128 devices in a mesh: seq: 8 (over x_lo, y), fsdp: 16 (over z, x_hi, core).
Axes of the slice: x: 4 (x_hi: 2, x_lo: 2; x = x_hi * 2 + x_lo), y: 4, z: 4, core: 2. Of those that a mesh axis runs over, the one named last changes fastest.
Arguments:
- tokens: bfloat16 [16, 2048, 1024], P('fsdp', 'seq'), may hold values from -6 to 6
- attn_gain: bfloat16 [1024], P(('seq', 'fsdp')), may hold values from 0.25 to 1.75
- qkv_weight: bfloat16 [1024, 2048], P(('seq', 'fsdp')), may hold values from -0.1875 to 0.1875
- qk_gain: bfloat16 [128], P(('seq', 'fsdp')), may hold values from 0.25 to 1.75
- out_weight: bfloat16 [1024, 1024], P(('seq', 'fsdp')), may hold values from -6 to 6
- ffn_gain: bfloat16 [1024], P(('seq', 'fsdp')), may hold values from 0.25 to 1.75
- router_weight: bfloat16 [1024, 32], P(('seq', 'fsdp')), may hold values from -0.09375 to 0.09375
- gate_up_weight: bfloat16 [32, 1024, 1024], P('fsdp'), may hold values from -0.1875 to 0.1875
- down_weight: bfloat16 [32, 1024, 512], P('fsdp'), may hold values from -1.5 to 1.5
- routes: int32 [16, 2048, 8], P('fsdp', 'seq'), may hold values from 0 to 31, all different within a row; in each aligned block of 256 rows (0 to 255, 256 to 511, ..., all dimensions but the last counted through in order) at most 88 rows name the same one
- cotangent: bfloat16 [16, 2048, 1024], P('fsdp', 'seq'), may hold values from -6 to 6
Outputs:
- layer_out: bfloat16 [16, 2048, 1024], P('fsdp', 'seq')
- token_grad: float32 [16, 2048, 1024], P('fsdp', 'seq')
- attn_gain_grad: float32 [1024], P(('seq', 'fsdp'))
- qkv_weight_grad: float32 [1024, 2048], P(('seq', 'fsdp'))
- qk_gain_grad: float32 [128], P(('seq', 'fsdp'))
- out_weight_grad: float32 [1024, 1024], P(('seq', 'fsdp'))
- ffn_gain_grad: float32 [1024], P(('seq', 'fsdp'))
- router_grad: float32 [1024, 32], P(('seq', 'fsdp'))
- gate_up_grad: float32 [32, 1024, 1024], P('fsdp', 'seq')
- down_grad: float32 [32, 1024, 512], P('fsdp', 'seq')
The draws below stay inside these ranges and needn't reach their ends.
Inputs may be any that keep to these rules, and one draw needn't show every extreme that they name: `routes`: each row names 8 different experts; among the rows of one device no expert is named by more than 88 rows, a bound that some block reaches.
All inputs are finite; a program needn't handle non-finite values.
Results may differ from the reference program's by a relative error of at most 0.035.
Values may be sent and summed in bfloat16 or wider, within the bound.
A program may use at most 192 MiB of HBM per device.

```python
import math
import jax
import jax.numpy as jnp
import numpy as np
from jax import lax

D = 1024
QUERY_HEADS = 16
KEY_VALUE_HEADS = 8
HEAD_SIZE = 64
F = 512
TOPK = 8
TOK_DEV = 256
EXPERTS = 32
SEQUENCE_TOKENS = 2048
SEQUENCE_COUNT = 16
QKW = 2048
CAP = 88


def levels(own_key, extent, cuts, low, high):
    def one(dim, shards_of):
        steps = jax.random.uniform(jax.random.fold_in(jax.random.fold_in(own_key, 6), dim), (shards_of,), jnp.float32, low / len(cuts), high / len(cuts))
        return jnp.repeat(jnp.exp(steps), extent[dim] // shards_of).reshape((-1,) + (1,) * (len(extent) - dim - 1))

    level = one(*cuts[0])
    for cut in cuts[1:]:
        level = level * one(*cut)
    return level


def shared_out(own_key, own, number, rows, number_of, top, reach, lean):
    sequence = jax.random.permutation(own_key, number_of)
    crowded, usual = portions_of(number_of, rows * top, reach, lean, True), portions_of(number_of, rows * top, reach, lean, False)
    places = jnp.arange(number_of)

    def named(tallies, turn):
        used = int((tallies > 0).sum())
        fixed = max(1, used // 4)
        moved = fixed + (places - fixed + turn * (used - fixed)) % max(1, number_of - fixed)
        return jnp.zeros((number_of,), jnp.int32).at[sequence[jnp.where(places < fixed, places, moved)]].set(jnp.asarray(tallies, jnp.int32))

    tallies = jnp.where(number % 4 == 0, named(crowded, number // 4), named(usual, number - number // 4 - 1))
    mixed = jax.random.permutation(jax.random.fold_in(own, 3), number_of)
    giver, taker = mixed[0:number_of // 2 * 2:2], mixed[1:number_of // 2 * 2:2]
    margin = jnp.minimum(tallies[giver] - 1, reach - tallies[taker]) // 2
    margin = jnp.where((giver == sequence[0]) | (taker == sequence[0]) | (tallies[taker] == 0), 0, jnp.maximum(margin, 0))
    moved = jax.random.randint(jax.random.fold_in(own, 4), (number_of // 2,), 0, 1 << 20) % (margin + 1)
    tallies = tallies.at[giver].add(-moved).at[taker].add(moved)
    members = jnp.searchsorted(jnp.cumsum(tallies), jnp.arange(rows * top), side="right").astype(jnp.int32)
    grid = members.reshape(top, rows).T
    grid = grid[jax.random.permutation(jax.random.fold_in(own, 1), rows)]
    turn = jax.random.randint(jax.random.fold_in(own, 2), (rows, 1), 0, top)
    return jnp.take_along_axis(grid, (jnp.arange(top)[None, :] + turn) % top, axis=1)


def portions_of(amount, total, limit, slope, full):
    loads = [(1 << 20) // math.isqrt(standing ** slope) + 1 for standing in range(1, amount + 1)]
    largest = limit if full else min(limit, max(-(-total // amount), total * loads[0] // sum(loads)))
    least = 1 if total - largest >= amount - 1 else 0
    holding, spare = [largest] + [least] * (amount - 1), total - largest - least * (amount - 1)
    while spare > 0:
        movable = [i for i in range(1, amount) if holding[i] < largest] or [i for i in range(1, amount) if holding[i] < limit]
        pool, left = sum([loads[i] for i in movable]), spare
        for i in movable:
            addition = min(limit - holding[i], max(1, left * loads[i] // pool), spare)
            holding[i] = holding[i] + addition
            spare = spare - addition
    return np.array(holding)


def noise(own_key, extent, spread, reach, shards=(), kind=jnp.bfloat16):
    factor_of = levels(own_key, extent, shards, -0.22, 0.18) if shards else 1.0
    values = jax.random.normal(own_key, extent, jnp.float32) * spread * factor_of
    return jnp.minimum(jnp.maximum(values, -reach), reach).astype(kind)


def setup_inputs(seed: int = 0) -> dict:
    arg_keys = jax.random.split(jax.random.key(seed), 12)
    tokens = noise(arg_keys[0], (SEQUENCE_COUNT, SEQUENCE_TOKENS, D), 1.0, 6.0, ((0, 16), (1, 8)))
    attn_gain = jnp.clip(1.0 + 0.15 * jax.random.normal(arg_keys[1], (D,), jnp.float32), 0.25, 1.75).astype(jnp.bfloat16)
    qkv_weight = noise(arg_keys[2], (D, QKW), D ** -0.5, 0.1875, ((0, 128),))
    qk_gain = jnp.clip(1.0 + 0.15 * jax.random.normal(arg_keys[3], (2 * HEAD_SIZE,), jnp.float32), 0.25, 1.75).astype(jnp.bfloat16)
    out_weight = noise(arg_keys[4], (QUERY_HEADS * HEAD_SIZE, D), (max(1, 3 * QUERY_HEADS * HEAD_SIZE // SEQUENCE_TOKENS)) ** -0.5, 6.0, ((0, 128),))
    ffn_gain = jnp.clip(1.0 + 0.15 * jax.random.normal(arg_keys[5], (D,), jnp.float32), 0.25, 1.75).astype(jnp.bfloat16)
    router_weight = noise(arg_keys[6], (D, EXPERTS), (4 * D) ** -0.5, 0.09375, ((0, 128),))
    gate_up_weight = noise(arg_keys[7], (EXPERTS, D, 2 * F), D ** -0.5, 0.1875, ((0, 16),))
    down_weight = noise(arg_keys[8], (EXPERTS, D, F), (max(1, F // 32)) ** -0.5, 1.5, ((0, 16),))
    routes_keys = jax.random.split(jax.random.fold_in(arg_keys[9], 1), SEQUENCE_COUNT * SEQUENCE_TOKENS // TOK_DEV)
    routes_turns = jax.random.permutation(jax.random.fold_in(arg_keys[9], 3), SEQUENCE_COUNT * SEQUENCE_TOKENS // TOK_DEV)
    routes = jax.vmap(lambda own, number: shared_out(jax.random.fold_in(arg_keys[9], 2), own, number, TOK_DEV, EXPERTS, TOPK, CAP, 0))(routes_keys, routes_turns).reshape((SEQUENCE_COUNT, SEQUENCE_TOKENS, TOPK))
    cotangent = noise(arg_keys[10], (SEQUENCE_COUNT, SEQUENCE_TOKENS, D), 1.0, 6.0, ((0, 16), (1, 8)))
    return {"tokens": tokens, "attn_gain": attn_gain, "qkv_weight": qkv_weight, "qk_gain": qk_gain, "out_weight": out_weight, "ffn_gain": ffn_gain, "router_weight": router_weight, "gate_up_weight": gate_up_weight, "down_weight": down_weight, "routes": routes, "cotangent": cotangent}


epsilon = 1e-06
rope_base = 10000.0
highest_precision = lax.Precision.HIGHEST

@jax.custom_vjp
def low(v):
    return lax.optimization_barrier(v.astype(jnp.bfloat16)).astype(jnp.float32)

@jax.custom_vjp
def reduced_backward(v):
    return v

def low_keep(v):
    return (low(v), None)

def low_pass(kept, grad):
    return (grad,)

def back_keep(v):
    return (v, None)

def back_low(kept, grad):
    return (low(grad),)
low.defvjp(low_keep, low_pass)
reduced_backward.defvjp(back_keep, back_low)

def rms_forward(values, weights):
    scaling = lax.rsqrt(lax.optimization_barrier(jnp.mean(values * values, axis=-1, keepdims=True)) + epsilon)
    return values * scaling * weights

def rotary_tables(positions, head_dim):
    half_dim = head_dim // 2
    freq_index = jnp.arange(half_dim, dtype=jnp.float32)
    inverse = jnp.exp(-(2.0 * freq_index / head_dim) * math.log(rope_base))
    angles = positions.astype(jnp.float32)[:, None] * inverse[None, :]
    return (jnp.cos(angles)[:, None, :], jnp.sin(angles)[:, None, :])

def rotate(values, cosine_values, sine_values):
    half_dim = values.shape[-1] // 2
    first_half = values[..., :half_dim]
    second_half = values[..., half_dim:]
    return jnp.concatenate([first_half * cosine_values - second_half * sine_values, second_half * cosine_values + first_half * sine_values], axis=-1)

def attend_sequence(pieces):
    query_sequence, key_seq, value_seq = pieces
    sequence_length = query_sequence.shape[0]
    group_count = QUERY_HEADS // KEY_VALUE_HEADS
    grouped_heads = query_sequence.reshape(sequence_length, KEY_VALUE_HEADS, group_count, HEAD_SIZE)
    scores = jnp.einsum('bkgd,lkd->kgbl', grouped_heads, key_seq, precision=highest_precision) * (1.0 / math.sqrt(HEAD_SIZE))
    scores = reduced_backward(scores)
    row_peak = lax.optimization_barrier(jnp.max(scores, axis=-1, keepdims=True))
    exp_scores = jnp.exp(scores - row_peak)
    attn_probs = low(exp_scores / lax.optimization_barrier(jnp.sum(exp_scores, axis=-1, keepdims=True)))
    attention_output = jnp.einsum('kgbl,lkd->bkgd', attn_probs, value_seq, precision=highest_precision)
    return attention_output.reshape(sequence_length, QUERY_HEADS * HEAD_SIZE)

def reference(tokens, attn_gain, qkv_weight, qk_gain, out_weight, ffn_gain, router_weight, gate_up_weight, down_weight, routes, cotangent):
    experts_all = router_weight.shape[1]
    cap_rows = TOK_DEV * TOPK * 11 // (8 * experts_all)
    token_total = SEQUENCE_COUNT * SEQUENCE_TOKENS
    pair_expert = routes.reshape(token_total // TOK_DEV, TOK_DEV * TOPK).astype(jnp.int32)
    block_count = pair_expert.shape[0]
    expert_ids = jnp.arange(experts_all, dtype=jnp.int32)
    onehot = (pair_expert[:, :, None] == expert_ids).astype(jnp.int32)
    running = jnp.cumsum(onehot, axis=1)
    slot_index = lax.optimization_barrier(jnp.sum(onehot * (running - 1), axis=2))
    block_ids = jnp.arange(block_count, dtype=jnp.int32)[:, None]
    position = ((pair_expert * block_count + block_ids) * cap_rows + slot_index).reshape(-1).astype(jnp.int32)
    pair_tokens = jnp.arange(token_total * TOPK, dtype=jnp.int32) // TOPK
    slot_table = jnp.full((experts_all * block_count * cap_rows,), token_total, dtype=jnp.int32).at[position].set(pair_tokens)
    slot_table = slot_table.reshape(experts_all, block_count * cap_rows)
    flat_routes = routes.reshape(token_total, TOPK).astype(jnp.int32)
    cosine_values, sine_values = rotary_tables(jnp.arange(SEQUENCE_TOKENS, dtype=jnp.int32), HEAD_SIZE)
    query_total_width = QUERY_HEADS * HEAD_SIZE
    key_total_width = KEY_VALUE_HEADS * HEAD_SIZE

    def forward(layer_inputs, attn_norm, query_key_value_projection, qk_norm, output_projection, ffn_norm, router_proj, gate_up, down_proj):
        normed_rows = low(rms_forward(layer_inputs, attn_norm))
        projected_rows = reduced_backward(jnp.einsum('xze,er->xzr', normed_rows, query_key_value_projection, precision=highest_precision))
        query_raw = projected_rows[..., :query_total_width].reshape(SEQUENCE_COUNT, SEQUENCE_TOKENS, QUERY_HEADS, HEAD_SIZE)
        unnormed_key = projected_rows[..., query_total_width:query_total_width + key_total_width].reshape(SEQUENCE_COUNT, SEQUENCE_TOKENS, KEY_VALUE_HEADS, HEAD_SIZE)
        unnormed_value = projected_rows[..., query_total_width + key_total_width:].reshape(SEQUENCE_COUNT, SEQUENCE_TOKENS, KEY_VALUE_HEADS, HEAD_SIZE)
        query_normed = rms_forward(query_raw, qk_norm[:HEAD_SIZE])
        key_normed = rms_forward(unnormed_key, qk_norm[HEAD_SIZE:])
        query_heads = reduced_backward(low(rotate(query_normed, cosine_values, sine_values)))
        key_heads = reduced_backward(low(rotate(key_normed, cosine_values, sine_values)))
        value_heads = reduced_backward(low(unnormed_value))
        attention_output = lax.map(jax.checkpoint(attend_sequence), (query_heads, key_heads, value_heads))
        attention_output = reduced_backward(low(attention_output))
        after_attention = layer_inputs + reduced_backward(jnp.einsum('kpn,nw->kpw', attention_output, output_projection, precision=highest_precision))
        normed_ffn = low(rms_forward(after_attention, ffn_norm)).reshape(token_total, D)
        logits = reduced_backward(jnp.dot(normed_ffn, router_proj, precision=highest_precision))
        chosen = jnp.take_along_axis(logits, flat_routes, axis=1)
        chosen_peak = lax.optimization_barrier(jnp.max(chosen, axis=1, keepdims=True))
        chosen_exp = jnp.exp(chosen - chosen_peak)
        gate_probs = chosen_exp / lax.optimization_barrier(jnp.sum(chosen_exp, axis=1, keepdims=True))
        padded_rows = jnp.concatenate([normed_ffn, jnp.zeros((1, D), normed_ffn.dtype)], axis=0)

        def run_expert(pieces):
            table_row, gate_up_one, down_one = pieces
            row_data = reduced_backward(padded_rows[table_row])
            gate_up_out = reduced_backward(jnp.dot(row_data, gate_up_one, precision=highest_precision))
            hidden = low(jax.nn.silu(gate_up_out[:, :F]) * gate_up_out[:, F:])
            return reduced_backward(low(jnp.einsum('rf,df->rd', hidden, down_one, precision=highest_precision)))
        expert_rows = lax.map(jax.checkpoint(run_expert), (slot_table, gate_up, down_proj))
        pair_out = expert_rows.reshape(-1, D)[position].reshape(token_total, TOPK, D)
        expert_sum = lax.optimization_barrier(jnp.sum(gate_probs[:, :, None] * pair_out, axis=1))
        return after_attention + expert_sum.reshape(SEQUENCE_COUNT, SEQUENCE_TOKENS, D)
    result, pullback = jax.vjp(forward, tokens.astype(jnp.float32), attn_gain.astype(jnp.float32), qkv_weight.astype(jnp.float32), qk_gain.astype(jnp.float32), out_weight.astype(jnp.float32), ffn_gain.astype(jnp.float32), router_weight.astype(jnp.float32), gate_up_weight.astype(jnp.float32), down_weight.astype(jnp.float32))
    gradients = pullback(cotangent.astype(jnp.float32))
    return (result.astype(jnp.bfloat16), gradients[0], gradients[1], gradients[2], gradients[3], gradients[4], gradients[5], gradients[6], gradients[7], gradients[8])
```

```python
import functools
import math

import jax
import jax.numpy as jnp
from jax import lax
from jax.experimental import pallas as pl
from jax.experimental.pallas import tpu as pltpu
from jax.sharding import PartitionSpec as P

D = 1024
QUERY_HEADS = 16
KEY_VALUE_HEADS = 8
HEAD_SIZE = 64
F = 512
TOPK = 8
EXPERTS = 32
CAP = 88
TOKENS = 256
SEQ = 8
FSDP = 16
LENGTH = SEQ * TOKENS
QKW = 2048
ROWS = FSDP * CAP
GROUP = 4
STEPS = FSDP // GROUP
STEP_ROWS = GROUP * CAP
VMEM = 60 * 1024 * 1024

epsilon = 1e-06
rope_base = 10000.0
f32 = jnp.float32
bf16 = jnp.bfloat16


def rms_forward(values, weights):
    scaling = lax.rsqrt(jnp.mean(values * values, axis=-1, keepdims=True) + epsilon)
    return (values * scaling * weights, scaling)


def rms_backward(values, scaling, weights, incoming):
    weighted = incoming * weights
    scaling_cube = scaling * scaling * scaling
    result = scaling * weighted - values * scaling_cube * jnp.mean(
        weighted * values, axis=-1, keepdims=True
    )
    return (result, incoming * values * scaling)


def rotary_tables(positions, head_dim):
    half_dim = head_dim // 2
    freq_index = jnp.arange(half_dim, dtype=f32)
    inverse = jnp.exp(-(2.0 * freq_index / head_dim) * math.log(rope_base))
    angles = positions.astype(f32)[:, None] * inverse[None, :]
    return (jnp.cos(angles)[:, None, :], jnp.sin(angles)[:, None, :])


def rotate(values, cosine_values, sine_values):
    half_dim = values.shape[-1] // 2
    first_half = values[..., :half_dim]
    second_half = values[..., half_dim:]
    return jnp.concatenate(
        [
            first_half * cosine_values - second_half * sine_values,
            second_half * cosine_values + first_half * sine_values,
        ],
        axis=-1,
    )


def dot(a, b):
    return lax.dot_general(a, b, (((1,), (0,)), ((), ())), preferred_element_type=f32)


def dot_t(a, b):
    return lax.dot_general(a, b, (((1,), (1,)), ((), ())), preferred_element_type=f32)


def t_dot(a, b):
    return lax.dot_general(a, b, (((0,), (0,)), ((), ())), preferred_element_type=f32)


def attend_kernel(heads_ref, out_ref, full_ref, logs_ref, key0, key1, value):
    step = pl.program_id(0)
    lanes = lax.broadcasted_iota(jnp.int32, (1, 128), 1)
    low_half = lanes < HEAD_SIZE

    @pl.when(step == 0)
    def _():
        pair = heads_ref[:, 128:256].astype(f32)
        key0[...] = jnp.where(low_half, pair, 0.0).astype(bf16)
        key1[...] = jnp.where(low_half, 0.0, pltpu.roll(pair, 64, 1)).astype(bf16)
        value[...] = jnp.where(low_half, jnp.where(lanes == 0, 1.0, 0.0), pair).astype(bf16)

    rows = pl.multiple_of(step * TOKENS, TOKENS)
    query = (heads_ref[pl.ds(rows, TOKENS), 0:128].astype(f32) * (1.0 / 8.0)).astype(bf16)
    results = []
    for key in (key0, key1):
        total = jnp.zeros((TOKENS, 128), f32)
        for c in range(4):
            part = pl.ds(c * 512, 512)
            weights = jnp.exp(dot_t(query, key[part, :]))
            total = total + dot(weights.astype(bf16), value[part, :])
        results.append(total)
    sum0, sum1 = results[0][:, 0:1], results[1][:, 0:1]
    full = jnp.where(low_half, pltpu.roll(results[0] / sum0, 64, 1), results[1] / sum1)
    full_ref[...] = full
    out_ref[...] = full.astype(bf16)
    logs_ref[...] = jnp.where(low_half, jnp.log(sum0), jnp.log(sum1))


def attend(heads):
    return pl.pallas_call(
        attend_kernel,
        grid=(LENGTH // TOKENS,),
        in_specs=[pl.BlockSpec((LENGTH, 256), lambda i: (0, 0))],
        out_specs=[pl.BlockSpec((TOKENS, 128), lambda i: (i, 0))] * 3,
        out_shape=[
            jax.ShapeDtypeStruct((LENGTH, 128), bf16),
            jax.ShapeDtypeStruct((LENGTH, 128), f32),
            jax.ShapeDtypeStruct((LENGTH, 128), f32),
        ],
        scratch_shapes=[pltpu.VMEM((LENGTH, 128), bf16)] * 3,
        compiler_params=pltpu.CompilerParams(vmem_limit_bytes=VMEM),
        cost_estimate=pl.CostEstimate(
            flops=4 * LENGTH * LENGTH * 128, bytes_accessed=4 << 20, transcendentals=2 * LENGTH * LENGTH
        ),
        name="attend",
    )(heads)


def split3(values):
    high = values.astype(bf16).astype(f32)
    rest = values - high
    middle = rest.astype(bf16).astype(f32)
    return high, middle, rest - middle


def with_terms(base, lanes, start, parts):
    high, middle, low = parts
    tail = jnp.where(
        lanes == start,
        high,
        jnp.where(lanes == start + 1, middle, jnp.where(lanes == start + 2, low, 0.0)),
    )
    return tail


def attend_back_kernel(
    heads_ref, full_ref, logs_ref, grad_ref, dq_ref, dkv_ref,
    key0, key1, value0, value1, key_t, dk_total, dv_total,
):
    step = pl.program_id(0)
    lanes = lax.broadcasted_iota(jnp.int32, (1, 128), 1)
    low_half = lanes < HEAD_SIZE

    @pl.when(step == 0)
    def _():
        pair = heads_ref[:, 128:256].astype(f32)
        swapped = pltpu.roll(pair, 64, 1)
        ones_high = jnp.where((lanes >= 64) & (lanes < 67), 1.0, 0.0)
        ones_low = jnp.where(lanes < 3, 1.0, 0.0)
        key0[...] = jnp.where(low_half, pair, ones_high).astype(bf16)
        key1[...] = jnp.where(low_half, ones_low, swapped).astype(bf16)
        value0[...] = jnp.where(low_half, swapped, ones_high).astype(bf16)
        value1[...] = jnp.where(low_half, ones_low, pair).astype(bf16)
        key_t[...] = jnp.transpose(pair)[0:64, :].astype(bf16)
        dk_total[...] = jnp.zeros_like(dk_total)
        dv_total[...] = jnp.zeros_like(dv_total)

    rows = pl.multiple_of(step * TOKENS, TOKENS)
    query = heads_ref[pl.ds(rows, TOKENS), 0:128].astype(f32) * (1.0 / 8.0)
    grad = grad_ref[...].astype(f32)
    logs = logs_ref[...]
    product = grad * full_ref[...]
    delta0 = jnp.sum(jnp.where(low_half, product, 0.0), axis=1, keepdims=True)
    delta1 = jnp.sum(jnp.where(low_half, 0.0, product), axis=1, keepdims=True)
    query0 = jnp.where(low_half, query, with_terms(query, lanes, 64, split3(-logs[:, 0:1]))).astype(bf16)
    query1 = jnp.where(low_half, with_terms(query, lanes, 0, split3(-logs[:, 64:65])), query).astype(bf16)
    grad0 = jnp.where(low_half, grad, with_terms(grad, lanes, 64, split3(-delta0))).astype(bf16)
    grad1 = jnp.where(low_half, with_terms(grad, lanes, 0, split3(-delta1)), grad).astype(bf16)
    only_query = (jnp.where(low_half, query, 0.0).astype(bf16), jnp.where(low_half, 0.0, query).astype(bf16))
    only_grad = (jnp.where(low_half, grad, 0.0).astype(bf16), jnp.where(low_half, 0.0, grad).astype(bf16))
    dq = [jnp.zeros((64, TOKENS), f32), jnp.zeros((64, TOKENS), f32)]
    for c in range(4):
        part = pl.ds(c * 512, 512)
        dv = dv_total[part, :]
        dk = dk_total[part, :]
        for h, (key, value, query_h, grad_h) in enumerate(
            ((key0, value0, query0, grad0), (key1, value1, query1, grad1))
        ):
            probs = jnp.exp(dot_t(key[part, :], query_h))
            inner = dot_t(value[part, :], grad_h)
            dv = dv + dot(probs.astype(bf16), only_grad[h])
            scores = (probs * inner).astype(bf16)
            dk = dk + dot(scores, only_query[h])
            dq[h] = dq[h] + dot(key_t[:, c * 512 : (c + 1) * 512], scores)
        dv_total[part, :] = dv
        dk_total[part, :] = dk
    both = jnp.concatenate(dq, axis=0) * (1.0 / 8.0)
    dq_ref[...] = jnp.transpose(both).astype(bf16)

    @pl.when(step == pl.num_programs(0) - 1)
    def _():
        dk = dk_total[...]
        dv = dv_total[...]
        dk = dk + pltpu.roll(dk, 64, 1)
        dv = dv + pltpu.roll(dv, 64, 1)
        dkv_ref[...] = jnp.where(low_half, dk, dv).astype(bf16)


def attend_back(heads, full, logs, grad):
    return pl.pallas_call(
        attend_back_kernel,
        grid=(LENGTH // TOKENS,),
        in_specs=[
            pl.BlockSpec((LENGTH, 256), lambda i: (0, 0)),
            pl.BlockSpec((TOKENS, 128), lambda i: (i, 0)),
            pl.BlockSpec((TOKENS, 128), lambda i: (i, 0)),
            pl.BlockSpec((TOKENS, 128), lambda i: (i, 0)),
        ],
        out_specs=[
            pl.BlockSpec((TOKENS, 128), lambda i: (i, 0)),
            pl.BlockSpec((LENGTH, 128), lambda i: (0, 0)),
        ],
        out_shape=[
            jax.ShapeDtypeStruct((LENGTH, 128), bf16),
            jax.ShapeDtypeStruct((LENGTH, 128), bf16),
        ],
        scratch_shapes=[pltpu.VMEM((LENGTH, 128), bf16)] * 4
        + [pltpu.VMEM((64, LENGTH), bf16)]
        + [pltpu.VMEM((LENGTH, 128), f32)] * 2,
        compiler_params=pltpu.CompilerParams(vmem_limit_bytes=VMEM),
        cost_estimate=pl.CostEstimate(
            flops=10 * LENGTH * LENGTH * 128, bytes_accessed=5 << 20, transcendentals=2 * LENGTH * LENGTH
        ),
        name="attend_back",
    )(heads, full, logs, grad)


def expert_kernel(
    x_ref, g_ref, gates_ref, up_ref, down_ref,
    y_ref, r_ref, gg_ref, dup_ref, ddown_ref,
    rows_x, rows_p, rows_h, rows_u, stage_x, stage_g, stage_gate, places,
):
    step = pl.program_id(0)

    @pl.when(step < STEPS)
    def _():
        gates = gates_ref[0]
        chosen = gates > 0.0
        before = (
            lax.broadcasted_iota(jnp.int32, (TOKENS, TOKENS), 0)
            < lax.broadcasted_iota(jnp.int32, (TOKENS, TOKENS), 1)
        ).astype(f32).astype(bf16)
        rank = dot(chosen.astype(f32).astype(bf16), before)
        rank = jnp.where(chosen, rank, -1000.0)
        slot = lax.broadcasted_iota(jnp.int32, (2 * CAP, TOKENS), 0)
        slot_place = slot.astype(f32)
        first = slot < CAP
        for s in range(GROUP):
            wanted = jnp.where(first, rank[2 * s : 2 * s + 1, :], rank[2 * s + 1 : 2 * s + 2, :] + CAP)
            wanted = jnp.where(
                (wanted < CAP) & jnp.logical_not(first), -1.0, wanted
            )
            hot = jnp.where(slot_place == wanted, 1.0, 0.0)
            gate = jnp.where(first, gates[2 * s : 2 * s + 1, :], gates[2 * s + 1 : 2 * s + 2, :])
            slot_gate = jnp.sum(hot * gate, axis=1, keepdims=True)
            hot = hot.astype(bf16)
            places[s] = hot
            picked = dot(hot, x_ref[TOKENS * s : TOKENS * (s + 1), :])
            for e in range(2):
                stage_x[e, CAP * s : CAP * (s + 1), :] = picked[CAP * e : CAP * (e + 1), :]
                stage_gate[e, CAP * s : CAP * (s + 1), :] = jnp.broadcast_to(
                    slot_gate[CAP * e : CAP * (e + 1), :], (CAP, 128)
                )
            picked = dot(hot, g_ref[TOKENS * s : TOKENS * (s + 1), :])
            for e in range(2):
                stage_g[e, CAP * s : CAP * (s + 1), :] = picked[CAP * e : CAP * (e + 1), :]
        here = pl.ds(pl.multiple_of(step * STEP_ROWS, 16), STEP_ROWS)
        for e in range(2):
            x_rows = stage_x[e].astype(bf16)
            rows_x[e, here, :] = x_rows
            gate = stage_gate[e][:, 0:1]
            grads = stage_g[e]
            pair = (grads * gate).astype(bf16)
            rows_p[e, here, :] = pair
            gate_part = dot(x_rows, up_ref[e, :, 0:F])
            up_part = dot(x_rows, up_ref[e, :, F : 2 * F])
            sigmoid = 1.0 / (1.0 + jnp.exp(-gate_part))
            silu = gate_part * sigmoid
            hidden = (silu * up_part).astype(bf16)
            rows_h[e, here, :] = hidden
            hidden_grad = dot(pair, down_ref[e])
            slope = sigmoid * (1.0 + gate_part * (1.0 - sigmoid))
            rows_u[e, here, 0:F] = (hidden_grad * up_part * slope).astype(bf16)
            rows_u[e, here, F : 2 * F] = (hidden_grad * silu).astype(bf16)
            out = dot_t(hidden, down_ref[e]).astype(bf16).astype(f32)
            gate_grad = jnp.sum(out * grads, axis=1, keepdims=True)
            for s in range(GROUP):
                hot = places[s, CAP * e : CAP * (e + 1), :].astype(f32)
                gg_ref[0, 2 * s + e : 2 * s + e + 1, :] = jnp.sum(
                    hot * gate_grad[CAP * s : CAP * (s + 1), :], axis=0, keepdims=True
                )
            stage_x[e] = out * gate
            stage_g[e] = dot_t(rows_u[e, here, :], up_ref[e])
        for s in range(GROUP):
            part = slice(CAP * s, CAP * (s + 1))
            both = jnp.concatenate([stage_x[0, part, :], stage_x[1, part, :]], axis=0).astype(bf16)
            y_ref[TOKENS * s : TOKENS * (s + 1), :] = t_dot(places[s], both).astype(bf16)
            both = jnp.concatenate([stage_g[0, part, :], stage_g[1, part, :]], axis=0).astype(bf16)
            r_ref[TOKENS * s : TOKENS * (s + 1), :] = t_dot(places[s], both).astype(bf16)

    @pl.when(step >= STEPS)
    def _():
        turn = step - STEPS
        e = turn // 4
        columns = pl.ds(pl.multiple_of((turn % 4) * 256, 256), 256)
        dup_ref[0] = t_dot(rows_x[e, :, columns], rows_u[e]).astype(bf16)
        ddown_ref[0] = t_dot(rows_p[e, :, columns], rows_h[e]).astype(bf16)


def experts(x_all, g_all, gates, up, down):
    last = STEPS - 1
    return pl.pallas_call(
        expert_kernel,
        grid=(STEPS + 8,),
        in_specs=[
            pl.BlockSpec((GROUP * TOKENS, D), lambda i: (jnp.minimum(i, last), 0)),
            pl.BlockSpec((GROUP * TOKENS, D), lambda i: (jnp.minimum(i, last), 0)),
            pl.BlockSpec((1, 2 * GROUP, TOKENS), lambda i: (jnp.minimum(i, last), 0, 0)),
            pl.BlockSpec((2, D, 2 * F), lambda i: (0, 0, 0), pipeline_mode=pl.Buffered(1)),
            pl.BlockSpec((2, D, F), lambda i: (0, 0, 0), pipeline_mode=pl.Buffered(1)),
        ],
        out_specs=[
            pl.BlockSpec((GROUP * TOKENS, D), lambda i: (jnp.minimum(i, last), 0)),
            pl.BlockSpec((GROUP * TOKENS, D), lambda i: (jnp.minimum(i, last), 0)),
            pl.BlockSpec((1, 2 * GROUP, TOKENS), lambda i: (jnp.minimum(i, last), 0, 0)),
            pl.BlockSpec((1, 256, 2 * F), lambda i: (jnp.maximum(i - STEPS, 0) // 4, jnp.maximum(i - STEPS, 0) % 4, 0)),
            pl.BlockSpec((1, 256, F), lambda i: (jnp.maximum(i - STEPS, 0) // 4, jnp.maximum(i - STEPS, 0) % 4, 0)),
        ],
        out_shape=[
            jax.ShapeDtypeStruct((FSDP * TOKENS, D), bf16),
            jax.ShapeDtypeStruct((FSDP * TOKENS, D), bf16),
            jax.ShapeDtypeStruct((STEPS, 2 * GROUP, TOKENS), f32),
            jax.ShapeDtypeStruct((2, D, 2 * F), bf16),
            jax.ShapeDtypeStruct((2, D, F), bf16),
        ],
        scratch_shapes=[
            pltpu.VMEM((2, ROWS, D), bf16),
            pltpu.VMEM((2, ROWS, D), bf16),
            pltpu.VMEM((2, ROWS, F), bf16),
            pltpu.VMEM((2, ROWS, 2 * F), bf16),
            pltpu.VMEM((2, STEP_ROWS, D), f32),
            pltpu.VMEM((2, STEP_ROWS, D), f32),
            pltpu.VMEM((2, STEP_ROWS, 128), f32),
            pltpu.VMEM((GROUP, 2 * CAP, TOKENS), bf16),
        ],
        compiler_params=pltpu.CompilerParams(vmem_limit_bytes=VMEM),
        cost_estimate=pl.CostEstimate(flops=30 * 10**9, bytes_accessed=40 << 20, transcendentals=1 << 21),
        name="experts",
    )(x_all, g_all, gates, up, down)


def on_device(
    tokens, attn_gain, qkv_weight, qk_gain, out_weight, ffn_gain, router_weight,
    gate_up_weight, down_weight, routes, cotangent,
):
    layer_inputs = tokens.reshape(TOKENS, D).astype(f32)
    query_total_width = QUERY_HEADS * HEAD_SIZE
    key_total_width = KEY_VALUE_HEADS * HEAD_SIZE
    seq_place = lax.axis_index("seq")

    small = jnp.concatenate(
        [router_weight.reshape(256), attn_gain, ffn_gain, qk_gain, jnp.zeros((2048 - 273,), bf16)]
    ).reshape(16, 128)
    packed = jnp.concatenate([qkv_weight.reshape(16, 1024), out_weight.reshape(16, 512), small], axis=1)
    packed = lax.all_gather(packed, "fsdp", axis=0, tiled=True)
    packed = lax.all_gather(packed, "seq", axis=0, tiled=True).reshape(128, 16, 1664)
    full_qkv = packed[:, :, :1024].reshape(D, QKW)
    full_out = packed[:, :, 1024:1536].reshape(D, D)
    small = packed[:, :, 1536:].reshape(128, 2048)
    full_router = small[:, :256].reshape(D, EXPERTS)
    attn_norm = small[:, 256:264].reshape(D).astype(f32)
    ffn_norm = small[:, 264:272].reshape(D).astype(f32)
    qk_norm = small[:, 272].astype(f32)

    cot = cotangent.reshape(TOKENS, D)
    g_all = lax.all_gather(cot, "fsdp", axis=0, tiled=True)

    normed_attn, attn_scaling = rms_forward(layer_inputs, attn_norm)
    normed_attn = normed_attn.astype(bf16)
    projected_rows = jnp.dot(normed_attn, full_qkv, preferred_element_type=f32)
    query_raw = projected_rows[:, :query_total_width].reshape(TOKENS, QUERY_HEADS, HEAD_SIZE)
    key_raw = projected_rows[:, query_total_width : query_total_width + key_total_width].reshape(
        TOKENS, KEY_VALUE_HEADS, HEAD_SIZE
    )
    value_low = projected_rows[:, query_total_width + key_total_width :].astype(bf16)
    query_normed, query_scaling = rms_forward(query_raw, qk_norm[:HEAD_SIZE])
    key_normed, key_scaling = rms_forward(key_raw, qk_norm[HEAD_SIZE:])
    positions = seq_place * TOKENS + jnp.arange(TOKENS, dtype=jnp.int32)
    cosine_values, sine_values = rotary_tables(positions, HEAD_SIZE)
    query_low = rotate(query_normed, cosine_values, sine_values).astype(bf16)
    key_low = rotate(key_normed, cosine_values, sine_values).astype(bf16)
    send = jnp.concatenate(
        [
            query_low.reshape(TOKENS, 8, 128),
            key_low.reshape(TOKENS, 8, 64),
            value_low.reshape(TOKENS, 8, 64),
        ],
        axis=2,
    ).transpose(1, 0, 2)
    heads = lax.all_to_all(send, "seq", split_axis=0, concat_axis=0, tiled=True).reshape(LENGTH, 256)
    attended_low, attended_full, logs = attend(heads)
    attended_tokens = (
        lax.all_to_all(attended_low.reshape(8, TOKENS, 128), "seq", split_axis=0, concat_axis=0, tiled=True)
        .transpose(1, 0, 2)
        .reshape(TOKENS, D)
    )
    after_attention = layer_inputs + jnp.dot(attended_tokens, full_out, preferred_element_type=f32)
    normed_ffn, ffn_scaling = rms_forward(after_attention, ffn_norm)
    normed_ffn = normed_ffn.astype(bf16)
    logits = lax.dot_general(full_router, normed_ffn, (((0,), (1,)), ((), ())), preferred_element_type=f32)
    route_ids = routes.reshape(TOKENS, TOPK)
    expert_ids = jnp.arange(EXPERTS, dtype=jnp.int32)
    named = jnp.any(route_ids[None, :, :] == expert_ids[:, None, None], axis=2)
    peak = jnp.max(jnp.where(named, logits, -jnp.inf), axis=0, keepdims=True)
    chosen_exp = jnp.where(named, jnp.exp(logits - peak), 0.0)
    gates = chosen_exp / jnp.sum(chosen_exp, axis=0, keepdims=True)

    x_all = lax.all_gather(normed_ffn, "fsdp", axis=0, tiled=True)
    my_gates = lax.all_to_all(gates.reshape(FSDP, 2, TOKENS), "fsdp", split_axis=0, concat_axis=0, tiled=True)
    y_all, r_all, gate_grads, dup, ddown = experts(
        x_all, g_all, my_gates.reshape(STEPS, 2 * GROUP, TOKENS), gate_up_weight, down_weight
    )
    gate_grad = lax.all_to_all(
        gate_grads.reshape(FSDP, 2, TOKENS), "fsdp", split_axis=0, concat_axis=0, tiled=True
    ).reshape(EXPERTS, TOKENS)
    row_sum = lax.psum_scatter(r_all, "fsdp", scatter_dimension=0, tiled=True)
    expert_sum = lax.psum_scatter(y_all, "fsdp", scatter_dimension=0, tiled=True)
    layer_out = (after_attention + expert_sum.astype(f32)).astype(bf16).reshape(1, TOKENS, D)

    incoming = cot.astype(f32)
    chosen_grad = gates * (gate_grad - jnp.sum(gates * gate_grad, axis=0, keepdims=True))
    logits_grad = chosen_grad.astype(bf16)
    router_grad = lax.dot_general(normed_ffn, logits_grad, (((0,), (1,)), ((), ())), preferred_element_type=f32)
    normed_ffn_grad = row_sum.astype(f32) + lax.dot_general(
        logits_grad, full_router, (((0,), (1,)), ((), ())), preferred_element_type=f32
    )
    after_extra, ffn_terms = rms_backward(after_attention, ffn_scaling, ffn_norm, normed_ffn_grad)
    after_grad = incoming + after_extra
    ffn_gain_grad = jnp.sum(ffn_terms, axis=0)
    after_low = after_grad.astype(bf16)
    out_weight_grad = t_dot(attended_tokens, after_low)
    attended_grad = dot_t(after_low, full_out).astype(bf16)
    grad_heads = lax.all_to_all(
        attended_grad.reshape(TOKENS, 8, 128).transpose(1, 0, 2), "seq", split_axis=0, concat_axis=0, tiled=True
    ).reshape(LENGTH, 128)
    dq, dkv = attend_back(heads, attended_full, logs, grad_heads)
    back = jnp.concatenate([dq, dkv], axis=1).reshape(8, TOKENS, 256)
    back = lax.all_to_all(back, "seq", split_axis=0, concat_axis=0, tiled=True)
    token_query_grad = back[:, :, :128].transpose(1, 0, 2).reshape(TOKENS, QUERY_HEADS, HEAD_SIZE)
    token_key_grad = back[:, :, 128:192].transpose(1, 0, 2)
    token_value_grad = back[:, :, 192:].transpose(1, 0, 2).reshape(TOKENS, key_total_width)
    query_normed_grad = rotate(token_query_grad.astype(f32), cosine_values, -sine_values)
    key_normed_grad = rotate(token_key_grad.astype(f32), cosine_values, -sine_values)
    query_raw_grad, query_terms = rms_backward(query_raw, query_scaling, qk_norm[:HEAD_SIZE], query_normed_grad)
    key_raw_grad, key_terms = rms_backward(key_raw, key_scaling, qk_norm[HEAD_SIZE:], key_normed_grad)
    qk_gain_grad = jnp.concatenate(
        [jnp.sum(query_terms, axis=(0, 1)), jnp.sum(key_terms, axis=(0, 1))], axis=0
    )
    projected_grad = jnp.concatenate(
        [
            query_raw_grad.reshape(TOKENS, query_total_width).astype(bf16),
            key_raw_grad.reshape(TOKENS, key_total_width).astype(bf16),
            token_value_grad,
        ],
        axis=1,
    )
    qkv_weight_grad = t_dot(normed_attn, projected_grad)
    normed_attn_grad = dot_t(projected_grad, full_qkv)
    input_extra, attn_terms = rms_backward(layer_inputs, attn_scaling, attn_norm, normed_attn_grad)
    token_grad = (after_grad + input_extra).reshape(1, TOKENS, D)
    attn_gain_grad = jnp.sum(attn_terms, axis=0)

    axes = ("seq", "fsdp")
    early = lax.all_to_all(
        out_weight_grad.astype(bf16).reshape(128, 16, 512), axes, split_axis=0, concat_axis=0, tiled=True
    )
    out_part = jnp.sum(early.astype(f32), axis=0).reshape(8, 1024)
    late = lax.all_to_all(
        qkv_weight_grad.astype(bf16).reshape(128, 16, 1024), axes, split_axis=0, concat_axis=0, tiled=True
    )
    qkv_part = jnp.sum(late.astype(f32), axis=0).reshape(8, 2048)
    small = jnp.concatenate(
        [
            router_grad.reshape(128, 256),
            attn_gain_grad.reshape(128, 8),
            ffn_gain_grad.reshape(128, 8),
            qk_gain_grad.reshape(128, 1),
            jnp.zeros((128, 111), f32),
        ],
        axis=1,
    )
    small = jnp.sum(lax.all_to_all(small, axes, split_axis=0, concat_axis=0, tiled=True), axis=0)
    router_part = small[:256].reshape(8, 32)
    attn_part = small[256:264]
    ffn_part = small[264:272]
    qk_part = small[272:273]
    gate_up_part = lax.psum_scatter(dup, "seq", scatter_dimension=1, tiled=True).astype(f32)
    down_part = lax.psum_scatter(ddown, "seq", scatter_dimension=1, tiled=True).astype(f32)
    return (
        layer_out, token_grad, attn_part, qkv_part, qk_part, out_part, ffn_part, router_part,
        gate_up_part, down_part,
    )


def solution(mesh):
    return jax.shard_map(
        on_device,
        mesh=mesh,
        in_specs=(
            P("fsdp", "seq", None),
            P(("seq", "fsdp")),
            P(("seq", "fsdp"), None),
            P(("seq", "fsdp")),
            P(("seq", "fsdp"), None),
            P(("seq", "fsdp")),
            P(("seq", "fsdp"), None),
            P("fsdp", None, None),
            P("fsdp", None, None),
            P("fsdp", "seq", None),
            P("fsdp", "seq", None),
        ),
        out_specs=(
            P("fsdp", "seq", None),
            P("fsdp", "seq", None),
            P(("seq", "fsdp")),
            P(("seq", "fsdp"), None),
            P(("seq", "fsdp")),
            P(("seq", "fsdp"), None),
            P(("seq", "fsdp")),
            P(("seq", "fsdp"), None),
            P("fsdp", "seq", None),
            P("fsdp", "seq", None),
        ),
        check_vma=False,
    )
```

```python
import functools
import math

import jax
import jax.numpy as jnp
from jax import lax
from jax.experimental import pallas as pl
from jax.experimental.pallas import tpu as pltpu
from jax.sharding import PartitionSpec as P

D = 1024
QUERY_HEADS = 16
KEY_VALUE_HEADS = 8
HEAD_SIZE = 64
F = 512
TOPK = 8
EXPERTS = 32
TOKENS = 256
SEQ = 8
FSDP = 16
LENGTH = SEQ * TOKENS
QKW = 2048
VMEM = 60 * 1024 * 1024

epsilon = 1e-06
rope_base = 10000.0
f32 = jnp.float32
bf16 = jnp.bfloat16


def rms_forward(values, weights):
    scaling = lax.rsqrt(jnp.mean(values * values, axis=-1, keepdims=True) + epsilon)
    return (values * scaling * weights, scaling)


def rms_backward(values, scaling, weights, incoming):
    weighted = incoming * weights
    scaling_cube = scaling * scaling * scaling
    result = scaling * weighted - values * scaling_cube * jnp.mean(
        weighted * values, axis=-1, keepdims=True
    )
    return (result, incoming * values * scaling)


def rotary_tables(positions, head_dim):
    half_dim = head_dim // 2
    freq_index = jnp.arange(half_dim, dtype=f32)
    inverse = jnp.exp(-(2.0 * freq_index / head_dim) * math.log(rope_base))
    angles = positions.astype(f32)[:, None] * inverse[None, :]
    return (jnp.cos(angles)[:, None, :], jnp.sin(angles)[:, None, :])


def rotate(values, cosine_values, sine_values):
    half_dim = values.shape[-1] // 2
    first_half = values[..., :half_dim]
    second_half = values[..., half_dim:]
    return jnp.concatenate(
        [
            first_half * cosine_values - second_half * sine_values,
            second_half * cosine_values + first_half * sine_values,
        ],
        axis=-1,
    )


def dot(a, b):
    return lax.dot_general(a, b, (((1,), (0,)), ((), ())), preferred_element_type=f32)


def dot_t(a, b):
    return lax.dot_general(a, b, (((1,), (1,)), ((), ())), preferred_element_type=f32)


def t_dot(a, b):
    return lax.dot_general(a, b, (((0,), (0,)), ((), ())), preferred_element_type=f32)


def attend_kernel(heads_ref, out_ref, full_ref, logs_ref, key0, key1, value):
    step = pl.program_id(0)
    lanes = lax.broadcasted_iota(jnp.int32, (1, 128), 1)
    low_half = lanes < HEAD_SIZE

    @pl.when(step == 0)
    def _():
        pair = heads_ref[:, 128:256].astype(f32)
        key0[...] = jnp.where(low_half, pair, 0.0).astype(bf16)
        key1[...] = jnp.where(low_half, 0.0, pltpu.roll(pair, 64, 1)).astype(bf16)
        value[...] = jnp.where(low_half, jnp.where(lanes == 0, 1.0, 0.0), pair).astype(bf16)

    rows = pl.multiple_of(step * TOKENS, TOKENS)
    query = (heads_ref[pl.ds(rows, TOKENS), 0:128].astype(f32) * (1.0 / 8.0)).astype(bf16)
    results = []
    for key in (key0, key1):
        total = jnp.zeros((TOKENS, 128), f32)
        for c in range(4):
            part = pl.ds(c * 512, 512)
            weights = jnp.exp(dot_t(query, key[part, :]))
            total = total + dot(weights.astype(bf16), value[part, :])
        results.append(total)
    sum0, sum1 = results[0][:, 0:1], results[1][:, 0:1]
    full = jnp.where(low_half, pltpu.roll(results[0] / sum0, 64, 1), results[1] / sum1)
    full_ref[...] = full
    out_ref[...] = full.astype(bf16)
    logs_ref[...] = jnp.where(low_half, jnp.log(sum0), jnp.log(sum1))


def attend(heads):
    return pl.pallas_call(
        attend_kernel,
        grid=(LENGTH // TOKENS,),
        in_specs=[pl.BlockSpec((LENGTH, 256), lambda i: (0, 0))],
        out_specs=[pl.BlockSpec((TOKENS, 128), lambda i: (i, 0))] * 3,
        out_shape=[
            jax.ShapeDtypeStruct((LENGTH, 128), bf16),
            jax.ShapeDtypeStruct((LENGTH, 128), f32),
            jax.ShapeDtypeStruct((LENGTH, 128), f32),
        ],
        scratch_shapes=[pltpu.VMEM((LENGTH, 128), bf16)] * 3,
        compiler_params=pltpu.CompilerParams(vmem_limit_bytes=VMEM),
        cost_estimate=pl.CostEstimate(
            flops=4 * LENGTH * LENGTH * 128, bytes_accessed=4 << 20, transcendentals=2 * LENGTH * LENGTH
        ),
        name="attend",
    )(heads)


def split3(values):
    high = values.astype(bf16).astype(f32)
    rest = values - high
    middle = rest.astype(bf16).astype(f32)
    return high, middle, rest - middle


def with_terms(lanes, start, parts):
    high, middle, low = parts
    tail = jnp.where(
        lanes == start,
        high,
        jnp.where(lanes == start + 1, middle, jnp.where(lanes == start + 2, low, 0.0)),
    )
    return tail


MESH = pl.DeviceIdType.MESH


class Place:
    def __init__(self):
        self.seq = lax.axis_index("seq")
        self.fsdp = lax.axis_index("fsdp")
        self.core = lax.rem(self.fsdp, 2)
        self.xh = lax.rem(self.fsdp // 2, 2)
        self.z = self.fsdp // 4
        self.y = lax.rem(self.seq, 4)
        self.xl = self.seq // 4

    def sibling(self):
        return {"fsdp": self.fsdp + 1 - 2 * self.core}

    def fsdp_at(self, ring, pair):
        z = lax.rem(self.z + ring + 4, 4)
        xh = 1 - self.xh if pair else self.xh
        return z * 4 + xh * 2 + self.core

    def seq_at(self, ring, pair):
        y = lax.rem(self.y + ring + 4, 4)
        xl = 1 - self.xl if pair else self.xl
        return xl * 4 + y

    def plane(self, axis):
        at = self.fsdp_at if axis == "fsdp" else self.seq_at
        return {
            "up": {axis: at(1, 0)},
            "down": {axis: at(-1, 0)},
            "across": {axis: at(0, 1)},
        }


def meet(targets):
    barrier = pltpu.get_barrier_semaphore()
    for target in targets:
        pl.semaphore_signal(barrier, inc=1, device_id=target, device_id_type=MESH)
    pl.semaphore_wait(barrier, len(targets))


class Copies:
    def __init__(self, send_sems, recv_sems):
        self.send_sems, self.recv_sems, self.count, self.all = send_sems, recv_sems, 0, []

    def start(self, src, dst, target):
        k = self.count
        self.count += 1
        copy = pltpu.make_async_remote_copy(
            src_ref=src, dst_ref=dst, send_sem=self.send_sems.at[k], recv_sem=self.recv_sems.at[k],
            device_id=target, device_id_type=MESH,
        )
        copy.start()
        self.all.append(copy)
        return copy

    def finish(self):
        for copy in self.all:
            copy.wait_send()


WCOLS = 1664

def attend_back_kernel(
    heads_ref, full_ref, logs_ref, grad_ref, y_ref, dq_ref, dkv_ref, sum_ref,
    key0, key1, value0, value1, key_t, dk_total, dv_total,
    slots, sib_in, hop_in, local_sems, send_sems, recv_sems,
):
    here = Place()
    sib = here.sibling()
    way = here.plane("fsdp")
    loads = [
        pltpu.make_async_copy(y_ref.at[2 * k], slots.at[k], local_sems.at[k]) for k in (6, 7, 5, 3, 4, 2, 1, 0)
    ]
    for copy in loads:
        copy.start()
    meet([sib, *way.values()])
    net = Copies(send_sems, recv_sems)
    joins = {k: net.start(y_ref.at[2 * k + 1], sib_in.at[k], sib) for k in (7, 6, 5, 3, 4, 2, 1, 0)}
    lanes = lax.broadcasted_iota(jnp.int32, (1, 128), 1)
    low_half = lanes < HEAD_SIZE
    pair = heads_ref[:, 128:256].astype(f32)
    swapped = pltpu.roll(pair, 64, 1)
    ones_high = jnp.where((lanes >= 64) & (lanes < 67), 1.0, 0.0)
    ones_low = jnp.where(lanes < 3, 1.0, 0.0)
    key0[...] = jnp.where(low_half, pair, ones_high).astype(bf16)
    key1[...] = jnp.where(low_half, ones_low, swapped).astype(bf16)
    value0[...] = jnp.where(low_half, swapped, ones_high).astype(bf16)
    value1[...] = jnp.where(low_half, ones_low, pair).astype(bf16)
    key_t[...] = jnp.transpose(pair)[0:64, :].astype(bf16)
    dk_total[...] = jnp.zeros_like(dk_total)
    dv_total[...] = jnp.zeros_like(dv_total)

    def one(step, carry):
        rows = pl.ds(pl.multiple_of(step * TOKENS, TOKENS), TOKENS)
        query = heads_ref[rows, 0:128].astype(f32) * (1.0 / 8.0)
        grad = grad_ref[rows, :].astype(f32)
        logs = logs_ref[rows, :]
        product = grad * full_ref[rows, :]
        delta0 = jnp.sum(jnp.where(low_half, product, 0.0), axis=1, keepdims=True)
        delta1 = jnp.sum(jnp.where(low_half, 0.0, product), axis=1, keepdims=True)
        query0 = jnp.where(low_half, query, with_terms(lanes, 64, split3(-logs[:, 0:1]))).astype(bf16)
        query1 = jnp.where(low_half, with_terms(lanes, 0, split3(-logs[:, 64:65])), query).astype(bf16)
        grad0 = jnp.where(low_half, grad, with_terms(lanes, 64, split3(-delta0))).astype(bf16)
        grad1 = jnp.where(low_half, with_terms(lanes, 0, split3(-delta1)), grad).astype(bf16)
        only_query = (
            jnp.where(low_half, query, 0.0).astype(bf16), jnp.where(low_half, 0.0, query).astype(bf16)
        )
        only_grad = (jnp.where(low_half, grad, 0.0).astype(bf16), jnp.where(low_half, 0.0, grad).astype(bf16))
        dq = [jnp.zeros((64, TOKENS), f32), jnp.zeros((64, TOKENS), f32)]
        for c in range(4):
            part = pl.ds(c * 512, 512)
            dv = dv_total[part, :]
            dk = dk_total[part, :]
            for h, (key, value, query_h, grad_h) in enumerate(
                ((key0, value0, query0, grad0), (key1, value1, query1, grad1))
            ):
                probs = jnp.exp(dot_t(key[part, :], query_h))
                inner = dot_t(value[part, :], grad_h)
                dv = dv + dot(probs.astype(bf16), only_grad[h])
                scores = (probs * inner).astype(bf16)
                dk = dk + dot(scores, only_query[h])
                dq[h] = dq[h] + dot(key_t[:, c * 512 : (c + 1) * 512], scores)
            dv_total[part, :] = dv
            dk_total[part, :] = dk
        both = jnp.concatenate(dq, axis=0) * (1.0 / 8.0)
        dq_ref[rows, :] = jnp.transpose(both).astype(bf16)
        return carry

    def run(first, last):
        lax.fori_loop(first, last, one, 0)

    def add_to(ref, *values):
        result = ref[...].astype(f32)
        for value in values:
            result = result + value[...].astype(f32)
        ref[...] = result.astype(bf16)

    def join(k):
        joins[k].wait_recv()
        add_to(slots.at[k], sib_in.at[k])

    def half(ref, which):
        return ref.at[pl.ds(128 * which, 128)]

    run(0, 1)
    for copy in loads:
        copy.wait()
    join(7)
    a = net.start(slots.at[7], hop_in.at[0], way["across"])
    join(3)
    xd = net.start(slots.at[3], hop_in.at[2], way["down"])
    join(5)
    xu = net.start(slots.at[5], hop_in.at[3], way["up"])
    join(6)
    run(1, 4)
    a.wait_recv()
    add_to(slots.at[6], hop_in.at[0])
    u = net.start(half(slots.at[6], 0), half(hop_in.at[1], 0), way["up"])
    d = net.start(half(slots.at[6], 1), half(hop_in.at[1], 1), way["down"])
    join(1)
    xd.wait_recv()
    xu.wait_recv()
    add_to(slots.at[1], hop_in.at[2], hop_in.at[3])
    rx = net.start(slots.at[1], hop_in.at[6], way["across"])
    join(2)
    join(4)
    join(0)
    run(4, 6)
    u.wait_recv()
    add_to(half(slots.at[4], 0), half(hop_in.at[1], 0))
    ru = net.start(slots.at[4], hop_in.at[4], way["up"])
    d.wait_recv()
    add_to(half(slots.at[2], 1), half(hop_in.at[1], 1))
    rd = net.start(slots.at[2], hop_in.at[5], way["down"])
    run(6, 8)
    dk = dk_total[...]
    dv = dv_total[...]
    dk = dk + pltpu.roll(dk, 64, 1)
    dv = dv + pltpu.roll(dv, 64, 1)
    dkv_ref[...] = jnp.where(low_half, dk, dv).astype(bf16)
    rx.wait_recv()
    ru.wait_recv()
    rd.wait_recv()
    sum_ref[...] = (
        slots[0].astype(f32) + hop_in[4].astype(f32) + hop_in[5].astype(f32) + hop_in[6].astype(f32)
    )
    net.finish()


def attend_back(heads, full, logs, grad, y_all):
    vmem = pl.BlockSpec(memory_space=pltpu.VMEM)
    return pl.pallas_call(
        attend_back_kernel,
        in_specs=[vmem] * 4 + [pl.BlockSpec(memory_space=pl.ANY)],
        out_specs=[vmem] * 3,
        out_shape=[
            jax.ShapeDtypeStruct((LENGTH, 128), bf16),
            jax.ShapeDtypeStruct((LENGTH, 128), bf16),
            jax.ShapeDtypeStruct((TOKENS, D), f32),
        ],
        scratch_shapes=[pltpu.VMEM((LENGTH, 128), bf16)] * 4
        + [pltpu.VMEM((64, LENGTH), bf16)]
        + [pltpu.VMEM((LENGTH, 128), f32)] * 2
        + [pltpu.VMEM((8, TOKENS, D), bf16)] * 2
        + [pltpu.VMEM((7, TOKENS, D), bf16)]
        + [
            pltpu.SemaphoreType.DMA((8,)),
            pltpu.SemaphoreType.DMA((18,)),
            pltpu.SemaphoreType.DMA((18,)),
        ],
        compiler_params=pltpu.CompilerParams(collective_id=9, has_side_effects=True, vmem_limit_bytes=VMEM),
        cost_estimate=pl.CostEstimate(
            flops=10 * LENGTH * LENGTH * 128, bytes_accessed=16 << 20, transcendentals=2 * LENGTH * LENGTH
        ),
        name="attend_back",
    )(heads, full, logs, grad, y_all)


def gather_kernel(in_ref, mask_ref, out_ref, masks_out, stage, block, local_sems, send_sems, recv_sems):
    here = Place()
    c, s, f = here.core, here.seq, here.z * 2 + here.xh
    sib = here.sibling()
    ways = {"seq": here.plane("seq"), "fsdp": here.plane("fsdp")}
    others = [(2, 1), (2, 0), (0, 1), (1, 1), (-1, 1), (1, 0), (-1, 0)]

    def f_at(ring, pair):
        return lax.rem(here.z + ring + 4, 4) * 2 + (1 - here.xh if pair else here.xh)

    seq_peers = [{"seq": here.seq_at(ring, pair)} for ring, pair in others]
    fsdp_peers = [{"fsdp": here.fsdp_at(ring, pair)} for ring, pair in others]
    meet([sib, *seq_peers, *fsdp_peers])
    net = Copies(send_sems, recv_sems)
    rows = pl.ds(pl.multiple_of(8 * c, 8), 8)
    join = net.start(in_ref.at[1 - c], stage.at[rows], sib)
    stage[rows, :] = in_ref[c]
    join.wait_recv()
    block[...] = stage[...].astype(bf16)
    low, high = pl.ds(0, 896), pl.ds(896, 768)
    locals_ = [
        pltpu.make_async_copy(block, out_ref.at[c, s, f], local_sems.at[0]),
        pltpu.make_async_copy(mask_ref, masks_out.at[here.fsdp], local_sems.at[1]),
    ]
    for copy in locals_:
        copy.start()
    a = [net.start(block.at[:, low], out_ref.at[c, s, f, :, low], peer) for peer in fsdp_peers]
    b = [net.start(block.at[:, high], out_ref.at[c, s, f, :, high], peer) for peer in seq_peers]
    m = [net.start(mask_ref, masks_out.at[here.fsdp], peer) for peer in [sib, *fsdp_peers]]
    for copy in locals_:
        copy.wait()
    kin = []

    def plane(part, way):
        def half(ref, which):
            return ref.at[pl.ds(4 * which, 4)]

        def go(ref, target):
            return net.start(ref, ref, target)

        ref = part(0, 0)
        across, up, down = go(ref, way["across"]), go(ref, way["up"]), go(ref, way["down"])
        kin.append(go(ref, sib))
        yield
        up.wait_recv()
        ref = part(-1, 0)
        far_low = go(half(ref, 0), way["up"])
        kin.append(go(ref, sib))
        down.wait_recv()
        ref = part(1, 0)
        far_high = go(half(ref, 1), way["down"])
        kin.append(go(ref, sib))
        yield
        across.wait_recv()
        ref = part(0, 1)
        up, down = go(ref, way["up"]), go(ref, way["down"])
        kin.append(go(ref, sib))
        yield
        far_low.wait_recv()
        far_high.wait_recv()
        kin.append(go(part(2, 0), sib))
        up.wait_recv()
        ref = part(-1, 1)
        far_low = go(half(ref, 0), way["up"])
        kin.append(go(ref, sib))
        down.wait_recv()
        ref = part(1, 1)
        far_high = go(half(ref, 1), way["down"])
        kin.append(go(ref, sib))
        yield
        far_low.wait_recv()
        far_high.wait_recv()
        kin.append(go(part(2, 1), sib))

    for copy in a:
        copy.wait_recv()
    first = plane(lambda ring, pair: out_ref.at[c, here.seq_at(ring, pair), :, :, low], ways["seq"])
    next(first)
    for copy in b:
        copy.wait_recv()
    second = plane(lambda ring, pair: out_ref.at[c, :, f_at(ring, pair), :, high], ways["fsdp"])
    next(second)
    for i in range(8):
        m[i].wait_recv()
        if i:
            ring, pair = others[i - 1]
            ref = masks_out.at[here.fsdp_at(-ring, pair)]
            kin.append(net.start(ref, ref, sib))
    for _ in range(4):
        next(first, None)
        next(second, None)
    for copy in kin:
        copy.wait_recv()
    net.finish()


def gather_weights(halves, mask):
    n = 64
    return pl.pallas_call(
        gather_kernel,
        in_specs=[pl.BlockSpec(memory_space=pltpu.VMEM)] * 2,
        out_specs=[pl.BlockSpec(memory_space=pl.ANY)] * 2,
        out_shape=[
            jax.ShapeDtypeStruct((2, 8, 8, 16, WCOLS), bf16),
            jax.ShapeDtypeStruct((16, 32, 256), bf16),
        ],
        scratch_shapes=[
            pltpu.VMEM((16, WCOLS), f32),
            pltpu.VMEM((16, WCOLS), bf16),
            pltpu.SemaphoreType.DMA((2,)),
            pltpu.SemaphoreType.DMA((n,)),
            pltpu.SemaphoreType.DMA((n,)),
        ],
        compiler_params=pltpu.CompilerParams(collective_id=1, has_side_effects=True, vmem_limit_bytes=VMEM),
        name="gather_weights",
    )(halves, mask)


def swap_kernel(in_ref, out_ref, local_sem, send_sems, recv_sems):
    here = Place()
    others = [(ring, pair) for ring in (0, -1, 1, 2) for pair in (0, 1)][1:]
    others = [(2, 1), (2, 0), (0, 1), (1, 1), (-1, 1), (1, 0), (-1, 0)]
    meet([{"seq": here.seq_at(ring, pair)} for ring, pair in others])
    net = Copies(send_sems, recv_sems)
    copies = [
        net.start(in_ref.at[here.seq_at(ring, pair)], out_ref.at[here.seq], {"seq": here.seq_at(ring, pair)})
        for ring, pair in others
    ]
    local = pltpu.make_async_copy(in_ref.at[here.seq], out_ref.at[here.seq], local_sem.at[0])
    local.start()
    local.wait()
    for copy in copies:
        copy.wait_recv()
    net.finish()


def swap(values, ident):
    return pl.pallas_call(
        swap_kernel,
        in_specs=[pl.BlockSpec(memory_space=pl.ANY)],
        out_specs=pl.BlockSpec(memory_space=pl.ANY),
        out_shape=jax.ShapeDtypeStruct(values.shape, values.dtype),
        scratch_shapes=[
            pltpu.SemaphoreType.DMA((1,)),
            pltpu.SemaphoreType.DMA((7,)),
            pltpu.SemaphoreType.DMA((7,)),
        ],
        compiler_params=pltpu.CompilerParams(collective_id=ident, has_side_effects=True),
        name="swap",
    )(values)


SLOTS=96
GROUP_ROWS=4*SLOTS
ROWS=4*GROUP_ROWS
WIDE=D+128

def moe_kernel(
    x_ref, g_ref, masks_ref, router_ref, up_hbm, down_hbm,
    row_out, gate_out, y_out, grads_out,
    slots, sib_in, hop_in, g_rows, up_ref, down_ref,
    rows_x, rows_p, rows_h, rows_u, rows_g, slot_gate, places, stage_y, stage_r, y_stage, w_stage,
    local_sems, send_sems, recv_sems,
):
    here = Place()
    sib = here.sibling()
    way = here.plane("fsdp")
    own = here.fsdp
    counter = [0]

    def local(src, dst):
        copy = pltpu.make_async_copy(src, dst, local_sems.at[counter[0]])
        counter[0] += 1
        copy.start()
        return copy

    first_x = local(x_ref, slots.at[0, :, pl.ds(0, D)])
    weights = [local(up_hbm, up_ref), local(down_hbm, down_ref)]

    def source(k):
        ring, pair, c = (0, -1, 1, 2)[k // 4], (k // 2) % 2, k % 2
        z = lax.rem(here.z + ring + 4, 4)
        xh = 1 - here.xh if pair else here.xh
        return z * 4 + xh * 2 + (1 - here.core if c else here.core)

    def fetch_g(group):
        return [local(g_ref.at[source(4 * group + s)], g_rows.at[s]) for s in range(4)]

    g_copies = fetch_g(0)
    meet([sib, *way.values()])
    net = Copies(send_sems, recv_sems)

    def block(k, low=0, rows=TOKENS):
        return slots.at[k, pl.ds(low, rows), pl.ds(0, D)]

    sent = {k: [] for k in range(16)}

    def push(k, to, target, low=0, rows=TOKENS, src=None):
        copy = net.start(block(k, low, rows) if src is None else src, block(to, low, rows), target)
        sent[k].append(copy)
        return copy

    across = push(0, 2, way["across"], src=x_ref)
    up = push(0, 4, way["up"], src=x_ref)
    down = push(0, 8, way["down"], src=x_ref)
    kin = {1: push(0, 1, sib, src=x_ref)}
    across.wait_recv()
    up_x = push(2, 6, way["up"])
    down_x = push(2, 10, way["down"])
    kin[3] = push(2, 3, sib)
    state = {}

    lanes = lax.broadcasted_iota(jnp.int32, (1, 128), 1)
    slot = lax.broadcasted_iota(jnp.int32, (2 * SLOTS, TOKENS), 0)
    slot_place = slot.astype(f32)
    first = slot < SLOTS
    expert = lax.broadcasted_iota(jnp.int32, (EXPERTS, TOKENS), 0)

    def gather(group):
        before = (
            lax.broadcasted_iota(jnp.int32, (TOKENS, TOKENS), 0)
            < lax.broadcasted_iota(jnp.int32, (TOKENS, TOKENS), 1)
        ).astype(f32).astype(bf16)
        for s in range(4):
            k = 4 * group + s
            if k in kin:
                kin[k].wait_recv()
            g_copies[s].wait()
            x_rows = slots[k, :, 0:D]
            named = masks_ref[source(k)].astype(f32)
            logits = dot_t(router_ref[...], x_rows)
            peak = jnp.max(jnp.where(named > 0.0, logits, -1e30), axis=0, keepdims=True)
            parts = jnp.where(named > 0.0, jnp.exp(logits - peak), 0.0)
            gates = parts / jnp.sum(parts, axis=0, keepdims=True)
            rank = dot(named.astype(bf16), before)
            rank = jnp.where(named > 0.0, rank, -1000.0)

            def mine(values, i):
                return jnp.sum(jnp.where(expert == 2 * own + i, values, 0.0), axis=0, keepdims=True)

            wanted = jnp.where(first, mine(rank, 0), mine(rank, 1) + SLOTS)
            hot = jnp.where(slot_place == wanted, 1.0, 0.0)
            gate = jnp.sum(hot * jnp.where(first, mine(gates, 0), mine(gates, 1)), axis=1, keepdims=True)
            hot = hot.astype(bf16)
            places[s] = hot
            picked = dot(hot, x_rows).astype(bf16)
            grads = dot(hot, g_rows[s])
            pair = (grads * gate).astype(bf16)
            grads = grads.astype(bf16)
            for i in range(2):
                part = slice(SLOTS * i, SLOTS * (i + 1))
                there = slice(group * GROUP_ROWS + SLOTS * s, group * GROUP_ROWS + SLOTS * (s + 1))
                rows_x[i, there, :] = picked[part]
                rows_p[i, there, :] = pair[part]
                rows_g[i, SLOTS * s : SLOTS * (s + 1), :] = grads[part]
                slot_gate[i, SLOTS * s : SLOTS * (s + 1), :] = jnp.broadcast_to(gate[part], (SLOTS, 128))

    def run(group):
        here_rows = pl.ds(group * GROUP_ROWS, GROUP_ROWS)

        def one(e, carry):
            x_rows = rows_x[e, here_rows, :]
            gate_part = dot(x_rows, up_ref[e, :, 0:F])
            up_part = dot(x_rows, up_ref[e, :, F : 2 * F])
            sigmoid = 1.0 / (1.0 + jnp.exp(-gate_part))
            silu = gate_part * sigmoid
            hidden = (silu * up_part).astype(bf16)
            rows_h[e, here_rows, :] = hidden
            hidden_grad = dot(rows_p[e, here_rows, :], down_ref[e])
            slope = sigmoid * (1.0 + gate_part * (1.0 - sigmoid))
            rows_u[e, here_rows, 0:F] = (hidden_grad * up_part * slope).astype(bf16)
            rows_u[e, here_rows, F : 2 * F] = (hidden_grad * silu).astype(bf16)
            out = dot_t(hidden, down_ref[e]).astype(bf16).astype(f32)
            gate_grad = jnp.sum(out * rows_g[e].astype(f32), axis=1, keepdims=True)
            stage_y[e] = (out * slot_gate[e][:, 0:1]).astype(bf16)
            stage_r[e, :, 0:D] = dot_t(rows_u[e, here_rows, :], up_ref[e]).astype(bf16)
            high = gate_grad.astype(bf16).astype(f32)
            column = 2 * own + e
            stage_r[e, :, D:WIDE] = jnp.where(
                lanes == column, high, jnp.where(lanes == column + EXPERTS, gate_grad - high, 0.0)
            ).astype(bf16)
            return carry

        lax.fori_loop(0, 2, one, 0)

    def combine(group):
        for copy in state.pop("y", ()):
            copy.wait()
        for s in range(4):
            k = 4 * group + s
            for copy in sent[k]:
                copy.wait_send()
            part = slice(SLOTS * s, SLOTS * (s + 1))
            both = jnp.concatenate([stage_y[0, part, :], stage_y[1, part, :]], axis=0)
            y_stage[s] = t_dot(places[s], both).astype(bf16)
            both = jnp.concatenate([stage_r[0, part, :], stage_r[1, part, :]], axis=0)
            slots[k] = t_dot(places[s], both).astype(bf16)
        state["y"] = [local(y_stage.at[s], y_out.at[4 * group + s]) for s in range(4)]
        for j in range(2):
            k = 4 * group + 2 * j
            state["k", group, j] = net.start(slots.at[k + 1], sib_in.at[2 * group + j], sib)

    def join(group, j):
        state["k", group, j].wait_recv()
        k = 4 * group + 2 * j
        slots[k] = (slots[k].astype(f32) + sib_in[2 * group + j].astype(f32)).astype(bf16)

    first_x.wait()
    gather(0)
    g_copies = fetch_g(1)
    for copy in weights:
        copy.wait()
    up.wait_recv()
    far_low = push(4, 12, way["up"], 0, 128)
    kin[5] = push(4, 5, sib)
    down.wait_recv()
    far_high = push(8, 12, way["down"], 128, 128)
    kin[9] = push(8, 9, sib)
    run(0)
    up_x.wait_recv()
    kin[7] = push(6, 7, sib)
    down_x.wait_recv()
    kin[11] = push(10, 11, sib)
    combine(0)
    far_low.wait_recv()
    far_high.wait_recv()
    far_x = push(12, 14, way["across"])
    kin[13] = push(12, 13, sib)
    gather(1)
    g_copies = fetch_g(3)
    run(1)
    far_x.wait_recv()
    kin[15] = push(14, 15, sib)
    combine(1)
    gather(3)
    g_copies = fetch_g(2)
    run(3)
    combine(3)
    gather(2)
    join(3, 1)
    hop_a = net.start(slots.at[14], hop_in.at[0], way["across"])
    join(3, 0)
    run(2)
    hop_a.wait_recv()
    slots[12] = (slots[12].astype(f32) + hop_in[0].astype(f32)).astype(bf16)
    hop_u = net.start(slots.at[12, pl.ds(0, 128)], hop_in.at[1, pl.ds(0, 128)], way["up"])
    hop_d = net.start(slots.at[12, pl.ds(128, 128)], hop_in.at[1, pl.ds(128, 128)], way["down"])
    combine(2)

    w_copies = [[], []]

    def weight_grad(piece):
        e, dx = piece // 2, piece % 2
        buffer = 0
        for copy in w_copies[buffer]:
            copy.wait()
        xl = 1 - here.xl if dx else here.xl
        columns = pl.ds(pl.multiple_of(xl * 512, 512), 512)
        w_stage[buffer, :, 0 : 2 * F] = t_dot(rows_x[e, :, columns], rows_u[e]).astype(bf16)
        w_stage[buffer, :, 2 * F : 3 * F] = t_dot(rows_p[e, :, columns], rows_h[e]).astype(bf16)
        w_copies[buffer] = [
            local(
                w_stage.at[buffer, pl.ds(128 * y, 128)],
                grads_out.at[e, pl.ds(pl.multiple_of(xl * 512 + 128 * y, 128), 128)],
            )
            for y in range(4)
        ]

    join(1, 1)
    hop_xd = net.start(slots.at[6], hop_in.at[2], way["down"])
    join(2, 1)
    hop_xu = net.start(slots.at[10], hop_in.at[3], way["up"])
    join(1, 0)
    join(2, 0)
    weight_grad(0)
    hop_u.wait_recv()
    slots[8, 0:128, :] = (slots[8, 0:128, :].astype(f32) + hop_in[1, 0:128, :].astype(f32)).astype(bf16)
    hop_ru = net.start(slots.at[8], hop_in.at[4], way["up"])
    hop_d.wait_recv()
    slots[4, 128:256, :] = (slots[4, 128:256, :].astype(f32) + hop_in[1, 128:256, :].astype(f32)).astype(bf16)
    hop_rd = net.start(slots.at[4], hop_in.at[5], way["down"])
    join(0, 1)
    join(0, 0)
    weight_grad(1)
    hop_xd.wait_recv()
    hop_xu.wait_recv()
    slots[2] = (slots[2].astype(f32) + hop_in[2].astype(f32) + hop_in[3].astype(f32)).astype(bf16)
    hop_rx = net.start(slots.at[2], hop_in.at[6], way["across"])
    weight_grad(2)
    weight_grad(3)
    hop_ru.wait_recv()
    hop_rd.wait_recv()
    hop_rx.wait_recv()
    total = (
        slots[0].astype(f32) + hop_in[4].astype(f32) + hop_in[5].astype(f32) + hop_in[6].astype(f32)
    )
    row_out[...] = total[:, 0:D]
    gate_out[...] = total[:, D:WIDE]
    for copies in (*w_copies, state["y"]):
        for copy in copies:
            copy.wait()
    waited = {id(copy) for k in range(16) for copy in sent[k]}
    for copy in net.all:
        if id(copy) not in waited:
            copy.wait_send()


def moe(x, g_all, masks, router_t, up, down):
    any_space = pl.BlockSpec(memory_space=pl.ANY)
    vmem = pl.BlockSpec(memory_space=pltpu.VMEM)
    return pl.pallas_call(
        moe_kernel,
        in_specs=[any_space, any_space, vmem, vmem, any_space, any_space],
        out_specs=[vmem, vmem, any_space, any_space],
        out_shape=[
            jax.ShapeDtypeStruct((TOKENS, D), f32),
            jax.ShapeDtypeStruct((TOKENS, 128), f32),
            jax.ShapeDtypeStruct((16, TOKENS, D), bf16),
            jax.ShapeDtypeStruct((2, D, 3 * F), bf16),
        ],
        scratch_shapes=[
            pltpu.VMEM((16, TOKENS, WIDE), bf16),
            pltpu.VMEM((8, TOKENS, WIDE), bf16),
            pltpu.VMEM((7, TOKENS, WIDE), bf16),
            pltpu.VMEM((4, TOKENS, D), bf16),
            pltpu.VMEM((2, D, 2 * F), bf16),
            pltpu.VMEM((2, D, F), bf16),
            pltpu.VMEM((2, ROWS, D), bf16),
            pltpu.VMEM((2, ROWS, D), bf16),
            pltpu.VMEM((2, ROWS, F), bf16),
            pltpu.VMEM((2, ROWS, 2 * F), bf16),
            pltpu.VMEM((2, GROUP_ROWS, D), bf16),
            pltpu.VMEM((2, GROUP_ROWS, 128), f32),
            pltpu.VMEM((4, 2 * SLOTS, TOKENS), bf16),
            pltpu.VMEM((2, GROUP_ROWS, D), bf16),
            pltpu.VMEM((2, GROUP_ROWS, WIDE), bf16),
            pltpu.VMEM((4, TOKENS, D), bf16),
            pltpu.VMEM((1, 512, 3 * F), bf16),
            pltpu.SemaphoreType.DMA((56,)),
            pltpu.SemaphoreType.DMA((40,)),
            pltpu.SemaphoreType.DMA((40,)),
        ],
        compiler_params=pltpu.CompilerParams(
            collective_id=4, has_side_effects=True, vmem_limit_bytes=63 * 1024 * 1024
        ),
        cost_estimate=pl.CostEstimate(flops=32 * 10**9, bytes_accessed=40 << 20, transcendentals=1 << 21),
        name="moe",
    )(x, g_all, masks, router_t, up, down)


GCOLS = 1536


def reduce_kernel(
    parts_ref, small_ref, out_ref, small_out,
    acc, sib_in, small_acc, small_sib, hop_a, hop_b, late_a, late_b, small_s, small_f, total, local_sems,
    send_sems, recv_sems,
):
    here = Place()
    c, s = here.core, here.seq
    f = here.z * 2 + here.xh
    sib = here.sibling()
    ways = {"seq": here.plane("seq"), "fsdp": here.plane("fsdp")}
    others = [(2, 1), (2, 0), (0, 1), (1, 1), (-1, 1), (1, 0), (-1, 0)]

    def f_at(ring, pair):
        return lax.rem(here.z + ring + 4, 4) * 2 + (1 - here.xh if pair else here.xh)

    seq_peers = [{"seq": here.seq_at(ring, pair)} for ring, pair in others]
    fsdp_peers = [{"fsdp": here.fsdp_at(ring, pair)} for ring, pair in others]
    own = pltpu.make_async_copy(parts_ref.at[c], acc, local_sems.at[0])
    own.start()
    meet([sib, *seq_peers, *fsdp_peers])
    net = Copies(send_sems, recv_sems)
    joins = [
        net.start(parts_ref.at[1 - c, pl.ds(2 * i, 2)], sib_in.at[pl.ds(2 * i, 2)], sib) for i in range(4)
    ]
    small_join = net.start(small_ref.at[1 - c], small_sib, sib)
    own.wait()
    small_join.wait_recv()
    small_acc[...] = small_ref[c] + small_sib[...]
    small_copies = [
        net.start(small_acc.at[here.seq_at(*others[i])], small_s.at[i], seq_peers[i]) for i in range(7)
    ]
    for i in range(4):
        joins[i].wait_recv()
        part = slice(2 * i, 2 * i + 2)
        acc[part] = (acc[part].astype(f32) + sib_in[part].astype(f32)).astype(bf16)

    def add_to(ref, *values):
        result = ref[...].astype(f32)
        for value in values:
            result = result + value[...].astype(f32)
        ref[...] = result.astype(bf16)

    def plane(part, hop, way):
        def half(ref, high):
            return ref.at[pl.ds(4 * high, 4)]

        a = net.start(part(2, 1), hop.at[0], way["across"])
        xd = net.start(part(-1, 1), hop.at[2], way["down"])
        xu = net.start(part(1, 1), hop.at[3], way["up"])
        yield
        a.wait_recv()
        add_to(part(2, 0), hop.at[0])
        u = net.start(half(part(2, 0), 0), half(hop.at[1], 0), way["up"])
        d = net.start(half(part(2, 0), 1), half(hop.at[1], 1), way["down"])
        yield
        xd.wait_recv()
        xu.wait_recv()
        add_to(part(0, 1), hop.at[2], hop.at[3])
        rx = net.start(part(0, 1), hop.at[6], way["across"])
        yield
        u.wait_recv()
        add_to(half(part(1, 0), 0), half(hop.at[1], 0))
        ru = net.start(part(1, 0), hop.at[4], way["up"])
        d.wait_recv()
        add_to(half(part(-1, 0), 1), half(hop.at[1], 1))
        rd = net.start(part(-1, 0), hop.at[5], way["down"])
        yield
        rx.wait_recv()
        ru.wait_recv()
        rd.wait_recv()
        add_to(part(0, 0), hop.at[4], hop.at[5], hop.at[6])

    low, high = pl.ds(0, GCOLS // 2), pl.ds(GCOLS // 2, GCOLS // 2)
    first = plane(lambda ring, pair: acc.at[here.seq_at(ring, pair), :, :, low], hop_a, ways["seq"])
    second = plane(lambda ring, pair: acc.at[:, f_at(ring, pair), :, high], hop_b, ways["fsdp"])
    for _ in range(4):
        next(first)
        next(second)
    for copy in small_copies:
        copy.wait_recv()
    mine = small_acc[s]
    for i in range(7):
        mine = mine + small_s[i]
    small_acc[s] = mine
    small_copies = [
        net.start(small_acc.at[s, f_at(*others[i])], small_f.at[i], fsdp_peers[i]) for i in range(7)
    ]
    next(first, None)
    a = [
        net.start(acc.at[s, f_at(*others[i]), :, low], late_a.at[i], fsdp_peers[i]) for i in range(7)
    ]
    next(second, None)
    b = [
        net.start(acc.at[here.seq_at(*others[i]), f, :, high], late_b.at[i], seq_peers[i]) for i in range(7)
    ]
    for copy in small_copies:
        copy.wait_recv()
    mine = small_acc[s, f]
    for i in range(7):
        mine = mine + small_f[i]
    small_out[...] = mine
    for cols, copies, late in ((slice(0, GCOLS // 2), a, late_a), (slice(GCOLS // 2, GCOLS), b, late_b)):
        for copy in copies:
            copy.wait_recv()
        result = acc[s, f, :, cols].astype(f32)
        for i in range(7):
            result = result + late[i].astype(f32)
        total[:, cols] = result
    theirs = pl.ds(pl.multiple_of(8 * (1 - c), 8), 8)
    last = net.start(total.at[theirs], out_ref.at[c], sib)
    out_ref[c] = total[pl.ds(pl.multiple_of(8 * c, 8), 8), :]
    last.wait_recv()
    net.finish()


def reduce_weights(parts, small):
    vmem = pl.BlockSpec(memory_space=pltpu.VMEM)
    n = 1 + 4 + 7 + 7 + 14 + 16 + 4
    return pl.pallas_call(
        reduce_kernel,
        in_specs=[pl.BlockSpec(memory_space=pl.ANY), vmem],
        out_specs=[vmem, vmem],
        out_shape=[jax.ShapeDtypeStruct((2, 8, GCOLS), f32), jax.ShapeDtypeStruct((8, 128), f32)],
        scratch_shapes=[
            pltpu.VMEM((8, 8, 16, GCOLS), bf16),
            pltpu.VMEM((8, 8, 16, GCOLS), bf16),
            pltpu.VMEM((8, 8, 8, 128), f32),
            pltpu.VMEM((8, 8, 8, 128), f32),
            pltpu.VMEM((7, 8, 16, GCOLS // 2), bf16),
            pltpu.VMEM((7, 8, 16, GCOLS // 2), bf16),
            pltpu.VMEM((7, 16, GCOLS // 2), bf16),
            pltpu.VMEM((7, 16, GCOLS // 2), bf16),
            pltpu.VMEM((7, 8, 8, 128), f32),
            pltpu.VMEM((7, 8, 128), f32),
            pltpu.VMEM((16, GCOLS), f32),
            pltpu.SemaphoreType.DMA((1,)),
            pltpu.SemaphoreType.DMA((n,)),
            pltpu.SemaphoreType.DMA((n,)),
        ],
        compiler_params=pltpu.CompilerParams(collective_id=3, has_side_effects=True, vmem_limit_bytes=VMEM),
        name="reduce_weights",
    )(parts, small)


def on_device(
    tokens, attn_gain, qkv_weight, qk_gain, out_weight, ffn_gain, router_weight,
    gate_up_weight, down_weight, routes, cotangent,
):
    layer_inputs = tokens.reshape(TOKENS, D).astype(f32)
    query_total_width = QUERY_HEADS * HEAD_SIZE
    key_total_width = KEY_VALUE_HEADS * HEAD_SIZE
    seq_place = lax.axis_index("seq")

    fsdp_place = lax.axis_index("fsdp")
    core = fsdp_place % 2
    route_ids = routes.reshape(TOKENS, TOPK)
    expert_ids = jnp.arange(EXPERTS, dtype=jnp.int32)
    named = jnp.any(route_ids[:, :, None] == expert_ids[None, None, :], axis=1)
    small = jnp.concatenate(
        [
            router_weight,
            attn_gain[:, None],
            ffn_gain[:, None],
            jnp.broadcast_to(qk_gain[:, None], (8, 1)),
            jnp.zeros((8, 93), bf16),
        ],
        axis=1,
    )
    halves = jnp.stack(
        [
            jnp.concatenate([qkv_weight[:, :1024], out_weight[:, :512], small], axis=1),
            jnp.concatenate([qkv_weight[:, 1024:], out_weight[:, 512:], small], axis=1),
        ]
    ).astype(f32)
    whole, masks = gather_weights(halves, named.T.astype(bf16))
    whole = whole.reshape(2, D, 1664)
    full_qkv = jnp.concatenate([whole[0, :, :1024], whole[1, :, :1024]], axis=1)
    full_out = jnp.concatenate([whole[0, :, 1024:1536], whole[1, :, 1024:1536]], axis=1)
    small = whole[0, :, 1536:]
    full_router = small[:, :32]
    attn_norm = small[:, 32].astype(f32)
    ffn_norm = small[:, 33].astype(f32)
    qk_norm = small[:, 34].reshape(128, 8)[:, 0].astype(f32)
    z_place, xh_place = fsdp_place // 4, (fsdp_place // 2) % 2
    y_place, xl_place = seq_place % 4, seq_place // 4

    cot = cotangent.reshape(TOKENS, D)
    g_all = lax.all_gather(cot[None], "fsdp", axis=0, tiled=True)

    normed_attn, attn_scaling = rms_forward(layer_inputs, attn_norm)
    normed_attn = normed_attn.astype(bf16)
    projected_rows = jnp.dot(normed_attn, full_qkv, preferred_element_type=f32)
    query_raw = projected_rows[:, :query_total_width].reshape(TOKENS, QUERY_HEADS, HEAD_SIZE)
    key_raw = projected_rows[:, query_total_width : query_total_width + key_total_width].reshape(
        TOKENS, KEY_VALUE_HEADS, HEAD_SIZE
    )
    value_low = projected_rows[:, query_total_width + key_total_width :].astype(bf16)
    query_normed, query_scaling = rms_forward(query_raw, qk_norm[:HEAD_SIZE])
    key_normed, key_scaling = rms_forward(key_raw, qk_norm[HEAD_SIZE:])
    positions = seq_place * TOKENS + jnp.arange(TOKENS, dtype=jnp.int32)
    cosine_values, sine_values = rotary_tables(positions, HEAD_SIZE)
    query_low = rotate(query_normed, cosine_values, sine_values).astype(bf16)
    key_low = rotate(key_normed, cosine_values, sine_values).astype(bf16)
    send = jnp.concatenate(
        [
            query_low.reshape(TOKENS, 8, 128),
            key_low.reshape(TOKENS, 8, 64),
            value_low.reshape(TOKENS, 8, 64),
        ],
        axis=2,
    ).transpose(1, 0, 2)
    heads = swap(send, 5).reshape(LENGTH, 256)
    attended_low, attended_full, logs = attend(heads)
    attended_tokens = (
        swap(attended_low.reshape(8, TOKENS, 128), 6)
        .transpose(1, 0, 2)
        .reshape(TOKENS, D)
    )
    after_attention = layer_inputs + jnp.dot(attended_tokens, full_out, preferred_element_type=f32)
    normed_ffn, ffn_scaling = rms_forward(after_attention, ffn_norm)
    normed_ffn = normed_ffn.astype(bf16)
    logits = jnp.dot(normed_ffn, full_router, preferred_element_type=f32)
    peak = jnp.max(jnp.where(named, logits, -jnp.inf), axis=1, keepdims=True)
    chosen_exp = jnp.where(named, jnp.exp(logits - peak), 0.0)
    gates = chosen_exp / jnp.sum(chosen_exp, axis=1, keepdims=True)

    g_all, masks = lax.optimization_barrier((g_all, masks))
    row_sum, gate_sum, y_all, grads = moe(normed_ffn, g_all, masks, full_router.T, gate_up_weight, down_weight)
    gate_grad = gate_sum[:, 0:32] + gate_sum[:, 32:64]
    expert_part = lax.psum_scatter(grads, "seq", scatter_dimension=1, tiled=True).astype(f32)
    gate_up_part, down_part = expert_part[:, :, : 2 * F], expert_part[:, :, 2 * F :]
    incoming = cot.astype(f32)
    chosen_grad = gates * (gate_grad - jnp.sum(gates * gate_grad, axis=1, keepdims=True))
    logits_grad = chosen_grad.astype(bf16)
    router_grad = t_dot(normed_ffn, logits_grad)
    normed_ffn_grad = row_sum + dot_t(logits_grad, full_router)
    after_extra, ffn_terms = rms_backward(after_attention, ffn_scaling, ffn_norm, normed_ffn_grad)
    after_grad = incoming + after_extra
    ffn_gain_grad = jnp.sum(ffn_terms, axis=0)
    after_low = after_grad.astype(bf16)
    out_weight_grad = t_dot(attended_tokens, after_low)
    attended_grad = dot_t(after_low, full_out).astype(bf16)
    grad_heads = swap(attended_grad.reshape(TOKENS, 8, 128).transpose(1, 0, 2), 7).reshape(LENGTH, 128)
    dq, dkv, expert_sum = attend_back(heads, attended_full, logs, grad_heads, y_all)
    layer_out = (after_attention + expert_sum).astype(bf16).reshape(1, TOKENS, D)
    back = jnp.concatenate([dq, dkv], axis=1).reshape(8, TOKENS, 256)
    back = swap(back, 8)
    token_query_grad = back[:, :, :128].transpose(1, 0, 2).reshape(TOKENS, QUERY_HEADS, HEAD_SIZE)
    token_key_grad = back[:, :, 128:192].transpose(1, 0, 2)
    token_value_grad = back[:, :, 192:].transpose(1, 0, 2).reshape(TOKENS, key_total_width)
    query_normed_grad = rotate(token_query_grad.astype(f32), cosine_values, -sine_values)
    key_normed_grad = rotate(token_key_grad.astype(f32), cosine_values, -sine_values)
    query_raw_grad, query_terms = rms_backward(query_raw, query_scaling, qk_norm[:HEAD_SIZE], query_normed_grad)
    key_raw_grad, key_terms = rms_backward(key_raw, key_scaling, qk_norm[HEAD_SIZE:], key_normed_grad)
    qk_gain_grad = jnp.concatenate(
        [jnp.sum(query_terms, axis=(0, 1)), jnp.sum(key_terms, axis=(0, 1))], axis=0
    )
    projected_grad = jnp.concatenate(
        [
            query_raw_grad.reshape(TOKENS, query_total_width).astype(bf16),
            key_raw_grad.reshape(TOKENS, key_total_width).astype(bf16),
            token_value_grad,
        ],
        axis=1,
    )
    qkv_weight_grad = t_dot(normed_attn, projected_grad)
    normed_attn_grad = dot_t(projected_grad, full_qkv)
    input_extra, attn_terms = rms_backward(layer_inputs, attn_scaling, attn_norm, normed_attn_grad)
    token_grad = (after_grad + input_extra).reshape(1, TOKENS, D)
    attn_gain_grad = jnp.sum(attn_terms, axis=0)

    qkv_low, out_low = qkv_weight_grad.astype(bf16), out_weight_grad.astype(bf16)
    parts = jnp.stack(
        [
            jnp.concatenate([qkv_low[:, :1024], out_low[:, :512]], axis=1),
            jnp.concatenate([qkv_low[:, 1024:], out_low[:, 512:]], axis=1),
        ]
    ).reshape(2, 8, 8, 16, GCOLS)
    small = jnp.concatenate(
        [
            router_grad.reshape(128, 256),
            attn_gain_grad.reshape(128, 8),
            ffn_gain_grad.reshape(128, 8),
            qk_gain_grad.reshape(128, 1),
            jnp.zeros((128, 751), f32),
        ],
        axis=1,
    ).reshape(8, 8, 2, 8, 128).transpose(2, 0, 1, 3, 4)
    parts, small = reduce_weights(parts, small)
    qkv_part = jnp.concatenate([parts[0, :, :1024], parts[1, :, :1024]], axis=1)
    out_part = jnp.concatenate([parts[0, :, 1024:], parts[1, :, 1024:]], axis=1)
    small = small.reshape(1024)
    router_part = small[:256].reshape(8, 32)
    attn_part = small[256:264]
    ffn_part = small[264:272]
    qk_part = small[272:273]
    return (
        layer_out, token_grad, attn_part, qkv_part, qk_part, out_part, ffn_part, router_part,
        gate_up_part, down_part,
    )


def solution(mesh):
    return jax.shard_map(
        on_device,
        mesh=mesh,
        in_specs=(
            P("fsdp", "seq", None),
            P(("seq", "fsdp")),
            P(("seq", "fsdp"), None),
            P(("seq", "fsdp")),
            P(("seq", "fsdp"), None),
            P(("seq", "fsdp")),
            P(("seq", "fsdp"), None),
            P("fsdp", None, None),
            P("fsdp", None, None),
            P("fsdp", "seq", None),
            P("fsdp", "seq", None),
        ),
        out_specs=(
            P("fsdp", "seq", None),
            P("fsdp", "seq", None),
            P(("seq", "fsdp")),
            P(("seq", "fsdp"), None),
            P(("seq", "fsdp")),
            P(("seq", "fsdp"), None),
            P(("seq", "fsdp")),
            P(("seq", "fsdp"), None),
            P("fsdp", "seq", None),
            P("fsdp", "seq", None),
        ),
        check_vma=False,
    )
```

```python
import math

import jax
import jax.numpy as jnp
from jax import lax
from jax.experimental import pallas as pl
from jax.experimental.pallas import tpu as pltpu
from jax.sharding import PartitionSpec as P

D = 1024
HEAD_SIZE = 64
F = 512
TOPK = 8
EXPERTS = 32
SLOTS = 96
TOKENS = 256
SEQ = 8
FSDP = 16
LENGTH = SEQ * TOKENS
GROUP_ROWS = 4 * SLOTS
ROWS = 4 * GROUP_ROWS
WIDE = D + 128
GCOLS = 1536
VMEM = 60 * 1024 * 1024

epsilon = 1e-06
rope_base = 10000.0
f32 = jnp.float32
bf16 = jnp.bfloat16


def dot(a, b):
    return lax.dot_general(a, b, (((1,), (0,)), ((), ())), preferred_element_type=f32)


def dot_t(a, b):
    return lax.dot_general(a, b, (((1,), (1,)), ((), ())), preferred_element_type=f32)


def t_dot(a, b):
    return lax.dot_general(a, b, (((0,), (0,)), ((), ())), preferred_element_type=f32)


MESH = pl.DeviceIdType.MESH


class Place:
    def __init__(self):
        self.seq = lax.axis_index("seq")
        self.fsdp = lax.axis_index("fsdp")
        self.core = lax.rem(self.fsdp, 2)
        self.xh = lax.rem(self.fsdp // 2, 2)
        self.z = self.fsdp // 4
        self.y = lax.rem(self.seq, 4)
        self.xl = self.seq // 4

    def sibling(self):
        return {"fsdp": self.fsdp + 1 - 2 * self.core}

    def fsdp_at(self, ring, pair):
        z = lax.rem(self.z + ring + 4, 4)
        xh = 1 - self.xh if pair else self.xh
        return z * 4 + xh * 2 + self.core

    def seq_at(self, ring, pair):
        y = lax.rem(self.y + ring + 4, 4)
        xl = 1 - self.xl if pair else self.xl
        return xl * 4 + y

    def plane(self, axis):
        at = self.fsdp_at if axis == "fsdp" else self.seq_at
        return {
            "up": {axis: at(1, 0)},
            "down": {axis: at(-1, 0)},
            "across": {axis: at(0, 1)},
        }


def meet(targets):
    barrier = pltpu.get_barrier_semaphore()
    for target in targets:
        pl.semaphore_signal(barrier, inc=1, device_id=target, device_id_type=MESH)
    pl.semaphore_wait(barrier, len(targets))


class Copies:
    def __init__(self, send_sems, recv_sems):
        self.send_sems, self.recv_sems, self.count, self.all = send_sems, recv_sems, 0, []

    def start(self, src, dst, target):
        k = self.count
        self.count += 1
        copy = pltpu.make_async_remote_copy(
            src_ref=src, dst_ref=dst, send_sem=self.send_sems.at[k], recv_sem=self.recv_sems.at[k],
            device_id=target, device_id_type=MESH,
        )
        copy.start()
        self.all.append(copy)
        return copy

    def finish(self):
        for copy in self.all:
            copy.wait_send()


OTHERS = ((2, 1), (2, 0), (0, 1), (1, 1), (-1, 1), (1, 0), (-1, 0))
WCOLS = 1664


def lane_halves():
    lanes = lax.broadcasted_iota(jnp.int32, (1, 128), 1)
    return lanes, lanes < HEAD_SIZE


def head_mean(values, low_half):
    low = jnp.sum(jnp.where(low_half, values, 0.0), axis=1, keepdims=True)
    high = jnp.sum(jnp.where(low_half, 0.0, values), axis=1, keepdims=True)
    return jnp.where(low_half, low, high) * (1.0 / HEAD_SIZE)


def partner(values, lanes):
    return jnp.where(
        lax.rem(lanes, HEAD_SIZE) < HEAD_SIZE // 2, pltpu.roll(values, 96, 1), pltpu.roll(values, 32, 1)
    )


def row_scale(values):
    return lax.rsqrt(jnp.mean(values * values, axis=1, keepdims=True) + epsilon)


def gain_tiles(small_t, lanes):
    pick = (
        lax.broadcasted_iota(jnp.int32, (D, 128), 0) == 8 * lax.broadcasted_iota(jnp.int32, (D, 128), 1)
    ).astype(f32).astype(bf16)
    gains = dot(small_t[32:48, :], pick)[2:3, :]
    other = pltpu.roll(gains, 64, 1)
    low_half = lanes < HEAD_SIZE
    return jnp.where(low_half, gains, other), jnp.where(low_half, other, gains)


def front_kernel(
    x_ref, w_ref, routes_ref, cos_ref, sin_ref,
    heads_out, full_ref, logs_ref, att_ref, after_ref, normed_ref, gates_ref, small_t_ref, raw_ref,
    wq, wkv, wo, small, send, heads, out_buf, att, key0, key1, value,
    local_sems, send_sems, recv_sems,
):
    here = Place()
    me = here.seq
    loads = [
        pltpu.make_async_copy(w_ref.at[h, :, pl.ds(start, width)], there, local_sems.at[k])
        for k, (h, start, width, there) in enumerate(
            (
                (0, 1536, 128, small),
                (0, 0, 1024, wq),
                (1, 0, 1024, wkv),
                (0, 1024, 512, wo.at[0]),
                (1, 1024, 512, wo.at[1]),
            )
        )
    ]
    for copy in loads:
        copy.start()
    peers = [here.seq_at(*other) for other in OTHERS]
    meet([{"seq": peer} for peer in peers])
    net = Copies(send_sems, recv_sems)
    lanes, low_half = lane_halves()
    loads[0].wait()
    small_t = jnp.transpose(small[...].astype(f32)).astype(bf16)
    small_t_ref[...] = small_t
    x = x_ref[...].astype(f32)
    normed = (x * row_scale(x) * small_t[32:33, :].astype(f32)).astype(bf16)
    query_gain, key_gain = gain_tiles(small_t, lanes)
    cos, sin = cos_ref[...], sin_ref[...]
    loads[1].wait()
    raw_ref[:, 0:1024] = dot(normed, wq[...])
    loads[2].wait()
    kv = dot(normed, wkv[...])
    raw_ref[:, 1024:1536] = kv[:, 0:512]

    def turned(tile, gain):
        normal = tile * lax.rsqrt(head_mean(tile * tile, low_half) + epsilon) * gain
        return normal * cos + partner(normal, lanes) * sin

    for j in range(4):
        part = slice(128 * j, 128 * (j + 1))
        keys = turned(kv[:, part], key_gain)
        values = kv[:, 512 + 128 * j : 640 + 128 * j]
        send[2 * j, :, 128:256] = jnp.where(low_half, keys, pltpu.roll(values, 64, 1)).astype(bf16)
        send[2 * j + 1, :, 128:256] = jnp.where(low_half, pltpu.roll(keys, 64, 1), values).astype(bf16)
    for h in range(8):
        send[h, :, 0:128] = turned(raw_ref[:, 128 * h : 128 * (h + 1)], query_gain).astype(bf16)
    copies = [net.start(send.at[peer], heads.at[me], {"seq": peer}) for peer in peers]
    heads[me] = send[me]
    for copy in copies:
        copy.wait_recv()
    save = pltpu.make_async_copy(heads, heads_out, local_sems.at[5])
    save.start()
    for c in range(8):
        rows = slice(TOKENS * c, TOKENS * (c + 1))
        pair = heads[c, :, 128:256].astype(f32)
        key0[rows, :] = jnp.where(low_half, pair, 0.0).astype(bf16)
        key1[rows, :] = jnp.where(low_half, 0.0, pltpu.roll(pair, 64, 1)).astype(bf16)
        value[rows, :] = jnp.where(low_half, jnp.where(lanes == 0, 1.0, 0.0), pair).astype(bf16)

    def block(i, carry):
        j = lax.rem(me + 1 + i, 8)
        query = (heads[j, :, 0:128].astype(f32) * (1.0 / 8.0)).astype(bf16)
        results = []
        for key in (key0, key1):
            total = jnp.zeros((TOKENS, 128), f32)
            for c in range(4):
                part = pl.ds(c * 512, 512)
                weights = jnp.exp(dot_t(query, key[part, :]))
                total = total + dot(weights.astype(bf16), value[part, :])
            results.append(total)
        sum0, sum1 = results[0][:, 0:1], results[1][:, 0:1]
        full = jnp.where(low_half, pltpu.roll(results[0] / sum0, 64, 1), results[1] / sum1)
        rows = pl.ds(pl.multiple_of(j * TOKENS, TOKENS), TOKENS)
        full_ref[rows, :] = full
        logs_ref[rows, :] = jnp.where(low_half, jnp.log(sum0), jnp.log(sum1))
        out_buf[j] = full.astype(bf16)

        @pl.when(i < 7)
        def _():
            answer(i).start()

        return carry

    columns = pl.ds(pl.multiple_of(me * 128, 128), 128)

    def answer(i):
        j = lax.rem(me + 1 + i, 8)
        return pltpu.make_async_remote_copy(
            src_ref=out_buf.at[j], dst_ref=att.at[:, columns], send_sem=send_sems.at[7 + i],
            recv_sem=recv_sems.at[7 + i], device_id={"seq": j}, device_id_type=MESH,
        )

    lax.fori_loop(0, 8, block, 0)
    att[:, columns] = out_buf[me]
    for k in (3, 4):
        loads[k].wait()
    for i in range(7):
        answer(i).wait_recv()
    attended = att[...]
    att_ref[...] = attended
    squares = jnp.zeros((TOKENS, 1), f32)
    for h in range(2):
        part = slice(512 * h, 512 * (h + 1))
        after = x_ref[:, part].astype(f32) + dot(attended, wo[h])
        after_ref[:, part] = after
        squares = squares + jnp.sum(after * after, axis=1, keepdims=True)
    scaling = lax.rsqrt(squares * (1.0 / D) + epsilon)
    normed = (after_ref[...] * scaling * small_t[33:34, :].astype(f32)).astype(bf16)
    normed_ref[...] = normed
    logits = dot(normed, small[...])
    named = jnp.zeros((TOKENS, 128), f32)
    for k in range(TOPK):
        named = jnp.where(routes_ref[:, k : k + 1] == lanes, 1.0, named)
    peak = jnp.max(jnp.where(named > 0.0, logits, -1e30), axis=1, keepdims=True)
    chosen = jnp.where(named > 0.0, jnp.exp(logits - peak), 0.0)
    gates_ref[...] = chosen / jnp.sum(chosen, axis=1, keepdims=True)
    save.wait()
    for i in range(7):
        answer(i).wait_send()
    net.finish()


def front(x, whole, routes, cos, sin):
    vmem = pl.BlockSpec(memory_space=pltpu.VMEM)
    hbm = pl.BlockSpec(memory_space=pl.ANY)
    return pl.pallas_call(
        front_kernel,
        in_specs=[vmem, hbm, vmem, vmem, vmem],
        out_specs=[hbm] + [vmem] * 8,
        out_shape=[
            jax.ShapeDtypeStruct((8, TOKENS, 256), bf16),
            jax.ShapeDtypeStruct((LENGTH, 128), f32),
            jax.ShapeDtypeStruct((LENGTH, 128), f32),
            jax.ShapeDtypeStruct((TOKENS, D), bf16),
            jax.ShapeDtypeStruct((TOKENS, D), f32),
            jax.ShapeDtypeStruct((TOKENS, D), bf16),
            jax.ShapeDtypeStruct((TOKENS, 128), f32),
            jax.ShapeDtypeStruct((128, D), bf16),
            jax.ShapeDtypeStruct((TOKENS, 1536), f32),
        ],
        scratch_shapes=[
            pltpu.VMEM((D, 1024), bf16),
            pltpu.VMEM((D, 1024), bf16),
            pltpu.VMEM((2, D, 512), bf16),
            pltpu.VMEM((D, 128), bf16),
            pltpu.VMEM((8, TOKENS, 256), bf16),
            pltpu.VMEM((8, TOKENS, 256), bf16),
            pltpu.VMEM((8, TOKENS, 128), bf16),
            pltpu.VMEM((TOKENS, D), bf16),
            pltpu.VMEM((LENGTH, 128), bf16),
            pltpu.VMEM((LENGTH, 128), bf16),
            pltpu.VMEM((LENGTH, 128), bf16),
            pltpu.SemaphoreType.DMA((6,)),
            pltpu.SemaphoreType.DMA((14,)),
            pltpu.SemaphoreType.DMA((14,)),
        ],
        compiler_params=pltpu.CompilerParams(collective_id=2, has_side_effects=True, vmem_limit_bytes=VMEM),
        cost_estimate=pl.CostEstimate(
            flops=4 * 10**9, bytes_accessed=16 << 20, transcendentals=2 * LENGTH * LENGTH
        ),
        name="front",
    )(x, whole, routes, cos, sin)


def split3(values):
    high = values.astype(bf16).astype(f32)
    rest = values - high
    middle = rest.astype(bf16).astype(f32)
    return high, middle, rest - middle


def with_terms(lanes, start, parts):
    high, middle, low = parts
    return jnp.where(
        lanes == start,
        high,
        jnp.where(lanes == start + 1, middle, jnp.where(lanes == start + 2, low, 0.0)),
    )


def back_kernel(
    row_ref, gate_sum_ref, gates_ref, after_ref, x_ref, cot_ref, att_ref, normed_ref, small_t_ref, raw_ref,
    heads_ref, full_ref, logs_ref, cos_ref, sin_ref, w_ref, y_ref,
    layer_ref, token_ref, parts_ref, small_ref,
    wq, wkv, wo, send, grads, dq_buf, dkv_buf, back_q, back_kv, pg_q, pg_kv, after_grad,
    key0, key1, value0, value1, key_t, dk_total, dv_total,
    slots, sib_in, hop_in, local_sems, send_sems, recv_sems,
):
    here = Place()
    me = here.seq
    sib = here.sibling()
    way = here.plane("fsdp")
    loads = [
        pltpu.make_async_copy(w_ref.at[h, :, pl.ds(start, width)], there, local_sems.at[k])
        for k, (h, start, width, there) in enumerate(
            ((0, 1024, 512, wo.at[0]), (1, 1024, 512, wo.at[1]), (0, 0, 1024, wq), (1, 0, 1024, wkv))
        )
    ]
    for copy in loads:
        copy.start()
    order = (6, 7, 3, 5, 2, 4, 1, 0)
    y_loads = {k: pltpu.make_async_copy(y_ref.at[2 * k], slots.at[k], local_sems.at[4 + k]) for k in order}
    for copy in y_loads.values():
        copy.start()
    peers = [here.seq_at(*other) for other in OTHERS]
    meet([sib, *way.values()] + [{"seq": peer} for peer in peers])
    net = Copies(send_sems, recv_sems)
    joins = {k: net.start(y_ref.at[2 * k + 1], sib_in.at[k], sib) for k in order}
    lanes, low_half = lane_halves()

    gate_sum = gate_sum_ref[...]
    gate_grad = gate_sum + pltpu.roll(gate_sum, 96, 1)
    gates = gates_ref[...]
    gate_grad = jnp.where(lanes < EXPERTS, gate_grad, 0.0)
    chosen = gates * (gate_grad - jnp.sum(gates * gate_grad, axis=1, keepdims=True))
    logits_grad = chosen.astype(bf16)
    normed_grad = row_ref[...] + dot(logits_grad, small_t_ref[...])
    after = after_ref[...]
    scaling = row_scale(after)
    weighted = normed_grad * small_t_ref[33:34, :].astype(f32)
    middle = jnp.mean(weighted * after, axis=1, keepdims=True)
    total = cot_ref[...].astype(f32) + scaling * weighted - after * (scaling * scaling * scaling * middle)
    after_grad[...] = total
    after_low = total.astype(bf16)
    ffn_gain = jnp.sum(normed_grad * after * scaling, axis=0, keepdims=True)
    for k in (0, 1):
        loads[k].wait()
    for q in range(2):
        rows = slice(512 * q, 512 * (q + 1))
        attended_grad = dot_t(after_low[:, 0:512], wo[0, rows, :]) + dot_t(after_low[:, 512:1024], wo[1, rows, :])
        for h in range(4):
            send[4 * q + h] = attended_grad[:, 128 * h : 128 * (h + 1)].astype(bf16)
    to_heads = [net.start(send.at[peer], grads.at[me], {"seq": peer}) for peer in peers]
    grads[me] = send[me]
    small_ref[...] = t_dot(normed_ref[...], logits_grad)
    for h in range(2):
        parts_ref[h, :, 1024:1536] = t_dot(att_ref[...], after_low[:, 512 * h : 512 * (h + 1)]).astype(bf16)

    def add_to(ref, *values):
        result = ref[...].astype(f32)
        for value in values:
            result = result + value[...].astype(f32)
        ref[...] = result.astype(bf16)

    def join(k):
        y_loads[k].wait()
        joins[k].wait_recv()
        add_to(slots.at[k], sib_in.at[k])

    def half(ref, which):
        return ref.at[pl.ds(128 * which, 128)]

    def expert_sum():
        join(6)
        join(7)
        up = [net.start(half(slots.at[6 + j], 0), half(hop_in.at[j], 0), way["up"]) for j in range(2)]
        down = [net.start(half(slots.at[6 + j], 1), half(hop_in.at[j], 1), way["down"]) for j in range(2)]
        yield
        for k in (3, 5, 2, 4):
            join(k)
        up[1].wait_recv()
        down[1].wait_recv()
        add_to(half(slots.at[5], 0), half(hop_in.at[1], 0))
        add_to(half(slots.at[3], 1), half(hop_in.at[1], 1))
        beside = [
            net.start(slots.at[5], hop_in.at[2], way["up"]), net.start(slots.at[3], hop_in.at[3], way["down"])
        ]
        up[0].wait_recv()
        down[0].wait_recv()
        add_to(half(slots.at[4], 0), half(hop_in.at[0], 0))
        add_to(half(slots.at[2], 1), half(hop_in.at[0], 1))
        own = [
            net.start(slots.at[4], hop_in.at[4], way["up"]), net.start(slots.at[2], hop_in.at[5], way["down"])
        ]
        yield
        join(1)
        join(0)
        for copy in beside:
            copy.wait_recv()
        add_to(slots.at[1], hop_in.at[2], hop_in.at[3])
        own.append(net.start(slots.at[1], hop_in.at[6], way["across"]))
        yield
        for copy in own:
            copy.wait_recv()
        layer_ref[...] = (
            after_ref[...]
            + slots[0].astype(f32)
            + hop_in[4].astype(f32)
            + hop_in[5].astype(f32)
            + hop_in[6].astype(f32)
        ).astype(bf16)

    moves = expert_sum()
    next(moves)
    ones_high = jnp.where((lanes >= 64) & (lanes < 67), 1.0, 0.0)
    ones_low = jnp.where(lanes < 3, 1.0, 0.0)
    for c in range(8):
        rows = slice(TOKENS * c, TOKENS * (c + 1))
        pair = heads_ref[c, :, 128:256].astype(f32)
        swapped = pltpu.roll(pair, 64, 1)
        key0[rows, :] = jnp.where(low_half, pair, ones_high).astype(bf16)
        key1[rows, :] = jnp.where(low_half, ones_low, swapped).astype(bf16)
        value0[rows, :] = jnp.where(low_half, swapped, ones_high).astype(bf16)
        value1[rows, :] = jnp.where(low_half, ones_low, pair).astype(bf16)
        key_t[:, rows] = jnp.transpose(pair)[0:64, :].astype(bf16)
    dk_total[...] = jnp.zeros_like(dk_total)
    dv_total[...] = jnp.zeros_like(dv_total)
    for copy in to_heads:
        copy.wait_recv()
    columns = pl.ds(pl.multiple_of(me * 128, 128), 128)

    def answer(i):
        j = lax.rem(me + 1 + i, 8)
        return pltpu.make_async_remote_copy(
            src_ref=dq_buf.at[j], dst_ref=back_q.at[:, columns], send_sem=send_sems.at[32 + i],
            recv_sem=recv_sems.at[32 + i], device_id={"seq": j}, device_id_type=MESH,
        )

    def block(i, carry):
        j = lax.rem(me + 1 + i, 8)
        rows = pl.ds(pl.multiple_of(j * TOKENS, TOKENS), TOKENS)
        query = heads_ref[j, :, 0:128].astype(f32) * (1.0 / 8.0)
        grad = grads[j].astype(f32)
        logs = logs_ref[rows, :]
        product = grad * full_ref[rows, :]
        delta0 = jnp.sum(jnp.where(low_half, product, 0.0), axis=1, keepdims=True)
        delta1 = jnp.sum(jnp.where(low_half, 0.0, product), axis=1, keepdims=True)
        query0 = jnp.where(low_half, query, with_terms(lanes, 64, split3(-logs[:, 0:1]))).astype(bf16)
        query1 = jnp.where(low_half, with_terms(lanes, 0, split3(-logs[:, 64:65])), query).astype(bf16)
        grad0 = jnp.where(low_half, grad, with_terms(lanes, 64, split3(-delta0))).astype(bf16)
        grad1 = jnp.where(low_half, with_terms(lanes, 0, split3(-delta1)), grad).astype(bf16)
        only_query = (
            jnp.where(low_half, query, 0.0).astype(bf16), jnp.where(low_half, 0.0, query).astype(bf16)
        )
        only_grad = (jnp.where(low_half, grad, 0.0).astype(bf16), jnp.where(low_half, 0.0, grad).astype(bf16))
        dq = [jnp.zeros((64, TOKENS), f32), jnp.zeros((64, TOKENS), f32)]
        for c in range(4):
            part = pl.ds(c * 512, 512)
            dv = dv_total[part, :]
            dk = dk_total[part, :]
            for h, (key, value, query_h, grad_h) in enumerate(
                ((key0, value0, query0, grad0), (key1, value1, query1, grad1))
            ):
                probs = jnp.exp(dot_t(key[part, :], query_h))
                inner = dot_t(value[part, :], grad_h)
                dv = dv + dot(probs.astype(bf16), only_grad[h])
                scores = (probs * inner).astype(bf16)
                dk = dk + dot(scores, only_query[h])
                dq[h] = dq[h] + dot(key_t[:, c * 512 : (c + 1) * 512], scores)
            dv_total[part, :] = dv
            dk_total[part, :] = dk
        both = jnp.concatenate(dq, axis=0) * (1.0 / 8.0)
        dq_buf[j] = jnp.transpose(both).astype(bf16)

        @pl.when(i < 7)
        def _():
            answer(i).start()

        return carry

    lax.fori_loop(0, 3, block, 0)
    next(moves)
    lax.fori_loop(3, 6, block, 0)
    next(moves)
    lax.fori_loop(6, 8, block, 0)
    for c in range(8):
        rows = slice(TOKENS * c, TOKENS * (c + 1))
        dk = dk_total[rows, :]
        dv = dv_total[rows, :]
        dk = dk + pltpu.roll(dk, 64, 1)
        dv = dv + pltpu.roll(dv, 64, 1)
        dkv_buf[c] = jnp.where(low_half, dk, dv).astype(bf16)
    to_tokens = [net.start(dkv_buf.at[peer], back_kv.at[me], {"seq": peer}) for peer in peers]
    back_kv[me] = dkv_buf[me]
    back_q[:, columns] = dq_buf[me]
    x = x_ref[...].astype(f32)
    x_scaling = row_scale(x)
    attn_gain = small_t_ref[32:33, :].astype(f32)
    normed = (x * x_scaling * attn_gain).astype(bf16)
    query_gain, key_gain = gain_tiles(small_t_ref[...], lanes)
    cos, sin = cos_ref[...], sin_ref[...]
    for i in range(7):
        answer(i).wait_recv()

    def unturned(grad, tile, gain):
        grad = grad * cos - partner(grad, lanes) * sin
        scale = lax.rsqrt(head_mean(tile * tile, low_half) + epsilon)
        weighted = grad * gain
        middle = head_mean(weighted * tile, low_half)
        result = scale * weighted - tile * (scale * scale * scale * middle)
        return result.astype(bf16), jnp.sum(grad * tile * scale, axis=0, keepdims=True)

    query_terms = jnp.zeros((1, 128), f32)
    for h in range(8):
        part = slice(128 * h, 128 * (h + 1))
        pg_q[:, part], terms = unturned(back_q[:, part].astype(f32), raw_ref[:, part], query_gain)
        query_terms = query_terms + terms
    for copy in loads[2:]:
        copy.wait()
    for r in range(4):
        part = slice(256 * r, 256 * (r + 1))
        parts_ref[0, part, 0:1024] = t_dot(normed[:, part], pg_q[...]).astype(bf16)
    normed_grad = dot_t(pg_q[...], wq[...])
    for copy in to_tokens:
        copy.wait_recv()
    key_terms = jnp.zeros((1, 128), f32)
    for j in range(4):
        first, second = back_kv[2 * j].astype(f32), back_kv[2 * j + 1].astype(f32)
        keys = jnp.where(low_half, first, pltpu.roll(second, 64, 1))
        values = jnp.where(low_half, pltpu.roll(first, 64, 1), second)
        part = slice(128 * j, 128 * (j + 1))
        pg_kv[:, part], terms = unturned(keys, raw_ref[:, 1024 + 128 * j : 1152 + 128 * j], key_gain)
        key_terms = key_terms + terms
        pg_kv[:, 512 + 128 * j : 640 + 128 * j] = values.astype(bf16)
    for r in range(4):
        part = slice(256 * r, 256 * (r + 1))
        parts_ref[1, part, 0:1024] = t_dot(normed[:, part], pg_kv[...]).astype(bf16)
    normed_grad = normed_grad + dot_t(pg_kv[...], wkv[...])
    weighted = normed_grad * attn_gain
    middle = jnp.mean(weighted * x, axis=1, keepdims=True)
    token_ref[...] = after_grad[...] + x_scaling * weighted - x * (x_scaling * x_scaling * x_scaling * middle)
    attn_gain_grad = jnp.sum(normed_grad * x * x_scaling, axis=0, keepdims=True)
    query_terms = query_terms + pltpu.roll(query_terms, 64, 1)
    key_terms = key_terms + pltpu.roll(key_terms, 64, 1)
    head_terms = jnp.where(low_half, query_terms, key_terms)
    spread = (
        8 * lax.broadcasted_iota(jnp.int32, (128, D), 0) == lax.broadcasted_iota(jnp.int32, (128, D), 1)
    ).astype(f32).astype(bf16)
    head_row = jnp.zeros((1, D), f32)
    for term in split3(head_terms):
        head_row = head_row + dot(jnp.broadcast_to(term, (16, 128)).astype(bf16), spread)[0:1, :]
    row = lax.broadcasted_iota(jnp.int32, (128, D), 0)
    gain_rows = jnp.where(
        row == 32, attn_gain_grad, jnp.where(row == 33, ffn_gain, jnp.where(row == 34, head_row, 0.0))
    )
    small_ref[...] = small_ref[...] + jnp.transpose(gain_rows)
    for _ in moves:
        pass
    for i in range(7):
        answer(i).wait_send()
    net.finish()


def back(*operands):
    vmem = pl.BlockSpec(memory_space=pltpu.VMEM)
    hbm = pl.BlockSpec(memory_space=pl.ANY)
    return pl.pallas_call(
        back_kernel,
        in_specs=[vmem] * 15 + [hbm] * 2,
        out_specs=[vmem] * 4,
        out_shape=[
            jax.ShapeDtypeStruct((TOKENS, D), bf16),
            jax.ShapeDtypeStruct((TOKENS, D), f32),
            jax.ShapeDtypeStruct((2, D, 1536), bf16),
            jax.ShapeDtypeStruct((D, 128), f32),
        ],
        scratch_shapes=[
            pltpu.VMEM((D, 1024), bf16),
            pltpu.VMEM((D, 1024), bf16),
            pltpu.VMEM((2, D, 512), bf16),
            pltpu.VMEM((8, TOKENS, 128), bf16),
            pltpu.VMEM((8, TOKENS, 128), bf16),
            pltpu.VMEM((8, TOKENS, 128), bf16),
            pltpu.VMEM((8, TOKENS, 128), bf16),
            pltpu.VMEM((TOKENS, D), bf16),
            pltpu.VMEM((8, TOKENS, 128), bf16),
            pltpu.VMEM((TOKENS, D), bf16),
            pltpu.VMEM((TOKENS, D), bf16),
            pltpu.VMEM((TOKENS, D), f32),
        ]
        + [pltpu.VMEM((LENGTH, 128), bf16)] * 4
        + [pltpu.VMEM((64, LENGTH), bf16)]
        + [pltpu.VMEM((LENGTH, 128), f32)] * 2
        + [pltpu.VMEM((8, TOKENS, D), bf16)] * 2
        + [pltpu.VMEM((7, TOKENS, D), bf16)]
        + [
            pltpu.SemaphoreType.DMA((12,)),
            pltpu.SemaphoreType.DMA((40,)),
            pltpu.SemaphoreType.DMA((40,)),
        ],
        compiler_params=pltpu.CompilerParams(collective_id=5, has_side_effects=True, vmem_limit_bytes=VMEM),
        cost_estimate=pl.CostEstimate(
            flops=9 * 10**9, bytes_accessed=32 << 20, transcendentals=2 * LENGTH * LENGTH
        ),
        name="back",
    )(*operands)


def gather_kernel(in_ref, mask_ref, out_ref, masks_out, stage, block, local_sems, send_sems, recv_sems):
    here = Place()
    c, s, f = here.core, here.seq, here.z * 2 + here.xh
    sib = here.sibling()
    ways = {"seq": here.plane("seq"), "fsdp": here.plane("fsdp")}
    others = [(2, 1), (2, 0), (0, 1), (1, 1), (-1, 1), (1, 0), (-1, 0)]

    def f_at(ring, pair):
        return lax.rem(here.z + ring + 4, 4) * 2 + (1 - here.xh if pair else here.xh)

    seq_peers = [{"seq": here.seq_at(ring, pair)} for ring, pair in others]
    fsdp_peers = [{"fsdp": here.fsdp_at(ring, pair)} for ring, pair in others]
    meet([sib, *seq_peers, *fsdp_peers])
    net = Copies(send_sems, recv_sems)
    rows = pl.ds(pl.multiple_of(8 * c, 8), 8)
    join = net.start(in_ref.at[1 - c], stage.at[rows], sib)
    stage[rows, :] = in_ref[c]
    join.wait_recv()
    block[...] = stage[...].astype(bf16)
    low, high = pl.ds(0, 896), pl.ds(896, 768)
    locals_ = [
        pltpu.make_async_copy(block, out_ref.at[c, s, f], local_sems.at[0]),
        pltpu.make_async_copy(mask_ref, masks_out.at[here.fsdp], local_sems.at[1]),
    ]
    for copy in locals_:
        copy.start()
    a = [net.start(block.at[:, low], out_ref.at[c, s, f, :, low], peer) for peer in fsdp_peers]
    b = [net.start(block.at[:, high], out_ref.at[c, s, f, :, high], peer) for peer in seq_peers]
    m = [net.start(mask_ref, masks_out.at[here.fsdp], peer) for peer in [sib, *fsdp_peers]]
    for copy in locals_:
        copy.wait()
    kin = []

    def plane(part, way):
        def half(ref, which):
            return ref.at[pl.ds(4 * which, 4)]

        def go(ref, target):
            return net.start(ref, ref, target)

        ref = part(0, 0)
        across, up, down = go(ref, way["across"]), go(ref, way["up"]), go(ref, way["down"])
        kin.append(go(ref, sib))
        yield
        up.wait_recv()
        ref = part(-1, 0)
        far_low = go(half(ref, 0), way["up"])
        kin.append(go(ref, sib))
        down.wait_recv()
        ref = part(1, 0)
        far_high = go(half(ref, 1), way["down"])
        kin.append(go(ref, sib))
        yield
        across.wait_recv()
        ref = part(0, 1)
        up, down = go(ref, way["up"]), go(ref, way["down"])
        kin.append(go(ref, sib))
        yield
        far_low.wait_recv()
        far_high.wait_recv()
        kin.append(go(part(2, 0), sib))
        up.wait_recv()
        ref = part(-1, 1)
        far_low = go(half(ref, 0), way["up"])
        kin.append(go(ref, sib))
        down.wait_recv()
        ref = part(1, 1)
        far_high = go(half(ref, 1), way["down"])
        kin.append(go(ref, sib))
        yield
        far_low.wait_recv()
        far_high.wait_recv()
        kin.append(go(part(2, 1), sib))

    for copy in a:
        copy.wait_recv()
    first = plane(lambda ring, pair: out_ref.at[c, here.seq_at(ring, pair), :, :, low], ways["seq"])
    next(first)
    for copy in b:
        copy.wait_recv()
    second = plane(lambda ring, pair: out_ref.at[c, :, f_at(ring, pair), :, high], ways["fsdp"])
    next(second)
    for i in range(8):
        m[i].wait_recv()
        if i:
            ring, pair = others[i - 1]
            ref = masks_out.at[here.fsdp_at(-ring, pair)]
            kin.append(net.start(ref, ref, sib))
    for _ in range(4):
        next(first, None)
        next(second, None)
    for copy in kin:
        copy.wait_recv()
    net.finish()


def gather_weights(halves, mask):
    n = 64
    return pl.pallas_call(
        gather_kernel,
        in_specs=[pl.BlockSpec(memory_space=pltpu.VMEM)] * 2,
        out_specs=[pl.BlockSpec(memory_space=pl.ANY)] * 2,
        out_shape=[
            jax.ShapeDtypeStruct((2, 8, 8, 16, WCOLS), bf16),
            jax.ShapeDtypeStruct((16, 32, 256), bf16),
        ],
        scratch_shapes=[
            pltpu.VMEM((16, WCOLS), f32),
            pltpu.VMEM((16, WCOLS), bf16),
            pltpu.SemaphoreType.DMA((2,)),
            pltpu.SemaphoreType.DMA((n,)),
            pltpu.SemaphoreType.DMA((n,)),
        ],
        compiler_params=pltpu.CompilerParams(collective_id=1, has_side_effects=True, vmem_limit_bytes=VMEM),
        name="gather_weights",
    )(halves, mask)


def moe_kernel(
    x_ref, g_ref, masks_ref, router_ref, up_hbm, down_hbm,
    row_out, gate_out, y_out, grads_out,
    slots, sib_in, hop_in, g_rows, up_ref, down_ref,
    rows_x, rows_p, rows_h, rows_u, rows_g, slot_gate, places, stage_y, stage_r, y_stage, w_stage,
    local_sems, send_sems, recv_sems,
):
    here = Place()
    sib = here.sibling()
    way = here.plane("fsdp")
    own = here.fsdp
    counter = [0]

    def local(src, dst):
        copy = pltpu.make_async_copy(src, dst, local_sems.at[counter[0]])
        counter[0] += 1
        copy.start()
        return copy

    first_x = local(x_ref, slots.at[0, :, pl.ds(0, D)])
    weights = [local(up_hbm, up_ref), local(down_hbm, down_ref)]

    def source(k):
        ring, pair, c = (0, -1, 1, 2)[k // 4], (k // 2) % 2, k % 2
        z = lax.rem(here.z + ring + 4, 4)
        xh = 1 - here.xh if pair else here.xh
        return z * 4 + xh * 2 + (1 - here.core if c else here.core)

    def fetch_g(group):
        return [local(g_ref.at[source(4 * group + s)], g_rows.at[s]) for s in range(4)]

    g_copies = fetch_g(0)
    meet([sib, *way.values()])
    net = Copies(send_sems, recv_sems)

    def block(k, low=0, rows=TOKENS):
        return slots.at[k, pl.ds(low, rows), pl.ds(0, D)]

    sent = {k: [] for k in range(16)}

    def push(k, to, target, low=0, rows=TOKENS, src=None):
        copy = net.start(block(k, low, rows) if src is None else src, block(to, low, rows), target)
        sent[k].append(copy)
        return copy

    across = push(0, 2, way["across"], src=x_ref)
    up = push(0, 4, way["up"], src=x_ref)
    down = push(0, 8, way["down"], src=x_ref)
    kin = {1: push(0, 1, sib, src=x_ref)}
    across.wait_recv()
    up_x = push(2, 6, way["up"])
    down_x = push(2, 10, way["down"])
    kin[3] = push(2, 3, sib)
    state = {}

    lanes = lax.broadcasted_iota(jnp.int32, (1, 128), 1)
    slot = lax.broadcasted_iota(jnp.int32, (2 * SLOTS, TOKENS), 0)
    slot_place = slot.astype(f32)
    first = slot < SLOTS
    expert = lax.broadcasted_iota(jnp.int32, (EXPERTS, TOKENS), 0)

    def gather(group):
        before = (
            lax.broadcasted_iota(jnp.int32, (TOKENS, TOKENS), 0)
            < lax.broadcasted_iota(jnp.int32, (TOKENS, TOKENS), 1)
        ).astype(f32).astype(bf16)
        for s in range(4):
            k = 4 * group + s
            if k in kin:
                kin[k].wait_recv()
            g_copies[s].wait()
            x_rows = slots[k, :, 0:D]
            named = masks_ref[source(k)].astype(f32)
            logits = dot_t(router_ref[...], x_rows)
            peak = jnp.max(jnp.where(named > 0.0, logits, -1e30), axis=0, keepdims=True)
            parts = jnp.where(named > 0.0, jnp.exp(logits - peak), 0.0)
            gates = parts / jnp.sum(parts, axis=0, keepdims=True)
            rank = dot(named.astype(bf16), before)
            rank = jnp.where(named > 0.0, rank, -1000.0)

            def mine(values, i):
                return jnp.sum(jnp.where(expert == 2 * own + i, values, 0.0), axis=0, keepdims=True)

            wanted = jnp.where(first, mine(rank, 0), mine(rank, 1) + SLOTS)
            hot = jnp.where(slot_place == wanted, 1.0, 0.0)
            gate = jnp.sum(hot * jnp.where(first, mine(gates, 0), mine(gates, 1)), axis=1, keepdims=True)
            hot = hot.astype(bf16)
            places[s] = hot
            picked = dot(hot, x_rows).astype(bf16)
            grads = dot(hot, g_rows[s])
            pair = (grads * gate).astype(bf16)
            grads = grads.astype(bf16)
            for i in range(2):
                part = slice(SLOTS * i, SLOTS * (i + 1))
                there = slice(group * GROUP_ROWS + SLOTS * s, group * GROUP_ROWS + SLOTS * (s + 1))
                rows_x[i, there, :] = picked[part]
                rows_p[i, there, :] = pair[part]
                rows_g[i, SLOTS * s : SLOTS * (s + 1), :] = grads[part]
                slot_gate[i, SLOTS * s : SLOTS * (s + 1), :] = jnp.broadcast_to(gate[part], (SLOTS, 128))

    def run(group):
        here_rows = pl.ds(group * GROUP_ROWS, GROUP_ROWS)

        def one(e, carry):
            x_rows = rows_x[e, here_rows, :]
            gate_part = dot(x_rows, up_ref[e, :, 0:F])
            up_part = dot(x_rows, up_ref[e, :, F : 2 * F])
            sigmoid = 1.0 / (1.0 + jnp.exp(-gate_part))
            silu = gate_part * sigmoid
            hidden = (silu * up_part).astype(bf16)
            rows_h[e, here_rows, :] = hidden
            hidden_grad = dot(rows_p[e, here_rows, :], down_ref[e])
            slope = sigmoid * (1.0 + gate_part * (1.0 - sigmoid))
            rows_u[e, here_rows, 0:F] = (hidden_grad * up_part * slope).astype(bf16)
            rows_u[e, here_rows, F : 2 * F] = (hidden_grad * silu).astype(bf16)
            out = dot_t(hidden, down_ref[e]).astype(bf16).astype(f32)
            gate_grad = jnp.sum(out * rows_g[e].astype(f32), axis=1, keepdims=True)
            stage_y[e] = (out * slot_gate[e][:, 0:1]).astype(bf16)
            stage_r[e, :, 0:D] = dot_t(rows_u[e, here_rows, :], up_ref[e]).astype(bf16)
            high = gate_grad.astype(bf16).astype(f32)
            column = 2 * own + e
            stage_r[e, :, D:WIDE] = jnp.where(
                lanes == column, high, jnp.where(lanes == column + EXPERTS, gate_grad - high, 0.0)
            ).astype(bf16)
            return carry

        lax.fori_loop(0, 2, one, 0)

    def combine(group):
        for copy in state.pop("y", ()):
            copy.wait()
        for s in range(4):
            k = 4 * group + s
            for copy in sent[k]:
                copy.wait_send()
            part = slice(SLOTS * s, SLOTS * (s + 1))
            both = jnp.concatenate([stage_y[0, part, :], stage_y[1, part, :]], axis=0)
            y_stage[s] = t_dot(places[s], both).astype(bf16)
            both = jnp.concatenate([stage_r[0, part, :], stage_r[1, part, :]], axis=0)
            slots[k] = t_dot(places[s], both).astype(bf16)
        state["y"] = [local(y_stage.at[s], y_out.at[4 * group + s]) for s in range(4)]
        for j in range(2):
            k = 4 * group + 2 * j
            state["k", group, j] = net.start(slots.at[k + 1], sib_in.at[2 * group + j], sib)

    def join(group, j):
        state["k", group, j].wait_recv()
        k = 4 * group + 2 * j
        slots[k] = (slots[k].astype(f32) + sib_in[2 * group + j].astype(f32)).astype(bf16)

    first_x.wait()
    gather(0)
    g_copies = fetch_g(1)
    for copy in weights:
        copy.wait()
    up.wait_recv()
    far_low = push(4, 12, way["up"], 0, 128)
    kin[5] = push(4, 5, sib)
    down.wait_recv()
    far_high = push(8, 12, way["down"], 128, 128)
    kin[9] = push(8, 9, sib)
    run(0)
    up_x.wait_recv()
    kin[7] = push(6, 7, sib)
    down_x.wait_recv()
    kin[11] = push(10, 11, sib)
    combine(0)
    far_low.wait_recv()
    far_high.wait_recv()
    far_x = push(12, 14, way["across"])
    kin[13] = push(12, 13, sib)
    gather(1)
    g_copies = fetch_g(3)
    run(1)
    far_x.wait_recv()
    kin[15] = push(14, 15, sib)
    combine(1)
    gather(3)
    g_copies = fetch_g(2)
    run(3)
    combine(3)
    gather(2)
    join(3, 1)
    hop_a = net.start(slots.at[14], hop_in.at[0], way["across"])
    join(3, 0)
    run(2)
    hop_a.wait_recv()
    slots[12] = (slots[12].astype(f32) + hop_in[0].astype(f32)).astype(bf16)
    hop_u = net.start(slots.at[12, pl.ds(0, 128)], hop_in.at[1, pl.ds(0, 128)], way["up"])
    hop_d = net.start(slots.at[12, pl.ds(128, 128)], hop_in.at[1, pl.ds(128, 128)], way["down"])
    combine(2)

    w_copies = [[], []]

    def weight_grad(piece):
        e, dx = piece // 2, piece % 2
        buffer = 0
        for copy in w_copies[buffer]:
            copy.wait()
        xl = 1 - here.xl if dx else here.xl
        columns = pl.ds(pl.multiple_of(xl * 512, 512), 512)
        w_stage[buffer, :, 0 : 2 * F] = t_dot(rows_x[e, :, columns], rows_u[e]).astype(bf16)
        w_stage[buffer, :, 2 * F : 3 * F] = t_dot(rows_p[e, :, columns], rows_h[e]).astype(bf16)
        w_copies[buffer] = [
            local(
                w_stage.at[buffer, pl.ds(128 * y, 128)],
                grads_out.at[e, pl.ds(pl.multiple_of(xl * 512 + 128 * y, 128), 128)],
            )
            for y in range(4)
        ]

    join(1, 1)
    hop_xd = net.start(slots.at[6], hop_in.at[2], way["down"])
    join(2, 1)
    hop_xu = net.start(slots.at[10], hop_in.at[3], way["up"])
    join(1, 0)
    join(2, 0)
    weight_grad(0)
    hop_u.wait_recv()
    slots[8, 0:128, :] = (slots[8, 0:128, :].astype(f32) + hop_in[1, 0:128, :].astype(f32)).astype(bf16)
    hop_ru = net.start(slots.at[8], hop_in.at[4], way["up"])
    hop_d.wait_recv()
    slots[4, 128:256, :] = (slots[4, 128:256, :].astype(f32) + hop_in[1, 128:256, :].astype(f32)).astype(bf16)
    hop_rd = net.start(slots.at[4], hop_in.at[5], way["down"])
    join(0, 1)
    join(0, 0)
    weight_grad(1)
    hop_xd.wait_recv()
    hop_xu.wait_recv()
    slots[2] = (slots[2].astype(f32) + hop_in[2].astype(f32) + hop_in[3].astype(f32)).astype(bf16)
    hop_rx = net.start(slots.at[2], hop_in.at[6], way["across"])
    weight_grad(2)
    weight_grad(3)
    hop_ru.wait_recv()
    hop_rd.wait_recv()
    hop_rx.wait_recv()
    total = (
        slots[0].astype(f32) + hop_in[4].astype(f32) + hop_in[5].astype(f32) + hop_in[6].astype(f32)
    )
    row_out[...] = total[:, 0:D]
    gate_out[...] = total[:, D:WIDE]
    for copies in (*w_copies, state["y"]):
        for copy in copies:
            copy.wait()
    waited = {id(copy) for k in range(16) for copy in sent[k]}
    for copy in net.all:
        if id(copy) not in waited:
            copy.wait_send()


def moe(x, g_all, masks, router_t, up, down):
    any_space = pl.BlockSpec(memory_space=pl.ANY)
    vmem = pl.BlockSpec(memory_space=pltpu.VMEM)
    return pl.pallas_call(
        moe_kernel,
        in_specs=[any_space, any_space, vmem, vmem, any_space, any_space],
        out_specs=[vmem, vmem, any_space, any_space],
        out_shape=[
            jax.ShapeDtypeStruct((TOKENS, D), f32),
            jax.ShapeDtypeStruct((TOKENS, 128), f32),
            jax.ShapeDtypeStruct((16, TOKENS, D), bf16),
            jax.ShapeDtypeStruct((2, D, 3 * F), bf16),
        ],
        scratch_shapes=[
            pltpu.VMEM((16, TOKENS, WIDE), bf16),
            pltpu.VMEM((8, TOKENS, WIDE), bf16),
            pltpu.VMEM((7, TOKENS, WIDE), bf16),
            pltpu.VMEM((4, TOKENS, D), bf16),
            pltpu.VMEM((2, D, 2 * F), bf16),
            pltpu.VMEM((2, D, F), bf16),
            pltpu.VMEM((2, ROWS, D), bf16),
            pltpu.VMEM((2, ROWS, D), bf16),
            pltpu.VMEM((2, ROWS, F), bf16),
            pltpu.VMEM((2, ROWS, 2 * F), bf16),
            pltpu.VMEM((2, GROUP_ROWS, D), bf16),
            pltpu.VMEM((2, GROUP_ROWS, 128), f32),
            pltpu.VMEM((4, 2 * SLOTS, TOKENS), bf16),
            pltpu.VMEM((2, GROUP_ROWS, D), bf16),
            pltpu.VMEM((2, GROUP_ROWS, WIDE), bf16),
            pltpu.VMEM((4, TOKENS, D), bf16),
            pltpu.VMEM((1, 512, 3 * F), bf16),
            pltpu.SemaphoreType.DMA((56,)),
            pltpu.SemaphoreType.DMA((40,)),
            pltpu.SemaphoreType.DMA((40,)),
        ],
        compiler_params=pltpu.CompilerParams(
            collective_id=4, has_side_effects=True, vmem_limit_bytes=63 * 1024 * 1024
        ),
        cost_estimate=pl.CostEstimate(flops=32 * 10**9, bytes_accessed=40 << 20, transcendentals=1 << 21),
        name="moe",
    )(x, g_all, masks, router_t, up, down)
def reduce_kernel(
    parts_ref, small_ref, out_ref, small_out,
    acc, sib_in, small_acc, small_sib, hop_a, hop_b, late_a, late_b, small_s, small_f, total, local_sems,
    send_sems, recv_sems,
):
    here = Place()
    c, s = here.core, here.seq
    f = here.z * 2 + here.xh
    sib = here.sibling()
    ways = {"seq": here.plane("seq"), "fsdp": here.plane("fsdp")}
    others = [(2, 1), (2, 0), (0, 1), (1, 1), (-1, 1), (1, 0), (-1, 0)]

    def f_at(ring, pair):
        return lax.rem(here.z + ring + 4, 4) * 2 + (1 - here.xh if pair else here.xh)

    seq_peers = [{"seq": here.seq_at(ring, pair)} for ring, pair in others]
    fsdp_peers = [{"fsdp": here.fsdp_at(ring, pair)} for ring, pair in others]
    own = pltpu.make_async_copy(parts_ref.at[c], acc, local_sems.at[0])
    own.start()
    meet([sib, *seq_peers, *fsdp_peers])
    net = Copies(send_sems, recv_sems)
    joins = [
        net.start(parts_ref.at[1 - c, pl.ds(2 * i, 2)], sib_in.at[pl.ds(2 * i, 2)], sib) for i in range(4)
    ]
    small_join = net.start(small_ref.at[:, :, 1 - c], small_sib, sib)
    own.wait()
    small_join.wait_recv()
    small_acc[...] = small_ref[:, :, c] + small_sib[...]
    small_copies = [
        net.start(small_acc.at[here.seq_at(*others[i])], small_s.at[i], seq_peers[i]) for i in range(7)
    ]
    for i in range(4):
        joins[i].wait_recv()
        part = slice(2 * i, 2 * i + 2)
        acc[part] = (acc[part].astype(f32) + sib_in[part].astype(f32)).astype(bf16)

    def add_to(ref, *values):
        result = ref[...].astype(f32)
        for value in values:
            result = result + value[...].astype(f32)
        ref[...] = result.astype(bf16)

    def plane(part, hop, way):
        def half(ref, high):
            return ref.at[pl.ds(4 * high, 4)]

        a = net.start(part(2, 1), hop.at[0], way["across"])
        xd = net.start(part(-1, 1), hop.at[2], way["down"])
        xu = net.start(part(1, 1), hop.at[3], way["up"])
        yield
        a.wait_recv()
        add_to(part(2, 0), hop.at[0])
        u = net.start(half(part(2, 0), 0), half(hop.at[1], 0), way["up"])
        d = net.start(half(part(2, 0), 1), half(hop.at[1], 1), way["down"])
        yield
        xd.wait_recv()
        xu.wait_recv()
        add_to(part(0, 1), hop.at[2], hop.at[3])
        rx = net.start(part(0, 1), hop.at[6], way["across"])
        yield
        u.wait_recv()
        add_to(half(part(1, 0), 0), half(hop.at[1], 0))
        ru = net.start(part(1, 0), hop.at[4], way["up"])
        d.wait_recv()
        add_to(half(part(-1, 0), 1), half(hop.at[1], 1))
        rd = net.start(part(-1, 0), hop.at[5], way["down"])
        yield
        rx.wait_recv()
        ru.wait_recv()
        rd.wait_recv()
        add_to(part(0, 0), hop.at[4], hop.at[5], hop.at[6])

    low, high = pl.ds(0, GCOLS // 2), pl.ds(GCOLS // 2, GCOLS // 2)
    first = plane(lambda ring, pair: acc.at[here.seq_at(ring, pair), :, :, low], hop_a, ways["seq"])
    second = plane(lambda ring, pair: acc.at[:, f_at(ring, pair), :, high], hop_b, ways["fsdp"])
    for _ in range(4):
        next(first)
        next(second)
    for copy in small_copies:
        copy.wait_recv()
    mine = small_acc[s]
    for i in range(7):
        mine = mine + small_s[i]
    small_acc[s] = mine
    small_copies = [
        net.start(small_acc.at[s, f_at(*others[i])], small_f.at[i], fsdp_peers[i]) for i in range(7)
    ]
    next(first, None)
    a = [
        net.start(acc.at[s, f_at(*others[i]), :, low], late_a.at[i], fsdp_peers[i]) for i in range(7)
    ]
    next(second, None)
    b = [
        net.start(acc.at[here.seq_at(*others[i]), f, :, high], late_b.at[i], seq_peers[i]) for i in range(7)
    ]
    for copy in small_copies:
        copy.wait_recv()
    mine = small_acc[s, f]
    for i in range(7):
        mine = mine + small_f[i]
    small_out[...] = mine
    for cols, copies, late in ((slice(0, GCOLS // 2), a, late_a), (slice(GCOLS // 2, GCOLS), b, late_b)):
        for copy in copies:
            copy.wait_recv()
        result = acc[s, f, :, cols].astype(f32)
        for i in range(7):
            result = result + late[i].astype(f32)
        total[:, cols] = result
    theirs = pl.ds(pl.multiple_of(8 * (1 - c), 8), 8)
    last = net.start(total.at[theirs], out_ref.at[c], sib)
    out_ref[c] = total[pl.ds(pl.multiple_of(8 * c, 8), 8), :]
    last.wait_recv()
    net.finish()


def reduce_weights(parts, small):
    vmem = pl.BlockSpec(memory_space=pltpu.VMEM)
    n = 1 + 4 + 7 + 7 + 14 + 16 + 4
    return pl.pallas_call(
        reduce_kernel,
        in_specs=[pl.BlockSpec(memory_space=pl.ANY), vmem],
        out_specs=[vmem, vmem],
        out_shape=[jax.ShapeDtypeStruct((2, 8, GCOLS), f32), jax.ShapeDtypeStruct((8, 128), f32)],
        scratch_shapes=[
            pltpu.VMEM((8, 8, 16, GCOLS), bf16),
            pltpu.VMEM((8, 8, 16, GCOLS), bf16),
            pltpu.VMEM((8, 8, 8, 128), f32),
            pltpu.VMEM((8, 8, 8, 128), f32),
            pltpu.VMEM((7, 8, 16, GCOLS // 2), bf16),
            pltpu.VMEM((7, 8, 16, GCOLS // 2), bf16),
            pltpu.VMEM((7, 16, GCOLS // 2), bf16),
            pltpu.VMEM((7, 16, GCOLS // 2), bf16),
            pltpu.VMEM((7, 8, 8, 128), f32),
            pltpu.VMEM((7, 8, 128), f32),
            pltpu.VMEM((16, GCOLS), f32),
            pltpu.SemaphoreType.DMA((1,)),
            pltpu.SemaphoreType.DMA((n,)),
            pltpu.SemaphoreType.DMA((n,)),
        ],
        compiler_params=pltpu.CompilerParams(collective_id=3, has_side_effects=True, vmem_limit_bytes=VMEM),
        name="reduce_weights",
    )(parts, small)


def on_device(
    tokens, attn_gain, qkv_weight, qk_gain, out_weight, ffn_gain, router_weight,
    gate_up_weight, down_weight, routes, cotangent,
):
    x = tokens.reshape(TOKENS, D)
    cot = cotangent.reshape(TOKENS, D)
    route_ids = routes.reshape(TOKENS, TOPK)
    expert_ids = jnp.arange(EXPERTS, dtype=jnp.int32)
    named = jnp.any(route_ids[:, :, None] == expert_ids[None, None, :], axis=1)
    small = jnp.concatenate(
        [
            router_weight,
            attn_gain[:, None],
            ffn_gain[:, None],
            jnp.broadcast_to(qk_gain[:, None], (8, 1)),
            jnp.zeros((8, 93), bf16),
        ],
        axis=1,
    )
    halves = jnp.stack(
        [
            jnp.concatenate([qkv_weight[:, :1024], out_weight[:, :512], small], axis=1),
            jnp.concatenate([qkv_weight[:, 1024:], out_weight[:, 512:], small], axis=1),
        ]
    ).astype(f32)
    whole, masks = gather_weights(halves, named.T.astype(bf16))
    whole = whole.reshape(2, D, WCOLS)
    g_all = lax.all_gather(cot[None], "fsdp", axis=0, tiled=True)

    positions = lax.axis_index("seq") * TOKENS + jnp.arange(TOKENS, dtype=jnp.int32)
    half_dim = HEAD_SIZE // 2
    freq_index = jnp.arange(half_dim, dtype=f32)
    inverse = jnp.exp(-(2.0 * freq_index / HEAD_SIZE) * math.log(rope_base))
    angles = positions.astype(f32)[:, None] * inverse[None, :]
    cos, sin = jnp.cos(angles), jnp.sin(angles)
    cos = jnp.concatenate([cos, cos, cos, cos], axis=1)
    sin = jnp.concatenate([-sin, sin, -sin, sin], axis=1)

    heads, full, logs, attended, after, normed_ffn, gates, small_t, raw = front(x, whole, route_ids, cos, sin)
    row_sum, gate_sum, y_all, expert_grads = moe(
        normed_ffn, g_all, masks, small_t[:EXPERTS], gate_up_weight, down_weight
    )
    expert_part = lax.psum_scatter(expert_grads, "seq", scatter_dimension=1, tiled=True).astype(f32)
    layer_out, token_grad, parts, small = back(
        row_sum, gate_sum, gates, after, x, cot, attended, normed_ffn, small_t, raw,
        heads, full, logs, cos, sin, whole, y_all,
    )
    parts, small = reduce_weights(parts.reshape(2, 8, 8, 16, GCOLS), small.reshape(8, 8, 2, 8, 128))
    qkv_part = jnp.concatenate([parts[0, :, :1024], parts[1, :, :1024]], axis=1)
    out_part = jnp.concatenate([parts[0, :, 1024:], parts[1, :, 1024:]], axis=1)
    return (
        layer_out.reshape(1, TOKENS, D),
        token_grad.reshape(1, TOKENS, D),
        small[:, EXPERTS],
        qkv_part,
        small[0:1, EXPERTS + 2],
        out_part,
        small[:, EXPERTS + 1],
        small[:, :EXPERTS],
        expert_part[:, :, : 2 * F],
        expert_part[:, :, 2 * F :],
    )


def solution(mesh):
    return jax.shard_map(
        on_device,
        mesh=mesh,
        in_specs=(
            P("fsdp", "seq", None),
            P(("seq", "fsdp")),
            P(("seq", "fsdp"), None),
            P(("seq", "fsdp")),
            P(("seq", "fsdp"), None),
            P(("seq", "fsdp")),
            P(("seq", "fsdp"), None),
            P("fsdp", None, None),
            P("fsdp", None, None),
            P("fsdp", "seq", None),
            P("fsdp", "seq", None),
        ),
        out_specs=(
            P("fsdp", "seq", None),
            P("fsdp", "seq", None),
            P(("seq", "fsdp")),
            P(("seq", "fsdp"), None),
            P(("seq", "fsdp")),
            P(("seq", "fsdp"), None),
            P(("seq", "fsdp")),
            P(("seq", "fsdp"), None),
            P("fsdp", "seq", None),
            P("fsdp", "seq", None),
        ),
        check_vma=False,
    )
```

```python
import math

import jax
import jax.numpy as jnp
from jax import lax
from jax.experimental import pallas as pl
from jax.experimental.pallas import tpu as pltpu
from jax.sharding import PartitionSpec as P

D = 1024
HEAD_SIZE = 64
F = 512
TOPK = 8
EXPERTS = 32
SLOTS = 96
TOKENS = 256
SEQ = 8
FSDP = 16
LENGTH = SEQ * TOKENS
GROUP_ROWS = 4 * SLOTS
ROWS = 4 * GROUP_ROWS
WIDE = D + 128
GCOLS = 1536
VMEM = 60 * 1024 * 1024

epsilon = 1e-06
rope_base = 10000.0
f32 = jnp.float32
bf16 = jnp.bfloat16


def dot(a, b):
    return lax.dot_general(a, b, (((1,), (0,)), ((), ())), preferred_element_type=f32)


def dot_t(a, b):
    return lax.dot_general(a, b, (((1,), (1,)), ((), ())), preferred_element_type=f32)


def t_dot(a, b):
    return lax.dot_general(a, b, (((0,), (0,)), ((), ())), preferred_element_type=f32)


MESH = pl.DeviceIdType.MESH


class Place:
    def __init__(self):
        self.seq = lax.axis_index("seq")
        self.fsdp = lax.axis_index("fsdp")
        self.core = lax.rem(self.fsdp, 2)
        self.xh = lax.rem(self.fsdp // 2, 2)
        self.z = self.fsdp // 4
        self.y = lax.rem(self.seq, 4)
        self.xl = self.seq // 4

    def sibling(self):
        return {"fsdp": self.fsdp + 1 - 2 * self.core}

    def fsdp_at(self, ring, pair):
        z = lax.rem(self.z + ring + 4, 4)
        xh = 1 - self.xh if pair else self.xh
        return z * 4 + xh * 2 + self.core

    def seq_at(self, ring, pair):
        y = lax.rem(self.y + ring + 4, 4)
        xl = 1 - self.xl if pair else self.xl
        return xl * 4 + y

    def plane(self, axis):
        at = self.fsdp_at if axis == "fsdp" else self.seq_at
        return {
            "up": {axis: at(1, 0)},
            "down": {axis: at(-1, 0)},
            "across": {axis: at(0, 1)},
        }


def meet(targets):
    barrier = pltpu.get_barrier_semaphore()
    for target in targets:
        pl.semaphore_signal(barrier, inc=1, device_id=target, device_id_type=MESH)
    pl.semaphore_wait(barrier, len(targets))


class Copies:
    def __init__(self, send_sems, recv_sems):
        self.send_sems, self.recv_sems, self.count, self.all = send_sems, recv_sems, 0, []

    def start(self, src, dst, target):
        k = self.count
        self.count += 1
        copy = pltpu.make_async_remote_copy(
            src_ref=src, dst_ref=dst, send_sem=self.send_sems.at[k], recv_sem=self.recv_sems.at[k],
            device_id=target, device_id_type=MESH,
        )
        copy.start()
        self.all.append(copy)
        return copy

    def finish(self, done=()):
        for copy in self.all:
            if all(copy is not other for other in done):
                copy.wait_send()


OTHERS = ((2, 1), (2, 0), (0, 1), (1, 1), (-1, 1), (1, 0), (-1, 0))
WCOLS = 1664


def lane_halves():
    lanes = lax.broadcasted_iota(jnp.int32, (1, 128), 1)
    return lanes, lanes < HEAD_SIZE


def head_mean(values, low_half):
    low = jnp.sum(jnp.where(low_half, values, 0.0), axis=1, keepdims=True)
    high = jnp.sum(jnp.where(low_half, 0.0, values), axis=1, keepdims=True)
    return jnp.where(low_half, low, high) * (1.0 / HEAD_SIZE)


def partner(values, lanes):
    return jnp.where(
        lax.rem(lanes, HEAD_SIZE) < HEAD_SIZE // 2, pltpu.roll(values, 96, 1), pltpu.roll(values, 32, 1)
    )


def row_scale(values):
    return lax.rsqrt(jnp.mean(values * values, axis=1, keepdims=True) + epsilon)


def gain_tiles(small_t, lanes):
    pick = (
        lax.broadcasted_iota(jnp.int32, (D, 128), 0) == 8 * lax.broadcasted_iota(jnp.int32, (D, 128), 1)
    ).astype(f32).astype(bf16)
    gains = dot(small_t[32:48, :], pick)[2:3, :]
    other = pltpu.roll(gains, 64, 1)
    low_half = lanes < HEAD_SIZE
    return jnp.where(low_half, gains, other), jnp.where(low_half, other, gains)


def front_kernel(
    x_ref, w_ref, routes_ref, cos_ref, sin_ref, cot_ref, side_ref,
    heads_out, g_out, full_ref, logs_ref, att_ref, after_ref, normed_ref, gates_ref, small_t_ref, raw_ref,
    wq, wkv, wo, small, send, heads, out_buf, att, key0, key1, value,
    local_sems, send_sems, recv_sems,
):
    here = Place()
    me = here.seq
    loads = [
        pltpu.make_async_copy(w_ref.at[h, :, pl.ds(start, width)], there, local_sems.at[k])
        for k, (h, start, width, there) in enumerate(
            (
                (0, 1536, 128, small),
                (0, 0, 1024, wq),
                (1, 0, 1024, wkv),
                (0, 1024, 512, wo.at[0]),
                (1, 1024, 512, wo.at[1]),
            )
        )
    ]
    for copy in loads:
        copy.start()
    own_g = [
        pltpu.make_async_copy(cot_ref, g_out.at[here.fsdp], local_sems.at[6]),
        pltpu.make_async_copy(side_ref, g_out.at[here.fsdp_at(0, 1)], local_sems.at[7]),
    ]
    for copy in own_g:
        copy.start()
    peers = [here.seq_at(*other) for other in OTHERS]
    sib = here.sibling()
    way = here.plane("fsdp")
    meet([sib, *way.values()] + [{"seq": peer} for peer in peers])
    net = Copies(send_sems, recv_sems)

    def gather_cotangent():
        def at(ring, pair):
            return g_out.at[here.fsdp_at(ring, pair)]

        def half(ref, which):
            return ref.at[pl.ds(128 * which, 128)]

        def go(ref, target):
            return net.start(ref, ref, target)

        up, down = [net.start(cot_ref, at(0, 0), way[w]) for w in ("up", "down")]
        kin = [net.start(cot_ref, at(0, 0), sib), net.start(side_ref, at(0, 1), sib)]
        yield
        up.wait_recv()
        far = [go(half(at(-1, 0), 0), way["up"])]
        kin.append(go(at(-1, 0), sib))
        down.wait_recv()
        far.append(go(half(at(1, 0), 1), way["down"]))
        kin.append(go(at(1, 0), sib))
        up, down = [net.start(side_ref, at(0, 1), way[w]) for w in ("up", "down")]
        yield
        for copy in far:
            copy.wait_recv()
        across = go(at(2, 0), way["across"])
        kin.append(go(at(2, 0), sib))
        yield
        up.wait_recv()
        kin.append(go(at(-1, 1), sib))
        down.wait_recv()
        kin.append(go(at(1, 1), sib))
        across.wait_recv()
        kin.append(go(at(2, 1), sib))
        yield
        for copy in kin:
            copy.wait_recv()

    moves = gather_cotangent()
    next(moves)
    lanes, low_half = lane_halves()
    loads[0].wait()
    small_t = jnp.transpose(small[...].astype(f32)).astype(bf16)
    small_t_ref[...] = small_t
    x = x_ref[...].astype(f32)
    normed = (x * row_scale(x) * small_t[32:33, :].astype(f32)).astype(bf16)
    query_gain, key_gain = gain_tiles(small_t, lanes)
    cos, sin = cos_ref[...], sin_ref[...]
    loads[1].wait()
    queries = dot(normed, wq[...])
    loads[2].wait()
    kv = dot(normed, wkv[...])

    def turned(tile, gain):
        normal = tile * lax.rsqrt(head_mean(tile * tile, low_half) + epsilon) * gain
        return normal * cos + partner(normal, lanes) * sin

    for j in range(4):
        part = slice(128 * j, 128 * (j + 1))
        raw_ref[8 + j] = kv[:, part]
        keys = turned(kv[:, part], key_gain)
        values = kv[:, 512 + 128 * j : 640 + 128 * j]
        send[2 * j, :, 128:256] = jnp.where(low_half, keys, pltpu.roll(values, 64, 1)).astype(bf16)
        send[2 * j + 1, :, 128:256] = jnp.where(low_half, pltpu.roll(keys, 64, 1), values).astype(bf16)
    for h in range(8):
        raw_ref[h] = queries[:, 128 * h : 128 * (h + 1)]
        send[h, :, 0:128] = turned(raw_ref[h], query_gain).astype(bf16)
    copies = [net.start(send.at[peer], heads.at[me], {"seq": peer}) for peer in peers]
    heads[me] = send[me]
    next(moves)
    for copy in copies:
        copy.wait_recv()
    save = pltpu.make_async_copy(heads, heads_out, local_sems.at[5])
    save.start()
    for c in range(8):
        rows = slice(TOKENS * c, TOKENS * (c + 1))
        pair = heads[c, :, 128:256].astype(f32)
        key0[rows, :] = jnp.where(low_half, pair, 0.0).astype(bf16)
        key1[rows, :] = jnp.where(low_half, 0.0, pltpu.roll(pair, 64, 1)).astype(bf16)
        value[rows, :] = jnp.where(low_half, jnp.where(lanes == 0, 1.0, 0.0), pair).astype(bf16)

    def block(i, carry):
        j = lax.rem(me + 1 + i, 8)
        query = (heads[j, :, 0:128].astype(f32) * (1.0 / 8.0)).astype(bf16)
        results = []
        for key in (key0, key1):
            total = jnp.zeros((TOKENS, 128), f32)
            for c in range(4):
                part = pl.ds(c * 512, 512)
                weights = jnp.exp(dot_t(query, key[part, :]))
                total = total + dot(weights.astype(bf16), value[part, :])
            results.append(total)
        sum0, sum1 = results[0][:, 0:1], results[1][:, 0:1]
        full = jnp.where(low_half, pltpu.roll(results[0] / sum0, 64, 1), results[1] / sum1)
        rows = pl.ds(pl.multiple_of(j * TOKENS, TOKENS), TOKENS)
        full_ref[rows, :] = full
        logs_ref[rows, :] = jnp.where(low_half, jnp.log(sum0), jnp.log(sum1))
        out_buf[j] = full.astype(bf16)

        @pl.when(i < 7)
        def _():
            answer(i).start()

        return carry

    columns = pl.ds(pl.multiple_of(me * 128, 128), 128)

    def answer(i):
        j = lax.rem(me + 1 + i, 8)
        return pltpu.make_async_remote_copy(
            src_ref=out_buf.at[j], dst_ref=att.at[:, columns], send_sem=send_sems.at[24 + i],
            recv_sem=recv_sems.at[24 + i], device_id={"seq": j}, device_id_type=MESH,
        )

    lax.fori_loop(0, 1, block, 0)
    next(moves)
    lax.fori_loop(1, 7, block, 0)
    next(moves)
    lax.fori_loop(7, 8, block, 0)
    att[:, columns] = out_buf[me]
    for k in (3, 4):
        loads[k].wait()
    for i in range(7):
        answer(i).wait_recv()
    attended = att[...]
    att_ref[...] = attended
    squares = jnp.zeros((TOKENS, 1), f32)
    for h in range(2):
        part = slice(512 * h, 512 * (h + 1))
        after = x_ref[:, part].astype(f32) + dot(attended, wo[h])
        after_ref[:, part] = after
        squares = squares + jnp.sum(after * after, axis=1, keepdims=True)
    scaling = lax.rsqrt(squares * (1.0 / D) + epsilon)
    normed = (after_ref[...] * scaling * small_t[33:34, :].astype(f32)).astype(bf16)
    normed_ref[...] = normed
    logits = dot(normed, small[...])
    named = jnp.zeros((TOKENS, 128), f32)
    for k in range(TOPK):
        named = jnp.where(routes_ref[:, k : k + 1] == lanes, 1.0, named)
    peak = jnp.max(jnp.where(named > 0.0, logits, -1e30), axis=1, keepdims=True)
    chosen = jnp.where(named > 0.0, jnp.exp(logits - peak), 0.0)
    gates_ref[...] = chosen / jnp.sum(chosen, axis=1, keepdims=True)
    for _ in moves:
        pass
    save.wait()
    for copy in own_g:
        copy.wait()
    for i in range(7):
        answer(i).wait_send()
    net.finish()


def front(x, whole, routes, cos, sin, cot, side):
    vmem = pl.BlockSpec(memory_space=pltpu.VMEM)
    hbm = pl.BlockSpec(memory_space=pl.ANY)
    return pl.pallas_call(
        front_kernel,
        in_specs=[vmem, hbm, vmem, vmem, vmem, hbm, hbm],
        out_specs=[hbm] * 2 + [vmem] * 8,
        out_shape=[
            jax.ShapeDtypeStruct((8, TOKENS, 256), bf16),
            jax.ShapeDtypeStruct((FSDP, TOKENS, D), bf16),
            jax.ShapeDtypeStruct((LENGTH, 128), f32),
            jax.ShapeDtypeStruct((LENGTH, 128), f32),
            jax.ShapeDtypeStruct((TOKENS, D), bf16),
            jax.ShapeDtypeStruct((TOKENS, D), f32),
            jax.ShapeDtypeStruct((TOKENS, D), bf16),
            jax.ShapeDtypeStruct((TOKENS, 128), f32),
            jax.ShapeDtypeStruct((128, D), bf16),
            jax.ShapeDtypeStruct((12, TOKENS, 128), f32),
        ],
        scratch_shapes=[
            pltpu.VMEM((D, 1024), bf16),
            pltpu.VMEM((D, 1024), bf16),
            pltpu.VMEM((2, D, 512), bf16),
            pltpu.VMEM((D, 128), bf16),
            pltpu.VMEM((8, TOKENS, 256), bf16),
            pltpu.VMEM((8, TOKENS, 256), bf16),
            pltpu.VMEM((8, TOKENS, 128), bf16),
            pltpu.VMEM((TOKENS, D), bf16),
            pltpu.VMEM((LENGTH, 128), bf16),
            pltpu.VMEM((LENGTH, 128), bf16),
            pltpu.VMEM((LENGTH, 128), bf16),
            pltpu.SemaphoreType.DMA((8,)),
            pltpu.SemaphoreType.DMA((31,)),
            pltpu.SemaphoreType.DMA((31,)),
        ],
        compiler_params=pltpu.CompilerParams(collective_id=2, has_side_effects=True, vmem_limit_bytes=VMEM),
        cost_estimate=pl.CostEstimate(
            flops=4 * 10**9, bytes_accessed=16 << 20, transcendentals=2 * LENGTH * LENGTH
        ),
        name="front",
    )(x, whole, routes, cos, sin, cot, side)


def split3(values):
    high = values.astype(bf16).astype(f32)
    rest = values - high
    middle = rest.astype(bf16).astype(f32)
    return high, middle, rest - middle


def with_terms(lanes, start, parts):
    high, middle, low = parts
    return jnp.where(
        lanes == start,
        high,
        jnp.where(lanes == start + 1, middle, jnp.where(lanes == start + 2, low, 0.0)),
    )


def back_kernel(
    gate_sum_ref, gates_ref, after_ref, x_ref, cot_ref, att_ref, normed_ref, small_t_ref,
    heads_ref, full_ref, logs_ref, cos_ref, sin_ref, row_ref, raw_ref, w_ref, y_ref, y_other, grads_ref, far_ref,
    layer_ref, token_ref, qkv_out, wo_out, small_out, up_out, down_out,
    wqkv, wo, send, grads, back_q, back_kv, pg, after_grad,
    key0, key1, value0, value1, key_t, dk_total, dv_total,
    slots, y_stage, hop_in,
    parts, parts_in, small, small_in, hop_a, hop_b, late_a, late_b, small_s, small_f, total, total_in,
    chunks, far_in, chunk_in, local_sems, send_sems, recv_sems,
):
    here = Place()
    me = here.seq
    sib = here.sibling()
    way = here.plane("fsdp")
    loads = [
        pltpu.make_async_copy(w_ref.at[h, :, pl.ds(start, width)], there, local_sems.at[k])
        for k, (h, start, width, there) in enumerate(
            (
                (0, 1024, 512, wo.at[0]),
                (1, 1024, 512, wo.at[1]),
                (0, 0, 1024, wqkv.at[0]),
                (1, 0, 1024, wqkv.at[1]),
            )
        )
    ]
    loads.append(pltpu.make_async_copy(row_ref, after_grad, local_sems.at[19]))
    for copy in loads:
        copy.start()
    e_loads = [
        pltpu.make_async_copy(
            grads_ref.at[:, pl.ds(pl.multiple_of(here.seq_at(ring, pair) * 128, 128), 128)],
            chunks.at[i, pair], local_sems.at[12 + 2 * i + pair],
        )
        for i, ring in enumerate((-1, 1, 0)) for pair in range(2)
    ]
    e_loads.append(pltpu.make_async_copy(far_ref, far_in, local_sems.at[18]))
    order = (6, 7, 3, 5, 2, 4, 1, 0)
    y_loads = {k: pltpu.make_async_copy(y_ref.at[k], slots.at[k], local_sems.at[4 + k]) for k in order}
    y_more = {
        k: pltpu.make_async_copy(y_other.at[k], y_stage.at[i % 2], local_sems.at[20 + k]) for i, k in enumerate(order)
    }
    for copy in y_loads.values():
        copy.start()
    for k in order[:2]:
        y_more[k].start()
    peers = [here.seq_at(*other) for other in OTHERS]
    seq_peers = [{"seq": peer} for peer in peers]
    fsdp_peers = [{"fsdp": here.fsdp_at(*other)} for other in OTHERS]
    meet([sib, *seq_peers, *fsdp_peers])
    net = Copies(send_sems, recv_sems)
    for copy in e_loads:
        copy.start()
    lanes, low_half = lane_halves()

    gate_sum = gate_sum_ref[...]
    gate_grad = gate_sum + pltpu.roll(gate_sum, 96, 1)
    gates = gates_ref[...]
    gate_grad = jnp.where(lanes < EXPERTS, gate_grad, 0.0)
    chosen = gates * (gate_grad - jnp.sum(gates * gate_grad, axis=1, keepdims=True))
    logits_grad = chosen.astype(bf16)
    loads[4].wait()
    normed_grad = after_grad[...] + dot(logits_grad, small_t_ref[...])
    after = after_ref[...]
    scaling = row_scale(after)
    weighted = normed_grad * small_t_ref[33:34, :].astype(f32)
    middle = jnp.mean(weighted * after, axis=1, keepdims=True)
    after_grad[...] = (
        cot_ref[...].astype(f32) + scaling * weighted - after * (scaling * scaling * scaling * middle)
    )
    after_low = after_grad[...].astype(bf16)
    ffn_gain = jnp.sum(normed_grad * after * scaling, axis=0, keepdims=True)
    for k in (0, 1):
        loads[k].wait()
    for q in range(2):
        rows = slice(512 * q, 512 * (q + 1))
        attended_grad = dot_t(after_low[:, 0:512], wo[0, rows, :]) + dot_t(after_low[:, 512:1024], wo[1, rows, :])
        for h in range(4):
            send[4 * q + h] = attended_grad[:, 128 * h : 128 * (h + 1)].astype(bf16)
    to_heads = [net.start(send.at[peer], grads.at[me], {"seq": peer}) for peer in peers]
    grads[me] = send[me]
    router_grad = t_dot(normed_ref[...], logits_grad)
    small[...] = router_grad.reshape(8, 8, 2, 8, 128)
    for h in range(2):
        out_grad = t_dot(att_ref[...], after_low[:, 512 * h : 512 * (h + 1)]).astype(bf16)
        parts[h, :, :, :, 1024:1536] = out_grad.reshape(8, 8, 16, 512)

    def add_to(ref, *values):
        result = ref[...].astype(f32)
        for value in values:
            result = result + value[...].astype(f32)
        ref[...] = result.astype(bf16)

    def join(k):
        i = order.index(k)
        y_loads[k].wait()
        y_more[k].wait()
        add_to(slots.at[k], y_stage.at[i % 2])
        if i + 2 < 8:
            y_more[order[i + 2]].start()

    def half(ref, which):
        return ref.at[pl.ds(128 * which, 128)]

    def expert_sum():
        join(6)
        join(7)
        up = [net.start(half(slots.at[6 + j], 0), half(hop_in.at[j], 0), way["up"]) for j in range(2)]
        down = [net.start(half(slots.at[6 + j], 1), half(hop_in.at[j], 1), way["down"]) for j in range(2)]
        yield
        for k in (3, 5, 2, 4):
            join(k)
        up[1].wait_recv()
        down[1].wait_recv()
        add_to(half(slots.at[5], 0), half(hop_in.at[1], 0))
        add_to(half(slots.at[3], 1), half(hop_in.at[1], 1))
        beside = [
            net.start(slots.at[5], hop_in.at[2], way["up"]), net.start(slots.at[3], hop_in.at[3], way["down"])
        ]
        up[0].wait_recv()
        down[0].wait_recv()
        add_to(half(slots.at[4], 0), half(hop_in.at[0], 0))
        add_to(half(slots.at[2], 1), half(hop_in.at[0], 1))
        own = [
            net.start(slots.at[4], hop_in.at[4], way["up"]), net.start(slots.at[2], hop_in.at[5], way["down"])
        ]
        yield
        join(1)
        join(0)
        for copy in beside:
            copy.wait_recv()
        add_to(slots.at[1], hop_in.at[2], hop_in.at[3])
        own.append(net.start(slots.at[1], hop_in.at[6], way["across"]))
        yield
        for copy in own:
            copy.wait_recv()
        layer_ref[...] = (
            after_ref[...]
            + slots[0].astype(f32)
            + hop_in[4].astype(f32)
            + hop_in[5].astype(f32)
            + hop_in[6].astype(f32)
        ).astype(bf16)

    def expert_grads():
        ring = here.plane("seq")
        for copy in e_loads:
            copy.wait()
        for pair in (1, 0):
            add_to(chunks.at[0, pair, 1], far_in.at[pair, 1])
            add_to(chunks.at[1, pair, 0], far_in.at[pair, 0])
        beside = [
            net.start(chunks.at[0, 1], chunk_in.at[0], ring["down"]),
            net.start(chunks.at[1, 1], chunk_in.at[1], ring["up"]),
        ]
        yield
        own = [
            net.start(chunks.at[0, 0], chunk_in.at[2], ring["down"]),
            net.start(chunks.at[1, 0], chunk_in.at[3], ring["up"]),
        ]
        for copy in beside:
            copy.wait_recv()
        add_to(chunks.at[2, 1], chunk_in.at[0], chunk_in.at[1])
        own.append(net.start(chunks.at[2, 1], chunk_in.at[4], ring["across"]))
        yield
        for copy in own:
            copy.wait_recv()
        result = chunks[2, 0].astype(f32)
        for i in range(2, 5):
            result = result + chunk_in[i].astype(f32)
        up_out[...] = result[:, :, 0 : 2 * F]
        down_out[...] = result[:, :, 2 * F : 3 * F]

    moves = expert_sum()
    more_moves = expert_grads()
    next(moves)
    ones_high = jnp.where((lanes >= 64) & (lanes < 67), 1.0, 0.0)
    ones_low = jnp.where(lanes < 3, 1.0, 0.0)
    for c in range(8):
        rows = slice(TOKENS * c, TOKENS * (c + 1))
        pair = heads_ref[c, :, 128:256].astype(f32)
        swapped = pltpu.roll(pair, 64, 1)
        key0[rows, :] = jnp.where(low_half, pair, ones_high).astype(bf16)
        key1[rows, :] = jnp.where(low_half, ones_low, swapped).astype(bf16)
        value0[rows, :] = jnp.where(low_half, swapped, ones_high).astype(bf16)
        value1[rows, :] = jnp.where(low_half, ones_low, pair).astype(bf16)
        key_t[:, rows] = jnp.transpose(pair)[0:64, :].astype(bf16)
    dk_total[...] = jnp.zeros_like(dk_total)
    dv_total[...] = jnp.zeros_like(dv_total)
    for copy in to_heads:
        copy.wait_recv()
    columns = pl.ds(pl.multiple_of(me * 128, 128), 128)

    def answer(i):
        j = lax.rem(me + 1 + i, 8)
        return pltpu.make_async_remote_copy(
            src_ref=grads.at[j], dst_ref=back_q.at[:, columns], send_sem=send_sems.at[92 + i],
            recv_sem=recv_sems.at[92 + i], device_id={"seq": j}, device_id_type=MESH,
        )

    def block(i, carry):
        j = lax.rem(me + 1 + i, 8)
        rows = pl.ds(pl.multiple_of(j * TOKENS, TOKENS), TOKENS)
        query = heads_ref[j, :, 0:128].astype(f32) * (1.0 / 8.0)
        grad = grads[j].astype(f32)
        logs = logs_ref[rows, :]
        product = grad * full_ref[rows, :]
        delta0 = jnp.sum(jnp.where(low_half, product, 0.0), axis=1, keepdims=True)
        delta1 = jnp.sum(jnp.where(low_half, 0.0, product), axis=1, keepdims=True)
        query0 = jnp.where(low_half, query, with_terms(lanes, 64, split3(-logs[:, 0:1]))).astype(bf16)
        query1 = jnp.where(low_half, with_terms(lanes, 0, split3(-logs[:, 64:65])), query).astype(bf16)
        grad0 = jnp.where(low_half, grad, with_terms(lanes, 64, split3(-delta0))).astype(bf16)
        grad1 = jnp.where(low_half, with_terms(lanes, 0, split3(-delta1)), grad).astype(bf16)
        only_query = (
            jnp.where(low_half, query, 0.0).astype(bf16), jnp.where(low_half, 0.0, query).astype(bf16)
        )
        only_grad = (jnp.where(low_half, grad, 0.0).astype(bf16), jnp.where(low_half, 0.0, grad).astype(bf16))
        dq = [jnp.zeros((64, TOKENS), f32), jnp.zeros((64, TOKENS), f32)]
        for c in range(4):
            part = pl.ds(c * 512, 512)
            dv = dv_total[part, :]
            dk = dk_total[part, :]
            for h, (key, value, query_h, grad_h) in enumerate(
                ((key0, value0, query0, grad0), (key1, value1, query1, grad1))
            ):
                probs = jnp.exp(dot_t(key[part, :], query_h))
                inner = dot_t(value[part, :], grad_h)
                dv = dv + dot(probs.astype(bf16), only_grad[h])
                scores = (probs * inner).astype(bf16)
                dk = dk + dot(scores, only_query[h])
                dq[h] = dq[h] + dot(key_t[:, c * 512 : (c + 1) * 512], scores)
            dv_total[part, :] = dv
            dk_total[part, :] = dk
        both = jnp.concatenate(dq, axis=0) * (1.0 / 8.0)
        grads[j] = jnp.transpose(both).astype(bf16)

        @pl.when(i < 7)
        def _():
            answer(i).start()

        return carry

    next(more_moves)
    lax.fori_loop(0, 3, block, 0)
    next(moves)
    lax.fori_loop(3, 6, block, 0)
    next(moves)
    next(more_moves)
    lax.fori_loop(6, 8, block, 0)
    for copy in to_heads:
        copy.wait_send()
    for c in range(8):
        rows = slice(TOKENS * c, TOKENS * (c + 1))
        dk = dk_total[rows, :]
        dv = dv_total[rows, :]
        dk = dk + pltpu.roll(dk, 64, 1)
        dv = dv + pltpu.roll(dv, 64, 1)
        send[c] = jnp.where(low_half, dk, dv).astype(bf16)
    to_tokens = [net.start(send.at[peer], back_kv.at[me], {"seq": peer}) for peer in peers]
    raw = [
        pltpu.make_async_copy(raw_ref.at[h], there.at[pl.ds(TOKENS * (h % 8), TOKENS)], local_sems.at[28 + h])
        for h, there in [(h, dk_total) for h in range(8)] + [(h, dv_total) for h in range(8, 12)]
    ]
    for copy in raw:
        copy.start()
    back_kv[me] = send[me]
    back_q[:, columns] = grads[me]
    x = x_ref[...].astype(f32)
    x_scaling = row_scale(x)
    attn_gain = small_t_ref[32:33, :].astype(f32)
    normed = (x * x_scaling * attn_gain).astype(bf16)
    query_gain, key_gain = gain_tiles(small_t_ref[...], lanes)
    cos, sin = cos_ref[...], sin_ref[...]
    for i in range(7):
        answer(i).wait_recv()

    def unturned(grad, tile, gain):
        grad = grad * cos - partner(grad, lanes) * sin
        scale = lax.rsqrt(head_mean(tile * tile, low_half) + epsilon)
        weighted = grad * gain
        middle = head_mean(weighted * tile, low_half)
        result = scale * weighted - tile * (scale * scale * scale * middle)
        return result.astype(bf16), jnp.sum(grad * tile * scale, axis=0, keepdims=True)

    for copy in raw:
        copy.wait()
    query_terms = jnp.zeros((1, 128), f32)
    for h in range(8):
        part = slice(128 * h, 128 * (h + 1))
        pg[0, :, part], terms = unturned(back_q[:, part].astype(f32), dk_total[TOKENS * h : TOKENS * (h + 1), :], query_gain)
        query_terms = query_terms + terms
    for copy in to_tokens:
        copy.wait_recv()
    key_terms = jnp.zeros((1, 128), f32)
    for j in range(4):
        first, second = back_kv[2 * j].astype(f32), back_kv[2 * j + 1].astype(f32)
        keys = jnp.where(low_half, first, pltpu.roll(second, 64, 1))
        values = jnp.where(low_half, pltpu.roll(first, 64, 1), second)
        part = slice(128 * j, 128 * (j + 1))
        pg[1, :, part], terms = unturned(keys, dv_total[TOKENS * j : TOKENS * (j + 1), :], key_gain)
        key_terms = key_terms + terms
        pg[1, :, 512 + 128 * j : 640 + 128 * j] = values.astype(bf16)

    core = here.core
    f = here.z * 2 + here.xh
    sib_joins = []
    for turn in range(2):
        h = 1 - core if turn == 0 else core
        for r in range(4):
            result = t_dot(normed[:, 256 * r : 256 * (r + 1)], pg[h]).astype(bf16)
            parts[h, 2 * r : 2 * r + 2, :, :, 0:1024] = result.reshape(2, 8, 16, 1024)
            if turn == 0:
                sib_joins.append(
                    net.start(parts.at[h, pl.ds(2 * r, 2)], parts_in.at[pl.ds(2 * r, 2)], sib)
                )
    for r in range(4):
        sib_joins[r].wait_recv()
        for q in (2 * r, 2 * r + 1):
            parts[core, q] = (parts[core, q].astype(f32) + parts_in[q].astype(f32)).astype(bf16)

    def f_at(ring, pair):
        return lax.rem(here.z + ring + 4, 4) * 2 + (1 - here.xh if pair else here.xh)

    def plane(part, hop, way):
        def half(ref, which):
            return ref.at[pl.ds(4 * which, 4)]

        a = net.start(part(2, 1), hop.at[0], way["across"])
        xd = net.start(part(-1, 1), hop.at[2], way["down"])
        xu = net.start(part(1, 1), hop.at[3], way["up"])
        yield
        a.wait_recv()
        add_to(part(2, 0), hop.at[0])
        u = net.start(half(part(2, 0), 0), half(hop.at[1], 0), way["up"])
        d = net.start(half(part(2, 0), 1), half(hop.at[1], 1), way["down"])
        yield
        xd.wait_recv()
        xu.wait_recv()
        add_to(part(0, 1), hop.at[2], hop.at[3])
        rx = net.start(part(0, 1), hop.at[6], way["across"])
        u.wait_recv()
        add_to(half(part(1, 0), 0), half(hop.at[1], 0))
        ru = net.start(part(1, 0), hop.at[4], way["up"])
        d.wait_recv()
        add_to(half(part(-1, 0), 1), half(hop.at[1], 1))
        rd = net.start(part(-1, 0), hop.at[5], way["down"])
        yield
        rx.wait_recv()
        ru.wait_recv()
        rd.wait_recv()
        add_to(part(0, 0), hop.at[4], hop.at[5], hop.at[6])

    low, high = pl.ds(0, GCOLS // 2), pl.ds(GCOLS // 2, GCOLS // 2)
    first_plane = plane(
        lambda ring, pair: parts.at[core, here.seq_at(ring, pair), :, :, low], hop_a, here.plane("seq")
    )
    second_plane = plane(lambda ring, pair: parts.at[core, :, f_at(ring, pair), :, high], hop_b, way)
    next(first_plane)
    next(second_plane)
    for copy in loads[2:4]:
        copy.wait()
    normed_grad = dot_t(pg[0], wqkv[0]) + dot_t(pg[1], wqkv[1])
    attn_gain_grad = jnp.sum(normed_grad * x * x_scaling, axis=0, keepdims=True)
    query_terms = query_terms + pltpu.roll(query_terms, 64, 1)
    key_terms = key_terms + pltpu.roll(key_terms, 64, 1)
    head_terms = jnp.where(low_half, query_terms, key_terms)
    spread = (
        8 * lax.broadcasted_iota(jnp.int32, (128, D), 0) == lax.broadcasted_iota(jnp.int32, (128, D), 1)
    ).astype(f32).astype(bf16)
    head_row = jnp.zeros((1, D), f32)
    for term in split3(head_terms):
        head_row = head_row + dot(jnp.broadcast_to(term, (16, 128)).astype(bf16), spread)[0:1, :]
    row = lax.broadcasted_iota(jnp.int32, (128, D), 0)
    gain_rows = jnp.where(
        row == 32, attn_gain_grad, jnp.where(row == 33, ffn_gain, jnp.where(row == 34, head_row, 0.0))
    )
    small[...] = small[...] + jnp.transpose(gain_rows).reshape(8, 8, 2, 8, 128)
    small_join = net.start(small.at[:, :, 1 - core], small_in, sib)
    next(first_plane)
    next(second_plane)
    weighted = normed_grad * attn_gain
    middle = jnp.mean(weighted * x, axis=1, keepdims=True)
    token_ref[...] = after_grad[...] + x_scaling * weighted - x * (x_scaling * x_scaling * x_scaling * middle)
    small_join.wait_recv()
    small_in[...] = small_in[...] + small[:, :, core]
    small_copies = [
        net.start(small_in.at[peers[i]], small_s.at[i], seq_peers[i]) for i in range(7)
    ]
    next(first_plane)
    next(second_plane)
    for _ in moves:
        pass
    for _ in more_moves:
        pass
    for copy in small_copies:
        copy.wait_recv()
    mine = small_in[me]
    for i in range(7):
        mine = mine + small_s[i]
    small_in[me] = mine
    small_copies = [
        net.start(small_in.at[me, f_at(*OTHERS[i])], small_f.at[i], fsdp_peers[i]) for i in range(7)
    ]
    next(first_plane, None)
    late = [
        [net.start(parts.at[core, me, f_at(*OTHERS[i]), :, low], late_a.at[i], fsdp_peers[i]) for i in range(7)]
    ]
    next(second_plane, None)
    late.append(
        [net.start(parts.at[core, peers[i], f, :, high], late_b.at[i], seq_peers[i]) for i in range(7)]
    )
    for copy in small_copies:
        copy.wait_recv()
    mine = small_in[me, f]
    for i in range(7):
        mine = mine + small_f[i]
    small_out[...] = mine
    for cols, copies, there in (
        (slice(0, GCOLS // 2), late[0], late_a), (slice(GCOLS // 2, GCOLS), late[1], late_b)
    ):
        for copy in copies:
            copy.wait_recv()
        result = parts[core, me, f, :, cols].astype(f32)
        for i in range(7):
            result = result + there[i].astype(f32)
        total[:, cols] = result
    last = net.start(total.at[pl.ds(pl.multiple_of(8 * (1 - core), 8), 8)], total_in, sib)
    mine = total[pl.ds(pl.multiple_of(8 * core, 8), 8), :]
    last.wait_recv()
    theirs = total_in[...]
    is_low = core == 0
    left, right = jnp.where(is_low, mine, theirs), jnp.where(is_low, theirs, mine)
    qkv_out[:, 0:1024] = left[:, 0:1024]
    qkv_out[:, 1024:2048] = right[:, 0:1024]
    wo_out[:, 0:512] = left[:, 1024:1536]
    wo_out[:, 512:1024] = right[:, 1024:1536]
    for i in range(7):
        answer(i).wait_send()
    net.finish(to_heads)


def back(*operands):
    vmem = pl.BlockSpec(memory_space=pltpu.VMEM)
    hbm = pl.BlockSpec(memory_space=pl.ANY)
    return pl.pallas_call(
        back_kernel,
        in_specs=[vmem] * 13 + [hbm] * 7,
        out_specs=[vmem] * 7,
        out_shape=[
            jax.ShapeDtypeStruct((TOKENS, D), bf16),
            jax.ShapeDtypeStruct((TOKENS, D), f32),
            jax.ShapeDtypeStruct((8, 2048), f32),
            jax.ShapeDtypeStruct((8, 1024), f32),
            jax.ShapeDtypeStruct((8, 128), f32),
            jax.ShapeDtypeStruct((2, 128, 2 * F), f32),
            jax.ShapeDtypeStruct((2, 128, F), f32),
        ],
        scratch_shapes=[
            pltpu.VMEM((2, D, 1024), bf16),
            pltpu.VMEM((2, D, 512), bf16),
            pltpu.VMEM((8, TOKENS, 128), bf16),
            pltpu.VMEM((8, TOKENS, 128), bf16),
            pltpu.VMEM((TOKENS, D), bf16),
            pltpu.VMEM((8, TOKENS, 128), bf16),
            pltpu.VMEM((2, TOKENS, D), bf16),
            pltpu.VMEM((TOKENS, D), f32),
        ]
        + [pltpu.VMEM((LENGTH, 128), bf16)] * 4
        + [pltpu.VMEM((64, LENGTH), bf16)]
        + [pltpu.VMEM((LENGTH, 128), f32)] * 2
        + [pltpu.VMEM((8, TOKENS, D), bf16), pltpu.VMEM((2, TOKENS, D), bf16)]
        + [pltpu.VMEM((7, TOKENS, D), bf16)]
        + [
            pltpu.VMEM((2, 8, 8, 16, GCOLS), bf16),
            pltpu.VMEM((8, 8, 16, GCOLS), bf16),
            pltpu.VMEM((8, 8, 2, 8, 128), f32),
            pltpu.VMEM((8, 8, 8, 128), f32),
            pltpu.VMEM((7, 8, 16, GCOLS // 2), bf16),
            pltpu.VMEM((7, 8, 16, GCOLS // 2), bf16),
            pltpu.VMEM((7, 16, GCOLS // 2), bf16),
            pltpu.VMEM((7, 16, GCOLS // 2), bf16),
            pltpu.VMEM((7, 8, 8, 128), f32),
            pltpu.VMEM((7, 8, 128), f32),
            pltpu.VMEM((16, GCOLS), f32),
            pltpu.VMEM((8, GCOLS), f32),
            pltpu.VMEM((3, 2, 2, 128, 3 * F), bf16),
            pltpu.VMEM((2, 2, 128, 3 * F), bf16),
            pltpu.VMEM((5, 2, 128, 3 * F), bf16),
            pltpu.SemaphoreType.DMA((40,)),
            pltpu.SemaphoreType.DMA((100,)),
            pltpu.SemaphoreType.DMA((100,)),
        ],
        compiler_params=pltpu.CompilerParams(collective_id=5, has_side_effects=True, vmem_limit_bytes=63 * 1024 * 1024),
        cost_estimate=pl.CostEstimate(
            flops=9 * 10**9, bytes_accessed=32 << 20, transcendentals=2 * LENGTH * LENGTH
        ),
        name="back",
    )(*operands)


def gather_kernel(
    qkv_ref, wo_ref, router_ref, attn_ref, ffn_ref, head_ref, routes_ref, cot_ref, out_ref, masks_out, side_out,
    in_ref, mask_ref, stage, block, local_sems, send_sems, recv_sems,
):
    lanes = lax.broadcasted_iota(jnp.int32, (1, 128), 1)
    same = lax.broadcasted_iota(jnp.int32, (8, 8), 0) == lax.broadcasted_iota(jnp.int32, (8, 8), 1)

    def column(row):
        return jnp.sum(jnp.where(same, row[...].astype(f32), 0.0), axis=1, keepdims=True)

    gains = jnp.where(
        lanes == 32,
        column(attn_ref),
        jnp.where(lanes == 33, column(ffn_ref), jnp.where(lanes == 34, head_ref[...].astype(f32), 0.0)),
    )
    for h in range(2):
        in_ref[h, :, 0:1024] = qkv_ref[:, 1024 * h : 1024 * (h + 1)].astype(f32)
        in_ref[h, :, 1024:1536] = wo_ref[:, 512 * h : 512 * (h + 1)].astype(f32)
        in_ref[h, :, 1536:1664] = gains
        in_ref[h, :, 1536:1568] = router_ref[...].astype(f32)
    named = jnp.zeros((256, 128), f32)
    for k in range(8):
        named = jnp.where(routes_ref[:, k : k + 1] == lanes, 1.0, named)
    mask_ref[...] = jnp.transpose(named)[0:32, :].astype(bf16)
    here = Place()
    c, s, f = here.core, here.seq, here.z * 2 + here.xh
    sib = here.sibling()
    ways = {"seq": here.plane("seq"), "fsdp": here.plane("fsdp")}
    others = [(2, 1), (2, 0), (0, 1), (1, 1), (-1, 1), (1, 0), (-1, 0)]

    def f_at(ring, pair):
        return lax.rem(here.z + ring + 4, 4) * 2 + (1 - here.xh if pair else here.xh)

    seq_peers = [{"seq": here.seq_at(ring, pair)} for ring, pair in others]
    fsdp_peers = [{"fsdp": here.fsdp_at(ring, pair)} for ring, pair in others]
    meet([sib, *seq_peers, *fsdp_peers])
    net = Copies(send_sems, recv_sems)
    rows = pl.ds(pl.multiple_of(8 * c, 8), 8)
    join = net.start(in_ref.at[1 - c], stage.at[rows], sib)
    stage[rows, :] = in_ref[c]
    join.wait_recv()
    block[...] = stage[...].astype(bf16)
    low, high = pl.ds(0, 896), pl.ds(896, 768)
    locals_ = [
        pltpu.make_async_copy(block, out_ref.at[c, s, f], local_sems.at[0]),
        pltpu.make_async_copy(mask_ref, masks_out.at[here.fsdp], local_sems.at[1]),
    ]
    for copy in locals_:
        copy.start()
    a = [net.start(block.at[:, low], out_ref.at[c, s, f, :, low], peer) for peer in fsdp_peers]
    b = [net.start(block.at[:, high], out_ref.at[c, s, f, :, high], peer) for peer in seq_peers]
    m = [net.start(mask_ref, masks_out.at[here.fsdp], peer) for peer in [sib, *fsdp_peers]]
    for copy in locals_:
        copy.wait()
    kin = []

    def plane(part, way):
        def half(ref, which):
            return ref.at[pl.ds(4 * which, 4)]

        def go(ref, target):
            return net.start(ref, ref, target)

        ref = part(0, 0)
        across, up, down = go(ref, way["across"]), go(ref, way["up"]), go(ref, way["down"])
        kin.append(go(ref, sib))
        yield
        up.wait_recv()
        ref = part(-1, 0)
        far_low = go(half(ref, 0), way["up"])
        kin.append(go(ref, sib))
        down.wait_recv()
        ref = part(1, 0)
        far_high = go(half(ref, 1), way["down"])
        kin.append(go(ref, sib))
        yield
        across.wait_recv()
        ref = part(0, 1)
        up, down = go(ref, way["up"]), go(ref, way["down"])
        kin.append(go(ref, sib))
        yield
        far_low.wait_recv()
        far_high.wait_recv()
        kin.append(go(part(2, 0), sib))
        up.wait_recv()
        ref = part(-1, 1)
        far_low = go(half(ref, 0), way["up"])
        kin.append(go(ref, sib))
        down.wait_recv()
        ref = part(1, 1)
        far_high = go(half(ref, 1), way["down"])
        kin.append(go(ref, sib))
        yield
        far_low.wait_recv()
        far_high.wait_recv()
        kin.append(go(part(2, 1), sib))

    for copy in a:
        copy.wait_recv()
    first = plane(lambda ring, pair: out_ref.at[c, here.seq_at(ring, pair), :, :, low], ways["seq"])
    next(first)
    for copy in b:
        copy.wait_recv()
    second = plane(lambda ring, pair: out_ref.at[c, :, f_at(ring, pair), :, high], ways["fsdp"])
    next(second)
    for i in range(8):
        m[i].wait_recv()
        if i:
            ring, pair = others[i - 1]
            ref = masks_out.at[here.fsdp_at(-ring, pair)]
            kin.append(net.start(ref, ref, sib))
    for turn in range(4):
        next(first, None)
        next(second, None)
        if turn == 1:
            kin.append(net.start(cot_ref, side_out, ways["fsdp"]["across"]))
    for copy in kin:
        copy.wait_recv()
    net.finish()


def gather_weights(*operands):
    n = 65
    return pl.pallas_call(
        gather_kernel,
        in_specs=[pl.BlockSpec(memory_space=pltpu.VMEM)] * 7 + [pl.BlockSpec(memory_space=pl.ANY)],
        out_specs=[pl.BlockSpec(memory_space=pl.ANY)] * 3,
        out_shape=[
            jax.ShapeDtypeStruct((2, 8, 8, 16, WCOLS), bf16),
            jax.ShapeDtypeStruct((16, 32, 256), bf16),
            jax.ShapeDtypeStruct((256, 1024), bf16),
        ],
        scratch_shapes=[
            pltpu.VMEM((2, 8, WCOLS), f32),
            pltpu.VMEM((32, 256), bf16),
            pltpu.VMEM((16, WCOLS), f32),
            pltpu.VMEM((16, WCOLS), bf16),
            pltpu.SemaphoreType.DMA((2,)),
            pltpu.SemaphoreType.DMA((n,)),
            pltpu.SemaphoreType.DMA((n,)),
        ],
        compiler_params=pltpu.CompilerParams(collective_id=1, has_side_effects=True, vmem_limit_bytes=VMEM),
        name="gather_weights",
    )(*operands)


def moe_kernel(
    x_ref, g_ref, masks_ref, router_ref, up_hbm, down_hbm,
    row_out, gate_out, y_out, y_in, grads_out, far_out,
    slots, sib_in, hop_in, g_rows, up_ref, down_ref,
    rows_x, rows_p, rows_h, rows_u, rows_g, slot_gate, places, stage_y, stage_r, stage,
    local_sems, send_sems, recv_sems,
):
    here = Place()
    sib = here.sibling()
    way = here.plane("fsdp")
    own = here.fsdp
    counter = [0]

    def local(src, dst):
        copy = pltpu.make_async_copy(src, dst, local_sems.at[counter[0]])
        counter[0] += 1
        copy.start()
        return copy

    first_x = local(x_ref, slots.at[0, :, pl.ds(0, D)])
    weights = [local(up_hbm, up_ref), local(down_hbm, down_ref)]

    def source(k):
        ring, pair, c = (0, -1, 1, 2)[k // 4], (k // 2) % 2, k % 2
        z = lax.rem(here.z + ring + 4, 4)
        xh = 1 - here.xh if pair else here.xh
        return z * 4 + xh * 2 + (1 - here.core if c else here.core)

    groups = ((4, 5, 8, 9), (6, 7, 10, 11), (12, 13, 14, 15), (0, 1, 2, 3))

    def fetch_g(group):
        return [local(g_ref.at[source(groups[group][s])], g_rows.at[s]) for s in range(4)]

    g_copies = fetch_g(0)
    ring = here.plane("seq")
    meet([sib, *way.values(), ring["up"], ring["down"]])
    net = Copies(send_sems, recv_sems)

    def block(k, low=0, rows=TOKENS):
        return slots.at[k, pl.ds(low, rows), pl.ds(0, D)]

    sent = {k: [] for k in range(16)}

    def push(k, to, target, low=0, rows=TOKENS, src=None):
        copy = net.start(block(k, low, rows) if src is None else src, block(to, low, rows), target)
        sent[k].append(copy)
        return copy

    across = push(0, 2, way["across"], src=x_ref)
    up = push(0, 4, way["up"], src=x_ref)
    down = push(0, 8, way["down"], src=x_ref)
    kin = {1: push(0, 1, sib, src=x_ref)}
    up.wait_recv()
    far_low = push(4, 12, way["up"], 0, 128)
    kin[5] = push(4, 5, sib)
    down.wait_recv()
    far_high = push(8, 12, way["down"], 128, 128)
    kin[9] = push(8, 9, sib)
    across.wait_recv()
    up_x = push(2, 6, way["up"])
    down_x = push(2, 10, way["down"])
    kin[3] = push(2, 3, sib)
    state = {}

    lanes = lax.broadcasted_iota(jnp.int32, (1, 128), 1)
    slot = lax.broadcasted_iota(jnp.int32, (2 * SLOTS, TOKENS), 0)
    slot_place = slot.astype(f32)
    first = slot < SLOTS
    expert = lax.broadcasted_iota(jnp.int32, (EXPERTS, TOKENS), 0)

    def gather(group):
        before = (
            lax.broadcasted_iota(jnp.int32, (TOKENS, TOKENS), 0)
            < lax.broadcasted_iota(jnp.int32, (TOKENS, TOKENS), 1)
        ).astype(f32).astype(bf16)
        for s in range(4):
            k = groups[group][s]
            if k in kin:
                kin[k].wait_recv()
            g_copies[s].wait()
            x_rows = slots[k, :, 0:D]
            named = masks_ref[source(k)].astype(f32)
            logits = dot_t(router_ref[0:EXPERTS, :], x_rows)
            peak = jnp.max(jnp.where(named > 0.0, logits, -1e30), axis=0, keepdims=True)
            parts = jnp.where(named > 0.0, jnp.exp(logits - peak), 0.0)
            gates = parts / jnp.sum(parts, axis=0, keepdims=True)
            rank = dot(named.astype(bf16), before)
            rank = jnp.where(named > 0.0, rank, -1000.0)

            def mine(values, i):
                return jnp.sum(jnp.where(expert == 2 * own + i, values, 0.0), axis=0, keepdims=True)

            wanted = jnp.where(first, mine(rank, 0), mine(rank, 1) + SLOTS)
            hot = jnp.where(slot_place == wanted, 1.0, 0.0)
            gate = jnp.sum(hot * jnp.where(first, mine(gates, 0), mine(gates, 1)), axis=1, keepdims=True)
            hot = hot.astype(bf16)
            places[s] = hot
            picked = dot(hot, x_rows).astype(bf16)
            grads = dot(hot, g_rows[s])
            pair = (grads * gate).astype(bf16)
            grads = grads.astype(bf16)
            for i in range(2):
                part = slice(SLOTS * i, SLOTS * (i + 1))
                there = slice(group * GROUP_ROWS + SLOTS * s, group * GROUP_ROWS + SLOTS * (s + 1))
                rows_x[i, there, :] = picked[part]
                rows_p[i, there, :] = pair[part]
                rows_g[i, SLOTS * s : SLOTS * (s + 1), :] = grads[part]
                slot_gate[i, SLOTS * s : SLOTS * (s + 1), :] = jnp.broadcast_to(gate[part], (SLOTS, 128))

    def run(group):
        here_rows = pl.ds(group * GROUP_ROWS, GROUP_ROWS)

        def one(e, carry):
            x_rows = rows_x[e, here_rows, :]
            gate_part = dot(x_rows, up_ref[e, :, 0:F])
            up_part = dot(x_rows, up_ref[e, :, F : 2 * F])
            sigmoid = 1.0 / (1.0 + jnp.exp(-gate_part))
            silu = gate_part * sigmoid
            hidden = (silu * up_part).astype(bf16)
            rows_h[e, here_rows, :] = hidden
            hidden_grad = dot(rows_p[e, here_rows, :], down_ref[e])
            slope = sigmoid * (1.0 + gate_part * (1.0 - sigmoid))
            rows_u[e, here_rows, 0:F] = (hidden_grad * up_part * slope).astype(bf16)
            rows_u[e, here_rows, F : 2 * F] = (hidden_grad * silu).astype(bf16)
            out = dot_t(hidden, down_ref[e]).astype(bf16).astype(f32)
            gate_grad = jnp.sum(out * rows_g[e].astype(f32), axis=1, keepdims=True)
            stage_y[e] = (out * slot_gate[e][:, 0:1]).astype(bf16)
            stage_r[e, :, 0:D] = dot_t(rows_u[e, here_rows, :], up_ref[e]).astype(bf16)
            high = gate_grad.astype(bf16).astype(f32)
            column = 2 * own + e
            stage_r[e, :, D:WIDE] = jnp.where(
                lanes == column, high, jnp.where(lanes == column + EXPERTS, gate_grad - high, 0.0)
            ).astype(bf16)
            return carry

        lax.fori_loop(0, 2, one, 0)

    y_sent = []

    def free_stage():
        for copy, remote in state.pop("y", ()):
            if remote:
                copy.wait_send()
            else:
                copy.wait()

    def combine(group):
        free_stage()
        for s in range(4):
            k = groups[group][s]
            for copy in sent[k]:
                copy.wait_send()
            part = slice(SLOTS * s, SLOTS * (s + 1))
            both = jnp.concatenate([stage_y[0, part, :], stage_y[1, part, :]], axis=0)
            stage[s, :, 0:D] = t_dot(places[s], both).astype(bf16)
            both = jnp.concatenate([stage_r[0, part, :], stage_r[1, part, :]], axis=0)
            slots[k] = t_dot(places[s], both).astype(bf16)
        state["y"] = []
        for s in range(4):
            k = groups[group][s]
            ready = stage.at[s, :, pl.ds(0, D)]
            if k % 2:
                y_sent.append(net.start(ready, y_in.at[k // 2], sib))
                state["y"].append((y_sent[-1], True))
            else:
                state["y"].append((local(ready, y_out.at[k // 2]), False))
        for k in groups[group][::2]:
            state[k] = net.start(slots.at[k + 1], sib_in.at[k // 2], sib)

    def join(k):
        state[k].wait_recv()
        slots[k] = (slots[k].astype(f32) + sib_in[k // 2].astype(f32)).astype(bf16)

    def half(ref, which):
        return ref.at[pl.ds(128 * which, 128)]

    gather(0)
    g_copies = fetch_g(1)
    for copy in weights:
        copy.wait()
    run(0)
    far_low.wait_recv()
    far_high.wait_recv()
    far_x = push(12, 14, way["across"])
    kin[13] = push(12, 13, sib)
    up_x.wait_recv()
    kin[7] = push(6, 7, sib)
    down_x.wait_recv()
    kin[11] = push(10, 11, sib)
    combine(0)
    gather(1)
    g_copies = fetch_g(2)
    join(4)
    hop_rd = net.start(slots.at[4], hop_in.at[5], way["down"])
    join(8)
    hop_ru = net.start(slots.at[8], hop_in.at[4], way["up"])
    run(1)
    far_x.wait_recv()
    kin[15] = push(14, 15, sib)
    combine(1)
    gather(2)
    g_copies = fetch_g(3)
    join(6)
    hop_xd = net.start(slots.at[6], hop_in.at[2], way["down"])
    join(10)
    hop_xu = net.start(slots.at[10], hop_in.at[3], way["up"])
    run(2)
    combine(2)
    first_x.wait()
    gather(3)
    join(14)
    hop_a = [net.start(half(slots.at[14], i), half(hop_in.at[0], i), way["across"]) for i in range(2)]
    join(12)
    run(3)
    far = []
    for i, to in enumerate(("up", "down")):
        hop_a[i].wait_recv()
        ref, other = half(slots.at[12], i), half(hop_in.at[0], i)
        ref[...] = (ref[...].astype(f32) + other[...].astype(f32)).astype(bf16)
        far.append(net.start(ref, half(hop_in.at[1], i), way[to]))
    combine(3)

    w_copies = []

    far_grads = []

    def send_far(dx):
        for copy in w_copies:
            copy.wait()
        w_copies.clear()
        rows = pl.ds(pl.multiple_of(here.seq_at(2, dx) * 128, 128), 128)
        for e, to in enumerate(("up", "down")):
            far_grads.append(net.start(grads_out.at[e, rows], far_out.at[dx, e], ring[to]))

    def weight_grad(e, dx):
        free_stage()
        for copy in w_copies:
            copy.wait()
        xl = 1 - here.xl if dx else here.xl
        columns = pl.ds(pl.multiple_of(xl * 512, 512), 512)
        for wide, left, right in (
            (slice(0, 2 * F), rows_x, rows_u), (slice(2 * F, 3 * F), rows_p, rows_h)
        ):
            result = t_dot(left[e, :, columns], right[e]).astype(bf16)
            for y in range(4):
                stage[y, 0:128, wide] = result[128 * y : 128 * (y + 1)]
        w_copies[:] = [
            local(
                stage.at[y, pl.ds(0, 128)],
                grads_out.at[e, pl.ds(pl.multiple_of(xl * 512 + 128 * y, 128), 128)],
            )
            for y in range(4)
        ]

    weight_grad(0, 1)
    relay = []
    for i, to in enumerate(("up", "down")):
        far[i].wait_recv()
        relay.append(net.start(half(hop_in.at[1], i), half(hop_in.at[7], i), way[to]))
    join(2)
    hop_xd.wait_recv()
    hop_xu.wait_recv()
    slots[2] = (slots[2].astype(f32) + hop_in[2].astype(f32) + hop_in[3].astype(f32)).astype(bf16)
    hop_rx = net.start(slots.at[2], hop_in.at[6], way["across"])
    join(0)
    weight_grad(1, 1)
    send_far(1)
    weight_grad(0, 0)
    weight_grad(1, 0)
    send_far(0)
    for copy in (hop_ru, hop_rd, hop_rx, *relay, *far_grads, *y_sent):
        copy.wait_recv()
    total = (
        slots[0].astype(f32)
        + hop_in[4].astype(f32)
        + hop_in[5].astype(f32)
        + hop_in[6].astype(f32)
        + hop_in[7].astype(f32)
    )
    row_out[...] = total[:, 0:D]
    gate_out[...] = total[:, D:WIDE]
    waited = {id(copy) for copies in (*sent.values(), y_sent) for copy in copies}
    for copy in net.all:
        if id(copy) not in waited:
            copy.wait_send()


def moe(x, g_all, masks, router_t, up, down):
    any_space = pl.BlockSpec(memory_space=pl.ANY)
    vmem = pl.BlockSpec(memory_space=pltpu.VMEM)
    return pl.pallas_call(
        moe_kernel,
        in_specs=[any_space, any_space, vmem, vmem, any_space, any_space],
        out_specs=[vmem, vmem, any_space, any_space, any_space, any_space],
        out_shape=[
            jax.ShapeDtypeStruct((TOKENS, D), f32),
            jax.ShapeDtypeStruct((TOKENS, 128), f32),
            jax.ShapeDtypeStruct((8, TOKENS, D), bf16),
            jax.ShapeDtypeStruct((8, TOKENS, D), bf16),
            jax.ShapeDtypeStruct((2, D, 3 * F), bf16),
            jax.ShapeDtypeStruct((2, 2, 128, 3 * F), bf16),
        ],
        scratch_shapes=[
            pltpu.VMEM((16, TOKENS, WIDE), bf16),
            pltpu.VMEM((8, TOKENS, WIDE), bf16),
            pltpu.VMEM((8, TOKENS, WIDE), bf16),
            pltpu.VMEM((4, TOKENS, D), bf16),
            pltpu.VMEM((2, D, 2 * F), bf16),
            pltpu.VMEM((2, D, F), bf16),
            pltpu.VMEM((2, ROWS, D), bf16),
            pltpu.VMEM((2, ROWS, D), bf16),
            pltpu.VMEM((2, ROWS, F), bf16),
            pltpu.VMEM((2, ROWS, 2 * F), bf16),
            pltpu.VMEM((2, GROUP_ROWS, D), bf16),
            pltpu.VMEM((2, GROUP_ROWS, 128), f32),
            pltpu.VMEM((4, 2 * SLOTS, TOKENS), bf16),
            pltpu.VMEM((2, GROUP_ROWS, D), bf16),
            pltpu.VMEM((2, GROUP_ROWS, WIDE), bf16),
            pltpu.VMEM((4, TOKENS, 3 * F), bf16),
            pltpu.SemaphoreType.DMA((56,)),
            pltpu.SemaphoreType.DMA((50,)),
            pltpu.SemaphoreType.DMA((50,)),
        ],
        compiler_params=pltpu.CompilerParams(
            collective_id=4, has_side_effects=True, vmem_limit_bytes=63 * 1024 * 1024
        ),
        cost_estimate=pl.CostEstimate(flops=32 * 10**9, bytes_accessed=40 << 20, transcendentals=1 << 21),
        name="moe",
    )(x, g_all, masks, router_t, up, down)


def on_device(
    tokens, attn_gain, qkv_weight, qk_gain, out_weight, ffn_gain, router_weight,
    gate_up_weight, down_weight, routes, cotangent,
):
    x = tokens.reshape(TOKENS, D)
    cot = cotangent.reshape(TOKENS, D)
    route_ids = routes.reshape(TOKENS, TOPK)
    whole, masks, side = gather_weights(
        qkv_weight, out_weight, router_weight, attn_gain.reshape(1, 8), ffn_gain.reshape(1, 8),
        qk_gain.reshape(1, 1), route_ids, cot,
    )
    whole = whole.reshape(2, D, WCOLS)

    positions = lax.axis_index("seq") * TOKENS + jnp.arange(TOKENS, dtype=jnp.int32)
    half_dim = HEAD_SIZE // 2
    freq_index = jnp.arange(half_dim, dtype=f32)
    inverse = jnp.exp(-(2.0 * freq_index / HEAD_SIZE) * math.log(rope_base))
    angles = positions.astype(f32)[:, None] * inverse[None, :]
    cos, sin = jnp.cos(angles), jnp.sin(angles)
    cos = jnp.concatenate([cos, cos, cos, cos], axis=1)
    sin = jnp.concatenate([-sin, sin, -sin, sin], axis=1)

    heads, g_all, full, logs, attended, after, normed_ffn, gates, small_t, raw = front(
        x, whole, route_ids, cos, sin, cot, side
    )
    row_sum, gate_sum, y_own, y_other, expert_grads, far = moe(
        normed_ffn, g_all, masks, small_t, gate_up_weight, down_weight
    )
    layer_out, token_grad, qkv_part, out_part, small, up_part, down_part = back(
        gate_sum, gates, after, x, cot, attended, normed_ffn, small_t, heads, full, logs, cos, sin,
        row_sum, raw, whole, y_own, y_other, expert_grads, far,
    )
    return (
        layer_out.reshape(1, TOKENS, D),
        token_grad.reshape(1, TOKENS, D),
        small[:, EXPERTS],
        qkv_part,
        small[0:1, EXPERTS + 2],
        out_part,
        small[:, EXPERTS + 1],
        small[:, :EXPERTS],
        up_part,
        down_part,
    )


def solution(mesh):
    return jax.shard_map(
        on_device,
        mesh=mesh,
        in_specs=(
            P("fsdp", "seq", None),
            P(("seq", "fsdp")),
            P(("seq", "fsdp"), None),
            P(("seq", "fsdp")),
            P(("seq", "fsdp"), None),
            P(("seq", "fsdp")),
            P(("seq", "fsdp"), None),
            P("fsdp", None, None),
            P("fsdp", None, None),
            P("fsdp", "seq", None),
            P("fsdp", "seq", None),
        ),
        out_specs=(
            P("fsdp", "seq", None),
            P("fsdp", "seq", None),
            P(("seq", "fsdp")),
            P(("seq", "fsdp"), None),
            P(("seq", "fsdp")),
            P(("seq", "fsdp"), None),
            P(("seq", "fsdp")),
            P(("seq", "fsdp"), None),
            P("fsdp", "seq", None),
            P("fsdp", "seq", None),
        ),
        check_vma=False,
    )
```

```python
import jax
import jax.numpy as jnp
import numpy as np
from jax import lax
from jax.experimental import pallas as pl
from jax.experimental.pallas import tpu as pltpu
from jax.sharding import PartitionSpec as P

D = 1024
HEAD_SIZE = 64
F = 512
TOPK = 8
EXPERTS = 32
SLOTS = 96
TOKENS = 256
SEQ = 8
FSDP = 16
LENGTH = SEQ * TOKENS
GROUP_ROWS = 4 * SLOTS
ROWS = 4 * GROUP_ROWS
GCOLS = 1536
VMEM = 60 * 1024 * 1024

epsilon = 1e-06
rope_base = 10000.0
f32 = jnp.float32
bf16 = jnp.bfloat16


def dot(a, b):
    return lax.dot_general(a, b, (((1,), (0,)), ((), ())), preferred_element_type=f32)


def dot_t(a, b):
    return lax.dot_general(a, b, (((1,), (1,)), ((), ())), preferred_element_type=f32)


def t_dot(a, b):
    return lax.dot_general(a, b, (((0,), (0,)), ((), ())), preferred_element_type=f32)


MESH = pl.DeviceIdType.MESH


class Place:
    def __init__(self):
        self.seq = lax.axis_index("seq")
        self.fsdp = lax.axis_index("fsdp")
        self.core = lax.rem(self.fsdp, 2)
        self.xh = lax.rem(self.fsdp // 2, 2)
        self.z = self.fsdp // 4
        self.y = lax.rem(self.seq, 4)
        self.xl = self.seq // 4

    def sibling(self):
        return {"fsdp": self.fsdp + 1 - 2 * self.core}

    def fsdp_at(self, ring, pair):
        z = lax.rem(self.z + ring + 4, 4)
        xh = 1 - self.xh if pair else self.xh
        return z * 4 + xh * 2 + self.core

    def seq_at(self, ring, pair):
        y = lax.rem(self.y + ring + 4, 4)
        xl = 1 - self.xl if pair else self.xl
        return xl * 4 + y

    def plane(self, axis):
        at = self.fsdp_at if axis == "fsdp" else self.seq_at
        return {
            "up": {axis: at(1, 0)},
            "down": {axis: at(-1, 0)},
            "across": {axis: at(0, 1)},
        }


def meet(targets):
    barrier = pltpu.get_barrier_semaphore()
    for target in targets:
        pl.semaphore_signal(barrier, inc=1, device_id=target, device_id_type=MESH)
    pl.semaphore_wait(barrier, len(targets))


class Copies:
    def __init__(self, send_sems, recv_sems):
        self.send_sems, self.recv_sems, self.count, self.all = send_sems, recv_sems, 0, []

    def start(self, src, dst, target):
        k = self.count
        self.count += 1
        copy = pltpu.make_async_remote_copy(
            src_ref=src, dst_ref=dst, send_sem=self.send_sems.at[k], recv_sem=self.recv_sems.at[k],
            device_id=target, device_id_type=MESH,
        )
        copy.start()
        self.all.append(copy)
        return copy

    def finish(self, done=()):
        for copy in self.all:
            if all(copy is not other for other in done):
                copy.wait_send()


OTHERS = ((2, 1), (2, 0), (0, 1), (1, 1), (-1, 1), (1, 0), (-1, 0))
WCOLS = 1664


def lane_halves():
    lanes = lax.broadcasted_iota(jnp.int32, (1, 128), 1)
    return lanes, lanes < HEAD_SIZE


def head_mean(values, low_half):
    low = jnp.sum(jnp.where(low_half, values, 0.0), axis=1, keepdims=True)
    high = jnp.sum(jnp.where(low_half, 0.0, values), axis=1, keepdims=True)
    return jnp.where(low_half, low, high) * (1.0 / HEAD_SIZE)


def partner(values, lanes):
    return jnp.where(
        lax.rem(lanes, HEAD_SIZE) < HEAD_SIZE // 2, pltpu.roll(values, 96, 1), pltpu.roll(values, 32, 1)
    )


def rotary_tables():
    inverse = rope_base ** (-2.0 * (np.arange(128) % 32) / HEAD_SIZE)
    near = np.arange(TOKENS)[:, None] * inverse[None, :]
    far = TOKENS * np.arange(SEQ)[:, None] * inverse[None, :]
    return [jnp.asarray(np.stack([np.cos(a), np.sin(a)]), f32) for a in (near, far)]


def rotary(near_ref, far_ref, block, lanes):
    pick = lax.broadcasted_iota(jnp.int32, (SEQ, 128), 0) == block
    far_cos = jnp.sum(jnp.where(pick, far_ref[0], 0.0), axis=0, keepdims=True)
    far_sin = jnp.sum(jnp.where(pick, far_ref[1], 0.0), axis=0, keepdims=True)
    cos = near_ref[0] * far_cos - near_ref[1] * far_sin
    sin = near_ref[1] * far_cos + near_ref[0] * far_sin
    return cos, jnp.where(lax.rem(lanes, HEAD_SIZE) < HEAD_SIZE // 2, -sin, sin)


def row_scale(values):
    return lax.rsqrt(jnp.mean(values * values, axis=1, keepdims=True) + epsilon)


def gain_tiles(small_t, lanes):
    pick = (
        lax.broadcasted_iota(jnp.int32, (D, 128), 0) == 8 * lax.broadcasted_iota(jnp.int32, (D, 128), 1)
    ).astype(f32).astype(bf16)
    gains = dot(small_t[32:48, :], pick)[2:3, :]
    other = pltpu.roll(gains, 64, 1)
    low_half = lanes < HEAD_SIZE
    return jnp.where(low_half, gains, other), jnp.where(low_half, other, gains)


def front_kernel(
    x_ref, w_ref, routes_ref, near_ref, far_place_ref, cot_ref, side_ref,
    heads_out, g_out, full_ref, logs_ref, att_ref, after_ref, normed_ref, gates_ref, small_t_ref, raw_ref, gates_t_ref,
    wq, wkv, wo, small, send, heads, out_buf, att, key0, key1, value,
    local_sems, send_sems, recv_sems,
):
    here = Place()
    me = here.seq
    loads = [
        pltpu.make_async_copy(w_ref.at[h, :, pl.ds(start, width)], there, local_sems.at[k])
        for k, (h, start, width, there) in enumerate(
            (
                (0, 1536, 128, small),
                (0, 0, 1024, wq),
                (1, 0, 1024, wkv),
                (0, 1024, 512, wo.at[0]),
                (1, 1024, 512, wo.at[1]),
            )
        )
    ]
    for copy in loads:
        copy.start()
    peers = [here.seq_at(*other) for other in OTHERS]
    sib = here.sibling()
    way = here.plane("fsdp")
    meet([sib, *way.values()] + [{"seq": peer} for peer in peers])
    net = Copies(send_sems, recv_sems)

    def gather_cotangent():
        def at(ring, pair):
            return g_out.at[here.fsdp_at(ring, pair)]

        def half(ref, which):
            return ref.at[pl.ds(128 * which, 128)]

        def go(ref, target):
            return net.start(ref, ref, target)

        up, down = [net.start(cot_ref, at(0, 0), way[w]) for w in ("up", "down")]
        kin = [net.start(cot_ref, at(0, 0), sib), net.start(side_ref, at(0, 1), sib)]
        yield
        up.wait_recv()
        far = [go(half(at(-1, 0), 0), way["up"])]
        kin.append(go(at(-1, 0), sib))
        down.wait_recv()
        far.append(go(half(at(1, 0), 1), way["down"]))
        kin.append(go(at(1, 0), sib))
        up, down = [net.start(side_ref, at(0, 1), way[w]) for w in ("up", "down")]
        yield
        for copy in far:
            copy.wait_recv()
        across = go(at(2, 0), way["across"])
        kin.append(go(at(2, 0), sib))
        yield
        up.wait_recv()
        kin.append(go(at(-1, 1), sib))
        down.wait_recv()
        kin.append(go(at(1, 1), sib))
        across.wait_recv()
        kin.append(go(at(2, 1), sib))
        yield
        for copy in kin:
            copy.wait_recv()

    moves = gather_cotangent()
    next(moves)
    lanes, low_half = lane_halves()
    loads[0].wait()
    small_t = jnp.transpose(small[...].astype(f32)).astype(bf16)
    small_t_ref[...] = small_t
    x = x_ref[...].astype(f32)
    normed = (x * row_scale(x) * small_t[32:33, :].astype(f32)).astype(bf16)
    query_gain, key_gain = gain_tiles(small_t, lanes)
    cos, sin = rotary(near_ref, far_place_ref, me, lanes)
    loads[1].wait()
    queries = dot(normed, wq[...])
    loads[2].wait()
    kv = dot(normed, wkv[...])

    def turned(tile, gain):
        normal = tile * lax.rsqrt(head_mean(tile * tile, low_half) + epsilon) * gain
        return normal * cos + partner(normal, lanes) * sin

    for j in range(4):
        part = slice(128 * j, 128 * (j + 1))
        raw_ref[8 + j] = kv[:, part]
        keys = turned(kv[:, part], key_gain)
        values = kv[:, 512 + 128 * j : 640 + 128 * j]
        send[2 * j, :, 128:256] = jnp.where(low_half, keys, pltpu.roll(values, 64, 1)).astype(bf16)
        send[2 * j + 1, :, 128:256] = jnp.where(low_half, pltpu.roll(keys, 64, 1), values).astype(bf16)
    for h in range(8):
        raw_ref[h] = queries[:, 128 * h : 128 * (h + 1)]
        send[h, :, 0:128] = turned(raw_ref[h], query_gain).astype(bf16)
    copies = [net.start(send.at[peer], heads.at[me], {"seq": peer}) for peer in peers]
    heads[me] = send[me]
    next(moves)
    for copy in copies:
        copy.wait_recv()
    save = pltpu.make_async_copy(heads, heads_out, local_sems.at[5])
    save.start()
    for c in range(8):
        rows = slice(TOKENS * c, TOKENS * (c + 1))
        pair = heads[c, :, 128:256].astype(f32)
        key0[rows, :] = jnp.where(low_half, pair, 0.0).astype(bf16)
        key1[rows, :] = jnp.where(low_half, 0.0, pltpu.roll(pair, 64, 1)).astype(bf16)
        value[rows, :] = jnp.where(low_half, jnp.where(lanes == 0, 1.0, 0.0), pair).astype(bf16)

    def block(i, carry):
        j = lax.rem(me + 1 + i, 8)
        query = (heads[j, :, 0:128].astype(f32) * (1.0 / 8.0)).astype(bf16)
        results = []
        for key in (key0, key1):
            total = jnp.zeros((TOKENS, 128), f32)
            for c in range(4):
                part = pl.ds(c * 512, 512)
                weights = jnp.exp(dot_t(query, key[part, :]))
                total = total + dot(weights.astype(bf16), value[part, :])
            results.append(total)
        sum0, sum1 = results[0][:, 0:1], results[1][:, 0:1]
        full = jnp.where(low_half, pltpu.roll(results[0] / sum0, 64, 1), results[1] / sum1)
        rows = pl.ds(pl.multiple_of(j * TOKENS, TOKENS), TOKENS)
        full_ref[rows, :] = full
        logs_ref[rows, :] = jnp.where(low_half, jnp.log(sum0), jnp.log(sum1))
        out_buf[j] = full.astype(bf16)

        @pl.when(i < 7)
        def _():
            answer(i).start()

        return carry

    columns = pl.ds(pl.multiple_of(me * 128, 128), 128)

    def answer(i):
        j = lax.rem(me + 1 + i, 8)
        return pltpu.make_async_remote_copy(
            src_ref=out_buf.at[j], dst_ref=att.at[:, columns], send_sem=send_sems.at[24 + i],
            recv_sem=recv_sems.at[24 + i], device_id={"seq": j}, device_id_type=MESH,
        )

    lax.fori_loop(0, 1, block, 0)
    next(moves)
    lax.fori_loop(1, 7, block, 0)
    next(moves)
    lax.fori_loop(7, 8, block, 0)
    att[:, columns] = out_buf[me]
    for k in (3, 4):
        loads[k].wait()
    for i in range(7):
        answer(i).wait_recv()
    attended = att[...]
    att_ref[...] = attended
    squares = jnp.zeros((TOKENS, 1), f32)
    for h in range(2):
        part = slice(512 * h, 512 * (h + 1))
        after = x_ref[:, part].astype(f32) + dot(attended, wo[h])
        after_ref[:, part] = after
        squares = squares + jnp.sum(after * after, axis=1, keepdims=True)
    scaling = lax.rsqrt(squares * (1.0 / D) + epsilon)
    normed = (after_ref[...] * scaling * small_t[33:34, :].astype(f32)).astype(bf16)
    normed_ref[...] = normed
    logits = dot(normed, small[...])
    expert = lax.broadcasted_iota(jnp.int32, (128, TOKENS), 0)
    named = jnp.zeros((128, TOKENS), f32)
    for k in range(TOPK):
        named = jnp.where(routes_ref[k : k + 1, :] == expert, 1.0, named)
    named = jnp.transpose(named)
    peak = jnp.max(jnp.where(named > 0.0, logits, -1e30), axis=1, keepdims=True)
    chosen = jnp.where(named > 0.0, jnp.exp(logits - peak), 0.0)
    gates = chosen / jnp.sum(chosen, axis=1, keepdims=True)
    gates_ref[...] = gates
    across = jnp.transpose(gates)
    gates_t_ref[...] = jnp.zeros_like(gates_t_ref)
    for i in range(FSDP):
        gates_t_ref[i, 0:2, :] = across[2 * i : 2 * i + 2, :]
    for _ in moves:
        pass
    save.wait()
    for i in range(7):
        answer(i).wait_send()
    net.finish()


def front(x, whole, routes, near, far, cot, side):
    vmem = pl.BlockSpec(memory_space=pltpu.VMEM)
    hbm = pl.BlockSpec(memory_space=pl.ANY)
    return pl.pallas_call(
        front_kernel,
        in_specs=[vmem, hbm, vmem, vmem, vmem, hbm, hbm],
        out_specs=[hbm] * 2 + [vmem] * 9,
        out_shape=[
            jax.ShapeDtypeStruct((8, TOKENS, 256), bf16),
            jax.ShapeDtypeStruct((FSDP, TOKENS, D), bf16),
            jax.ShapeDtypeStruct((LENGTH, 128), f32),
            jax.ShapeDtypeStruct((LENGTH, 128), f32),
            jax.ShapeDtypeStruct((TOKENS, D), bf16),
            jax.ShapeDtypeStruct((TOKENS, D), f32),
            jax.ShapeDtypeStruct((TOKENS, D), bf16),
            jax.ShapeDtypeStruct((TOKENS, 128), f32),
            jax.ShapeDtypeStruct((128, D), bf16),
            jax.ShapeDtypeStruct((12, TOKENS, 128), f32),
            jax.ShapeDtypeStruct((FSDP, 8, TOKENS), f32),
        ],
        scratch_shapes=[
            pltpu.VMEM((D, 1024), bf16),
            pltpu.VMEM((D, 1024), bf16),
            pltpu.VMEM((2, D, 512), bf16),
            pltpu.VMEM((D, 128), bf16),
            pltpu.VMEM((8, TOKENS, 256), bf16),
            pltpu.VMEM((8, TOKENS, 256), bf16),
            pltpu.VMEM((8, TOKENS, 128), bf16),
            pltpu.VMEM((TOKENS, D), bf16),
            pltpu.VMEM((LENGTH, 128), bf16),
            pltpu.VMEM((LENGTH, 128), bf16),
            pltpu.VMEM((LENGTH, 128), bf16),
            pltpu.SemaphoreType.DMA((8,)),
            pltpu.SemaphoreType.DMA((31,)),
            pltpu.SemaphoreType.DMA((31,)),
        ],
        compiler_params=pltpu.CompilerParams(collective_id=2, has_side_effects=True, vmem_limit_bytes=VMEM),
        cost_estimate=pl.CostEstimate(
            flops=4 * 10**9, bytes_accessed=16 << 20, transcendentals=2 * LENGTH * LENGTH
        ),
        name="front",
    )(x, whole, routes, near, far, cot, side)


def split3(values):
    high = values.astype(bf16).astype(f32)
    rest = values - high
    middle = rest.astype(bf16).astype(f32)
    return high, middle, rest - middle


def with_terms(lanes, start, parts):
    high, middle, low = parts
    return jnp.where(
        lanes == start,
        high,
        jnp.where(lanes == start + 1, middle, jnp.where(lanes == start + 2, low, 0.0)),
    )


def back_kernel(
    gate_sum_ref, gates_ref, after_ref, x_ref, cot_ref, att_ref, normed_ref, small_t_ref,
    heads_ref, full_ref, logs_ref, near_ref, far_place_ref, row_ref, raw_ref, w_ref, y_ref, y_other, grads_ref, far_ref,
    layer_ref, token_ref, qkv_out, wo_out, small_out, up_out, down_out,
    wqkv, wo, send, grads, back_q, back_kv, pg, after_grad,
    key0, key1, value0, value1, key_t, dk_total, dv_total,
    slots, y_stage, hop_in,
    parts, parts_in, small, small_in, hop_a, hop_b, late_a, late_b, small_s, small_f, total, total_in,
    chunks, far_in, chunk_in, local_sems, send_sems, recv_sems,
):
    here = Place()
    me = here.seq
    sib = here.sibling()
    way = here.plane("fsdp")
    loads = [
        pltpu.make_async_copy(w_ref.at[h, :, pl.ds(start, width)], there, local_sems.at[k])
        for k, (h, start, width, there) in enumerate(
            (
                (0, 1024, 512, wo.at[0]),
                (1, 1024, 512, wo.at[1]),
                (0, 0, 1024, wqkv.at[0]),
                (1, 0, 1024, wqkv.at[1]),
            )
        )
    ]
    loads.append(pltpu.make_async_copy(row_ref, after_grad, local_sems.at[19]))
    for copy in loads:
        copy.start()
    e_loads = [
        pltpu.make_async_copy(
            grads_ref.at[:, pl.ds(pl.multiple_of(here.seq_at(ring, pair) * 128, 128), 128)],
            chunks.at[i, pair], local_sems.at[12 + 2 * i + pair],
        )
        for i, ring in enumerate((-1, 1, 0)) for pair in range(2)
    ]
    e_loads.append(pltpu.make_async_copy(far_ref, far_in, local_sems.at[18]))
    order = (6, 7, 3, 5, 2, 4, 1, 0)
    y_loads = {k: pltpu.make_async_copy(y_ref.at[k], slots.at[k], local_sems.at[4 + k]) for k in order}
    y_more = {
        k: pltpu.make_async_copy(y_other.at[k], y_stage.at[i % 2], local_sems.at[20 + k]) for i, k in enumerate(order)
    }
    for copy in y_loads.values():
        copy.start()
    for k in order[:2]:
        y_more[k].start()
    peers = [here.seq_at(*other) for other in OTHERS]
    seq_peers = [{"seq": peer} for peer in peers]
    fsdp_peers = [{"fsdp": here.fsdp_at(*other)} for other in OTHERS]
    meet([sib, *seq_peers, *fsdp_peers])
    net = Copies(send_sems, recv_sems)
    for copy in e_loads:
        copy.start()
    lanes, low_half = lane_halves()

    gate_grad = gate_sum_ref[...]
    gates = gates_ref[...]
    chosen = gates * (gate_grad - jnp.sum(gates * gate_grad, axis=1, keepdims=True))
    logits_grad = chosen.astype(bf16)
    loads[4].wait()
    normed_grad = after_grad[...] + dot(logits_grad, small_t_ref[...])
    after = after_ref[...]
    scaling = row_scale(after)
    weighted = normed_grad * small_t_ref[33:34, :].astype(f32)
    middle = jnp.mean(weighted * after, axis=1, keepdims=True)
    after_grad[...] = (
        cot_ref[...].astype(f32) + scaling * weighted - after * (scaling * scaling * scaling * middle)
    )
    after_low = after_grad[...].astype(bf16)
    ffn_gain = jnp.sum(normed_grad * after * scaling, axis=0, keepdims=True)
    for k in (0, 1):
        loads[k].wait()
    for q in range(2):
        rows = slice(512 * q, 512 * (q + 1))
        attended_grad = dot_t(after_low[:, 0:512], wo[0, rows, :]) + dot_t(after_low[:, 512:1024], wo[1, rows, :])
        for h in range(4):
            send[4 * q + h] = attended_grad[:, 128 * h : 128 * (h + 1)].astype(bf16)

    def delivery(d):
        peer = lax.rem(me + d, 8)
        return pltpu.make_async_remote_copy(
            src_ref=send.at[peer], dst_ref=grads.at[me], send_sem=send_sems.at[92 + d],
            recv_sem=recv_sems.at[92 + d], device_id={"seq": peer}, device_id_type=MESH,
        )

    for d in range(7, 0, -1):
        delivery(d).start()
    grads[me] = send[me]
    router_grad = t_dot(normed_ref[...], logits_grad)
    small[...] = router_grad.reshape(8, 8, 2, 8, 128)
    for h in range(2):
        out_grad = t_dot(att_ref[...], after_low[:, 512 * h : 512 * (h + 1)]).astype(bf16)
        parts[h, :, :, :, 1024:1536] = out_grad.reshape(8, 8, 16, 512)
    out_join = net.start(
        parts.at[1 - here.core, :, :, :, pl.ds(1024, 512)], parts_in.at[:, :, :, pl.ds(1024, 512)], sib
    )

    def add_to(ref, *values):
        result = ref[...].astype(f32)
        for value in values:
            result = result + value[...].astype(f32)
        ref[...] = result.astype(bf16)

    def join(k):
        i = order.index(k)
        y_loads[k].wait()
        y_more[k].wait()
        add_to(slots.at[k], y_stage.at[i % 2])
        if i + 2 < 8:
            y_more[order[i + 2]].start()

    def half(ref, which):
        return ref.at[pl.ds(128 * which, 128)]

    def expert_sum():
        join(6)
        join(7)
        up = [net.start(half(slots.at[6 + j], 0), half(hop_in.at[j], 0), way["up"]) for j in range(2)]
        down = [net.start(half(slots.at[6 + j], 1), half(hop_in.at[j], 1), way["down"]) for j in range(2)]
        yield
        for k in (3, 5, 2, 4):
            join(k)
        up[1].wait_recv()
        down[1].wait_recv()
        add_to(half(slots.at[5], 0), half(hop_in.at[1], 0))
        add_to(half(slots.at[3], 1), half(hop_in.at[1], 1))
        beside = [
            net.start(slots.at[5], hop_in.at[2], way["up"]), net.start(slots.at[3], hop_in.at[3], way["down"])
        ]
        up[0].wait_recv()
        down[0].wait_recv()
        add_to(half(slots.at[4], 0), half(hop_in.at[0], 0))
        add_to(half(slots.at[2], 1), half(hop_in.at[0], 1))
        own = [
            net.start(slots.at[4], hop_in.at[4], way["up"]), net.start(slots.at[2], hop_in.at[5], way["down"])
        ]
        yield
        join(1)
        join(0)
        for copy in beside:
            copy.wait_recv()
        add_to(slots.at[1], hop_in.at[2], hop_in.at[3])
        own.append(net.start(slots.at[1], hop_in.at[6], way["across"]))
        yield
        for copy in own:
            copy.wait_recv()
        layer_ref[...] = (
            after_ref[...]
            + slots[0].astype(f32)
            + hop_in[4].astype(f32)
            + hop_in[5].astype(f32)
            + hop_in[6].astype(f32)
        ).astype(bf16)

    def expert_grads():
        ring = here.plane("seq")
        for copy in e_loads:
            copy.wait()
        for pair in (1, 0):
            add_to(chunks.at[0, pair, 1], far_in.at[pair, 1])
            add_to(chunks.at[1, pair, 0], far_in.at[pair, 0])
        beside = [
            net.start(chunks.at[0, 1], chunk_in.at[0], ring["down"]),
            net.start(chunks.at[1, 1], chunk_in.at[1], ring["up"]),
        ]
        yield
        own = [
            net.start(chunks.at[0, 0], chunk_in.at[2], ring["down"]),
            net.start(chunks.at[1, 0], chunk_in.at[3], ring["up"]),
        ]
        for copy in beside:
            copy.wait_recv()
        add_to(chunks.at[2, 1], chunk_in.at[0], chunk_in.at[1])
        own.append(net.start(chunks.at[2, 1], chunk_in.at[4], ring["across"]))
        yield
        for copy in own:
            copy.wait_recv()
        result = chunks[2, 0].astype(f32)
        for i in range(2, 5):
            result = result + chunk_in[i].astype(f32)
        up_out[...] = result[:, :, 0 : 2 * F]
        down_out[...] = result[:, :, 2 * F : 3 * F]

    moves = expert_sum()
    more_moves = expert_grads()
    next(moves)
    ones_high = jnp.where((lanes >= 64) & (lanes < 67), 1.0, 0.0)
    ones_low = jnp.where(lanes < 3, 1.0, 0.0)
    for c in range(8):
        rows = slice(TOKENS * c, TOKENS * (c + 1))
        pair = heads_ref[c, :, 128:256].astype(f32)
        swapped = pltpu.roll(pair, 64, 1)
        key0[rows, :] = jnp.where(low_half, pair, ones_high).astype(bf16)
        key1[rows, :] = jnp.where(low_half, ones_low, swapped).astype(bf16)
        value0[rows, :] = jnp.where(low_half, swapped, ones_high).astype(bf16)
        value1[rows, :] = jnp.where(low_half, ones_low, pair).astype(bf16)
        key_t[:, rows] = jnp.transpose(pair)[0:64, :].astype(bf16)
    dk_total[...] = jnp.zeros_like(dk_total)
    dv_total[...] = jnp.zeros_like(dv_total)
    columns = pl.ds(pl.multiple_of(me * 128, 128), 128)

    def answer(i):
        j = lax.rem(me + i, 8)
        return pltpu.make_async_remote_copy(
            src_ref=grads.at[j], dst_ref=back_q.at[:, columns], send_sem=send_sems.at[84 + i],
            recv_sem=recv_sems.at[84 + i], device_id={"seq": j}, device_id_type=MESH,
        )

    def block(i, carry):
        j = lax.rem(me + i, 8)

        @pl.when(i > 0)
        def _():
            delivery(8 - i).wait_recv()

        rows = pl.ds(pl.multiple_of(j * TOKENS, TOKENS), TOKENS)
        query = heads_ref[j, :, 0:128].astype(f32) * (1.0 / 8.0)
        grad = grads[j].astype(f32)
        logs = logs_ref[rows, :]
        product = grad * full_ref[rows, :]
        delta0 = jnp.sum(jnp.where(low_half, product, 0.0), axis=1, keepdims=True)
        delta1 = jnp.sum(jnp.where(low_half, 0.0, product), axis=1, keepdims=True)
        query0 = jnp.where(low_half, query, with_terms(lanes, 64, split3(-logs[:, 0:1]))).astype(bf16)
        query1 = jnp.where(low_half, with_terms(lanes, 0, split3(-logs[:, 64:65])), query).astype(bf16)
        grad0 = jnp.where(low_half, grad, with_terms(lanes, 64, split3(-delta0))).astype(bf16)
        grad1 = jnp.where(low_half, with_terms(lanes, 0, split3(-delta1)), grad).astype(bf16)
        only_query = (
            jnp.where(low_half, query, 0.0).astype(bf16), jnp.where(low_half, 0.0, query).astype(bf16)
        )
        only_grad = (jnp.where(low_half, grad, 0.0).astype(bf16), jnp.where(low_half, 0.0, grad).astype(bf16))
        dq = [jnp.zeros((64, TOKENS), f32), jnp.zeros((64, TOKENS), f32)]
        for c in range(4):
            part = pl.ds(c * 512, 512)
            dv = dv_total[part, :]
            dk = dk_total[part, :]
            for h, (key, value, query_h, grad_h) in enumerate(
                ((key0, value0, query0, grad0), (key1, value1, query1, grad1))
            ):
                probs = jnp.exp(dot_t(key[part, :], query_h))
                inner = dot_t(value[part, :], grad_h)
                dv = dv + dot(probs.astype(bf16), only_grad[h])
                scores = (probs * inner).astype(bf16)
                dk = dk + dot(scores, only_query[h])
                dq[h] = dq[h] + dot(key_t[:, c * 512 : (c + 1) * 512], scores)
            dv_total[part, :] = dv
            dk_total[part, :] = dk
        both = jnp.concatenate(dq, axis=0) * (1.0 / 8.0)
        grads[j] = jnp.transpose(both).astype(bf16)

        @pl.when(i > 0)
        def _():
            answer(i).start()

        return carry

    lax.fori_loop(0, 3, block, 0)
    next(more_moves)
    next(moves)
    lax.fori_loop(3, 6, block, 0)
    next(moves)
    lax.fori_loop(6, 8, block, 0)
    for d in range(1, 8):
        delivery(d).wait_send()
    for c in range(8):
        rows = slice(TOKENS * c, TOKENS * (c + 1))
        dk = dk_total[rows, :]
        dv = dv_total[rows, :]
        dk = dk + pltpu.roll(dk, 64, 1)
        dv = dv + pltpu.roll(dv, 64, 1)
        send[c] = jnp.where(low_half, dk, dv).astype(bf16)
    to_tokens = [net.start(send.at[peer], back_kv.at[me], {"seq": peer}) for peer in peers]
    raw = [
        pltpu.make_async_copy(raw_ref.at[h], there.at[pl.ds(TOKENS * (h % 8), TOKENS)], local_sems.at[28 + h])
        for h, there in [(h, dk_total) for h in range(8)] + [(h, dv_total) for h in range(8, 12)]
    ]
    for copy in raw:
        copy.start()
    back_kv[me] = send[me]
    back_q[:, columns] = grads[me]
    x = x_ref[...].astype(f32)
    x_scaling = row_scale(x)
    attn_gain = small_t_ref[32:33, :].astype(f32)
    normed = (x * x_scaling * attn_gain).astype(bf16)
    query_gain, key_gain = gain_tiles(small_t_ref[...], lanes)
    cos, sin = rotary(near_ref, far_place_ref, me, lanes)
    for i in range(1, 8):
        answer(i).wait_recv()

    def unturned(grad, tile, gain):
        grad = grad * cos - partner(grad, lanes) * sin
        scale = lax.rsqrt(head_mean(tile * tile, low_half) + epsilon)
        weighted = grad * gain
        middle = head_mean(weighted * tile, low_half)
        result = scale * weighted - tile * (scale * scale * scale * middle)
        return result.astype(bf16), jnp.sum(grad * tile * scale, axis=0, keepdims=True)

    for copy in raw:
        copy.wait()
    next(more_moves)
    query_terms = jnp.zeros((1, 128), f32)
    for h in range(8):
        part = slice(128 * h, 128 * (h + 1))
        pg[0, :, part], terms = unturned(back_q[:, part].astype(f32), dk_total[TOKENS * h : TOKENS * (h + 1), :], query_gain)
        query_terms = query_terms + terms
    for copy in to_tokens:
        copy.wait_recv()
    key_terms = jnp.zeros((1, 128), f32)
    for j in range(4):
        first, second = back_kv[2 * j].astype(f32), back_kv[2 * j + 1].astype(f32)
        keys = jnp.where(low_half, first, pltpu.roll(second, 64, 1))
        values = jnp.where(low_half, pltpu.roll(first, 64, 1), second)
        part = slice(128 * j, 128 * (j + 1))
        pg[1, :, part], terms = unturned(keys, dv_total[TOKENS * j : TOKENS * (j + 1), :], key_gain)
        key_terms = key_terms + terms
        pg[1, :, 512 + 128 * j : 640 + 128 * j] = values.astype(bf16)

    core = here.core
    f = here.z * 2 + here.xh
    sib_joins = []
    for turn in range(2):
        h = 1 - core if turn == 0 else core
        for r in range(4):
            result = t_dot(normed[:, 256 * r : 256 * (r + 1)], pg[h]).astype(bf16)
            parts[h, 2 * r : 2 * r + 2, :, :, 0:1024] = result.reshape(2, 8, 16, 1024)
            if turn == 0:
                sib_joins.append(
                    net.start(
                        parts.at[h, pl.ds(2 * r, 2), :, :, pl.ds(0, 1024)],
                        parts_in.at[pl.ds(2 * r, 2), :, :, pl.ds(0, 1024)],
                        sib,
                    )
                )
    out_join.wait_recv()
    for r in range(4):
        sib_joins[r].wait_recv()
        for q in (2 * r, 2 * r + 1):
            parts[core, q] = (parts[core, q].astype(f32) + parts_in[q].astype(f32)).astype(bf16)

    def f_at(ring, pair):
        return lax.rem(here.z + ring + 4, 4) * 2 + (1 - here.xh if pair else here.xh)

    def plane(part, hop, way):
        def half(ref, which):
            return ref.at[pl.ds(4 * which, 4)]

        a = net.start(part(2, 1), hop.at[0], way["across"])
        xd = net.start(part(-1, 1), hop.at[2], way["down"])
        xu = net.start(part(1, 1), hop.at[3], way["up"])
        yield
        a.wait_recv()
        add_to(part(2, 0), hop.at[0])
        u = net.start(half(part(2, 0), 0), half(hop.at[1], 0), way["up"])
        d = net.start(half(part(2, 0), 1), half(hop.at[1], 1), way["down"])
        yield
        xd.wait_recv()
        xu.wait_recv()
        add_to(part(0, 1), hop.at[2], hop.at[3])
        rx = net.start(part(0, 1), hop.at[6], way["across"])
        u.wait_recv()
        add_to(half(part(1, 0), 0), half(hop.at[1], 0))
        ru = net.start(part(1, 0), hop.at[4], way["up"])
        d.wait_recv()
        add_to(half(part(-1, 0), 1), half(hop.at[1], 1))
        rd = net.start(part(-1, 0), hop.at[5], way["down"])
        yield
        rx.wait_recv()
        ru.wait_recv()
        rd.wait_recv()
        add_to(part(0, 0), hop.at[4], hop.at[5], hop.at[6])

    low, high = pl.ds(0, GCOLS // 2), pl.ds(GCOLS // 2, GCOLS // 2)
    first_plane = plane(
        lambda ring, pair: parts.at[core, here.seq_at(ring, pair), :, :, low], hop_a, here.plane("seq")
    )
    second_plane = plane(lambda ring, pair: parts.at[core, :, f_at(ring, pair), :, high], hop_b, way)
    next(first_plane)
    next(second_plane)
    for copy in loads[2:4]:
        copy.wait()
    normed_grad = dot_t(pg[0], wqkv[0]) + dot_t(pg[1], wqkv[1])
    attn_gain_grad = jnp.sum(normed_grad * x * x_scaling, axis=0, keepdims=True)
    query_terms = query_terms + pltpu.roll(query_terms, 64, 1)
    key_terms = key_terms + pltpu.roll(key_terms, 64, 1)
    head_terms = jnp.where(low_half, query_terms, key_terms)
    spread = (
        8 * lax.broadcasted_iota(jnp.int32, (128, D), 0) == lax.broadcasted_iota(jnp.int32, (128, D), 1)
    ).astype(f32).astype(bf16)
    head_row = jnp.zeros((1, D), f32)
    for term in split3(head_terms):
        head_row = head_row + dot(jnp.broadcast_to(term, (16, 128)).astype(bf16), spread)[0:1, :]
    row = lax.broadcasted_iota(jnp.int32, (128, D), 0)
    gain_rows = jnp.where(
        row == 32, attn_gain_grad, jnp.where(row == 33, ffn_gain, jnp.where(row == 34, head_row, 0.0))
    )
    small[...] = small[...] + jnp.transpose(gain_rows).reshape(8, 8, 2, 8, 128)
    small_join = net.start(small.at[:, :, 1 - core], small_in, sib)
    next(first_plane)
    next(second_plane)
    weighted = normed_grad * attn_gain
    middle = jnp.mean(weighted * x, axis=1, keepdims=True)
    token_ref[...] = after_grad[...] + x_scaling * weighted - x * (x_scaling * x_scaling * x_scaling * middle)
    small_join.wait_recv()
    small_in[...] = small_in[...] + small[:, :, core]
    small_copies = [
        net.start(small_in.at[peers[i]], small_s.at[i], seq_peers[i]) for i in range(7)
    ]
    next(first_plane)
    next(second_plane)
    for _ in moves:
        pass
    for _ in more_moves:
        pass
    for copy in small_copies:
        copy.wait_recv()
    mine = small_in[me]
    for i in range(7):
        mine = mine + small_s[i]
    small_in[me] = mine
    small_copies = [
        net.start(small_in.at[me, f_at(*OTHERS[i])], small_f.at[i], fsdp_peers[i]) for i in range(7)
    ]
    next(first_plane, None)
    late = [
        [net.start(parts.at[core, me, f_at(*OTHERS[i]), :, low], late_a.at[i], fsdp_peers[i]) for i in range(7)]
    ]
    next(second_plane, None)
    late.append(
        [net.start(parts.at[core, peers[i], f, :, high], late_b.at[i], seq_peers[i]) for i in range(7)]
    )
    for copy in small_copies:
        copy.wait_recv()
    mine = small_in[me, f]
    for i in range(7):
        mine = mine + small_f[i]
    small_out[...] = mine
    for cols, copies, there in (
        (slice(0, GCOLS // 2), late[0], late_a), (slice(GCOLS // 2, GCOLS), late[1], late_b)
    ):
        for copy in copies:
            copy.wait_recv()
        result = parts[core, me, f, :, cols].astype(f32)
        for i in range(7):
            result = result + there[i].astype(f32)
        total[:, cols] = result
    last = net.start(total.at[pl.ds(pl.multiple_of(8 * (1 - core), 8), 8)], total_in, sib)
    mine = total[pl.ds(pl.multiple_of(8 * core, 8), 8), :]
    last.wait_recv()
    theirs = total_in[...]
    is_low = core == 0
    left, right = jnp.where(is_low, mine, theirs), jnp.where(is_low, theirs, mine)
    qkv_out[:, 0:1024] = left[:, 0:1024]
    qkv_out[:, 1024:2048] = right[:, 0:1024]
    wo_out[:, 0:512] = left[:, 1024:1536]
    wo_out[:, 512:1024] = right[:, 1024:1536]
    for i in range(1, 8):
        answer(i).wait_send()
    net.finish()


def back(*operands):
    vmem = pl.BlockSpec(memory_space=pltpu.VMEM)
    hbm = pl.BlockSpec(memory_space=pl.ANY)
    return pl.pallas_call(
        back_kernel,
        in_specs=[vmem] * 13 + [hbm] * 7,
        out_specs=[vmem] * 7,
        out_shape=[
            jax.ShapeDtypeStruct((TOKENS, D), bf16),
            jax.ShapeDtypeStruct((TOKENS, D), f32),
            jax.ShapeDtypeStruct((8, 2048), f32),
            jax.ShapeDtypeStruct((8, 1024), f32),
            jax.ShapeDtypeStruct((8, 128), f32),
            jax.ShapeDtypeStruct((2, 128, 2 * F), f32),
            jax.ShapeDtypeStruct((2, 128, F), f32),
        ],
        scratch_shapes=[
            pltpu.VMEM((2, D, 1024), bf16),
            pltpu.VMEM((2, D, 512), bf16),
            pltpu.VMEM((8, TOKENS, 128), bf16),
            pltpu.VMEM((8, TOKENS, 128), bf16),
            pltpu.VMEM((TOKENS, D), bf16),
            pltpu.VMEM((8, TOKENS, 128), bf16),
            pltpu.VMEM((2, TOKENS, D), bf16),
            pltpu.VMEM((TOKENS, D), f32),
        ]
        + [pltpu.VMEM((LENGTH, 128), bf16)] * 4
        + [pltpu.VMEM((64, LENGTH), bf16)]
        + [pltpu.VMEM((LENGTH, 128), f32)] * 2
        + [pltpu.VMEM((8, TOKENS, D), bf16), pltpu.VMEM((2, TOKENS, D), bf16)]
        + [pltpu.VMEM((7, TOKENS, D), bf16)]
        + [
            pltpu.VMEM((2, 8, 8, 16, GCOLS), bf16),
            pltpu.VMEM((8, 8, 16, GCOLS), bf16),
            pltpu.VMEM((8, 8, 2, 8, 128), f32),
            pltpu.VMEM((8, 8, 8, 128), f32),
            pltpu.VMEM((7, 8, 16, GCOLS // 2), bf16),
            pltpu.VMEM((7, 8, 16, GCOLS // 2), bf16),
            pltpu.VMEM((7, 16, GCOLS // 2), bf16),
            pltpu.VMEM((7, 16, GCOLS // 2), bf16),
            pltpu.VMEM((7, 8, 8, 128), f32),
            pltpu.VMEM((7, 8, 128), f32),
            pltpu.VMEM((16, GCOLS), f32),
            pltpu.VMEM((8, GCOLS), f32),
            pltpu.VMEM((3, 2, 2, 128, 3 * F), bf16),
            pltpu.VMEM((2, 2, 128, 3 * F), bf16),
            pltpu.VMEM((5, 2, 128, 3 * F), bf16),
            pltpu.SemaphoreType.DMA((40,)),
            pltpu.SemaphoreType.DMA((100,)),
            pltpu.SemaphoreType.DMA((100,)),
        ],
        compiler_params=pltpu.CompilerParams(collective_id=5, has_side_effects=True, vmem_limit_bytes=63 * 1024 * 1024),
        cost_estimate=pl.CostEstimate(
            flops=9 * 10**9, bytes_accessed=32 << 20, transcendentals=2 * LENGTH * LENGTH
        ),
        name="back",
    )(*operands)


def finish_kernel(layer, token, up, down, qkv, wo, small, *outs):
    for src, dst in zip((layer, token, up, down, qkv, wo), outs):
        dst[...] = src[...]
    router, attn, ffn, head = outs[6:]
    same = lax.broadcasted_iota(jnp.int32, (8, 8), 0) == lax.broadcasted_iota(jnp.int32, (8, 8), 1)
    values = small[...]
    router[...] = values[:, 0:EXPERTS]
    for ref, lane in ((attn, EXPERTS), (ffn, EXPERTS + 1)):
        ref[...] = jnp.sum(jnp.where(same, values[:, lane : lane + 1], 0.0), axis=0, keepdims=True)
    head[...] = values[0:1, EXPERTS + 2 : EXPERTS + 3]


def finish(*operands):
    vmem = pl.BlockSpec(memory_space=pltpu.VMEM)
    small = [(8, EXPERTS), (1, 8), (1, 8), (1, 1)]
    return pl.pallas_call(
        finish_kernel,
        in_specs=[vmem] * 7,
        out_specs=[vmem] * 10,
        out_shape=[jax.ShapeDtypeStruct(a.shape, a.dtype) for a in operands[:6]]
        + [jax.ShapeDtypeStruct(shape, f32) for shape in small],
        compiler_params=pltpu.CompilerParams(vmem_limit_bytes=VMEM),
        name="finish",
    )(*operands)


def gather_kernel(
    qkv_ref, wo_ref, router_ref, attn_ref, ffn_ref, head_ref, routes_ref, cot_ref, out_ref, masks_out, side_out,
    in_ref, mask_ref, stage, block, local_sems, send_sems, recv_sems,
):
    lanes = lax.broadcasted_iota(jnp.int32, (1, 128), 1)
    same = lax.broadcasted_iota(jnp.int32, (8, 8), 0) == lax.broadcasted_iota(jnp.int32, (8, 8), 1)

    def column(row):
        return jnp.sum(jnp.where(same, row[...].astype(f32), 0.0), axis=1, keepdims=True)

    gains = jnp.where(
        lanes == 32,
        column(attn_ref),
        jnp.where(lanes == 33, column(ffn_ref), jnp.where(lanes == 34, head_ref[...].astype(f32), 0.0)),
    )
    for h in range(2):
        in_ref[h, :, 0:1024] = qkv_ref[:, 1024 * h : 1024 * (h + 1)].astype(f32)
        in_ref[h, :, 1024:1536] = wo_ref[:, 512 * h : 512 * (h + 1)].astype(f32)
        in_ref[h, :, 1536:1664] = gains
        in_ref[h, :, 1536:1568] = router_ref[...].astype(f32)
    expert = lax.broadcasted_iota(jnp.int32, (32, 256), 0)
    named = jnp.zeros((32, 256), f32)
    for k in range(8):
        named = jnp.where(routes_ref[k : k + 1, :] == expert, 1.0, named)
    mask_ref[...] = named.astype(bf16)
    here = Place()
    c, s, f = here.core, here.seq, here.z * 2 + here.xh
    sib = here.sibling()
    ways = {"seq": here.plane("seq"), "fsdp": here.plane("fsdp")}
    others = [(2, 1), (2, 0), (0, 1), (1, 1), (-1, 1), (1, 0), (-1, 0)]

    def f_at(ring, pair):
        return lax.rem(here.z + ring + 4, 4) * 2 + (1 - here.xh if pair else here.xh)

    seq_peers = [{"seq": here.seq_at(ring, pair)} for ring, pair in others]
    fsdp_peers = [{"fsdp": here.fsdp_at(ring, pair)} for ring, pair in others]
    meet([sib, *seq_peers, *fsdp_peers])
    net = Copies(send_sems, recv_sems)
    rows = pl.ds(pl.multiple_of(8 * c, 8), 8)
    join = net.start(in_ref.at[1 - c], stage.at[rows], sib)
    stage[rows, :] = in_ref[c]
    join.wait_recv()
    block[...] = stage[...].astype(bf16)
    low, high = pl.ds(0, 896), pl.ds(896, 768)
    locals_ = [
        pltpu.make_async_copy(block, out_ref.at[c, s, f], local_sems.at[0]),
        pltpu.make_async_copy(mask_ref, masks_out.at[here.fsdp], local_sems.at[1]),
    ]
    for copy in locals_:
        copy.start()
    a = [net.start(block.at[:, low], out_ref.at[c, s, f, :, low], peer) for peer in fsdp_peers]
    b = [net.start(block.at[:, high], out_ref.at[c, s, f, :, high], peer) for peer in seq_peers]
    m = [net.start(mask_ref, masks_out.at[here.fsdp], peer) for peer in [sib, *fsdp_peers]]
    for copy in locals_:
        copy.wait()
    kin = []

    def plane(part, way):
        def half(ref, which):
            return ref.at[pl.ds(4 * which, 4)]

        def go(ref, target):
            return net.start(ref, ref, target)

        ref = part(0, 0)
        across, up, down = go(ref, way["across"]), go(ref, way["up"]), go(ref, way["down"])
        kin.append(go(ref, sib))
        yield
        up.wait_recv()
        ref = part(-1, 0)
        far_low = go(half(ref, 0), way["up"])
        kin.append(go(ref, sib))
        down.wait_recv()
        ref = part(1, 0)
        far_high = go(half(ref, 1), way["down"])
        kin.append(go(ref, sib))
        yield
        across.wait_recv()
        ref = part(0, 1)
        up, down = go(ref, way["up"]), go(ref, way["down"])
        kin.append(go(ref, sib))
        yield
        far_low.wait_recv()
        far_high.wait_recv()
        kin.append(go(part(2, 0), sib))
        up.wait_recv()
        ref = part(-1, 1)
        far_low = go(half(ref, 0), way["up"])
        kin.append(go(ref, sib))
        down.wait_recv()
        ref = part(1, 1)
        far_high = go(half(ref, 1), way["down"])
        kin.append(go(ref, sib))
        yield
        far_low.wait_recv()
        far_high.wait_recv()
        kin.append(go(part(2, 1), sib))

    for copy in a:
        copy.wait_recv()
    first = plane(lambda ring, pair: out_ref.at[c, here.seq_at(ring, pair), :, :, low], ways["seq"])
    next(first)
    for copy in b:
        copy.wait_recv()
    second = plane(lambda ring, pair: out_ref.at[c, :, f_at(ring, pair), :, high], ways["fsdp"])
    next(second)
    for i in range(8):
        m[i].wait_recv()
        if i:
            ring, pair = others[i - 1]
            ref = masks_out.at[here.fsdp_at(-ring, pair)]
            kin.append(net.start(ref, ref, sib))
    for turn in range(4):
        next(first, None)
        next(second, None)
        if turn == 1:
            kin.append(net.start(cot_ref, side_out, ways["fsdp"]["across"]))
    for copy in kin:
        copy.wait_recv()
    net.finish()


def gather_weights(*operands):
    n = 65
    return pl.pallas_call(
        gather_kernel,
        in_specs=[pl.BlockSpec(memory_space=pltpu.VMEM)] * 7 + [pl.BlockSpec(memory_space=pl.ANY)],
        out_specs=[pl.BlockSpec(memory_space=pl.ANY)] * 3,
        out_shape=[
            jax.ShapeDtypeStruct((2, 8, 8, 16, WCOLS), bf16),
            jax.ShapeDtypeStruct((16, 32, 256), bf16),
            jax.ShapeDtypeStruct((256, 1024), bf16),
        ],
        scratch_shapes=[
            pltpu.VMEM((2, 8, WCOLS), f32),
            pltpu.VMEM((32, 256), bf16),
            pltpu.VMEM((16, WCOLS), f32),
            pltpu.VMEM((16, WCOLS), bf16),
            pltpu.SemaphoreType.DMA((2,)),
            pltpu.SemaphoreType.DMA((n,)),
            pltpu.SemaphoreType.DMA((n,)),
        ],
        compiler_params=pltpu.CompilerParams(collective_id=1, has_side_effects=True, vmem_limit_bytes=VMEM),
        name="gather_weights",
    )(*operands)


def moe_kernel(
    x_ref, cot_ref, side_ref, g_ref, masks_ref, gates_ref, up_hbm, down_hbm,
    row_out, gate_out, y_out, y_in, grads_out, far_out,
    slots, spare, gates_in, grads_stage, grads_in, sib_in, hop_in, g_rows, up_ref, down_ref,
    rows_x, rows_p, rows_h, rows_u, rows_g, slot_gate, places, ranks, stage_y, stage_r, stage,
    local_sems, send_sems, recv_sems,
):
    here = Place()
    sib = here.sibling()
    way = here.plane("fsdp")
    own = here.fsdp
    counter = [0]

    def local(src, dst):
        copy = pltpu.make_async_copy(src, dst, local_sems.at[counter[0]])
        counter[0] += 1
        copy.start()
        return copy

    first_x = local(x_ref, slots.at[0])
    weights = [local(up_hbm, up_ref), local(down_hbm, down_ref)]

    def source(k):
        ring, pair, c = (0, -1, 1, 2)[k // 4], (k // 2) % 2, k % 2
        z = lax.rem(here.z + ring + 4, 4)
        xh = 1 - here.xh if pair else here.xh
        return z * 4 + xh * 2 + (1 - here.core if c else here.core)

    groups = ((4, 5, 8, 9), (0, 1, 2, 3), (6, 7, 10, 11), (12, 13, 14, 15))

    def fetch_g(group):
        near = {0: cot_ref, 2: side_ref}
        return [
            local(near[k] if k in near else g_ref.at[source(k)], g_rows.at[s])
            for s, k in enumerate(groups[group])
        ]

    g_copies = fetch_g(0)
    ring = here.plane("seq")
    others = [{"fsdp": source(k)} for k in range(1, 16)]
    meet([*others, ring["up"], ring["down"]])
    net = Copies(send_sems, recv_sems)

    def block(k, low=0, rows=TOKENS):
        return slots.at[k, pl.ds(low, rows)]

    sent = {k: [] for k in range(16)}

    def push(k, to, target, low=0, rows=TOKENS, src=None):
        copy = net.start(block(k, low, rows) if src is None else src, block(to, low, rows), target)
        sent[k].append(copy)
        return copy

    small = [net.start(gates_ref.at[source(k)], gates_in.at[own], others[k - 1]) for k in range(1, 16)]
    gates_in[own] = gates_ref[own]
    across = push(0, 2, way["across"], src=x_ref)
    up = push(0, 4, way["up"], src=x_ref)
    down = push(0, 8, way["down"], src=x_ref)
    kin = {1: push(0, 1, sib, src=x_ref)}
    expert = lax.broadcasted_iota(jnp.int32, (EXPERTS, TOKENS), 0)
    for k in range(16):
        named = masks_ref[source(k)].astype(f32)
        for i in range(2):
            ranks[2 * k + i : 2 * k + i + 1, :] = jnp.sum(
                jnp.where(expert == 2 * own + i, named, 0.0), axis=0, keepdims=True
            )
    before = (
        lax.broadcasted_iota(jnp.int32, (TOKENS, TOKENS), 0)
        < lax.broadcasted_iota(jnp.int32, (TOKENS, TOKENS), 1)
    ).astype(f32).astype(bf16)
    second = lax.rem(lax.broadcasted_iota(jnp.int32, (2 * 16, 1), 0), 2).astype(f32)
    named = ranks[...]
    ranks[...] = jnp.where(named > 0.0, dot(named.astype(bf16), before) + SLOTS * second, -1000.0)
    up.wait_recv()
    far_low = push(4, 12, way["up"], 0, 128)
    kin[5] = push(4, 5, sib)
    down.wait_recv()
    far_high = push(8, 12, way["down"], 128, 128)
    kin[9] = push(8, 9, sib)
    across.wait_recv()
    up_x = push(2, 6, way["up"])
    down_x = push(2, 10, way["down"])
    kin[3] = push(2, 3, sib)
    state = {}

    lanes = lax.broadcasted_iota(jnp.int32, (1, 128), 1)
    slot = lax.broadcasted_iota(jnp.int32, (2 * SLOTS, TOKENS), 0)
    slot_place = slot.astype(f32)
    first = slot < SLOTS
    expert = lax.broadcasted_iota(jnp.int32, (EXPERTS, TOKENS), 0)

    def gather(group):
        for s in range(4):
            k = groups[group][s]
            if k in kin:
                kin[k].wait_recv()
            g_copies[s].wait()
            wanted = jnp.where(first, ranks[2 * k : 2 * k + 1, :], ranks[2 * k + 1 : 2 * k + 2, :])
            hot = jnp.where(slot_place == wanted, 1.0, 0.0)
            gates = gates_in[source(k)]
            gate = jnp.sum(hot * jnp.where(first, gates[0:1, :], gates[1:2, :]), axis=1, keepdims=True)
            hot = hot.astype(bf16)
            places[s] = hot
            picked = dot(hot, slots[k]).astype(bf16)
            grads = dot(hot, g_rows[s])
            pair = (grads * gate).astype(bf16)
            grads = grads.astype(bf16)
            for i in range(2):
                part = slice(SLOTS * i, SLOTS * (i + 1))
                there = slice(group * GROUP_ROWS + SLOTS * s, group * GROUP_ROWS + SLOTS * (s + 1))
                rows_x[i, there, :] = picked[part]
                rows_p[i, there, :] = pair[part]
                rows_g[i, SLOTS * s : SLOTS * (s + 1), :] = grads[part]
                slot_gate[i, SLOTS * s : SLOTS * (s + 1), :] = jnp.broadcast_to(gate[part], (SLOTS, 128))

    def run(group):
        here_rows = pl.ds(group * GROUP_ROWS, GROUP_ROWS)

        def one(e, carry):
            x_rows = rows_x[e, here_rows, :]
            gate_part = dot(x_rows, up_ref[e, :, 0:F])
            up_part = dot(x_rows, up_ref[e, :, F : 2 * F])
            sigmoid = 1.0 / (1.0 + jnp.exp(-gate_part))
            silu = gate_part * sigmoid
            hidden = (silu * up_part).astype(bf16)
            rows_h[e, here_rows, :] = hidden
            hidden_grad = dot(rows_p[e, here_rows, :], down_ref[e])
            slope = sigmoid * (1.0 + gate_part * (1.0 - sigmoid))
            rows_u[e, here_rows, 0:F] = (hidden_grad * up_part * slope).astype(bf16)
            rows_u[e, here_rows, F : 2 * F] = (hidden_grad * silu).astype(bf16)
            out = dot_t(hidden, down_ref[e]).astype(bf16).astype(f32)
            gate_grad = jnp.sum(out * rows_g[e].astype(f32), axis=1, keepdims=True)
            stage_y[e] = (out * slot_gate[e][:, 0:1]).astype(bf16)
            stage_r[e] = dot_t(rows_u[e, here_rows, :], up_ref[e]).astype(bf16)
            for s in range(4):
                hot = places[s, pl.ds(pl.multiple_of(SLOTS * e, SLOTS), SLOTS), :].astype(f32)
                grads_stage[groups[group][s], e, 0:1, :] = jnp.sum(
                    hot * gate_grad[SLOTS * s : SLOTS * (s + 1)], axis=0, keepdims=True
                )
            return carry

        lax.fori_loop(0, 2, one, 0)
        for k in groups[group]:
            if k:
                small.append(net.start(grads_stage.at[k], grads_in.at[own], others[k - 1]))
            else:
                grads_in[own] = grads_stage[0]

    def result(k):
        return spare.at[k // 4 - 1] if k in (4, 8) else slots.at[k]

    y_sent = []

    def free_stage():
        for copy, remote in state.pop("y", ()):
            if remote:
                copy.wait_send()
            else:
                copy.wait()

    def combine(group):
        free_stage()
        for s in range(4):
            k = groups[group][s]
            if k not in (4, 8):
                for copy in sent[k]:
                    copy.wait_send()
            part = slice(SLOTS * s, SLOTS * (s + 1))
            both = jnp.concatenate([stage_y[0, part, :], stage_y[1, part, :]], axis=0)
            stage[s, :, 0:D] = t_dot(places[s], both).astype(bf16)
            both = jnp.concatenate([stage_r[0, part, :], stage_r[1, part, :]], axis=0)
            result(k)[...] = t_dot(places[s], both).astype(bf16)
        state["y"] = []
        for s in range(4):
            k = groups[group][s]
            ready = stage.at[s, :, pl.ds(0, D)]
            if k % 2:
                y_sent.append(net.start(ready, y_in.at[k // 2], sib))
                state["y"].append((y_sent[-1], True))
            else:
                state["y"].append((local(ready, y_out.at[k // 2]), False))
        for k in groups[group][::2]:
            state[k] = net.start(slots.at[k + 1], sib_in.at[k // 2], sib)

    def join(k):
        state[k].wait_recv()
        there = result(k)
        there[...] = (there[...].astype(f32) + sib_in[k // 2].astype(f32)).astype(bf16)

    def half(ref, which):
        return ref.at[pl.ds(128 * which, 128)]

    first_x.wait()
    for copy in small:
        copy.wait_recv()
    small.clear()
    gather(0)
    g_copies = fetch_g(1)
    for copy in weights:
        copy.wait()
    run(0)
    combine(0)
    far_low.wait_recv()
    far_high.wait_recv()
    far_x = push(12, 14, way["across"])
    kin[13] = push(12, 13, sib)
    gather(1)
    g_copies = fetch_g(2)
    join(4)
    hop_rd = net.start(result(4), hop_in.at[5], way["down"])
    join(8)
    hop_ru = net.start(result(8), hop_in.at[4], way["up"])
    run(1)
    up_x.wait_recv()
    kin[7] = push(6, 7, sib)
    down_x.wait_recv()
    kin[11] = push(10, 11, sib)
    combine(1)
    gather(2)
    g_copies = fetch_g(3)
    run(2)
    far_x.wait_recv()
    kin[15] = push(14, 15, sib)
    combine(2)
    gather(3)
    join(6)
    hop_xd = net.start(slots.at[6], hop_in.at[2], way["down"])
    join(10)
    hop_xu = net.start(slots.at[10], hop_in.at[3], way["up"])
    join(2)
    join(0)
    run(3)
    combine(3)

    w_copies = []

    far_grads = []

    def send_far(dx):
        for copy in w_copies:
            copy.wait()
        w_copies.clear()
        rows = pl.ds(pl.multiple_of(here.seq_at(2, dx) * 128, 128), 128)
        for e, to in enumerate(("up", "down")):
            far_grads.append(net.start(grads_out.at[e, rows], far_out.at[dx, e], ring[to]))

    def weight_grad(e, dx):
        free_stage()
        for copy in w_copies:
            copy.wait()
        xl = 1 - here.xl if dx else here.xl
        columns = pl.ds(pl.multiple_of(xl * 512, 512), 512)
        for wide, left, right in (
            (slice(0, 2 * F), rows_x, rows_u), (slice(2 * F, 3 * F), rows_p, rows_h)
        ):
            result = t_dot(left[e, :, columns], right[e]).astype(bf16)
            for y in range(4):
                stage[y, 0:128, wide] = result[128 * y : 128 * (y + 1)]
        w_copies[:] = [
            local(
                stage.at[y, pl.ds(0, 128)],
                grads_out.at[e, pl.ds(pl.multiple_of(xl * 512 + 128 * y, 128), 128)],
            )
            for y in range(4)
        ]

    weight_grad(0, 1)
    join(14)
    hop_a = [net.start(half(slots.at[14], i), half(hop_in.at[0], i), way["across"]) for i in range(2)]
    join(12)
    weight_grad(1, 1)
    send_far(1)
    far = []
    for i, to in enumerate(("up", "down")):
        hop_a[i].wait_recv()
        ref, other = half(slots.at[12], i), half(hop_in.at[0], i)
        ref[...] = (ref[...].astype(f32) + other[...].astype(f32)).astype(bf16)
        far.append(net.start(ref, half(hop_in.at[1], i), way[to]))
    weight_grad(0, 0)
    hop_xd.wait_recv()
    hop_xu.wait_recv()
    slots[2] = (slots[2].astype(f32) + hop_in[2].astype(f32) + hop_in[3].astype(f32)).astype(bf16)
    hop_rx = net.start(slots.at[2], hop_in.at[6], way["across"])
    relay = []
    for i, to in enumerate(("up", "down")):
        far[i].wait_recv()
        relay.append(net.start(half(hop_in.at[1], i), half(hop_in.at[7], i), way[to]))
    weight_grad(1, 0)
    send_far(0)
    for copy in (hop_ru, hop_rd, hop_rx, *relay, *far_grads, *y_sent, *small):
        copy.wait_recv()
    total = (
        slots[0].astype(f32)
        + hop_in[4].astype(f32)
        + hop_in[5].astype(f32)
        + hop_in[6].astype(f32)
        + hop_in[7].astype(f32)
    )
    row_out[...] = total
    row = lax.broadcasted_iota(jnp.int32, (128, TOKENS), 0)
    gate_grads = jnp.zeros((128, TOKENS), f32)
    for f in range(16):
        for e in range(2):
            gate_grads = jnp.where(row == 2 * f + e, grads_in[f, e, 0:1, :], gate_grads)
    gate_out[...] = jnp.transpose(gate_grads)
    waited = {id(copy) for copies in (*(sent[k] for k in sent if k not in (4, 8)), y_sent) for copy in copies}
    for copy in net.all:
        if id(copy) not in waited:
            copy.wait_send()


def moe(x, cot, side, g_all, masks, gates, up, down):
    any_space = pl.BlockSpec(memory_space=pl.ANY)
    vmem = pl.BlockSpec(memory_space=pltpu.VMEM)
    return pl.pallas_call(
        moe_kernel,
        in_specs=[any_space] * 4 + [vmem, vmem, any_space, any_space],
        out_specs=[vmem, vmem, any_space, any_space, any_space, any_space],
        out_shape=[
            jax.ShapeDtypeStruct((TOKENS, D), f32),
            jax.ShapeDtypeStruct((TOKENS, 128), f32),
            jax.ShapeDtypeStruct((8, TOKENS, D), bf16),
            jax.ShapeDtypeStruct((8, TOKENS, D), bf16),
            jax.ShapeDtypeStruct((2, D, 3 * F), bf16),
            jax.ShapeDtypeStruct((2, 2, 128, 3 * F), bf16),
        ],
        scratch_shapes=[
            pltpu.VMEM((16, TOKENS, D), bf16),
            pltpu.VMEM((2, TOKENS, D), bf16),
            pltpu.VMEM((16, 8, TOKENS), f32),
            pltpu.VMEM((16, 2, 8, TOKENS), f32),
            pltpu.VMEM((16, 2, 8, TOKENS), f32),
            pltpu.VMEM((8, TOKENS, D), bf16),
            pltpu.VMEM((8, TOKENS, D), bf16),
            pltpu.VMEM((4, TOKENS, D), bf16),
            pltpu.VMEM((2, D, 2 * F), bf16),
            pltpu.VMEM((2, D, F), bf16),
            pltpu.VMEM((2, ROWS, D), bf16),
            pltpu.VMEM((2, ROWS, D), bf16),
            pltpu.VMEM((2, ROWS, F), bf16),
            pltpu.VMEM((2, ROWS, 2 * F), bf16),
            pltpu.VMEM((2, GROUP_ROWS, D), bf16),
            pltpu.VMEM((2, GROUP_ROWS, 128), f32),
            pltpu.VMEM((4, 2 * SLOTS, TOKENS), bf16),
            pltpu.VMEM((2 * 16, TOKENS), f32),
            pltpu.VMEM((2, GROUP_ROWS, D), bf16),
            pltpu.VMEM((2, GROUP_ROWS, D), bf16),
            pltpu.VMEM((4, TOKENS, 3 * F), bf16),
            pltpu.SemaphoreType.DMA((56,)),
            pltpu.SemaphoreType.DMA((80,)),
            pltpu.SemaphoreType.DMA((80,)),
        ],
        compiler_params=pltpu.CompilerParams(
            collective_id=4, has_side_effects=True, vmem_limit_bytes=63 * 1024 * 1024
        ),
        cost_estimate=pl.CostEstimate(flops=32 * 10**9, bytes_accessed=40 << 20, transcendentals=1 << 21),
        name="moe",
    )(x, cot, side, g_all, masks, gates, up, down)


def on_device(
    tokens, attn_gain, qkv_weight, qk_gain, out_weight, ffn_gain, router_weight,
    gate_up_weight, down_weight, routes, cotangent,
):
    x = tokens.reshape(TOKENS, D)
    cot = cotangent.reshape(TOKENS, D)
    route_ids = routes.reshape(TOKENS, TOPK).T
    whole, masks, side = gather_weights(
        qkv_weight, out_weight, router_weight, attn_gain.reshape(1, 8), ffn_gain.reshape(1, 8),
        qk_gain.reshape(1, 1), route_ids, cot,
    )
    whole = whole.reshape(2, D, WCOLS)

    near, far_place = rotary_tables()
    heads, g_all, full, logs, attended, after, normed_ffn, gates, small_t, raw, gates_t = front(
        x, whole, route_ids, near, far_place, cot, side
    )
    row_sum, gate_sum, y_own, y_other, expert_grads, far = moe(
        normed_ffn, cot, side, g_all, masks, gates_t, gate_up_weight, down_weight
    )
    layer_out, token_grad, qkv_part, out_part, small, up_part, down_part = back(
        gate_sum, gates, after, x, cot, attended, normed_ffn, small_t, heads, full, logs, near, far_place,
        row_sum, raw, whole, y_own, y_other, expert_grads, far,
    )
    layer_out, token_grad, up_part, down_part, qkv_part, out_part, router_part, attn_part, ffn_part, head_part = finish(
        layer_out, token_grad, up_part, down_part, qkv_part, out_part, small
    )
    return (
        layer_out.reshape(1, TOKENS, D),
        token_grad.reshape(1, TOKENS, D),
        attn_part.reshape(8),
        qkv_part,
        head_part.reshape(1),
        out_part,
        ffn_part.reshape(8),
        router_part,
        up_part,
        down_part,
    )


def solution(mesh):
    return jax.shard_map(
        on_device,
        mesh=mesh,
        in_specs=(
            P("fsdp", "seq", None),
            P(("seq", "fsdp")),
            P(("seq", "fsdp"), None),
            P(("seq", "fsdp")),
            P(("seq", "fsdp"), None),
            P(("seq", "fsdp")),
            P(("seq", "fsdp"), None),
            P("fsdp", None, None),
            P("fsdp", None, None),
            P("fsdp", "seq", None),
            P("fsdp", "seq", None),
        ),
        out_specs=(
            P("fsdp", "seq", None),
            P("fsdp", "seq", None),
            P(("seq", "fsdp")),
            P(("seq", "fsdp"), None),
            P(("seq", "fsdp")),
            P(("seq", "fsdp"), None),
            P(("seq", "fsdp")),
            P(("seq", "fsdp"), None),
            P("fsdp", "seq", None),
            P("fsdp", "seq", None),
        ),
        check_vma=False,
    )
```

```python
import jax
import jax.numpy as jnp
import numpy as np
from jax import lax
from jax.experimental import pallas as pl
from jax.experimental.pallas import tpu as pltpu
from jax.sharding import PartitionSpec as P

D = 1024
HEAD_SIZE = 64
F = 512
TOPK = 8
EXPERTS = 32
SLOTS = 96
TOKENS = 256
SEQ = 8
FSDP = 16
LENGTH = SEQ * TOKENS
GROUP_ROWS = 4 * SLOTS
ROWS = 4 * GROUP_ROWS
GCOLS = 1536
VMEM = 60 * 1024 * 1024

epsilon = 1e-06
rope_base = 10000.0
f32 = jnp.float32
bf16 = jnp.bfloat16


def dot(a, b):
    return lax.dot_general(a, b, (((1,), (0,)), ((), ())), preferred_element_type=f32)


def dot_t(a, b):
    return lax.dot_general(a, b, (((1,), (1,)), ((), ())), preferred_element_type=f32)


def t_dot(a, b):
    return lax.dot_general(a, b, (((0,), (0,)), ((), ())), preferred_element_type=f32)


MESH = pl.DeviceIdType.MESH


class Place:
    def __init__(self):
        self.seq = lax.axis_index("seq")
        self.fsdp = lax.axis_index("fsdp")
        self.core = lax.rem(self.fsdp, 2)
        self.xh = lax.rem(self.fsdp // 2, 2)
        self.z = self.fsdp // 4
        self.y = lax.rem(self.seq, 4)
        self.xl = self.seq // 4

    def sibling(self):
        return {"fsdp": self.fsdp + 1 - 2 * self.core}

    def fsdp_at(self, ring, pair):
        z = lax.rem(self.z + ring + 4, 4)
        xh = 1 - self.xh if pair else self.xh
        return z * 4 + xh * 2 + self.core

    def seq_at(self, ring, pair):
        y = lax.rem(self.y + ring + 4, 4)
        xl = 1 - self.xl if pair else self.xl
        return xl * 4 + y

    def plane(self, axis):
        at = self.fsdp_at if axis == "fsdp" else self.seq_at
        return {
            "up": {axis: at(1, 0)},
            "down": {axis: at(-1, 0)},
            "across": {axis: at(0, 1)},
        }


def meet(targets):
    barrier = pltpu.get_barrier_semaphore()
    for target in targets:
        pl.semaphore_signal(barrier, inc=1, device_id=target, device_id_type=MESH)
    pl.semaphore_wait(barrier, len(targets))


class Copies:
    def __init__(self, send_sems, recv_sems):
        self.send_sems, self.recv_sems, self.count, self.all = send_sems, recv_sems, 0, []

    def start(self, src, dst, target):
        k = self.count
        self.count += 1
        copy = pltpu.make_async_remote_copy(
            src_ref=src, dst_ref=dst, send_sem=self.send_sems.at[k], recv_sem=self.recv_sems.at[k],
            device_id=target, device_id_type=MESH,
        )
        copy.start()
        self.all.append(copy)
        return copy

    def finish(self, done=()):
        for copy in self.all:
            if all(copy is not other for other in done):
                copy.wait_send()


OTHERS = ((2, 1), (2, 0), (0, 1), (1, 1), (-1, 1), (1, 0), (-1, 0))
WCOLS = 1664


def lane_halves():
    lanes = lax.broadcasted_iota(jnp.int32, (1, 128), 1)
    return lanes, lanes < HEAD_SIZE


def head_mean(values, low_half):
    low = jnp.sum(jnp.where(low_half, values, 0.0), axis=1, keepdims=True)
    high = jnp.sum(jnp.where(low_half, 0.0, values), axis=1, keepdims=True)
    return jnp.where(low_half, low, high) * (1.0 / HEAD_SIZE)


def partner(values, lanes):
    return jnp.where(
        lax.rem(lanes, HEAD_SIZE) < HEAD_SIZE // 2, pltpu.roll(values, 96, 1), pltpu.roll(values, 32, 1)
    )


def rotary_tables():
    inverse = rope_base ** (-2.0 * (np.arange(128) % 32) / HEAD_SIZE)
    near = np.arange(TOKENS)[:, None] * inverse[None, :]
    far = TOKENS * np.arange(SEQ)[:, None] * inverse[None, :]
    return [jnp.asarray(np.stack([np.cos(a), np.sin(a)]), f32) for a in (near, far)]


def rotary(near_ref, far_ref, block, lanes):
    pick = lax.broadcasted_iota(jnp.int32, (SEQ, 128), 0) == block
    far_cos = jnp.sum(jnp.where(pick, far_ref[0], 0.0), axis=0, keepdims=True)
    far_sin = jnp.sum(jnp.where(pick, far_ref[1], 0.0), axis=0, keepdims=True)
    cos = near_ref[0] * far_cos - near_ref[1] * far_sin
    sin = near_ref[1] * far_cos + near_ref[0] * far_sin
    return cos, jnp.where(lax.rem(lanes, HEAD_SIZE) < HEAD_SIZE // 2, -sin, sin)


def row_scale(values):
    return lax.rsqrt(jnp.mean(values * values, axis=1, keepdims=True) + epsilon)


def gain_tiles(small_t, lanes):
    pick = (
        lax.broadcasted_iota(jnp.int32, (D, 128), 0) == 8 * lax.broadcasted_iota(jnp.int32, (D, 128), 1)
    ).astype(f32).astype(bf16)
    gains = dot(small_t[32:48, :], pick)[2:3, :]
    other = pltpu.roll(gains, 64, 1)
    low_half = lanes < HEAD_SIZE
    return jnp.where(low_half, gains, other), jnp.where(low_half, other, gains)


def front_kernel(
    x_ref, w_ref, routes_ref, near_ref, far_place_ref, cot_ref, side_ref,
    heads_out, g_out, full_ref, logs_ref, att_ref, after_ref, normed_ref, gates_ref, small_t_ref, raw_ref, gates_t_ref,
    wq, wkv, wo, small, send, heads, out_buf, att, key0, key1, value,
    local_sems, send_sems, recv_sems,
):
    here = Place()
    me = here.seq
    loads = [
        pltpu.make_async_copy(w_ref.at[h, :, pl.ds(start, width)], there, local_sems.at[k])
        for k, (h, start, width, there) in enumerate(
            (
                (0, 1536, 128, small),
                (0, 0, 1024, wq),
                (1, 0, 1024, wkv),
                (0, 1024, 512, wo.at[0]),
                (1, 1024, 512, wo.at[1]),
            )
        )
    ]
    for copy in loads:
        copy.start()
    peers = [here.seq_at(*other) for other in OTHERS]
    sib = here.sibling()
    way = here.plane("fsdp")
    meet([sib, *way.values()] + [{"seq": peer} for peer in peers])
    net = Copies(send_sems, recv_sems)

    def gather_cotangent():
        def at(ring, pair):
            return g_out.at[here.fsdp_at(ring, pair)]

        def half(ref, which):
            return ref.at[pl.ds(128 * which, 128)]

        def go(ref, target):
            return net.start(ref, ref, target)

        up, down = [net.start(cot_ref, at(0, 0), way[w]) for w in ("up", "down")]
        kin = [net.start(cot_ref, at(0, 0), sib), net.start(side_ref, at(0, 1), sib)]
        yield
        up.wait_recv()
        far = [go(half(at(-1, 0), 0), way["up"])]
        kin.append(go(at(-1, 0), sib))
        down.wait_recv()
        far.append(go(half(at(1, 0), 1), way["down"]))
        kin.append(go(at(1, 0), sib))
        up, down = [net.start(side_ref, at(0, 1), way[w]) for w in ("up", "down")]
        yield
        for copy in far:
            copy.wait_recv()
        across = go(at(2, 0), way["across"])
        kin.append(go(at(2, 0), sib))
        yield
        up.wait_recv()
        kin.append(go(at(-1, 1), sib))
        down.wait_recv()
        kin.append(go(at(1, 1), sib))
        across.wait_recv()
        kin.append(go(at(2, 1), sib))
        yield
        for copy in kin:
            copy.wait_recv()

    moves = gather_cotangent()
    next(moves)
    lanes, low_half = lane_halves()
    loads[0].wait()
    small_t = jnp.transpose(small[...].astype(f32)).astype(bf16)
    small_t_ref[...] = small_t
    x = x_ref[...].astype(f32)
    normed = (x * row_scale(x) * small_t[32:33, :].astype(f32)).astype(bf16)
    query_gain, key_gain = gain_tiles(small_t, lanes)
    cos, sin = rotary(near_ref, far_place_ref, me, lanes)
    loads[1].wait()
    queries = dot(normed, wq[...])
    loads[2].wait()
    kv = dot(normed, wkv[...])

    def turned(tile, gain):
        normal = tile * lax.rsqrt(head_mean(tile * tile, low_half) + epsilon) * gain
        return normal * cos + partner(normal, lanes) * sin

    for j in range(4):
        part = slice(128 * j, 128 * (j + 1))
        raw_ref[8 + j] = kv[:, part]
        keys = turned(kv[:, part], key_gain)
        values = kv[:, 512 + 128 * j : 640 + 128 * j]
        send[2 * j, :, 128:256] = jnp.where(low_half, keys, pltpu.roll(values, 64, 1)).astype(bf16)
        send[2 * j + 1, :, 128:256] = jnp.where(low_half, pltpu.roll(keys, 64, 1), values).astype(bf16)
    for h in range(8):
        raw_ref[h] = queries[:, 128 * h : 128 * (h + 1)]
        send[h, :, 0:128] = turned(raw_ref[h], query_gain).astype(bf16)
    copies = [net.start(send.at[peer], heads.at[me], {"seq": peer}) for peer in peers]
    heads[me] = send[me]
    next(moves)
    for copy in copies:
        copy.wait_recv()
    save = pltpu.make_async_copy(heads, heads_out, local_sems.at[5])
    save.start()
    for c in range(8):
        rows = slice(TOKENS * c, TOKENS * (c + 1))
        pair = heads[c, :, 128:256].astype(f32)
        key0[rows, :] = jnp.where(low_half, pair, 0.0).astype(bf16)
        key1[rows, :] = jnp.where(low_half, 0.0, pltpu.roll(pair, 64, 1)).astype(bf16)
        value[rows, :] = jnp.where(low_half, jnp.where(lanes == 0, 1.0, 0.0), pair).astype(bf16)

    def block(i, carry):
        j = lax.rem(me + 1 + i, 8)
        query = (heads[j, :, 0:128].astype(f32) * (1.0 / 8.0)).astype(bf16)
        results = []
        for key in (key0, key1):
            total = jnp.zeros((TOKENS, 128), f32)
            for c in range(4):
                part = pl.ds(c * 512, 512)
                weights = jnp.exp(dot_t(query, key[part, :]))
                total = total + dot(weights.astype(bf16), value[part, :])
            results.append(total)
        sum0, sum1 = results[0][:, 0:1], results[1][:, 0:1]
        full = jnp.where(low_half, pltpu.roll(results[0] / sum0, 64, 1), results[1] / sum1)
        rows = pl.ds(pl.multiple_of(j * TOKENS, TOKENS), TOKENS)
        full_ref[rows, :] = full
        logs_ref[rows, :] = jnp.where(low_half, jnp.log(sum0), jnp.log(sum1))
        out_buf[j] = full.astype(bf16)

        @pl.when(i < 7)
        def _():
            answer(i).start()

        return carry

    columns = pl.ds(pl.multiple_of(me * 128, 128), 128)

    def answer(i):
        j = lax.rem(me + 1 + i, 8)
        return pltpu.make_async_remote_copy(
            src_ref=out_buf.at[j], dst_ref=att.at[:, columns], send_sem=send_sems.at[24 + i],
            recv_sem=recv_sems.at[24 + i], device_id={"seq": j}, device_id_type=MESH,
        )

    lax.fori_loop(0, 1, block, 0)
    next(moves)
    lax.fori_loop(1, 7, block, 0)
    next(moves)
    lax.fori_loop(7, 8, block, 0)
    att[:, columns] = out_buf[me]
    for k in (3, 4):
        loads[k].wait()
    for i in range(7):
        answer(i).wait_recv()
    attended = att[...]
    att_ref[...] = attended
    squares = jnp.zeros((TOKENS, 1), f32)
    for h in range(2):
        part = slice(512 * h, 512 * (h + 1))
        after = x_ref[:, part].astype(f32) + dot(attended, wo[h])
        after_ref[:, part] = after
        squares = squares + jnp.sum(after * after, axis=1, keepdims=True)
    scaling = lax.rsqrt(squares * (1.0 / D) + epsilon)
    normed = (after_ref[...] * scaling * small_t[33:34, :].astype(f32)).astype(bf16)
    normed_ref[...] = normed
    logits = dot(normed, small[...])
    expert = lax.broadcasted_iota(jnp.int32, (128, TOKENS), 0)
    named = jnp.zeros((128, TOKENS), f32)
    for k in range(TOPK):
        named = jnp.where(routes_ref[k : k + 1, :] == expert, 1.0, named)
    named = jnp.transpose(named)
    peak = jnp.max(jnp.where(named > 0.0, logits, -1e30), axis=1, keepdims=True)
    chosen = jnp.where(named > 0.0, jnp.exp(logits - peak), 0.0)
    gates = chosen / jnp.sum(chosen, axis=1, keepdims=True)
    gates_ref[...] = gates
    across = jnp.transpose(gates)
    gates_t_ref[...] = jnp.zeros_like(gates_t_ref)
    for i in range(FSDP):
        gates_t_ref[i, 0:2, :] = across[2 * i : 2 * i + 2, :]
    for _ in moves:
        pass
    save.wait()
    for i in range(7):
        answer(i).wait_send()
    net.finish()


def front(x, whole, routes, near, far, cot, side):
    vmem = pl.BlockSpec(memory_space=pltpu.VMEM)
    hbm = pl.BlockSpec(memory_space=pl.ANY)
    return pl.pallas_call(
        front_kernel,
        in_specs=[vmem, hbm, vmem, vmem, vmem, hbm, hbm],
        out_specs=[hbm] * 2 + [vmem] * 9,
        out_shape=[
            jax.ShapeDtypeStruct((8, TOKENS, 256), bf16),
            jax.ShapeDtypeStruct((FSDP, TOKENS, D), bf16),
            jax.ShapeDtypeStruct((LENGTH, 128), f32),
            jax.ShapeDtypeStruct((LENGTH, 128), f32),
            jax.ShapeDtypeStruct((TOKENS, D), bf16),
            jax.ShapeDtypeStruct((TOKENS, D), f32),
            jax.ShapeDtypeStruct((TOKENS, D), bf16),
            jax.ShapeDtypeStruct((TOKENS, 128), f32),
            jax.ShapeDtypeStruct((128, D), bf16),
            jax.ShapeDtypeStruct((12, TOKENS, 128), f32),
            jax.ShapeDtypeStruct((FSDP, 8, TOKENS), f32),
        ],
        scratch_shapes=[
            pltpu.VMEM((D, 1024), bf16),
            pltpu.VMEM((D, 1024), bf16),
            pltpu.VMEM((2, D, 512), bf16),
            pltpu.VMEM((D, 128), bf16),
            pltpu.VMEM((8, TOKENS, 256), bf16),
            pltpu.VMEM((8, TOKENS, 256), bf16),
            pltpu.VMEM((8, TOKENS, 128), bf16),
            pltpu.VMEM((TOKENS, D), bf16),
            pltpu.VMEM((LENGTH, 128), bf16),
            pltpu.VMEM((LENGTH, 128), bf16),
            pltpu.VMEM((LENGTH, 128), bf16),
            pltpu.SemaphoreType.DMA((8,)),
            pltpu.SemaphoreType.DMA((31,)),
            pltpu.SemaphoreType.DMA((31,)),
        ],
        compiler_params=pltpu.CompilerParams(collective_id=2, has_side_effects=True, vmem_limit_bytes=VMEM),
        cost_estimate=pl.CostEstimate(
            flops=4 * 10**9, bytes_accessed=16 << 20, transcendentals=2 * LENGTH * LENGTH
        ),
        name="front",
    )(x, whole, routes, near, far, cot, side)


def split3(values):
    high = values.astype(bf16).astype(f32)
    rest = values - high
    middle = rest.astype(bf16).astype(f32)
    return high, middle, rest - middle


def with_terms(lanes, start, parts):
    high, middle, low = parts
    return jnp.where(
        lanes == start,
        high,
        jnp.where(lanes == start + 1, middle, jnp.where(lanes == start + 2, low, 0.0)),
    )


def back_kernel(
    gate_sum_ref, gates_ref, after_ref, x_ref, cot_ref, att_ref, normed_ref, small_t_ref,
    heads_ref, full_ref, logs_ref, near_ref, far_place_ref, row_ref, raw_ref, w_ref, y_ref, y_other, grads_ref, far_ref,
    layer_ref, token_ref, qkv_out, wo_out, small_out, up_out, down_out,
    wqkv, wo, send, grads, back_q, back_kv, pg, after_grad,
    key0, key1, value0, value1, key_t, dk_total, dv_total,
    slots, y_stage, hop_in,
    parts, parts_in, small, small_in, hop_a, hop_b, late_a, late_b, small_s, small_f, total, total_in,
    chunks, far_in, chunk_in, local_sems, send_sems, recv_sems,
):
    here = Place()
    me = here.seq
    sib = here.sibling()
    way = here.plane("fsdp")
    loads = [
        pltpu.make_async_copy(w_ref.at[h, :, pl.ds(start, width)], there, local_sems.at[k])
        for k, (h, start, width, there) in enumerate(
            (
                (0, 1024, 512, wo.at[0]),
                (1, 1024, 512, wo.at[1]),
                (0, 0, 1024, wqkv.at[0]),
                (1, 0, 1024, wqkv.at[1]),
            )
        )
    ]
    loads.append(pltpu.make_async_copy(row_ref, after_grad, local_sems.at[19]))
    for copy in loads:
        copy.start()
    e_loads = [
        pltpu.make_async_copy(
            grads_ref.at[:, pl.ds(pl.multiple_of(here.seq_at(ring, pair) * 128, 128), 128)],
            chunks.at[i, pair], local_sems.at[12 + 2 * i + pair],
        )
        for i, ring in enumerate((-1, 1, 0)) for pair in range(2)
    ]
    e_loads.append(pltpu.make_async_copy(far_ref, far_in.at[1], local_sems.at[18]))
    order = (6, 7, 3, 5, 2, 4, 1, 0)
    y_loads = {k: pltpu.make_async_copy(y_ref.at[k], slots.at[k], local_sems.at[4 + k]) for k in order}
    y_more = {
        k: pltpu.make_async_copy(y_other.at[k], y_stage.at[i % 2], local_sems.at[20 + k]) for i, k in enumerate(order)
    }
    for copy in y_loads.values():
        copy.start()
    for k in order[:2]:
        y_more[k].start()
    peers = [here.seq_at(*other) for other in OTHERS]
    seq_peers = [{"seq": peer} for peer in peers]
    fsdp_peers = [{"fsdp": here.fsdp_at(*other)} for other in OTHERS]
    meet([sib, *seq_peers, *fsdp_peers])
    net = Copies(send_sems, recv_sems)
    for copy in e_loads:
        copy.start()
    rows = pl.ds(pl.multiple_of(here.seq_at(2, 0) * 128, 128), 128)
    ring = here.plane("seq")
    far_sent = [
        net.start(grads_ref.at[e, rows], far_in.at[0, e], ring[to]) for e, to in enumerate(("up", "down"))
    ]
    lanes, low_half = lane_halves()

    gate_grad = gate_sum_ref[...]
    gates = gates_ref[...]
    chosen = gates * (gate_grad - jnp.sum(gates * gate_grad, axis=1, keepdims=True))
    logits_grad = chosen.astype(bf16)
    loads[4].wait()
    normed_grad = after_grad[...] + dot(logits_grad, small_t_ref[...])
    after = after_ref[...]
    scaling = row_scale(after)
    weighted = normed_grad * small_t_ref[33:34, :].astype(f32)
    middle = jnp.mean(weighted * after, axis=1, keepdims=True)
    after_grad[...] = (
        cot_ref[...].astype(f32) + scaling * weighted - after * (scaling * scaling * scaling * middle)
    )
    after_low = after_grad[...].astype(bf16)
    ffn_gain = jnp.sum(normed_grad * after * scaling, axis=0, keepdims=True)
    for k in (0, 1):
        loads[k].wait()
    for q in range(2):
        rows = slice(512 * q, 512 * (q + 1))
        attended_grad = dot_t(after_low[:, 0:512], wo[0, rows, :]) + dot_t(after_low[:, 512:1024], wo[1, rows, :])
        for h in range(4):
            send[4 * q + h] = attended_grad[:, 128 * h : 128 * (h + 1)].astype(bf16)

    def delivery(d):
        peer = lax.rem(me + d, 8)
        return pltpu.make_async_remote_copy(
            src_ref=send.at[peer], dst_ref=grads.at[me], send_sem=send_sems.at[92 + d],
            recv_sem=recv_sems.at[92 + d], device_id={"seq": peer}, device_id_type=MESH,
        )

    for d in range(7, 0, -1):
        delivery(d).start()
    grads[me] = send[me]
    router_grad = t_dot(normed_ref[...], logits_grad)
    small[...] = router_grad.reshape(8, 8, 2, 8, 128)
    for h in range(2):
        out_grad = t_dot(att_ref[...], after_low[:, 512 * h : 512 * (h + 1)]).astype(bf16)
        parts[h, :, :, :, 1024:1536] = out_grad.reshape(8, 8, 16, 512)
    out_join = net.start(
        parts.at[1 - here.core, :, :, :, pl.ds(1024, 512)], parts_in.at[:, :, :, pl.ds(1024, 512)], sib
    )

    def add_to(ref, *values):
        result = ref[...].astype(f32)
        for value in values:
            result = result + value[...].astype(f32)
        ref[...] = result.astype(bf16)

    def join(k):
        i = order.index(k)
        y_loads[k].wait()
        y_more[k].wait()
        add_to(slots.at[k], y_stage.at[i % 2])
        if i + 2 < 8:
            y_more[order[i + 2]].start()

    def half(ref, which):
        return ref.at[pl.ds(128 * which, 128)]

    def expert_sum():
        join(6)
        join(7)
        up = [net.start(half(slots.at[6 + j], 0), half(hop_in.at[j], 0), way["up"]) for j in range(2)]
        down = [net.start(half(slots.at[6 + j], 1), half(hop_in.at[j], 1), way["down"]) for j in range(2)]
        yield
        for k in (3, 5, 2, 4):
            join(k)
        up[1].wait_recv()
        down[1].wait_recv()
        add_to(half(slots.at[5], 0), half(hop_in.at[1], 0))
        add_to(half(slots.at[3], 1), half(hop_in.at[1], 1))
        beside = [
            net.start(slots.at[5], hop_in.at[2], way["up"]), net.start(slots.at[3], hop_in.at[3], way["down"])
        ]
        up[0].wait_recv()
        down[0].wait_recv()
        add_to(half(slots.at[4], 0), half(hop_in.at[0], 0))
        add_to(half(slots.at[2], 1), half(hop_in.at[0], 1))
        own = [
            net.start(slots.at[4], hop_in.at[4], way["up"]), net.start(slots.at[2], hop_in.at[5], way["down"])
        ]
        yield
        join(1)
        join(0)
        for copy in beside:
            copy.wait_recv()
        add_to(slots.at[1], hop_in.at[2], hop_in.at[3])
        own.append(net.start(slots.at[1], hop_in.at[6], way["across"]))
        yield
        for copy in own:
            copy.wait_recv()
        layer_ref[...] = (
            after_ref[...]
            + slots[0].astype(f32)
            + hop_in[4].astype(f32)
            + hop_in[5].astype(f32)
            + hop_in[6].astype(f32)
        ).astype(bf16)

    def expert_grads():
        for copy in e_loads:
            copy.wait()
        for pair in (1, 0):
            if pair == 0:
                for copy in far_sent:
                    copy.wait_recv()
            add_to(chunks.at[0, pair, 1], far_in.at[pair, 1])
            add_to(chunks.at[1, pair, 0], far_in.at[pair, 0])
        beside = [
            net.start(chunks.at[0, 1], chunk_in.at[0], ring["down"]),
            net.start(chunks.at[1, 1], chunk_in.at[1], ring["up"]),
        ]
        yield
        own = [
            net.start(chunks.at[0, 0], chunk_in.at[2], ring["down"]),
            net.start(chunks.at[1, 0], chunk_in.at[3], ring["up"]),
        ]
        for copy in beside:
            copy.wait_recv()
        add_to(chunks.at[2, 1], chunk_in.at[0], chunk_in.at[1])
        own.append(net.start(chunks.at[2, 1], chunk_in.at[4], ring["across"]))
        yield
        for copy in own:
            copy.wait_recv()
        result = chunks[2, 0].astype(f32)
        for i in range(2, 5):
            result = result + chunk_in[i].astype(f32)
        up_out[...] = result[:, :, 0 : 2 * F]
        down_out[...] = result[:, :, 2 * F : 3 * F]

    moves = expert_sum()
    more_moves = expert_grads()
    next(moves)
    ones_high = jnp.where((lanes >= 64) & (lanes < 67), 1.0, 0.0)
    ones_low = jnp.where(lanes < 3, 1.0, 0.0)
    for c in range(8):
        rows = slice(TOKENS * c, TOKENS * (c + 1))
        pair = heads_ref[c, :, 128:256].astype(f32)
        swapped = pltpu.roll(pair, 64, 1)
        key0[rows, :] = jnp.where(low_half, pair, ones_high).astype(bf16)
        key1[rows, :] = jnp.where(low_half, ones_low, swapped).astype(bf16)
        value0[rows, :] = jnp.where(low_half, swapped, ones_high).astype(bf16)
        value1[rows, :] = jnp.where(low_half, ones_low, pair).astype(bf16)
        key_t[:, rows] = jnp.transpose(pair)[0:64, :].astype(bf16)
    dk_total[...] = jnp.zeros_like(dk_total)
    dv_total[...] = jnp.zeros_like(dv_total)
    columns = pl.ds(pl.multiple_of(me * 128, 128), 128)

    def answer(i):
        j = lax.rem(me + i, 8)
        return pltpu.make_async_remote_copy(
            src_ref=grads.at[j], dst_ref=back_q.at[:, columns], send_sem=send_sems.at[84 + i],
            recv_sem=recv_sems.at[84 + i], device_id={"seq": j}, device_id_type=MESH,
        )

    def block(i, carry):
        j = lax.rem(me + i, 8)

        @pl.when(i > 0)
        def _():
            delivery(8 - i).wait_recv()

        rows = pl.ds(pl.multiple_of(j * TOKENS, TOKENS), TOKENS)
        query = heads_ref[j, :, 0:128].astype(f32) * (1.0 / 8.0)
        grad = grads[j].astype(f32)
        logs = logs_ref[rows, :]
        product = grad * full_ref[rows, :]
        delta0 = jnp.sum(jnp.where(low_half, product, 0.0), axis=1, keepdims=True)
        delta1 = jnp.sum(jnp.where(low_half, 0.0, product), axis=1, keepdims=True)
        query0 = jnp.where(low_half, query, with_terms(lanes, 64, split3(-logs[:, 0:1]))).astype(bf16)
        query1 = jnp.where(low_half, with_terms(lanes, 0, split3(-logs[:, 64:65])), query).astype(bf16)
        grad0 = jnp.where(low_half, grad, with_terms(lanes, 64, split3(-delta0))).astype(bf16)
        grad1 = jnp.where(low_half, with_terms(lanes, 0, split3(-delta1)), grad).astype(bf16)
        only_query = (
            jnp.where(low_half, query, 0.0).astype(bf16), jnp.where(low_half, 0.0, query).astype(bf16)
        )
        only_grad = (jnp.where(low_half, grad, 0.0).astype(bf16), jnp.where(low_half, 0.0, grad).astype(bf16))
        dq = [jnp.zeros((64, TOKENS), f32), jnp.zeros((64, TOKENS), f32)]
        for c in range(4):
            part = pl.ds(c * 512, 512)
            dv = dv_total[part, :]
            dk = dk_total[part, :]
            for h, (key, value, query_h, grad_h) in enumerate(
                ((key0, value0, query0, grad0), (key1, value1, query1, grad1))
            ):
                probs = jnp.exp(dot_t(key[part, :], query_h))
                inner = dot_t(value[part, :], grad_h)
                dv = dv + dot(probs.astype(bf16), only_grad[h])
                scores = (probs * inner).astype(bf16)
                dk = dk + dot(scores, only_query[h])
                dq[h] = dq[h] + dot(key_t[:, c * 512 : (c + 1) * 512], scores)
            dv_total[part, :] = dv
            dk_total[part, :] = dk
        both = jnp.concatenate(dq, axis=0) * (1.0 / 8.0)
        grads[j] = jnp.transpose(both).astype(bf16)

        @pl.when(i > 0)
        def _():
            answer(i).start()

        return carry

    lax.fori_loop(0, 3, block, 0)
    next(more_moves)
    next(moves)
    lax.fori_loop(3, 6, block, 0)
    next(moves)
    lax.fori_loop(6, 8, block, 0)
    for d in range(1, 8):
        delivery(d).wait_send()
    for c in range(8):
        rows = slice(TOKENS * c, TOKENS * (c + 1))
        dk = dk_total[rows, :]
        dv = dv_total[rows, :]
        dk = dk + pltpu.roll(dk, 64, 1)
        dv = dv + pltpu.roll(dv, 64, 1)
        send[c] = jnp.where(low_half, dk, dv).astype(bf16)
    to_tokens = [net.start(send.at[peer], back_kv.at[me], {"seq": peer}) for peer in peers]
    raw = [
        pltpu.make_async_copy(raw_ref.at[h], there.at[pl.ds(TOKENS * (h % 8), TOKENS)], local_sems.at[28 + h])
        for h, there in [(h, dk_total) for h in range(8)] + [(h, dv_total) for h in range(8, 12)]
    ]
    for copy in raw:
        copy.start()
    back_kv[me] = send[me]
    back_q[:, columns] = grads[me]
    x = x_ref[...].astype(f32)
    x_scaling = row_scale(x)
    attn_gain = small_t_ref[32:33, :].astype(f32)
    normed = (x * x_scaling * attn_gain).astype(bf16)
    query_gain, key_gain = gain_tiles(small_t_ref[...], lanes)
    cos, sin = rotary(near_ref, far_place_ref, me, lanes)
    for i in range(1, 8):
        answer(i).wait_recv()

    def unturned(grad, tile, gain):
        grad = grad * cos - partner(grad, lanes) * sin
        scale = lax.rsqrt(head_mean(tile * tile, low_half) + epsilon)
        weighted = grad * gain
        middle = head_mean(weighted * tile, low_half)
        result = scale * weighted - tile * (scale * scale * scale * middle)
        return result.astype(bf16), jnp.sum(grad * tile * scale, axis=0, keepdims=True)

    for copy in raw:
        copy.wait()
    next(more_moves)
    query_terms = jnp.zeros((1, 128), f32)
    for h in range(8):
        part = slice(128 * h, 128 * (h + 1))
        pg[0, :, part], terms = unturned(back_q[:, part].astype(f32), dk_total[TOKENS * h : TOKENS * (h + 1), :], query_gain)
        query_terms = query_terms + terms
    core = here.core
    f = here.z * 2 + here.xh
    sib_joins = [out_join]

    def weight_part(i):
        columns = pl.ds(512 * i, 512)
        for r in range(4):
            result = t_dot(normed[:, 256 * r : 256 * (r + 1)], pg[i]).astype(bf16).reshape(2, 8, 16, 1024)
            for h in range(2):
                parts[h, 2 * r : 2 * r + 2, :, :, 512 * i : 512 * (i + 1)] = result[:, :, :, 512 * h : 512 * (h + 1)]
        sib_joins.append(
            net.start(parts.at[1 - core, :, :, :, columns], parts_in.at[:, :, :, columns], sib)
        )

    weight_part(0)
    for copy in to_tokens:
        copy.wait_recv()
    key_terms = jnp.zeros((1, 128), f32)
    for j in range(4):
        first, second = back_kv[2 * j].astype(f32), back_kv[2 * j + 1].astype(f32)
        keys = jnp.where(low_half, first, pltpu.roll(second, 64, 1))
        values = jnp.where(low_half, pltpu.roll(first, 64, 1), second)
        part = slice(128 * j, 128 * (j + 1))
        pg[1, :, part], terms = unturned(keys, dv_total[TOKENS * j : TOKENS * (j + 1), :], key_gain)
        key_terms = key_terms + terms
        pg[1, :, 512 + 128 * j : 640 + 128 * j] = values.astype(bf16)

    weight_part(1)
    for copy, columns in zip(sib_joins, (slice(1024, 1536), slice(0, 512), slice(512, 1024))):
        copy.wait_recv()
        for q in range(8):
            parts[core, q, :, :, columns] = (
                parts[core, q, :, :, columns].astype(f32) + parts_in[q, :, :, columns].astype(f32)
            ).astype(bf16)

    def f_at(ring, pair):
        return lax.rem(here.z + ring + 4, 4) * 2 + (1 - here.xh if pair else here.xh)

    def plane(part, hop, way):
        def half(ref, which):
            return ref.at[pl.ds(4 * which, 4)]

        up = [net.start(half(part(2, j), 0), half(hop.at[j], 0), way["up"]) for j in (1, 0)]
        down = [net.start(half(part(2, j), 1), half(hop.at[j], 1), way["down"]) for j in (1, 0)]
        yield
        on = []
        for i, j in enumerate((1, 0)):
            up[i].wait_recv()
            add_to(half(part(1, j), 0), half(hop.at[j], 0))
            on.append(net.start(part(1, j), hop.at[2 + 2 * i], way["up"]))
            down[i].wait_recv()
            add_to(half(part(-1, j), 1), half(hop.at[j], 1))
            on.append(net.start(part(-1, j), hop.at[3 + 2 * i], way["down"]))
        yield
        on[0].wait_recv()
        on[1].wait_recv()
        add_to(part(0, 1), hop.at[2], hop.at[3])
        across = net.start(part(0, 1), hop.at[6], way["across"])
        yield
        on[2].wait_recv()
        on[3].wait_recv()
        across.wait_recv()
        add_to(part(0, 0), hop.at[4], hop.at[5], hop.at[6])

    low, high = pl.ds(0, GCOLS // 2), pl.ds(GCOLS // 2, GCOLS // 2)
    first_plane = plane(
        lambda ring, pair: parts.at[core, here.seq_at(ring, pair), :, :, low], hop_a, here.plane("seq")
    )
    second_plane = plane(lambda ring, pair: parts.at[core, :, f_at(ring, pair), :, high], hop_b, way)
    next(first_plane)
    next(second_plane)
    for copy in loads[2:4]:
        copy.wait()
    normed_grad = dot_t(pg[0], wqkv[0]) + dot_t(pg[1], wqkv[1])
    attn_gain_grad = jnp.sum(normed_grad * x * x_scaling, axis=0, keepdims=True)
    query_terms = query_terms + pltpu.roll(query_terms, 64, 1)
    key_terms = key_terms + pltpu.roll(key_terms, 64, 1)
    head_terms = jnp.where(low_half, query_terms, key_terms)
    spread = (
        8 * lax.broadcasted_iota(jnp.int32, (128, D), 0) == lax.broadcasted_iota(jnp.int32, (128, D), 1)
    ).astype(f32).astype(bf16)
    head_row = jnp.zeros((1, D), f32)
    for term in split3(head_terms):
        head_row = head_row + dot(jnp.broadcast_to(term, (16, 128)).astype(bf16), spread)[0:1, :]
    row = lax.broadcasted_iota(jnp.int32, (128, D), 0)
    gain_rows = jnp.where(
        row == 32, attn_gain_grad, jnp.where(row == 33, ffn_gain, jnp.where(row == 34, head_row, 0.0))
    )
    small[...] = small[...] + jnp.transpose(gain_rows).reshape(8, 8, 2, 8, 128)
    small_join = net.start(small.at[:, :, 1 - core], small_in, sib)
    next(first_plane)
    next(second_plane)
    weighted = normed_grad * attn_gain
    middle = jnp.mean(weighted * x, axis=1, keepdims=True)
    token_ref[...] = after_grad[...] + x_scaling * weighted - x * (x_scaling * x_scaling * x_scaling * middle)
    small_join.wait_recv()
    small_in[...] = small_in[...] + small[:, :, core]
    small_copies = [
        net.start(small_in.at[peers[i]], small_s.at[i], seq_peers[i]) for i in range(7)
    ]
    next(first_plane)
    next(second_plane)
    for _ in moves:
        pass
    for _ in more_moves:
        pass
    for copy in small_copies:
        copy.wait_recv()
    mine = small_in[me]
    for i in range(7):
        mine = mine + small_s[i]
    small_in[me] = mine
    small_copies = [
        net.start(small_in.at[me, f_at(*OTHERS[i])], small_f.at[i], fsdp_peers[i]) for i in range(7)
    ]
    next(first_plane, None)
    late = [
        [net.start(parts.at[core, me, f_at(*OTHERS[i]), :, low], late_a.at[i], fsdp_peers[i]) for i in range(7)]
    ]
    next(second_plane, None)
    late.append(
        [net.start(parts.at[core, peers[i], f, :, high], late_b.at[i], seq_peers[i]) for i in range(7)]
    )
    for copy in small_copies:
        copy.wait_recv()
    mine = small_in[me, f]
    for i in range(7):
        mine = mine + small_f[i]
    small_out[...] = mine
    for cols, copies, there in (
        (slice(0, GCOLS // 2), late[0], late_a), (slice(GCOLS // 2, GCOLS), late[1], late_b)
    ):
        for copy in copies:
            copy.wait_recv()
        result = parts[core, me, f, :, cols].astype(f32)
        for i in range(7):
            result = result + there[i].astype(f32)
        total[:, cols] = result
    last = net.start(total.at[pl.ds(pl.multiple_of(8 * (1 - core), 8), 8)], total_in, sib)
    mine = total[pl.ds(pl.multiple_of(8 * core, 8), 8), :]
    last.wait_recv()
    theirs = total_in[...]
    is_low = core == 0
    left, right = jnp.where(is_low, mine, theirs), jnp.where(is_low, theirs, mine)
    for i in range(2):
        qkv_out[:, 1024 * i : 1024 * i + 512] = left[:, 512 * i : 512 * (i + 1)]
        qkv_out[:, 1024 * i + 512 : 1024 * (i + 1)] = right[:, 512 * i : 512 * (i + 1)]
    wo_out[:, 0:512] = left[:, 1024:1536]
    wo_out[:, 512:1024] = right[:, 1024:1536]
    for i in range(1, 8):
        answer(i).wait_send()
    net.finish()


def back(*operands):
    vmem = pl.BlockSpec(memory_space=pltpu.VMEM)
    hbm = pl.BlockSpec(memory_space=pl.ANY)
    return pl.pallas_call(
        back_kernel,
        in_specs=[vmem] * 13 + [hbm] * 7,
        out_specs=[vmem] * 7,
        out_shape=[
            jax.ShapeDtypeStruct((TOKENS, D), bf16),
            jax.ShapeDtypeStruct((TOKENS, D), f32),
            jax.ShapeDtypeStruct((8, 2048), f32),
            jax.ShapeDtypeStruct((8, 1024), f32),
            jax.ShapeDtypeStruct((8, 128), f32),
            jax.ShapeDtypeStruct((2, 128, 2 * F), f32),
            jax.ShapeDtypeStruct((2, 128, F), f32),
        ],
        scratch_shapes=[
            pltpu.VMEM((2, D, 1024), bf16),
            pltpu.VMEM((2, D, 512), bf16),
            pltpu.VMEM((8, TOKENS, 128), bf16),
            pltpu.VMEM((8, TOKENS, 128), bf16),
            pltpu.VMEM((TOKENS, D), bf16),
            pltpu.VMEM((8, TOKENS, 128), bf16),
            pltpu.VMEM((2, TOKENS, D), bf16),
            pltpu.VMEM((TOKENS, D), f32),
        ]
        + [pltpu.VMEM((LENGTH, 128), bf16)] * 4
        + [pltpu.VMEM((64, LENGTH), bf16)]
        + [pltpu.VMEM((LENGTH, 128), f32)] * 2
        + [pltpu.VMEM((8, TOKENS, D), bf16), pltpu.VMEM((2, TOKENS, D), bf16)]
        + [pltpu.VMEM((7, TOKENS, D), bf16)]
        + [
            pltpu.VMEM((2, 8, 8, 16, GCOLS), bf16),
            pltpu.VMEM((8, 8, 16, GCOLS), bf16),
            pltpu.VMEM((8, 8, 2, 8, 128), f32),
            pltpu.VMEM((8, 8, 8, 128), f32),
            pltpu.VMEM((7, 8, 16, GCOLS // 2), bf16),
            pltpu.VMEM((7, 8, 16, GCOLS // 2), bf16),
            pltpu.VMEM((7, 16, GCOLS // 2), bf16),
            pltpu.VMEM((7, 16, GCOLS // 2), bf16),
            pltpu.VMEM((7, 8, 8, 128), f32),
            pltpu.VMEM((7, 8, 128), f32),
            pltpu.VMEM((16, GCOLS), f32),
            pltpu.VMEM((8, GCOLS), f32),
            pltpu.VMEM((3, 2, 2, 128, 3 * F), bf16),
            pltpu.VMEM((2, 2, 128, 3 * F), bf16),
            pltpu.VMEM((5, 2, 128, 3 * F), bf16),
            pltpu.SemaphoreType.DMA((40,)),
            pltpu.SemaphoreType.DMA((100,)),
            pltpu.SemaphoreType.DMA((100,)),
        ],
        compiler_params=pltpu.CompilerParams(collective_id=5, has_side_effects=True, vmem_limit_bytes=63 * 1024 * 1024),
        cost_estimate=pl.CostEstimate(
            flops=9 * 10**9, bytes_accessed=32 << 20, transcendentals=2 * LENGTH * LENGTH
        ),
        name="back",
    )(*operands)


def finish_kernel(layer, token, up, down, qkv, wo, small, *outs):
    for src, dst in zip((layer, token, up, down, qkv, wo), outs):
        dst[...] = src[...]
    router, attn, ffn, head = outs[6:]
    same = lax.broadcasted_iota(jnp.int32, (8, 8), 0) == lax.broadcasted_iota(jnp.int32, (8, 8), 1)
    values = small[...]
    router[...] = values[:, 0:EXPERTS]
    for ref, lane in ((attn, EXPERTS), (ffn, EXPERTS + 1)):
        ref[...] = jnp.sum(jnp.where(same, values[:, lane : lane + 1], 0.0), axis=0, keepdims=True)
    head[...] = values[0:1, EXPERTS + 2 : EXPERTS + 3]


def finish(*operands):
    vmem = pl.BlockSpec(memory_space=pltpu.VMEM)
    small = [(8, EXPERTS), (1, 8), (1, 8), (1, 1)]
    return pl.pallas_call(
        finish_kernel,
        in_specs=[vmem] * 7,
        out_specs=[vmem] * 10,
        out_shape=[jax.ShapeDtypeStruct(a.shape, a.dtype) for a in operands[:6]]
        + [jax.ShapeDtypeStruct(shape, f32) for shape in small],
        compiler_params=pltpu.CompilerParams(vmem_limit_bytes=VMEM),
        name="finish",
    )(*operands)


def gather_kernel(
    qkv_ref, wo_ref, router_ref, attn_ref, ffn_ref, head_ref, routes_ref, cot_ref, out_ref, masks_out, side_out,
    in_ref, mask_ref, stage, block, local_sems, send_sems, recv_sems,
):
    lanes = lax.broadcasted_iota(jnp.int32, (1, 128), 1)
    same = lax.broadcasted_iota(jnp.int32, (8, 8), 0) == lax.broadcasted_iota(jnp.int32, (8, 8), 1)

    def column(row):
        return jnp.sum(jnp.where(same, row[...].astype(f32), 0.0), axis=1, keepdims=True)

    gains = jnp.where(
        lanes == 32,
        column(attn_ref),
        jnp.where(lanes == 33, column(ffn_ref), jnp.where(lanes == 34, head_ref[...].astype(f32), 0.0)),
    )
    for h in range(2):
        in_ref[h, :, 0:1024] = qkv_ref[:, 1024 * h : 1024 * (h + 1)].astype(f32)
        in_ref[h, :, 1024:1536] = wo_ref[:, 512 * h : 512 * (h + 1)].astype(f32)
        in_ref[h, :, 1536:1664] = gains
        in_ref[h, :, 1536:1568] = router_ref[...].astype(f32)
    expert = lax.broadcasted_iota(jnp.int32, (32, 256), 0)
    named = jnp.zeros((32, 256), f32)
    for k in range(8):
        named = jnp.where(routes_ref[k : k + 1, :] == expert, 1.0, named)
    mask_ref[...] = named.astype(bf16)
    here = Place()
    c, s, f = here.core, here.seq, here.z * 2 + here.xh
    sib = here.sibling()
    ways = {"seq": here.plane("seq"), "fsdp": here.plane("fsdp")}
    others = [(2, 1), (2, 0), (0, 1), (1, 1), (-1, 1), (1, 0), (-1, 0)]

    def f_at(ring, pair):
        return lax.rem(here.z + ring + 4, 4) * 2 + (1 - here.xh if pair else here.xh)

    seq_peers = [{"seq": here.seq_at(ring, pair)} for ring, pair in others]
    fsdp_peers = [{"fsdp": here.fsdp_at(ring, pair)} for ring, pair in others]
    meet([sib, *seq_peers, *fsdp_peers])
    net = Copies(send_sems, recv_sems)
    rows = pl.ds(pl.multiple_of(8 * c, 8), 8)
    join = net.start(in_ref.at[1 - c], stage.at[rows], sib)
    stage[rows, :] = in_ref[c]
    join.wait_recv()
    block[...] = stage[...].astype(bf16)
    low, high = pl.ds(0, 896), pl.ds(896, 768)
    locals_ = [
        pltpu.make_async_copy(block, out_ref.at[c, s, f], local_sems.at[0]),
        pltpu.make_async_copy(mask_ref, masks_out.at[here.fsdp], local_sems.at[1]),
    ]
    for copy in locals_:
        copy.start()
    a = [net.start(block.at[:, low], out_ref.at[c, s, f, :, low], peer) for peer in fsdp_peers]
    b = [net.start(block.at[:, high], out_ref.at[c, s, f, :, high], peer) for peer in seq_peers]
    m = [net.start(mask_ref, masks_out.at[here.fsdp], peer) for peer in [sib, *fsdp_peers]]
    for copy in locals_:
        copy.wait()
    kin = []

    def plane(part, way):
        def half(ref, which):
            return ref.at[pl.ds(4 * which, 4)]

        def go(ref, target):
            return net.start(ref, ref, target)

        ref = part(0, 0)
        across, up, down = go(ref, way["across"]), go(ref, way["up"]), go(ref, way["down"])
        kin.append(go(ref, sib))
        yield
        up.wait_recv()
        ref = part(-1, 0)
        far_low = go(half(ref, 0), way["up"])
        kin.append(go(ref, sib))
        down.wait_recv()
        ref = part(1, 0)
        far_high = go(half(ref, 1), way["down"])
        kin.append(go(ref, sib))
        yield
        across.wait_recv()
        ref = part(0, 1)
        up, down = go(ref, way["up"]), go(ref, way["down"])
        kin.append(go(ref, sib))
        yield
        far_low.wait_recv()
        far_high.wait_recv()
        kin.append(go(part(2, 0), sib))
        up.wait_recv()
        ref = part(-1, 1)
        far_low = go(half(ref, 0), way["up"])
        kin.append(go(ref, sib))
        down.wait_recv()
        ref = part(1, 1)
        far_high = go(half(ref, 1), way["down"])
        kin.append(go(ref, sib))
        yield
        far_low.wait_recv()
        far_high.wait_recv()
        kin.append(go(part(2, 1), sib))

    for copy in a:
        copy.wait_recv()
    first = plane(lambda ring, pair: out_ref.at[c, here.seq_at(ring, pair), :, :, low], ways["seq"])
    next(first)
    for copy in b:
        copy.wait_recv()
    second = plane(lambda ring, pair: out_ref.at[c, :, f_at(ring, pair), :, high], ways["fsdp"])
    next(second)
    for i in range(8):
        m[i].wait_recv()
        if i:
            ring, pair = others[i - 1]
            ref = masks_out.at[here.fsdp_at(-ring, pair)]
            kin.append(net.start(ref, ref, sib))
    for turn in range(4):
        next(first, None)
        next(second, None)
        if turn == 1:
            kin.append(net.start(cot_ref, side_out, ways["fsdp"]["across"]))
    for copy in kin:
        copy.wait_recv()
    net.finish()


def gather_weights(*operands):
    n = 65
    return pl.pallas_call(
        gather_kernel,
        in_specs=[pl.BlockSpec(memory_space=pltpu.VMEM)] * 7 + [pl.BlockSpec(memory_space=pl.ANY)],
        out_specs=[pl.BlockSpec(memory_space=pl.ANY)] * 3,
        out_shape=[
            jax.ShapeDtypeStruct((2, 8, 8, 16, WCOLS), bf16),
            jax.ShapeDtypeStruct((16, 32, 256), bf16),
            jax.ShapeDtypeStruct((256, 1024), bf16),
        ],
        scratch_shapes=[
            pltpu.VMEM((2, 8, WCOLS), f32),
            pltpu.VMEM((32, 256), bf16),
            pltpu.VMEM((16, WCOLS), f32),
            pltpu.VMEM((16, WCOLS), bf16),
            pltpu.SemaphoreType.DMA((2,)),
            pltpu.SemaphoreType.DMA((n,)),
            pltpu.SemaphoreType.DMA((n,)),
        ],
        compiler_params=pltpu.CompilerParams(collective_id=1, has_side_effects=True, vmem_limit_bytes=VMEM),
        name="gather_weights",
    )(*operands)


def moe_kernel(
    x_ref, cot_ref, side_ref, g_ref, masks_ref, gates_ref, up_hbm, down_hbm,
    row_out, gate_out, y_out, y_in, grads_out, far_out,
    slots, spare, gates_in, grads_stage, grads_in, sib_in, hop_in, g_rows, up_ref, down_ref,
    rows_x, rows_p, rows_h, rows_u, rows_g, slot_gate, places, ranks, stage_y, stage_r, stage,
    local_sems, send_sems, recv_sems,
):
    here = Place()
    sib = here.sibling()
    way = here.plane("fsdp")
    own = here.fsdp
    counter = [0]

    def local(src, dst):
        copy = pltpu.make_async_copy(src, dst, local_sems.at[counter[0]])
        counter[0] += 1
        copy.start()
        return copy

    first_x = local(x_ref, slots.at[0])
    weights = [local(up_hbm, up_ref), local(down_hbm, down_ref)]

    def source(k):
        ring, pair, c = (0, -1, 1, 2)[k // 4], (k // 2) % 2, k % 2
        z = lax.rem(here.z + ring + 4, 4)
        xh = 1 - here.xh if pair else here.xh
        return z * 4 + xh * 2 + (1 - here.core if c else here.core)

    groups = ((0, 1), (4, 5, 8, 9), (6, 7, 10, 11), (12, 13, 14, 15), (2, 3))
    starts = [SLOTS * sum(len(g) for g in groups[:i]) for i in range(5)]

    def fetch_g(group):
        near = {0: cot_ref, 2: side_ref}
        return [
            local(near[k] if k in near else g_ref.at[source(k)], g_rows.at[s])
            for s, k in enumerate(groups[group])
        ]

    g_copies = fetch_g(0)
    ring = here.plane("seq")
    others = [{"fsdp": source(k)} for k in range(1, 16)]
    meet([*others, ring["up"], ring["down"]])
    net = Copies(send_sems, recv_sems)

    def block(k, low=0, rows=TOKENS):
        return slots.at[k, pl.ds(low, rows)]

    sent = {k: [] for k in range(16)}

    def push(k, to, target, low=0, rows=TOKENS, src=None):
        copy = net.start(block(k, low, rows) if src is None else src, block(to, low, rows), target)
        sent[k].append(copy)
        return copy

    small = [net.start(gates_ref.at[source(k)], gates_in.at[own], others[k - 1]) for k in range(1, 16)]
    gates_in[own] = gates_ref[own]
    across = push(0, 2, way["across"], src=x_ref)
    up = push(0, 4, way["up"], src=x_ref)
    down = push(0, 8, way["down"], src=x_ref)
    kin = {1: push(0, 1, sib, src=x_ref)}
    expert = lax.broadcasted_iota(jnp.int32, (EXPERTS, TOKENS), 0)
    for k in range(16):
        named = masks_ref[source(k)].astype(f32)
        for i in range(2):
            ranks[2 * k + i : 2 * k + i + 1, :] = jnp.sum(
                jnp.where(expert == 2 * own + i, named, 0.0), axis=0, keepdims=True
            )
    before = (
        lax.broadcasted_iota(jnp.int32, (TOKENS, TOKENS), 0)
        < lax.broadcasted_iota(jnp.int32, (TOKENS, TOKENS), 1)
    ).astype(f32).astype(bf16)
    second = lax.rem(lax.broadcasted_iota(jnp.int32, (2 * 16, 1), 0), 2).astype(f32)
    named = ranks[...]
    ranks[...] = jnp.where(named > 0.0, dot(named.astype(bf16), before) + SLOTS * second, -1000.0)
    state = {}

    lanes = lax.broadcasted_iota(jnp.int32, (1, 128), 1)
    slot = lax.broadcasted_iota(jnp.int32, (2 * SLOTS, TOKENS), 0)
    slot_place = slot.astype(f32)
    first = slot < SLOTS
    expert = lax.broadcasted_iota(jnp.int32, (EXPERTS, TOKENS), 0)

    def gather(group):
        for s, k in enumerate(groups[group]):
            if k in kin:
                kin[k].wait_recv()
            g_copies[s].wait()
            wanted = jnp.where(first, ranks[2 * k : 2 * k + 1, :], ranks[2 * k + 1 : 2 * k + 2, :])
            hot = jnp.where(slot_place == wanted, 1.0, 0.0)
            gates = gates_in[source(k)]
            gate = jnp.sum(hot * jnp.where(first, gates[0:1, :], gates[1:2, :]), axis=1, keepdims=True)
            hot = hot.astype(bf16)
            places[s] = hot
            picked = dot(hot, slots[k]).astype(bf16)
            grads = dot(hot, g_rows[s])
            pair = (grads * gate).astype(bf16)
            grads = grads.astype(bf16)
            for i in range(2):
                part = slice(SLOTS * i, SLOTS * (i + 1))
                there = slice(starts[group] + SLOTS * s, starts[group] + SLOTS * (s + 1))
                rows_x[i, there, :] = picked[part]
                rows_p[i, there, :] = pair[part]
                rows_g[i, SLOTS * s : SLOTS * (s + 1), :] = grads[part]
                slot_gate[i, SLOTS * s : SLOTS * (s + 1), :] = jnp.broadcast_to(gate[part], (SLOTS, 128))

    def run(group):
        count = SLOTS * len(groups[group])
        here_rows = pl.ds(starts[group], count)

        def one(e, carry):
            x_rows = rows_x[e, here_rows, :]
            gate_part = dot(x_rows, up_ref[e, :, 0:F])
            up_part = dot(x_rows, up_ref[e, :, F : 2 * F])
            sigmoid = 1.0 / (1.0 + jnp.exp(-gate_part))
            silu = gate_part * sigmoid
            hidden = (silu * up_part).astype(bf16)
            rows_h[e, here_rows, :] = hidden
            hidden_grad = dot(rows_p[e, here_rows, :], down_ref[e])
            slope = sigmoid * (1.0 + gate_part * (1.0 - sigmoid))
            rows_u[e, here_rows, 0:F] = (hidden_grad * up_part * slope).astype(bf16)
            rows_u[e, here_rows, F : 2 * F] = (hidden_grad * silu).astype(bf16)
            out = dot_t(hidden, down_ref[e]).astype(bf16).astype(f32)
            gate_grad = jnp.sum(out * rows_g[e, 0:count, :].astype(f32), axis=1, keepdims=True)
            stage_y[e, 0:count, :] = (out * slot_gate[e, 0:count, 0:1]).astype(bf16)
            stage_r[e, 0:count, :] = dot_t(rows_u[e, here_rows, :], up_ref[e]).astype(bf16)
            for s, k in enumerate(groups[group]):
                hot = places[s, pl.ds(pl.multiple_of(SLOTS * e, SLOTS), SLOTS), :].astype(f32)
                grads_stage[k, e, 0:1, :] = jnp.sum(
                    hot * gate_grad[SLOTS * s : SLOTS * (s + 1)], axis=0, keepdims=True
                )
            return carry

        lax.fori_loop(0, 2, one, 0)
        for k in groups[group]:
            if k:
                small.append(net.start(grads_stage.at[k], grads_in.at[own], others[k - 1]))
            else:
                grads_in[own] = grads_stage[0]

    def result(k):
        return spare.at[k // 4 - 1] if k in (4, 8) else slots.at[k]

    y_sent = []

    def free_stage():
        for copy, remote in state.pop("y", ()):
            if remote:
                copy.wait_send()
            else:
                copy.wait()

    def combine(group):
        order = (2, 3, 0, 1) if group == 3 else range(len(groups[group]))
        for s in order:
            k = groups[group][s]
            if k not in (4, 8):
                for copy in sent[k]:
                    copy.wait_send()
            part = slice(SLOTS * s, SLOTS * (s + 1))
            both = jnp.concatenate([stage_r[0, part, :], stage_r[1, part, :]], axis=0)
            result(k)[...] = t_dot(places[s], both).astype(bf16)
            if k % 2:
                state[k - 1] = net.start(slots.at[k], sib_in.at[k // 2], sib)
        free_stage()
        state["y"] = []
        for s, k in enumerate(groups[group]):
            part = slice(SLOTS * s, SLOTS * (s + 1))
            both = jnp.concatenate([stage_y[0, part, :], stage_y[1, part, :]], axis=0)
            stage[s, :, 0:D] = t_dot(places[s], both).astype(bf16)
            ready = stage.at[s, :, pl.ds(0, D)]
            if k % 2:
                y_sent.append(net.start(ready, y_in.at[k // 2], sib))
                state["y"].append((y_sent[-1], True))
            else:
                state["y"].append((local(ready, y_out.at[k // 2]), False))

    def join(k):
        state[k].wait_recv()
        there = result(k)
        there[...] = (there[...].astype(f32) + sib_in[k // 2].astype(f32)).astype(bf16)

    first_x.wait()
    for copy in small:
        copy.wait_recv()
    small.clear()
    gather(0)
    g_copies = fetch_g(1)
    for copy in weights:
        copy.wait()
    run(0)
    up.wait_recv()
    far_low = push(4, 12, way["up"], 0, 128)
    kin[5] = push(4, 5, sib)
    down.wait_recv()
    far_high = push(8, 12, way["down"], 128, 128)
    kin[9] = push(8, 9, sib)
    across.wait_recv()
    up_x = push(2, 6, way["up"])
    down_x = push(2, 10, way["down"])
    kin[3] = push(2, 3, sib)
    combine(0)
    gather(1)
    g_copies = fetch_g(2)
    run(1)
    combine(1)
    far_low.wait_recv()
    far_high.wait_recv()
    far_x = push(12, 14, way["across"])
    kin[13] = push(12, 13, sib)
    up_x.wait_recv()
    kin[7] = push(6, 7, sib)
    down_x.wait_recv()
    kin[11] = push(10, 11, sib)
    gather(2)
    g_copies = fetch_g(3)
    join(4)
    hop_rd = net.start(result(4), hop_in.at[5], way["down"])
    join(8)
    hop_ru = net.start(result(8), hop_in.at[4], way["up"])
    run(2)
    far_x.wait_recv()
    kin[15] = push(14, 15, sib)
    combine(2)
    gather(3)
    g_copies = fetch_g(4)
    join(6)
    hop_xd = net.start(slots.at[6], hop_in.at[2], way["down"])
    join(10)
    hop_xu = net.start(slots.at[10], hop_in.at[3], way["up"])
    run(3)
    combine(3)
    gather(4)
    join(14)

    def quarter(ref, i):
        return ref.at[pl.ds((0, 128, 64, 192)[i], 64)]

    ways = ("up", "down", "up", "down")
    hop_a = [
        net.start(quarter(slots.at[14], i), quarter(hop_in.at[0], i), way["across"]) for i in range(4)
    ]
    join(12)
    join(0)
    run(4)
    combine(4)

    w_copies = []

    far_grads = []

    def send_far(dx):
        for copy in w_copies:
            copy.wait()
        w_copies.clear()
        rows = pl.ds(pl.multiple_of(here.seq_at(2, dx) * 128, 128), 128)
        for e, to in enumerate(("up", "down")):
            far_grads.append(net.start(grads_out.at[e, rows], far_out.at[e], ring[to]))

    def weight_grad(e, dx):
        free_stage()
        for copy in w_copies:
            copy.wait()
        xl = 1 - here.xl if dx else here.xl
        columns = pl.ds(pl.multiple_of(xl * 512, 512), 512)
        for wide, left, right in (
            (slice(0, 2 * F), rows_x, rows_u), (slice(2 * F, 3 * F), rows_p, rows_h)
        ):
            result = t_dot(left[e, :, columns], right[e]).astype(bf16)
            for y in range(4):
                stage[y, 0:128, wide] = result[128 * y : 128 * (y + 1)]
        w_copies[:] = [
            local(
                stage.at[y, pl.ds(0, 128)],
                grads_out.at[e, pl.ds(pl.multiple_of(xl * 512 + 128 * y, 128), 128)],
            )
            for y in range(4)
        ]

    weight_grad(0, 1)
    join(2)
    hop_xd.wait_recv()
    hop_xu.wait_recv()
    slots[2] = (slots[2].astype(f32) + hop_in[2].astype(f32) + hop_in[3].astype(f32)).astype(bf16)
    hop_rx = net.start(slots.at[2], hop_in.at[6], way["across"])
    far = []
    for i in range(4):
        hop_a[i].wait_recv()
        ref, other = quarter(slots.at[12], i), quarter(hop_in.at[0], i)
        ref[...] = (ref[...].astype(f32) + other[...].astype(f32)).astype(bf16)
        far.append(net.start(ref, quarter(hop_in.at[1], i), way[ways[i]]))
    weight_grad(1, 1)
    send_far(1)
    relay = []
    for i in range(4):
        far[i].wait_recv()
        relay.append(net.start(quarter(hop_in.at[1], i), quarter(hop_in.at[7], i), way[ways[i]]))
    weight_grad(0, 0)
    weight_grad(1, 0)
    for copy in w_copies:
        copy.wait()
    for copy in (hop_ru, hop_rd, hop_rx, *relay, *far_grads, *y_sent, *small):
        copy.wait_recv()
    total = (
        slots[0].astype(f32)
        + hop_in[4].astype(f32)
        + hop_in[5].astype(f32)
        + hop_in[6].astype(f32)
        + hop_in[7].astype(f32)
    )
    row_out[...] = total
    row = lax.broadcasted_iota(jnp.int32, (128, TOKENS), 0)
    gate_grads = jnp.zeros((128, TOKENS), f32)
    for f in range(16):
        for e in range(2):
            gate_grads = jnp.where(row == 2 * f + e, grads_in[f, e, 0:1, :], gate_grads)
    gate_out[...] = jnp.transpose(gate_grads)
    waited = {id(copy) for copies in (*(sent[k] for k in sent if k not in (4, 8)), y_sent) for copy in copies}
    for copy in net.all:
        if id(copy) not in waited:
            copy.wait_send()


def moe(x, cot, side, g_all, masks, gates, up, down):
    any_space = pl.BlockSpec(memory_space=pl.ANY)
    vmem = pl.BlockSpec(memory_space=pltpu.VMEM)
    return pl.pallas_call(
        moe_kernel,
        in_specs=[any_space] * 4 + [vmem, vmem, any_space, any_space],
        out_specs=[vmem, vmem, any_space, any_space, any_space, any_space],
        out_shape=[
            jax.ShapeDtypeStruct((TOKENS, D), f32),
            jax.ShapeDtypeStruct((TOKENS, 128), f32),
            jax.ShapeDtypeStruct((8, TOKENS, D), bf16),
            jax.ShapeDtypeStruct((8, TOKENS, D), bf16),
            jax.ShapeDtypeStruct((2, D, 3 * F), bf16),
            jax.ShapeDtypeStruct((2, 128, 3 * F), bf16),
        ],
        scratch_shapes=[
            pltpu.VMEM((16, TOKENS, D), bf16),
            pltpu.VMEM((2, TOKENS, D), bf16),
            pltpu.VMEM((16, 8, TOKENS), f32),
            pltpu.VMEM((16, 2, 8, TOKENS), f32),
            pltpu.VMEM((16, 2, 8, TOKENS), f32),
            pltpu.VMEM((8, TOKENS, D), bf16),
            pltpu.VMEM((8, TOKENS, D), bf16),
            pltpu.VMEM((4, TOKENS, D), bf16),
            pltpu.VMEM((2, D, 2 * F), bf16),
            pltpu.VMEM((2, D, F), bf16),
            pltpu.VMEM((2, ROWS, D), bf16),
            pltpu.VMEM((2, ROWS, D), bf16),
            pltpu.VMEM((2, ROWS, F), bf16),
            pltpu.VMEM((2, ROWS, 2 * F), bf16),
            pltpu.VMEM((2, GROUP_ROWS, D), bf16),
            pltpu.VMEM((2, GROUP_ROWS, 128), f32),
            pltpu.VMEM((4, 2 * SLOTS, TOKENS), bf16),
            pltpu.VMEM((2 * 16, TOKENS), f32),
            pltpu.VMEM((2, GROUP_ROWS, D), bf16),
            pltpu.VMEM((2, GROUP_ROWS, D), bf16),
            pltpu.VMEM((4, TOKENS, 3 * F), bf16),
            pltpu.SemaphoreType.DMA((56,)),
            pltpu.SemaphoreType.DMA((96,)),
            pltpu.SemaphoreType.DMA((96,)),
        ],
        compiler_params=pltpu.CompilerParams(
            collective_id=4, has_side_effects=True, vmem_limit_bytes=63 * 1024 * 1024
        ),
        cost_estimate=pl.CostEstimate(flops=32 * 10**9, bytes_accessed=40 << 20, transcendentals=1 << 21),
        name="moe",
    )(x, cot, side, g_all, masks, gates, up, down)


def on_device(
    tokens, attn_gain, qkv_weight, qk_gain, out_weight, ffn_gain, router_weight,
    gate_up_weight, down_weight, routes, cotangent,
):
    x = tokens.reshape(TOKENS, D)
    cot = cotangent.reshape(TOKENS, D)
    route_ids = routes.reshape(TOKENS, TOPK).T
    whole, masks, side = gather_weights(
        qkv_weight, out_weight, router_weight, attn_gain.reshape(1, 8), ffn_gain.reshape(1, 8),
        qk_gain.reshape(1, 1), route_ids, cot,
    )
    whole = whole.reshape(2, D, WCOLS)

    near, far_place = rotary_tables()
    heads, g_all, full, logs, attended, after, normed_ffn, gates, small_t, raw, gates_t = front(
        x, whole, route_ids, near, far_place, cot, side
    )
    row_sum, gate_sum, y_own, y_other, expert_grads, far = moe(
        normed_ffn, cot, side, g_all, masks, gates_t, gate_up_weight, down_weight
    )
    layer_out, token_grad, qkv_part, out_part, small, up_part, down_part = back(
        gate_sum, gates, after, x, cot, attended, normed_ffn, small_t, heads, full, logs, near, far_place,
        row_sum, raw, whole, y_own, y_other, expert_grads, far,
    )
    layer_out, token_grad, up_part, down_part, qkv_part, out_part, router_part, attn_part, ffn_part, head_part = finish(
        layer_out, token_grad, up_part, down_part, qkv_part, out_part, small
    )
    return (
        layer_out.reshape(1, TOKENS, D),
        token_grad.reshape(1, TOKENS, D),
        attn_part.reshape(8),
        qkv_part,
        head_part.reshape(1),
        out_part,
        ffn_part.reshape(8),
        router_part,
        up_part,
        down_part,
    )


def solution(mesh):
    return jax.shard_map(
        on_device,
        mesh=mesh,
        in_specs=(
            P("fsdp", "seq", None),
            P(("seq", "fsdp")),
            P(("seq", "fsdp"), None),
            P(("seq", "fsdp")),
            P(("seq", "fsdp"), None),
            P(("seq", "fsdp")),
            P(("seq", "fsdp"), None),
            P("fsdp", None, None),
            P("fsdp", None, None),
            P("fsdp", "seq", None),
            P("fsdp", "seq", None),
        ),
        out_specs=(
            P("fsdp", "seq", None),
            P("fsdp", "seq", None),
            P(("seq", "fsdp")),
            P(("seq", "fsdp"), None),
            P(("seq", "fsdp")),
            P(("seq", "fsdp"), None),
            P(("seq", "fsdp")),
            P(("seq", "fsdp"), None),
            P("fsdp", "seq", None),
            P("fsdp", "seq", None),
        ),
        check_vma=False,
    )
```

```python
import jax
import jax.numpy as jnp
import numpy as np
from jax import lax
from jax.experimental import pallas as pl
from jax.experimental.pallas import tpu as pltpu
from jax.sharding import PartitionSpec as P

D = 1024
HEAD_SIZE = 64
F = 512
TOPK = 8
EXPERTS = 32
SLOTS = 96
TOKENS = 256
SEQ = 8
FSDP = 16
LENGTH = SEQ * TOKENS
GROUP_ROWS = 4 * SLOTS
ROWS = 4 * GROUP_ROWS
GCOLS = 1536
VMEM = 60 * 1024 * 1024

epsilon = 1e-06
rope_base = 10000.0
f32 = jnp.float32
bf16 = jnp.bfloat16


def dot(a, b):
    return lax.dot_general(a, b, (((1,), (0,)), ((), ())), preferred_element_type=f32)


def dot_t(a, b):
    return lax.dot_general(a, b, (((1,), (1,)), ((), ())), preferred_element_type=f32)


def t_dot(a, b):
    return lax.dot_general(a, b, (((0,), (0,)), ((), ())), preferred_element_type=f32)


MESH = pl.DeviceIdType.MESH


class Place:
    def __init__(self):
        self.seq = lax.axis_index("seq")
        self.fsdp = lax.axis_index("fsdp")
        self.core = lax.rem(self.fsdp, 2)
        self.xh = lax.rem(self.fsdp // 2, 2)
        self.z = self.fsdp // 4
        self.y = lax.rem(self.seq, 4)
        self.xl = self.seq // 4

    def sibling(self):
        return {"fsdp": self.fsdp + 1 - 2 * self.core}

    def fsdp_at(self, ring, pair):
        z = lax.rem(self.z + ring + 4, 4)
        xh = 1 - self.xh if pair else self.xh
        return z * 4 + xh * 2 + self.core

    def seq_at(self, ring, pair):
        y = lax.rem(self.y + ring + 4, 4)
        xl = 1 - self.xl if pair else self.xl
        return xl * 4 + y

    def plane(self, axis):
        at = self.fsdp_at if axis == "fsdp" else self.seq_at
        return {
            "up": {axis: at(1, 0)},
            "down": {axis: at(-1, 0)},
            "across": {axis: at(0, 1)},
        }


def meet(targets):
    barrier = pltpu.get_barrier_semaphore()
    for target in targets:
        pl.semaphore_signal(barrier, inc=1, device_id=target, device_id_type=MESH)
    pl.semaphore_wait(barrier, len(targets))


class Copies:
    def __init__(self, send_sems, recv_sems):
        self.send_sems, self.recv_sems, self.count, self.all = send_sems, recv_sems, 0, []

    def start(self, src, dst, target):
        k = self.count
        self.count += 1
        copy = pltpu.make_async_remote_copy(
            src_ref=src, dst_ref=dst, send_sem=self.send_sems.at[k], recv_sem=self.recv_sems.at[k],
            device_id=target, device_id_type=MESH,
        )
        copy.start()
        self.all.append(copy)
        return copy

    def finish(self, done=()):
        for copy in self.all:
            if all(copy is not other for other in done):
                copy.wait_send()


OTHERS = ((2, 1), (2, 0), (0, 1), (1, 1), (-1, 1), (1, 0), (-1, 0))
WCOLS = 1664


def lane_halves():
    lanes = lax.broadcasted_iota(jnp.int32, (1, 128), 1)
    return lanes, lanes < HEAD_SIZE


def head_mean(values, low_half):
    low = jnp.sum(jnp.where(low_half, values, 0.0), axis=1, keepdims=True)
    high = jnp.sum(jnp.where(low_half, 0.0, values), axis=1, keepdims=True)
    return jnp.where(low_half, low, high) * (1.0 / HEAD_SIZE)


def partner(values, lanes):
    return jnp.where(
        lax.rem(lanes, HEAD_SIZE) < HEAD_SIZE // 2, pltpu.roll(values, 96, 1), pltpu.roll(values, 32, 1)
    )


def rotary_tables():
    inverse = rope_base ** (-2.0 * (np.arange(128) % 32) / HEAD_SIZE)
    near = np.arange(TOKENS)[:, None] * inverse[None, :]
    far = TOKENS * np.arange(SEQ)[:, None] * inverse[None, :]
    return [jnp.asarray(np.stack([np.cos(a), np.sin(a)]), f32) for a in (near, far)]


def rotary(near_ref, far_ref, block, lanes):
    pick = lax.broadcasted_iota(jnp.int32, (SEQ, 128), 0) == block
    far_cos = jnp.sum(jnp.where(pick, far_ref[0], 0.0), axis=0, keepdims=True)
    far_sin = jnp.sum(jnp.where(pick, far_ref[1], 0.0), axis=0, keepdims=True)
    cos = near_ref[0] * far_cos - near_ref[1] * far_sin
    sin = near_ref[1] * far_cos + near_ref[0] * far_sin
    return cos, jnp.where(lax.rem(lanes, HEAD_SIZE) < HEAD_SIZE // 2, -sin, sin)


def row_scale(values):
    return lax.rsqrt(jnp.mean(values * values, axis=1, keepdims=True) + epsilon)


def gain_tiles(small_t, lanes):
    pick = (
        lax.broadcasted_iota(jnp.int32, (D, 128), 0) == 8 * lax.broadcasted_iota(jnp.int32, (D, 128), 1)
    ).astype(f32).astype(bf16)
    gains = dot(small_t[32:48, :], pick)[2:3, :]
    other = pltpu.roll(gains, 64, 1)
    low_half = lanes < HEAD_SIZE
    return jnp.where(low_half, gains, other), jnp.where(low_half, other, gains)


def front_kernel(
    x_ref, w_ref, routes_ref, near_ref, far_place_ref, cot_ref, side_ref,
    heads_out, g_out, full_ref, logs_ref, att_ref, after_ref, normed_ref, gates_ref, small_t_ref, raw_ref, gates_t_ref,
    wq, wkv, wo, small, send, heads, out_buf, att, key0, key1, value,
    local_sems, send_sems, recv_sems,
):
    here = Place()
    me = here.seq
    loads = [
        pltpu.make_async_copy(w_ref.at[h, :, pl.ds(start, width)], there, local_sems.at[k])
        for k, (h, start, width, there) in enumerate(
            (
                (0, 1536, 128, small),
                (0, 0, 1024, wq),
                (1, 0, 1024, wkv),
                (0, 1024, 512, wo.at[0]),
                (1, 1024, 512, wo.at[1]),
            )
        )
    ]
    for copy in loads:
        copy.start()
    peers = [here.seq_at(*other) for other in OTHERS]
    sib = here.sibling()
    way = here.plane("fsdp")
    meet([sib, *way.values()] + [{"seq": peer} for peer in peers])
    net = Copies(send_sems, recv_sems)

    def gather_cotangent():
        def at(ring, pair):
            return g_out.at[here.fsdp_at(ring, pair)]

        def half(ref, which):
            return ref.at[pl.ds(128 * which, 128)]

        def go(ref, target):
            return net.start(ref, ref, target)

        up, down = [net.start(cot_ref, at(0, 0), way[w]) for w in ("up", "down")]
        kin = [net.start(cot_ref, at(0, 0), sib), net.start(side_ref, at(0, 1), sib)]
        yield
        up.wait_recv()
        far = [go(half(at(-1, 0), 0), way["up"])]
        kin.append(go(at(-1, 0), sib))
        down.wait_recv()
        far.append(go(half(at(1, 0), 1), way["down"]))
        kin.append(go(at(1, 0), sib))
        up, down = [net.start(side_ref, at(0, 1), way[w]) for w in ("up", "down")]
        yield
        for copy in far:
            copy.wait_recv()
        across = go(at(2, 0), way["across"])
        kin.append(go(at(2, 0), sib))
        yield
        up.wait_recv()
        kin.append(go(at(-1, 1), sib))
        down.wait_recv()
        kin.append(go(at(1, 1), sib))
        across.wait_recv()
        kin.append(go(at(2, 1), sib))
        yield
        for copy in kin:
            copy.wait_recv()

    moves = gather_cotangent()
    next(moves)
    lanes, low_half = lane_halves()
    loads[0].wait()
    small_t = jnp.transpose(small[...].astype(f32)).astype(bf16)
    small_t_ref[...] = small_t
    x = x_ref[...].astype(f32)
    normed = (x * row_scale(x) * small_t[32:33, :].astype(f32)).astype(bf16)
    query_gain, key_gain = gain_tiles(small_t, lanes)
    cos, sin = rotary(near_ref, far_place_ref, me, lanes)
    loads[1].wait()
    queries = dot(normed, wq[...])
    loads[2].wait()
    kv = dot(normed, wkv[...])

    def turned(tile, gain):
        normal = tile * lax.rsqrt(head_mean(tile * tile, low_half) + epsilon) * gain
        return normal * cos + partner(normal, lanes) * sin

    for j in range(4):
        part = slice(128 * j, 128 * (j + 1))
        raw_ref[8 + j] = kv[:, part]
        keys = turned(kv[:, part], key_gain)
        values = kv[:, 512 + 128 * j : 640 + 128 * j]
        send[2 * j, :, 128:256] = jnp.where(low_half, keys, pltpu.roll(values, 64, 1)).astype(bf16)
        send[2 * j + 1, :, 128:256] = jnp.where(low_half, pltpu.roll(keys, 64, 1), values).astype(bf16)
    for h in range(8):
        raw_ref[h] = queries[:, 128 * h : 128 * (h + 1)]
        send[h, :, 0:128] = turned(raw_ref[h], query_gain).astype(bf16)
    copies = [net.start(send.at[peer], heads.at[me], {"seq": peer}) for peer in peers]
    heads[me] = send[me]
    next(moves)
    for copy in copies:
        copy.wait_recv()
    save = pltpu.make_async_copy(heads, heads_out, local_sems.at[5])
    save.start()
    for c in range(8):
        rows = slice(TOKENS * c, TOKENS * (c + 1))
        pair = heads[c, :, 128:256].astype(f32)
        key0[rows, :] = jnp.where(low_half, pair, 0.0).astype(bf16)
        key1[rows, :] = jnp.where(low_half, 0.0, pltpu.roll(pair, 64, 1)).astype(bf16)
        value[rows, :] = jnp.where(low_half, jnp.where(lanes == 0, 1.0, 0.0), pair).astype(bf16)

    def block(i, carry):
        j = lax.rem(me + 1 + i, 8)
        query = (heads[j, :, 0:128].astype(f32) * (1.0 / 8.0)).astype(bf16)
        results = []
        for key in (key0, key1):
            total = jnp.zeros((TOKENS, 128), f32)
            for c in range(4):
                part = pl.ds(c * 512, 512)
                weights = jnp.exp(dot_t(query, key[part, :]))
                total = total + dot(weights.astype(bf16), value[part, :])
            results.append(total)
        sum0, sum1 = results[0][:, 0:1], results[1][:, 0:1]
        full = jnp.where(low_half, pltpu.roll(results[0] / sum0, 64, 1), results[1] / sum1)
        rows = pl.ds(pl.multiple_of(j * TOKENS, TOKENS), TOKENS)
        full_ref[rows, :] = full
        logs_ref[rows, :] = jnp.where(low_half, jnp.log(sum0), jnp.log(sum1))
        out_buf[j] = full.astype(bf16)

        @pl.when(i < 7)
        def _():
            answer(i).start()

        return carry

    columns = pl.ds(pl.multiple_of(me * 128, 128), 128)

    def answer(i):
        j = lax.rem(me + 1 + i, 8)
        return pltpu.make_async_remote_copy(
            src_ref=out_buf.at[j], dst_ref=att.at[:, columns], send_sem=send_sems.at[24 + i],
            recv_sem=recv_sems.at[24 + i], device_id={"seq": j}, device_id_type=MESH,
        )

    lax.fori_loop(0, 1, block, 0)
    next(moves)
    lax.fori_loop(1, 7, block, 0)
    next(moves)
    lax.fori_loop(7, 8, block, 0)
    att[:, columns] = out_buf[me]
    for k in (3, 4):
        loads[k].wait()
    for i in range(7):
        answer(i).wait_recv()
    attended = att[...]
    att_ref[...] = attended
    squares = jnp.zeros((TOKENS, 1), f32)
    for h in range(2):
        part = slice(512 * h, 512 * (h + 1))
        after = x_ref[:, part].astype(f32) + dot(attended, wo[h])
        after_ref[:, part] = after
        squares = squares + jnp.sum(after * after, axis=1, keepdims=True)
    scaling = lax.rsqrt(squares * (1.0 / D) + epsilon)
    normed = (after_ref[...] * scaling * small_t[33:34, :].astype(f32)).astype(bf16)
    normed_ref[...] = normed
    logits = dot(normed, small[...])
    expert = lax.broadcasted_iota(jnp.int32, (128, TOKENS), 0)
    named = jnp.zeros((128, TOKENS), f32)
    for k in range(TOPK):
        named = jnp.where(routes_ref[k : k + 1, :] == expert, 1.0, named)
    named = jnp.transpose(named)
    peak = jnp.max(jnp.where(named > 0.0, logits, -1e30), axis=1, keepdims=True)
    chosen = jnp.where(named > 0.0, jnp.exp(logits - peak), 0.0)
    gates = chosen / jnp.sum(chosen, axis=1, keepdims=True)
    gates_ref[...] = gates
    across = jnp.transpose(gates)
    gates_t_ref[...] = jnp.zeros_like(gates_t_ref)
    for i in range(FSDP):
        gates_t_ref[i, 0:2, :] = across[2 * i : 2 * i + 2, :]
    for _ in moves:
        pass
    save.wait()
    for i in range(7):
        answer(i).wait_send()
    net.finish()


def front(x, whole, routes, near, far, cot, side):
    vmem = pl.BlockSpec(memory_space=pltpu.VMEM)
    hbm = pl.BlockSpec(memory_space=pl.ANY)
    return pl.pallas_call(
        front_kernel,
        in_specs=[vmem, hbm, vmem, vmem, vmem, hbm, hbm],
        out_specs=[hbm] * 2 + [vmem] * 9,
        out_shape=[
            jax.ShapeDtypeStruct((8, TOKENS, 256), bf16),
            jax.ShapeDtypeStruct((FSDP, TOKENS, D), bf16),
            jax.ShapeDtypeStruct((LENGTH, 128), f32),
            jax.ShapeDtypeStruct((LENGTH, 128), f32),
            jax.ShapeDtypeStruct((TOKENS, D), bf16),
            jax.ShapeDtypeStruct((TOKENS, D), f32),
            jax.ShapeDtypeStruct((TOKENS, D), bf16),
            jax.ShapeDtypeStruct((TOKENS, 128), f32),
            jax.ShapeDtypeStruct((128, D), bf16),
            jax.ShapeDtypeStruct((12, TOKENS, 128), f32),
            jax.ShapeDtypeStruct((FSDP, 8, TOKENS), f32),
        ],
        scratch_shapes=[
            pltpu.VMEM((D, 1024), bf16),
            pltpu.VMEM((D, 1024), bf16),
            pltpu.VMEM((2, D, 512), bf16),
            pltpu.VMEM((D, 128), bf16),
            pltpu.VMEM((8, TOKENS, 256), bf16),
            pltpu.VMEM((8, TOKENS, 256), bf16),
            pltpu.VMEM((8, TOKENS, 128), bf16),
            pltpu.VMEM((TOKENS, D), bf16),
            pltpu.VMEM((LENGTH, 128), bf16),
            pltpu.VMEM((LENGTH, 128), bf16),
            pltpu.VMEM((LENGTH, 128), bf16),
            pltpu.SemaphoreType.DMA((8,)),
            pltpu.SemaphoreType.DMA((31,)),
            pltpu.SemaphoreType.DMA((31,)),
        ],
        compiler_params=pltpu.CompilerParams(collective_id=2, has_side_effects=True, vmem_limit_bytes=VMEM),
        cost_estimate=pl.CostEstimate(
            flops=4 * 10**9, bytes_accessed=16 << 20, transcendentals=2 * LENGTH * LENGTH
        ),
        name="front",
    )(x, whole, routes, near, far, cot, side)


def split3(values):
    high = values.astype(bf16).astype(f32)
    rest = values - high
    middle = rest.astype(bf16).astype(f32)
    return high, middle, rest - middle


def with_terms(lanes, start, parts):
    high, middle, low = parts
    return jnp.where(
        lanes == start,
        high,
        jnp.where(lanes == start + 1, middle, jnp.where(lanes == start + 2, low, 0.0)),
    )


def back_kernel(
    gate_sum_ref, gates_ref, after_ref, x_ref, cot_ref, att_ref, normed_ref, small_t_ref,
    heads_ref, full_ref, logs_ref, near_ref, far_place_ref, row_ref, raw_ref, w_ref, y_ref, y_other, grads_ref, far_ref,
    layer_ref, token_ref, qkv_out, wo_out, small_out, up_out, down_out,
    wqkv, wo, send, grads, back_q, back_kv, pg, after_grad,
    key0, key1, value0, value1, key_t, dk_total, dv_total,
    slots, y_stage, hop_in,
    parts, parts_in, small, small_in, hops, late, small_s, small_f, total, total_in,
    chunks, far_in, chunk_in, local_sems, send_sems, recv_sems,
):
    here = Place()
    me = here.seq
    sib = here.sibling()
    way = here.plane("fsdp")
    loads = [
        pltpu.make_async_copy(w_ref.at[h, :, pl.ds(start, width)], there, local_sems.at[k])
        for k, (h, start, width, there) in enumerate(
            (
                (0, 1024, 512, wo.at[0]),
                (1, 1024, 512, wo.at[1]),
                (0, 0, 1024, wqkv.at[0]),
                (1, 0, 1024, wqkv.at[1]),
            )
        )
    ]
    loads.append(pltpu.make_async_copy(row_ref, after_grad, local_sems.at[19]))
    for copy in loads:
        copy.start()
    e_loads = [
        pltpu.make_async_copy(
            grads_ref.at[:, pl.ds(pl.multiple_of(here.seq_at(ring, pair) * 128, 128), 128)],
            chunks.at[i, pair], local_sems.at[12 + 2 * i + pair],
        )
        for i, ring in enumerate((-1, 1, 0)) for pair in range(2)
    ]
    e_loads.append(pltpu.make_async_copy(far_ref, far_in.at[1], local_sems.at[18]))
    order = (6, 7, 3, 5, 2, 4, 1, 0)
    y_loads = {k: pltpu.make_async_copy(y_ref.at[k], slots.at[k], local_sems.at[4 + k]) for k in order}
    y_more = {
        k: pltpu.make_async_copy(y_other.at[k], y_stage.at[i % 2], local_sems.at[20 + k]) for i, k in enumerate(order)
    }
    for copy in y_loads.values():
        copy.start()
    for k in order[:2]:
        y_more[k].start()
    peers = [here.seq_at(*other) for other in OTHERS]
    seq_peers = [{"seq": peer} for peer in peers]
    fsdp_peers = [{"fsdp": here.fsdp_at(*other)} for other in OTHERS]
    meet([sib, *seq_peers, *fsdp_peers])
    net = Copies(send_sems, recv_sems)
    for copy in e_loads:
        copy.start()
    rows = pl.ds(pl.multiple_of(here.seq_at(2, 0) * 128, 128), 128)
    ring = here.plane("seq")
    far_sent = [
        net.start(grads_ref.at[e, rows], far_in.at[0, e], ring[to]) for e, to in enumerate(("up", "down"))
    ]
    lanes, low_half = lane_halves()

    gate_grad = gate_sum_ref[...]
    gates = gates_ref[...]
    chosen = gates * (gate_grad - jnp.sum(gates * gate_grad, axis=1, keepdims=True))
    logits_grad = chosen.astype(bf16)
    loads[4].wait()
    normed_grad = after_grad[...] + dot(logits_grad, small_t_ref[...])
    after = after_ref[...]
    scaling = row_scale(after)
    weighted = normed_grad * small_t_ref[33:34, :].astype(f32)
    middle = jnp.mean(weighted * after, axis=1, keepdims=True)
    after_grad[...] = (
        cot_ref[...].astype(f32) + scaling * weighted - after * (scaling * scaling * scaling * middle)
    )
    after_low = after_grad[...].astype(bf16)
    ffn_gain = jnp.sum(normed_grad * after * scaling, axis=0, keepdims=True)
    for k in (0, 1):
        loads[k].wait()
    for q in range(2):
        rows = slice(512 * q, 512 * (q + 1))
        attended_grad = dot_t(after_low[:, 0:512], wo[0, rows, :]) + dot_t(after_low[:, 512:1024], wo[1, rows, :])
        for h in range(4):
            send[4 * q + h] = attended_grad[:, 128 * h : 128 * (h + 1)].astype(bf16)

    def delivery(d):
        peer = lax.rem(me + d, 8)
        return pltpu.make_async_remote_copy(
            src_ref=send.at[peer], dst_ref=grads.at[me], send_sem=send_sems.at[104 + d],
            recv_sem=recv_sems.at[104 + d], device_id={"seq": peer}, device_id_type=MESH,
        )

    for d in range(7, 0, -1):
        delivery(d).start()
    grads[me] = send[me]
    router_grad = t_dot(normed_ref[...], logits_grad)
    small[...] = router_grad.reshape(8, 8, 2, 8, 128)
    for h in range(2):
        out_grad = t_dot(att_ref[...], after_low[:, 512 * h : 512 * (h + 1)]).astype(bf16)
        parts[h, :, :, :, 1024:1536] = out_grad.reshape(8, 8, 16, 512)
    out_join = net.start(
        parts.at[1 - here.core, :, :, :, pl.ds(1024, 512)], parts_in.at[:, :, :, pl.ds(1024, 512)], sib
    )

    def add_to(ref, *values):
        result = ref[...].astype(f32)
        for value in values:
            result = result + value[...].astype(f32)
        ref[...] = result.astype(bf16)

    def join(k):
        i = order.index(k)
        y_loads[k].wait()
        y_more[k].wait()
        add_to(slots.at[k], y_stage.at[i % 2])
        if i + 2 < 8:
            y_more[order[i + 2]].start()

    def half(ref, which):
        return ref.at[pl.ds(128 * which, 128)]

    def expert_sum():
        join(6)
        join(7)
        up = [net.start(half(slots.at[6 + j], 0), half(hop_in.at[j], 0), way["up"]) for j in range(2)]
        down = [net.start(half(slots.at[6 + j], 1), half(hop_in.at[j], 1), way["down"]) for j in range(2)]
        yield
        for k in (3, 5, 2, 4):
            join(k)
        up[1].wait_recv()
        down[1].wait_recv()
        add_to(half(slots.at[5], 0), half(hop_in.at[1], 0))
        add_to(half(slots.at[3], 1), half(hop_in.at[1], 1))
        beside = [
            net.start(slots.at[5], hop_in.at[2], way["up"]), net.start(slots.at[3], hop_in.at[3], way["down"])
        ]
        up[0].wait_recv()
        down[0].wait_recv()
        add_to(half(slots.at[4], 0), half(hop_in.at[0], 0))
        add_to(half(slots.at[2], 1), half(hop_in.at[0], 1))
        own = [
            net.start(slots.at[4], hop_in.at[4], way["up"]), net.start(slots.at[2], hop_in.at[5], way["down"])
        ]
        yield
        join(1)
        join(0)
        for copy in beside:
            copy.wait_recv()
        add_to(slots.at[1], hop_in.at[2], hop_in.at[3])
        own.append(net.start(slots.at[1], hop_in.at[6], way["across"]))
        yield
        for copy in own:
            copy.wait_recv()
        layer_ref[...] = (
            after_ref[...]
            + slots[0].astype(f32)
            + hop_in[4].astype(f32)
            + hop_in[5].astype(f32)
            + hop_in[6].astype(f32)
        ).astype(bf16)

    def expert_grads():
        for copy in e_loads:
            copy.wait()
        for pair in (1, 0):
            if pair == 0:
                for copy in far_sent:
                    copy.wait_recv()
            add_to(chunks.at[0, pair, 1], far_in.at[pair, 1])
            add_to(chunks.at[1, pair, 0], far_in.at[pair, 0])
        beside = [
            net.start(chunks.at[0, 1], chunk_in.at[0], ring["down"]),
            net.start(chunks.at[1, 1], chunk_in.at[1], ring["up"]),
        ]
        yield
        own = [
            net.start(chunks.at[0, 0], chunk_in.at[2], ring["down"]),
            net.start(chunks.at[1, 0], chunk_in.at[3], ring["up"]),
        ]
        for copy in beside:
            copy.wait_recv()
        add_to(chunks.at[2, 1], chunk_in.at[0], chunk_in.at[1])
        own.append(net.start(chunks.at[2, 1], chunk_in.at[4], ring["across"]))
        yield
        for copy in own:
            copy.wait_recv()
        result = chunks[2, 0].astype(f32)
        for i in range(2, 5):
            result = result + chunk_in[i].astype(f32)
        up_out[...] = result[:, :, 0 : 2 * F]
        down_out[...] = result[:, :, 2 * F : 3 * F]

    moves = expert_sum()
    more_moves = expert_grads()
    next(moves)
    ones_high = jnp.where((lanes >= 64) & (lanes < 67), 1.0, 0.0)
    ones_low = jnp.where(lanes < 3, 1.0, 0.0)
    for c in range(8):
        rows = slice(TOKENS * c, TOKENS * (c + 1))
        pair = heads_ref[c, :, 128:256].astype(f32)
        swapped = pltpu.roll(pair, 64, 1)
        key0[rows, :] = jnp.where(low_half, pair, ones_high).astype(bf16)
        key1[rows, :] = jnp.where(low_half, ones_low, swapped).astype(bf16)
        value0[rows, :] = jnp.where(low_half, swapped, ones_high).astype(bf16)
        value1[rows, :] = jnp.where(low_half, ones_low, pair).astype(bf16)
        key_t[:, rows] = jnp.transpose(pair)[0:64, :].astype(bf16)
    dk_total[...] = jnp.zeros_like(dk_total)
    dv_total[...] = jnp.zeros_like(dv_total)
    columns = pl.ds(pl.multiple_of(me * 128, 128), 128)

    def answer(i):
        j = lax.rem(me + i, 8)
        return pltpu.make_async_remote_copy(
            src_ref=grads.at[j], dst_ref=back_q.at[:, columns], send_sem=send_sems.at[96 + i],
            recv_sem=recv_sems.at[96 + i], device_id={"seq": j}, device_id_type=MESH,
        )

    def block(i, carry):
        j = lax.rem(me + i, 8)

        @pl.when(i > 0)
        def _():
            delivery(8 - i).wait_recv()

        rows = pl.ds(pl.multiple_of(j * TOKENS, TOKENS), TOKENS)
        query = heads_ref[j, :, 0:128].astype(f32) * (1.0 / 8.0)
        grad = grads[j].astype(f32)
        logs = logs_ref[rows, :]
        product = grad * full_ref[rows, :]
        delta0 = jnp.sum(jnp.where(low_half, product, 0.0), axis=1, keepdims=True)
        delta1 = jnp.sum(jnp.where(low_half, 0.0, product), axis=1, keepdims=True)
        query0 = jnp.where(low_half, query, with_terms(lanes, 64, split3(-logs[:, 0:1]))).astype(bf16)
        query1 = jnp.where(low_half, with_terms(lanes, 0, split3(-logs[:, 64:65])), query).astype(bf16)
        grad0 = jnp.where(low_half, grad, with_terms(lanes, 64, split3(-delta0))).astype(bf16)
        grad1 = jnp.where(low_half, with_terms(lanes, 0, split3(-delta1)), grad).astype(bf16)
        only_query = (
            jnp.where(low_half, query, 0.0).astype(bf16), jnp.where(low_half, 0.0, query).astype(bf16)
        )
        only_grad = (jnp.where(low_half, grad, 0.0).astype(bf16), jnp.where(low_half, 0.0, grad).astype(bf16))
        dq = [jnp.zeros((64, TOKENS), f32), jnp.zeros((64, TOKENS), f32)]
        for c in range(4):
            part = pl.ds(c * 512, 512)
            dv = dv_total[part, :]
            dk = dk_total[part, :]
            for h, (key, value, query_h, grad_h) in enumerate(
                ((key0, value0, query0, grad0), (key1, value1, query1, grad1))
            ):
                probs = jnp.exp(dot_t(key[part, :], query_h))
                inner = dot_t(value[part, :], grad_h)
                dv = dv + dot(probs.astype(bf16), only_grad[h])
                scores = (probs * inner).astype(bf16)
                dk = dk + dot(scores, only_query[h])
                dq[h] = dq[h] + dot(key_t[:, c * 512 : (c + 1) * 512], scores)
            dv_total[part, :] = dv
            dk_total[part, :] = dk
        both = jnp.concatenate(dq, axis=0) * (1.0 / 8.0)
        grads[j] = jnp.transpose(both).astype(bf16)

        @pl.when(i > 0)
        def _():
            answer(i).start()

        return carry

    lax.fori_loop(0, 2, block, 0)
    next(more_moves)
    lax.fori_loop(2, 3, block, 0)
    next(moves)
    lax.fori_loop(3, 6, block, 0)
    next(moves)
    lax.fori_loop(6, 8, block, 0)
    for d in range(1, 8):
        delivery(d).wait_send()
    for c in range(8):
        rows = slice(TOKENS * c, TOKENS * (c + 1))
        dk = dk_total[rows, :]
        dv = dv_total[rows, :]
        dk = dk + pltpu.roll(dk, 64, 1)
        dv = dv + pltpu.roll(dv, 64, 1)
        send[c] = jnp.where(low_half, dk, dv).astype(bf16)
    to_tokens = [net.start(send.at[peer], back_kv.at[me], {"seq": peer}) for peer in peers]
    raw = [
        pltpu.make_async_copy(raw_ref.at[h], there.at[pl.ds(TOKENS * (h % 8), TOKENS)], local_sems.at[28 + h])
        for h, there in [(h, dk_total) for h in range(8)] + [(h, dv_total) for h in range(8, 12)]
    ]
    for copy in raw:
        copy.start()
    back_kv[me] = send[me]
    back_q[:, columns] = grads[me]
    x = x_ref[...].astype(f32)
    x_scaling = row_scale(x)
    attn_gain = small_t_ref[32:33, :].astype(f32)
    normed = (x * x_scaling * attn_gain).astype(bf16)
    query_gain, key_gain = gain_tiles(small_t_ref[...], lanes)
    cos, sin = rotary(near_ref, far_place_ref, me, lanes)
    for i in range(1, 8):
        answer(i).wait_recv()

    def unturned(grad, tile, gain):
        grad = grad * cos - partner(grad, lanes) * sin
        scale = lax.rsqrt(head_mean(tile * tile, low_half) + epsilon)
        weighted = grad * gain
        middle = head_mean(weighted * tile, low_half)
        result = scale * weighted - tile * (scale * scale * scale * middle)
        return result.astype(bf16), jnp.sum(grad * tile * scale, axis=0, keepdims=True)

    for copy in raw:
        copy.wait()
    core = here.core
    f = here.z * 2 + here.xh

    def f_at(ring, pair):
        return lax.rem(here.z + ring + 4, 4) * 2 + (1 - here.xh if pair else here.xh)

    def plane(part, hop, way):
        def half(ref, which):
            return ref.at[pl.ds(4 * which, 4)]

        up = [net.start(half(part(2, j), 0), half(hop.at[j], 0), way["up"]) for j in (1, 0)]
        down = [net.start(half(part(2, j), 1), half(hop.at[j], 1), way["down"]) for j in (1, 0)]
        yield
        on = []
        for i, j in enumerate((1, 0)):
            up[i].wait_recv()
            add_to(half(part(1, j), 0), half(hop.at[j], 0))
            on.append(net.start(part(1, j), hop.at[2 + 2 * i], way["up"]))
            down[i].wait_recv()
            add_to(half(part(-1, j), 1), half(hop.at[j], 1))
            on.append(net.start(part(-1, j), hop.at[3 + 2 * i], way["down"]))
        yield
        on[0].wait_recv()
        on[1].wait_recv()
        add_to(part(0, 1), hop.at[2], hop.at[3])
        across = net.start(part(0, 1), hop.at[6], way["across"])
        yield
        on[2].wait_recv()
        on[3].wait_recv()
        across.wait_recv()
        add_to(part(0, 0), hop.at[4], hop.at[5], hop.at[6])

    def columns_of(group):
        return pl.ds(512 * group, 512)

    def by_seq(ring, pair):
        return parts.at[core, here.seq_at(ring, pair), :, :, columns_of(0)]

    def by_fsdp(group):
        return lambda ring, pair: parts.at[core, :, f_at(ring, pair), :, columns_of(group)]

    def joined(copy, group):
        copy.wait_recv()
        there = slice(512 * group, 512 * (group + 1))
        for q in range(8):
            parts[core, q, :, :, there] = (
                parts[core, q, :, :, there].astype(f32) + parts_in[q, :, :, there].astype(f32)
            ).astype(bf16)

    planes = [
        plane(by_seq, hops.at[0], here.plane("seq")),
        plane(by_fsdp(1), hops.at[1], way),
        plane(by_fsdp(2), hops.at[2], way),
    ]
    joined(out_join, 2)
    next(planes[2])
    next(more_moves)
    query_terms = jnp.zeros((1, 128), f32)
    for h in range(8):
        part = slice(128 * h, 128 * (h + 1))
        pg[0, :, part], terms = unturned(back_q[:, part].astype(f32), dk_total[TOKENS * h : TOKENS * (h + 1), :], query_gain)
        query_terms = query_terms + terms
    sib_joins = []

    def weight_part(i):
        columns = pl.ds(512 * i, 512)
        for r in range(4):
            result = t_dot(normed[:, 256 * r : 256 * (r + 1)], pg[i]).astype(bf16).reshape(2, 8, 16, 1024)
            for h in range(2):
                parts[h, 2 * r : 2 * r + 2, :, :, 512 * i : 512 * (i + 1)] = result[:, :, :, 512 * h : 512 * (h + 1)]
        sib_joins.append(
            net.start(parts.at[1 - core, :, :, :, columns], parts_in.at[:, :, :, columns], sib)
        )

    weight_part(0)
    for copy in to_tokens:
        copy.wait_recv()
    key_terms = jnp.zeros((1, 128), f32)
    for j in range(4):
        first, second = back_kv[2 * j].astype(f32), back_kv[2 * j + 1].astype(f32)
        keys = jnp.where(low_half, first, pltpu.roll(second, 64, 1))
        values = jnp.where(low_half, pltpu.roll(first, 64, 1), second)
        part = slice(128 * j, 128 * (j + 1))
        pg[1, :, part], terms = unturned(keys, dv_total[TOKENS * j : TOKENS * (j + 1), :], key_gain)
        key_terms = key_terms + terms
        pg[1, :, 512 + 128 * j : 640 + 128 * j] = values.astype(bf16)

    weight_part(1)
    next(planes[2])
    joined(sib_joins[0], 0)
    next(planes[0])
    joined(sib_joins[1], 1)
    next(planes[1])
    next(planes[2])
    for copy in loads[2:4]:
        copy.wait()
    normed_grad = dot_t(pg[0], wqkv[0]) + dot_t(pg[1], wqkv[1])
    attn_gain_grad = jnp.sum(normed_grad * x * x_scaling, axis=0, keepdims=True)
    query_terms = query_terms + pltpu.roll(query_terms, 64, 1)
    key_terms = key_terms + pltpu.roll(key_terms, 64, 1)
    head_terms = jnp.where(low_half, query_terms, key_terms)
    spread = (
        8 * lax.broadcasted_iota(jnp.int32, (128, D), 0) == lax.broadcasted_iota(jnp.int32, (128, D), 1)
    ).astype(f32).astype(bf16)
    head_row = jnp.zeros((1, D), f32)
    for term in split3(head_terms):
        head_row = head_row + dot(jnp.broadcast_to(term, (16, 128)).astype(bf16), spread)[0:1, :]
    row = lax.broadcasted_iota(jnp.int32, (128, D), 0)
    gain_rows = jnp.where(
        row == 32, attn_gain_grad, jnp.where(row == 33, ffn_gain, jnp.where(row == 34, head_row, 0.0))
    )
    small[...] = small[...] + jnp.transpose(gain_rows).reshape(8, 8, 2, 8, 128)
    small_join = net.start(small.at[:, :, 1 - core], small_in, sib)
    next(planes[0])
    next(planes[1])
    next(planes[2], None)
    weighted = normed_grad * attn_gain
    middle = jnp.mean(weighted * x, axis=1, keepdims=True)
    token_ref[...] = after_grad[...] + x_scaling * weighted - x * (x_scaling * x_scaling * x_scaling * middle)
    small_join.wait_recv()
    small_in[...] = small_in[...] + small[:, :, core]
    small_copies = [
        net.start(small_in.at[peers[i]], small_s.at[i], seq_peers[i]) for i in range(7)
    ]
    next(planes[0])
    next(planes[1])
    for _ in moves:
        pass
    for _ in more_moves:
        pass
    for copy in small_copies:
        copy.wait_recv()
    mine = small_in[me]
    for i in range(7):
        mine = mine + small_s[i]
    small_in[me] = mine
    small_copies = [
        net.start(small_in.at[me, f_at(*OTHERS[i])], small_f.at[i], fsdp_peers[i]) for i in range(7)
    ]
    def last_exchange(group):
        return [
            net.start(parts.at[core, me, f_at(*OTHERS[i]), :, columns_of(0)], late.at[0, i], fsdp_peers[i])
            if group == 0
            else net.start(parts.at[core, peers[i], f, :, columns_of(group)], late.at[group, i], seq_peers[i])
            for i in range(7)
        ]

    late_copies = {2: last_exchange(2)}
    next(planes[0], None)
    late_copies[0] = last_exchange(0)
    next(planes[1], None)
    late_copies[1] = last_exchange(1)
    for copy in small_copies:
        copy.wait_recv()
    mine = small_in[me, f]
    for i in range(7):
        mine = mine + small_f[i]
    small_out[...] = mine
    for group in (2, 0, 1):
        for copy in late_copies[group]:
            copy.wait_recv()
        cols = slice(512 * group, 512 * (group + 1))
        result = parts[core, me, f, :, cols].astype(f32)
        for i in range(7):
            result = result + late[group, i].astype(f32)
        total[:, cols] = result
    last = net.start(total.at[pl.ds(pl.multiple_of(8 * (1 - core), 8), 8)], total_in, sib)
    mine = total[pl.ds(pl.multiple_of(8 * core, 8), 8), :]
    last.wait_recv()
    theirs = total_in[...]
    is_low = core == 0
    left, right = jnp.where(is_low, mine, theirs), jnp.where(is_low, theirs, mine)
    for i in range(2):
        qkv_out[:, 1024 * i : 1024 * i + 512] = left[:, 512 * i : 512 * (i + 1)]
        qkv_out[:, 1024 * i + 512 : 1024 * (i + 1)] = right[:, 512 * i : 512 * (i + 1)]
    wo_out[:, 0:512] = left[:, 1024:1536]
    wo_out[:, 512:1024] = right[:, 1024:1536]
    for i in range(1, 8):
        answer(i).wait_send()
    net.finish()


def back(*operands):
    vmem = pl.BlockSpec(memory_space=pltpu.VMEM)
    hbm = pl.BlockSpec(memory_space=pl.ANY)
    return pl.pallas_call(
        back_kernel,
        in_specs=[vmem] * 13 + [hbm] * 7,
        out_specs=[vmem] * 7,
        out_shape=[
            jax.ShapeDtypeStruct((TOKENS, D), bf16),
            jax.ShapeDtypeStruct((TOKENS, D), f32),
            jax.ShapeDtypeStruct((8, 2048), f32),
            jax.ShapeDtypeStruct((8, 1024), f32),
            jax.ShapeDtypeStruct((8, 128), f32),
            jax.ShapeDtypeStruct((2, 128, 2 * F), f32),
            jax.ShapeDtypeStruct((2, 128, F), f32),
        ],
        scratch_shapes=[
            pltpu.VMEM((2, D, 1024), bf16),
            pltpu.VMEM((2, D, 512), bf16),
            pltpu.VMEM((8, TOKENS, 128), bf16),
            pltpu.VMEM((8, TOKENS, 128), bf16),
            pltpu.VMEM((TOKENS, D), bf16),
            pltpu.VMEM((8, TOKENS, 128), bf16),
            pltpu.VMEM((2, TOKENS, D), bf16),
            pltpu.VMEM((TOKENS, D), f32),
        ]
        + [pltpu.VMEM((LENGTH, 128), bf16)] * 4
        + [pltpu.VMEM((64, LENGTH), bf16)]
        + [pltpu.VMEM((LENGTH, 128), f32)] * 2
        + [pltpu.VMEM((8, TOKENS, D), bf16), pltpu.VMEM((2, TOKENS, D), bf16)]
        + [pltpu.VMEM((7, TOKENS, D), bf16)]
        + [
            pltpu.VMEM((2, 8, 8, 16, GCOLS), bf16),
            pltpu.VMEM((8, 8, 16, GCOLS), bf16),
            pltpu.VMEM((8, 8, 2, 8, 128), f32),
            pltpu.VMEM((8, 8, 8, 128), f32),
            pltpu.VMEM((3, 7, 8, 16, 512), bf16),
            pltpu.VMEM((3, 7, 16, 512), bf16),
            pltpu.VMEM((7, 8, 8, 128), f32),
            pltpu.VMEM((7, 8, 128), f32),
            pltpu.VMEM((16, GCOLS), f32),
            pltpu.VMEM((8, GCOLS), f32),
            pltpu.VMEM((3, 2, 2, 128, 3 * F), bf16),
            pltpu.VMEM((2, 2, 128, 3 * F), bf16),
            pltpu.VMEM((5, 2, 128, 3 * F), bf16),
            pltpu.SemaphoreType.DMA((40,)),
            pltpu.SemaphoreType.DMA((112,)),
            pltpu.SemaphoreType.DMA((112,)),
        ],
        compiler_params=pltpu.CompilerParams(collective_id=5, has_side_effects=True, vmem_limit_bytes=63 * 1024 * 1024),
        cost_estimate=pl.CostEstimate(
            flops=9 * 10**9, bytes_accessed=32 << 20, transcendentals=2 * LENGTH * LENGTH
        ),
        name="back",
    )(*operands)


def finish_kernel(layer, token, up, down, qkv, wo, small, *outs):
    for src, dst in zip((layer, token, up, down, qkv, wo), outs):
        dst[...] = src[...]
    router, attn, ffn, head = outs[6:]
    same = lax.broadcasted_iota(jnp.int32, (8, 8), 0) == lax.broadcasted_iota(jnp.int32, (8, 8), 1)
    values = small[...]
    router[...] = values[:, 0:EXPERTS]
    for ref, lane in ((attn, EXPERTS), (ffn, EXPERTS + 1)):
        ref[...] = jnp.sum(jnp.where(same, values[:, lane : lane + 1], 0.0), axis=0, keepdims=True)
    head[...] = values[0:1, EXPERTS + 2 : EXPERTS + 3]


def finish(*operands):
    vmem = pl.BlockSpec(memory_space=pltpu.VMEM)
    small = [(8, EXPERTS), (1, 8), (1, 8), (1, 1)]
    return pl.pallas_call(
        finish_kernel,
        in_specs=[vmem] * 7,
        out_specs=[vmem] * 10,
        out_shape=[jax.ShapeDtypeStruct(a.shape, a.dtype) for a in operands[:6]]
        + [jax.ShapeDtypeStruct(shape, f32) for shape in small],
        compiler_params=pltpu.CompilerParams(vmem_limit_bytes=VMEM),
        name="finish",
    )(*operands)


def gather_kernel(
    qkv_ref, wo_ref, router_ref, attn_ref, ffn_ref, head_ref, routes_ref, cot_ref, out_ref, masks_out, side_out,
    in_ref, mask_ref, stage, block, local_sems, send_sems, recv_sems,
):
    lanes = lax.broadcasted_iota(jnp.int32, (1, 128), 1)
    same = lax.broadcasted_iota(jnp.int32, (8, 8), 0) == lax.broadcasted_iota(jnp.int32, (8, 8), 1)

    def column(row):
        return jnp.sum(jnp.where(same, row[...].astype(f32), 0.0), axis=1, keepdims=True)

    gains = jnp.where(
        lanes == 32,
        column(attn_ref),
        jnp.where(lanes == 33, column(ffn_ref), jnp.where(lanes == 34, head_ref[...].astype(f32), 0.0)),
    )
    for h in range(2):
        in_ref[h, :, 0:1024] = qkv_ref[:, 1024 * h : 1024 * (h + 1)].astype(f32)
        in_ref[h, :, 1024:1536] = wo_ref[:, 512 * h : 512 * (h + 1)].astype(f32)
        in_ref[h, :, 1536:1664] = gains
        in_ref[h, :, 1536:1568] = router_ref[...].astype(f32)
    expert = lax.broadcasted_iota(jnp.int32, (32, 256), 0)
    named = jnp.zeros((32, 256), f32)
    for k in range(8):
        named = jnp.where(routes_ref[k : k + 1, :] == expert, 1.0, named)
    mask_ref[...] = named.astype(bf16)
    here = Place()
    c, s, f = here.core, here.seq, here.z * 2 + here.xh
    sib = here.sibling()
    ways = {"seq": here.plane("seq"), "fsdp": here.plane("fsdp")}
    others = [(2, 1), (2, 0), (0, 1), (1, 1), (-1, 1), (1, 0), (-1, 0)]

    def f_at(ring, pair):
        return lax.rem(here.z + ring + 4, 4) * 2 + (1 - here.xh if pair else here.xh)

    seq_peers = [{"seq": here.seq_at(ring, pair)} for ring, pair in others]
    fsdp_peers = [{"fsdp": here.fsdp_at(ring, pair)} for ring, pair in others]
    meet([sib, *seq_peers, *fsdp_peers])
    net = Copies(send_sems, recv_sems)
    rows = pl.ds(pl.multiple_of(8 * c, 8), 8)
    join = net.start(in_ref.at[1 - c], stage.at[rows], sib)
    stage[rows, :] = in_ref[c]
    join.wait_recv()
    block[...] = stage[...].astype(bf16)
    low, high = pl.ds(0, 896), pl.ds(896, 768)
    locals_ = [
        pltpu.make_async_copy(block, out_ref.at[c, s, f], local_sems.at[0]),
        pltpu.make_async_copy(mask_ref, masks_out.at[here.fsdp], local_sems.at[1]),
    ]
    for copy in locals_:
        copy.start()
    a = [net.start(block.at[:, low], out_ref.at[c, s, f, :, low], peer) for peer in fsdp_peers]
    b = [net.start(block.at[:, high], out_ref.at[c, s, f, :, high], peer) for peer in seq_peers]
    m = [net.start(mask_ref, masks_out.at[here.fsdp], peer) for peer in [sib, *fsdp_peers]]
    for copy in locals_:
        copy.wait()
    kin = []

    def plane(part, way):
        def half(ref, which):
            return ref.at[pl.ds(4 * which, 4)]

        def go(ref, target):
            return net.start(ref, ref, target)

        ref = part(0, 0)
        across, up, down = go(ref, way["across"]), go(ref, way["up"]), go(ref, way["down"])
        kin.append(go(ref, sib))
        yield
        up.wait_recv()
        ref = part(-1, 0)
        far_low = go(half(ref, 0), way["up"])
        kin.append(go(ref, sib))
        down.wait_recv()
        ref = part(1, 0)
        far_high = go(half(ref, 1), way["down"])
        kin.append(go(ref, sib))
        yield
        across.wait_recv()
        ref = part(0, 1)
        up, down = go(ref, way["up"]), go(ref, way["down"])
        kin.append(go(ref, sib))
        yield
        far_low.wait_recv()
        far_high.wait_recv()
        kin.append(go(part(2, 0), sib))
        up.wait_recv()
        ref = part(-1, 1)
        far_low = go(half(ref, 0), way["up"])
        kin.append(go(ref, sib))
        down.wait_recv()
        ref = part(1, 1)
        far_high = go(half(ref, 1), way["down"])
        kin.append(go(ref, sib))
        yield
        far_low.wait_recv()
        far_high.wait_recv()
        kin.append(go(part(2, 1), sib))

    for copy in a:
        copy.wait_recv()
    first = plane(lambda ring, pair: out_ref.at[c, here.seq_at(ring, pair), :, :, low], ways["seq"])
    next(first)
    for copy in b:
        copy.wait_recv()
    second = plane(lambda ring, pair: out_ref.at[c, :, f_at(ring, pair), :, high], ways["fsdp"])
    next(second)
    for i in range(8):
        m[i].wait_recv()
        if i:
            ring, pair = others[i - 1]
            ref = masks_out.at[here.fsdp_at(-ring, pair)]
            kin.append(net.start(ref, ref, sib))
    for turn in range(4):
        next(first, None)
        next(second, None)
        if turn == 1:
            kin.append(net.start(cot_ref, side_out, ways["fsdp"]["across"]))
    for copy in kin:
        copy.wait_recv()
    net.finish()


def gather_weights(*operands):
    n = 65
    return pl.pallas_call(
        gather_kernel,
        in_specs=[pl.BlockSpec(memory_space=pltpu.VMEM)] * 7 + [pl.BlockSpec(memory_space=pl.ANY)],
        out_specs=[pl.BlockSpec(memory_space=pl.ANY)] * 3,
        out_shape=[
            jax.ShapeDtypeStruct((2, 8, 8, 16, WCOLS), bf16),
            jax.ShapeDtypeStruct((16, 32, 256), bf16),
            jax.ShapeDtypeStruct((256, 1024), bf16),
        ],
        scratch_shapes=[
            pltpu.VMEM((2, 8, WCOLS), f32),
            pltpu.VMEM((32, 256), bf16),
            pltpu.VMEM((16, WCOLS), f32),
            pltpu.VMEM((16, WCOLS), bf16),
            pltpu.SemaphoreType.DMA((2,)),
            pltpu.SemaphoreType.DMA((n,)),
            pltpu.SemaphoreType.DMA((n,)),
        ],
        compiler_params=pltpu.CompilerParams(collective_id=1, has_side_effects=True, vmem_limit_bytes=VMEM),
        name="gather_weights",
    )(*operands)


def moe_kernel(
    x_ref, cot_ref, side_ref, g_ref, masks_ref, gates_ref, up_hbm, down_hbm,
    row_out, gate_out, y_out, y_in, grads_out, far_out,
    slots, spare, gates_in, grads_stage, grads_in, sib_in, hop_in, g_rows, up_ref, down_ref,
    rows_x, rows_p, rows_h, rows_u, rows_g, slot_gate, places, ranks, stage_y, stage_r, stage,
    local_sems, send_sems, recv_sems,
):
    here = Place()
    sib = here.sibling()
    way = here.plane("fsdp")
    own = here.fsdp
    counter = [0]

    def local(src, dst):
        copy = pltpu.make_async_copy(src, dst, local_sems.at[counter[0]])
        counter[0] += 1
        copy.start()
        return copy

    first_x = local(x_ref, slots.at[0])
    weights = [local(up_hbm, up_ref), local(down_hbm, down_ref)]

    def source(k):
        ring, pair, c = (0, -1, 1, 2)[k // 4], (k // 2) % 2, k % 2
        z = lax.rem(here.z + ring + 4, 4)
        xh = 1 - here.xh if pair else here.xh
        return z * 4 + xh * 2 + (1 - here.core if c else here.core)

    groups = ((0, 1), (4, 5, 8, 9), (6, 7, 10, 11), (12, 13, 14, 15), (2, 3))
    starts = [SLOTS * sum(len(g) for g in groups[:i]) for i in range(5)]

    def fetch_g(group):
        near = {0: cot_ref, 2: side_ref}
        return [
            local(near[k] if k in near else g_ref.at[source(k)], g_rows.at[s])
            for s, k in enumerate(groups[group])
        ]

    g_copies = fetch_g(0)
    ring = here.plane("seq")
    others = [{"fsdp": source(k)} for k in range(1, 16)]
    meet([*others, ring["up"], ring["down"]])
    net = Copies(send_sems, recv_sems)

    def block(k, low=0, rows=TOKENS):
        return slots.at[k, pl.ds(low, rows)]

    sent = {k: [] for k in range(16)}

    def push(k, to, target, low=0, rows=TOKENS, src=None):
        copy = net.start(block(k, low, rows) if src is None else src, block(to, low, rows), target)
        sent[k].append(copy)
        return copy

    small = [net.start(gates_ref.at[source(k)], gates_in.at[own], others[k - 1]) for k in range(1, 16)]
    gates_in[own] = gates_ref[own]
    across = push(0, 2, way["across"], src=x_ref)
    up = push(0, 4, way["up"], src=x_ref)
    down = push(0, 8, way["down"], src=x_ref)
    kin = {1: push(0, 1, sib, src=x_ref)}
    expert = lax.broadcasted_iota(jnp.int32, (EXPERTS, TOKENS), 0)
    for k in range(16):
        named = masks_ref[source(k)].astype(f32)
        for i in range(2):
            ranks[2 * k + i : 2 * k + i + 1, :] = jnp.sum(
                jnp.where(expert == 2 * own + i, named, 0.0), axis=0, keepdims=True
            )
    before = (
        lax.broadcasted_iota(jnp.int32, (TOKENS, TOKENS), 0)
        < lax.broadcasted_iota(jnp.int32, (TOKENS, TOKENS), 1)
    ).astype(f32).astype(bf16)
    second = lax.rem(lax.broadcasted_iota(jnp.int32, (2 * 16, 1), 0), 2).astype(f32)
    named = ranks[...]
    ranks[...] = jnp.where(named > 0.0, dot(named.astype(bf16), before) + SLOTS * second, -1000.0)
    state = {}

    lanes = lax.broadcasted_iota(jnp.int32, (1, 128), 1)
    slot = lax.broadcasted_iota(jnp.int32, (2 * SLOTS, TOKENS), 0)
    slot_place = slot.astype(f32)
    first = slot < SLOTS
    expert = lax.broadcasted_iota(jnp.int32, (EXPERTS, TOKENS), 0)

    def gather(group):
        for s, k in enumerate(groups[group]):
            if k in kin:
                kin[k].wait_recv()
            g_copies[s].wait()
            wanted = jnp.where(first, ranks[2 * k : 2 * k + 1, :], ranks[2 * k + 1 : 2 * k + 2, :])
            hot = jnp.where(slot_place == wanted, 1.0, 0.0)
            gates = gates_in[source(k)]
            gate = jnp.sum(hot * jnp.where(first, gates[0:1, :], gates[1:2, :]), axis=1, keepdims=True)
            hot = hot.astype(bf16)
            places[s] = hot
            picked = dot(hot, slots[k]).astype(bf16)
            grads = dot(hot, g_rows[s])
            pair = (grads * gate).astype(bf16)
            grads = grads.astype(bf16)
            for i in range(2):
                part = slice(SLOTS * i, SLOTS * (i + 1))
                there = slice(starts[group] + SLOTS * s, starts[group] + SLOTS * (s + 1))
                rows_x[i, there, :] = picked[part]
                rows_p[i, there, :] = pair[part]
                rows_g[i, SLOTS * s : SLOTS * (s + 1), :] = grads[part]
                slot_gate[i, SLOTS * s : SLOTS * (s + 1), :] = jnp.broadcast_to(gate[part], (SLOTS, 128))

    def run(group):
        count = SLOTS * len(groups[group])
        here_rows = pl.ds(starts[group], count)

        def one(e, carry):
            x_rows = rows_x[e, here_rows, :]
            gate_part = dot(x_rows, up_ref[e, :, 0:F])
            up_part = dot(x_rows, up_ref[e, :, F : 2 * F])
            sigmoid = 1.0 / (1.0 + jnp.exp(-gate_part))
            silu = gate_part * sigmoid
            hidden = (silu * up_part).astype(bf16)
            rows_h[e, here_rows, :] = hidden
            hidden_grad = dot(rows_p[e, here_rows, :], down_ref[e])
            slope = sigmoid * (1.0 + gate_part * (1.0 - sigmoid))
            rows_u[e, here_rows, 0:F] = (hidden_grad * up_part * slope).astype(bf16)
            rows_u[e, here_rows, F : 2 * F] = (hidden_grad * silu).astype(bf16)
            out = dot_t(hidden, down_ref[e]).astype(bf16).astype(f32)
            gate_grad = jnp.sum(out * rows_g[e, 0:count, :].astype(f32), axis=1, keepdims=True)
            stage_y[e, 0:count, :] = (out * slot_gate[e, 0:count, 0:1]).astype(bf16)
            stage_r[e, 0:count, :] = dot_t(rows_u[e, here_rows, :], up_ref[e]).astype(bf16)
            for s, k in enumerate(groups[group]):
                hot = places[s, pl.ds(pl.multiple_of(SLOTS * e, SLOTS), SLOTS), :].astype(f32)
                grads_stage[k, e, 0:1, :] = jnp.sum(
                    hot * gate_grad[SLOTS * s : SLOTS * (s + 1)], axis=0, keepdims=True
                )
            return carry

        lax.fori_loop(0, 2, one, 0)
        for k in groups[group]:
            if k:
                small.append(net.start(grads_stage.at[k], grads_in.at[own], others[k - 1]))
            else:
                grads_in[own] = grads_stage[0]

    def result(k):
        return spare.at[k // 4 - 1] if k in (4, 8) else slots.at[k]

    y_sent = []

    def free_stage():
        for copy, remote in state.pop("y", ()):
            if remote:
                copy.wait_send()
            else:
                copy.wait()

    def combine(group):
        order = (2, 3, 0, 1) if group == 3 else range(len(groups[group]))
        for s in order:
            k = groups[group][s]
            if k not in (4, 8):
                for copy in sent[k]:
                    copy.wait_send()
            part = slice(SLOTS * s, SLOTS * (s + 1))
            both = jnp.concatenate([stage_r[0, part, :], stage_r[1, part, :]], axis=0)
            result(k)[...] = t_dot(places[s], both).astype(bf16)
            if k % 2:
                state[k - 1] = net.start(slots.at[k], sib_in.at[k // 2], sib)
        free_stage()
        state["y"] = []
        for s, k in enumerate(groups[group]):
            part = slice(SLOTS * s, SLOTS * (s + 1))
            both = jnp.concatenate([stage_y[0, part, :], stage_y[1, part, :]], axis=0)
            stage[s, :, 0:D] = t_dot(places[s], both).astype(bf16)
            ready = stage.at[s, :, pl.ds(0, D)]
            if k % 2:
                y_sent.append(net.start(ready, y_in.at[k // 2], sib))
                state["y"].append((y_sent[-1], True))
            else:
                state["y"].append((local(ready, y_out.at[k // 2]), False))

    def join(k):
        state[k].wait_recv()
        there = result(k)
        there[...] = (there[...].astype(f32) + sib_in[k // 2].astype(f32)).astype(bf16)

    first_x.wait()
    for copy in small:
        copy.wait_recv()
    small.clear()
    gather(0)
    g_copies = fetch_g(1)
    for copy in weights:
        copy.wait()
    run(0)
    up.wait_recv()
    far_low = push(4, 12, way["up"], 0, 128)
    kin[5] = push(4, 5, sib)
    down.wait_recv()
    far_high = push(8, 12, way["down"], 128, 128)
    kin[9] = push(8, 9, sib)
    across.wait_recv()
    up_x = push(2, 6, way["up"])
    down_x = push(2, 10, way["down"])
    kin[3] = push(2, 3, sib)
    combine(0)
    gather(1)
    g_copies = fetch_g(2)
    run(1)
    combine(1)
    far_low.wait_recv()
    far_high.wait_recv()
    far_x = push(12, 14, way["across"])
    kin[13] = push(12, 13, sib)
    up_x.wait_recv()
    kin[7] = push(6, 7, sib)
    down_x.wait_recv()
    kin[11] = push(10, 11, sib)
    gather(2)
    g_copies = fetch_g(3)
    join(4)
    hop_rd = net.start(result(4), hop_in.at[5], way["down"])
    join(8)
    hop_ru = net.start(result(8), hop_in.at[4], way["up"])
    run(2)
    far_x.wait_recv()
    kin[15] = push(14, 15, sib)
    combine(2)
    gather(3)
    g_copies = fetch_g(4)
    join(6)
    hop_xd = net.start(slots.at[6], hop_in.at[2], way["down"])
    join(10)
    hop_xu = net.start(slots.at[10], hop_in.at[3], way["up"])
    run(3)
    combine(3)
    gather(4)
    join(14)

    def quarter(ref, i):
        return ref.at[pl.ds((0, 128, 64, 192)[i], 64)]

    ways = ("up", "down", "up", "down")
    hop_a = [
        net.start(quarter(slots.at[14], i), quarter(hop_in.at[0], i), way["across"]) for i in range(4)
    ]
    join(12)
    join(0)
    run(4)
    combine(4)

    w_copies = []

    far_grads = []

    def send_far(dx):
        for copy in w_copies:
            copy.wait()
        w_copies.clear()
        rows = pl.ds(pl.multiple_of(here.seq_at(2, dx) * 128, 128), 128)
        for e, to in enumerate(("up", "down")):
            far_grads.append(net.start(grads_out.at[e, rows], far_out.at[e], ring[to]))

    def weight_grad(e, dx):
        free_stage()
        for copy in w_copies:
            copy.wait()
        xl = 1 - here.xl if dx else here.xl
        columns = pl.ds(pl.multiple_of(xl * 512, 512), 512)
        for wide, left, right in (
            (slice(0, 2 * F), rows_x, rows_u), (slice(2 * F, 3 * F), rows_p, rows_h)
        ):
            result = t_dot(left[e, :, columns], right[e]).astype(bf16)
            for y in range(4):
                stage[y, 0:128, wide] = result[128 * y : 128 * (y + 1)]
        w_copies[:] = [
            local(
                stage.at[y, pl.ds(0, 128)],
                grads_out.at[e, pl.ds(pl.multiple_of(xl * 512 + 128 * y, 128), 128)],
            )
            for y in range(4)
        ]

    weight_grad(0, 1)
    join(2)
    hop_xd.wait_recv()
    hop_xu.wait_recv()
    slots[2] = (slots[2].astype(f32) + hop_in[2].astype(f32) + hop_in[3].astype(f32)).astype(bf16)
    hop_rx = net.start(slots.at[2], hop_in.at[6], way["across"])
    far = []
    for i in range(4):
        hop_a[i].wait_recv()
        ref, other = quarter(slots.at[12], i), quarter(hop_in.at[0], i)
        ref[...] = (ref[...].astype(f32) + other[...].astype(f32)).astype(bf16)
        far.append(net.start(ref, quarter(hop_in.at[1], i), way[ways[i]]))
    weight_grad(1, 1)
    send_far(1)
    relay = []
    for i in range(4):
        far[i].wait_recv()
        relay.append(net.start(quarter(hop_in.at[1], i), quarter(hop_in.at[7], i), way[ways[i]]))
    weight_grad(0, 0)
    weight_grad(1, 0)
    for copy in w_copies:
        copy.wait()
    for copy in (hop_ru, hop_rd, hop_rx, *relay, *far_grads, *y_sent, *small):
        copy.wait_recv()
    total = (
        slots[0].astype(f32)
        + hop_in[4].astype(f32)
        + hop_in[5].astype(f32)
        + hop_in[6].astype(f32)
        + hop_in[7].astype(f32)
    )
    row_out[...] = total
    row = lax.broadcasted_iota(jnp.int32, (128, TOKENS), 0)
    gate_grads = jnp.zeros((128, TOKENS), f32)
    for f in range(16):
        for e in range(2):
            gate_grads = jnp.where(row == 2 * f + e, grads_in[f, e, 0:1, :], gate_grads)
    gate_out[...] = jnp.transpose(gate_grads)
    waited = {id(copy) for copies in (*(sent[k] for k in sent if k not in (4, 8)), y_sent) for copy in copies}
    for copy in net.all:
        if id(copy) not in waited:
            copy.wait_send()


def moe(x, cot, side, g_all, masks, gates, up, down):
    any_space = pl.BlockSpec(memory_space=pl.ANY)
    vmem = pl.BlockSpec(memory_space=pltpu.VMEM)
    return pl.pallas_call(
        moe_kernel,
        in_specs=[any_space] * 4 + [vmem, vmem, any_space, any_space],
        out_specs=[vmem, vmem, any_space, any_space, any_space, any_space],
        out_shape=[
            jax.ShapeDtypeStruct((TOKENS, D), f32),
            jax.ShapeDtypeStruct((TOKENS, 128), f32),
            jax.ShapeDtypeStruct((8, TOKENS, D), bf16),
            jax.ShapeDtypeStruct((8, TOKENS, D), bf16),
            jax.ShapeDtypeStruct((2, D, 3 * F), bf16),
            jax.ShapeDtypeStruct((2, 128, 3 * F), bf16),
        ],
        scratch_shapes=[
            pltpu.VMEM((16, TOKENS, D), bf16),
            pltpu.VMEM((2, TOKENS, D), bf16),
            pltpu.VMEM((16, 8, TOKENS), f32),
            pltpu.VMEM((16, 2, 8, TOKENS), f32),
            pltpu.VMEM((16, 2, 8, TOKENS), f32),
            pltpu.VMEM((8, TOKENS, D), bf16),
            pltpu.VMEM((8, TOKENS, D), bf16),
            pltpu.VMEM((4, TOKENS, D), bf16),
            pltpu.VMEM((2, D, 2 * F), bf16),
            pltpu.VMEM((2, D, F), bf16),
            pltpu.VMEM((2, ROWS, D), bf16),
            pltpu.VMEM((2, ROWS, D), bf16),
            pltpu.VMEM((2, ROWS, F), bf16),
            pltpu.VMEM((2, ROWS, 2 * F), bf16),
            pltpu.VMEM((2, GROUP_ROWS, D), bf16),
            pltpu.VMEM((2, GROUP_ROWS, 128), f32),
            pltpu.VMEM((4, 2 * SLOTS, TOKENS), bf16),
            pltpu.VMEM((2 * 16, TOKENS), f32),
            pltpu.VMEM((2, GROUP_ROWS, D), bf16),
            pltpu.VMEM((2, GROUP_ROWS, D), bf16),
            pltpu.VMEM((4, TOKENS, 3 * F), bf16),
            pltpu.SemaphoreType.DMA((56,)),
            pltpu.SemaphoreType.DMA((96,)),
            pltpu.SemaphoreType.DMA((96,)),
        ],
        compiler_params=pltpu.CompilerParams(
            collective_id=4, has_side_effects=True, vmem_limit_bytes=63 * 1024 * 1024
        ),
        cost_estimate=pl.CostEstimate(flops=32 * 10**9, bytes_accessed=40 << 20, transcendentals=1 << 21),
        name="moe",
    )(x, cot, side, g_all, masks, gates, up, down)


def on_device(
    tokens, attn_gain, qkv_weight, qk_gain, out_weight, ffn_gain, router_weight,
    gate_up_weight, down_weight, routes, cotangent,
):
    x = tokens.reshape(TOKENS, D)
    cot = cotangent.reshape(TOKENS, D)
    route_ids = routes.reshape(TOKENS, TOPK).T
    whole, masks, side = gather_weights(
        qkv_weight, out_weight, router_weight, attn_gain.reshape(1, 8), ffn_gain.reshape(1, 8),
        qk_gain.reshape(1, 1), route_ids, cot,
    )
    whole = whole.reshape(2, D, WCOLS)

    near, far_place = rotary_tables()
    heads, g_all, full, logs, attended, after, normed_ffn, gates, small_t, raw, gates_t = front(
        x, whole, route_ids, near, far_place, cot, side
    )
    row_sum, gate_sum, y_own, y_other, expert_grads, far = moe(
        normed_ffn, cot, side, g_all, masks, gates_t, gate_up_weight, down_weight
    )
    layer_out, token_grad, qkv_part, out_part, small, up_part, down_part = back(
        gate_sum, gates, after, x, cot, attended, normed_ffn, small_t, heads, full, logs, near, far_place,
        row_sum, raw, whole, y_own, y_other, expert_grads, far,
    )
    layer_out, token_grad, up_part, down_part, qkv_part, out_part, router_part, attn_part, ffn_part, head_part = finish(
        layer_out, token_grad, up_part, down_part, qkv_part, out_part, small
    )
    return (
        layer_out.reshape(1, TOKENS, D),
        token_grad.reshape(1, TOKENS, D),
        attn_part.reshape(8),
        qkv_part,
        head_part.reshape(1),
        out_part,
        ffn_part.reshape(8),
        router_part,
        up_part,
        down_part,
    )


def solution(mesh):
    return jax.shard_map(
        on_device,
        mesh=mesh,
        in_specs=(
            P("fsdp", "seq", None),
            P(("seq", "fsdp")),
            P(("seq", "fsdp"), None),
            P(("seq", "fsdp")),
            P(("seq", "fsdp"), None),
            P(("seq", "fsdp")),
            P(("seq", "fsdp"), None),
            P("fsdp", None, None),
            P("fsdp", None, None),
            P("fsdp", "seq", None),
            P("fsdp", "seq", None),
        ),
        out_specs=(
            P("fsdp", "seq", None),
            P("fsdp", "seq", None),
            P(("seq", "fsdp")),
            P(("seq", "fsdp"), None),
            P(("seq", "fsdp")),
            P(("seq", "fsdp"), None),
            P(("seq", "fsdp")),
            P(("seq", "fsdp"), None),
            P("fsdp", "seq", None),
            P("fsdp", "seq", None),
        ),
        check_vma=False,
    )
```
